32 devices in a mesh: grp: 2 (over x), cell: 16 (over z, y, core).
Axes of the slice: x: 2, y: 2, z: 4, core: 2. Of those that a mesh axis runs over, the one named last changes fastest.
Arguments:
- windows: bfloat16 [3, 16, 1024, 256], P(None, 'cell', 'grp'), parts along dimension 2, may hold values from -6 to 6
- counts: int32 [32], P('grp'), parts along dimension 0, may hold values from 1 to 32, as said below
- pairs: int32 [2, 2, 16384], P(None, None, ('grp', 'cell')), parts along dimension 2, may hold values from 0 to 31, as said below
Outputs:
- lags: float32 [2, 16384, 256], P(None, ('grp', 'cell')), parts along dimension 1
The draws below stay inside these ranges and needn't reach their ends.
There are 2 independent parts, one for each index of `grp`. The reference program is written for one: setup_inputs(seed, part) draws one part's arguments, and reference() takes and returns one part's arrays. A program takes and returns all parts, laid end to end along the dimension named above; each array names one. Nothing has to cross between parts.
Inputs may be any that keep to these rules, and one draw needn't show every extreme that they name: `counts`: slots below a cell's count hold events, the rest are empty; some cell is full in every draw. `pairs`: slot numbers within a cell; every cell's list of every round names slot 0 and slot 31.
All inputs are finite; a program needn't handle non-finite values.
Results may differ from the reference program's by a relative error of at most 0.0052.
Values may be sent and summed in bfloat16 or wider, within the bound.
No kernel may reach another device: no remote copies, remote signals or barrier semaphores. Data moves between devices by JAX's collectives and lax.ppermute only.
A program may use at most 64 MiB of HBM per device.

```python
import math
import jax
import jax.numpy as jnp
from jax import lax

W = 256
EV_DEV = 32
PAIRS = 512
ROUNDS = 2
CELLS = 16
STATIONS = 16
EVENTS = 512
PAIRS_ALL = 8192
N_CELL = 16


def draw_counts(key, part):
    key = jax.random.fold_in(key, 11)
    base_key, heavy_key, force_key = jax.random.split(key, 3)
    light = jax.random.randint(base_key, (CELLS,), 1, EV_DEV // 4 + 2)
    heavy = jax.random.randint(heavy_key, (CELLS,), 0, 6) == 0
    forced = jnp.arange(CELLS, dtype=jnp.int32) == jax.random.randint(force_key, (), 0, CELLS)
    return jnp.where(heavy | forced, EV_DEV, light).astype(jnp.int32)


def draw_pairs(key, part):
    key = jax.random.fold_in(key, 23)
    slot_key, spot_key = jax.random.split(key)
    slots = jax.random.randint(slot_key, (ROUNDS, 2, PAIRS_ALL), 0, EV_DEV)
    spots = jax.random.randint(spot_key, (ROUNDS, 1, CELLS), 0, PAIRS)
    place = jnp.arange(PAIRS_ALL, dtype=jnp.int32) % PAIRS
    hit = place[None, None, :] == jnp.repeat(spots, PAIRS, axis=2)
    ends = jnp.array([0, EV_DEV - 1], dtype=jnp.int32)[None, :, None]
    return jnp.where(hit, ends, slots).astype(jnp.int32)


def block_scale(rng, shape, shards, least, top_value):
    def one(position, shards_of):
        steps = jax.random.uniform(jax.random.fold_in(jax.random.fold_in(rng, 6), position), (shards_of,), jnp.float32, least / len(shards), top_value / len(shards))
        return jnp.repeat(jnp.exp(steps), shape[position] // shards_of).reshape((-1,) + (1,) * (len(shape) - position - 1))

    loudness = one(*shards[0])
    for cut in shards[1:]:
        loudness = loudness * one(*cut)
    return loudness


def normal_values(rng, shape, spread, reach, cuts=(), held_as=jnp.bfloat16):
    values = spread * jax.random.normal(rng, shape, jnp.float32)
    if cuts:
        values = values * block_scale(rng, shape, cuts, -0.22, 0.18)
    return jnp.clip(values, -reach, reach).astype(held_as)


def setup_inputs(seed: int = 0, part: int = 0) -> dict:
    arg_keys = jax.random.split(jax.random.key(seed), 4)
    part_splits = jax.random.split(jax.random.fold_in(arg_keys[3], part), 4)
    windows = normal_values(part_splits[0], (3, STATIONS, EVENTS, W), 1.0, 6.0, ((1, 16),))
    counts = draw_counts(jax.random.fold_in(jax.random.fold_in(arg_keys[3], part), 71), part)
    pairs = draw_pairs(jax.random.fold_in(jax.random.fold_in(arg_keys[3], part), 71), part)
    return dict(windows=windows, counts=counts, pairs=pairs)


EPSILON = 1e-06

def phase_angles(samples, count):
    moments = jnp.arange(samples, dtype=jnp.int32)
    freq_bins = jnp.arange(count, dtype=jnp.int32)
    product = moments[:, None] * freq_bins[None, :] % samples
    return product.astype(jnp.float32) * (2.0 * math.pi / samples)

def forward_matrix(samples):
    angles = phase_angles(samples, samples // 2)
    return jnp.concatenate([jnp.cos(angles), -jnp.sin(angles)], axis=1).astype(jnp.bfloat16)

def inverse_matrices(samples):
    angles = phase_angles(samples, samples // 2).T
    weights = jnp.where(jnp.arange(samples // 2) == 0, 1.0, 2.0).astype(jnp.float32) / samples
    return (weights[:, None] * jnp.cos(angles), -weights[:, None] * jnp.sin(angles))

def spectra_of(block, forward):
    flat_block = block.reshape(-1, block.shape[-1])
    energy = lax.optimization_barrier(jnp.sum(jnp.square(flat_block.astype(jnp.float32)), axis=1, keepdims=True))
    raw_spectra = jnp.dot(flat_block, forward, preferred_element_type=jnp.float32)
    return (raw_spectra / jnp.sqrt(energy + EPSILON)).astype(jnp.bfloat16).reshape(block.shape)

def contract(left, right):
    return jnp.einsum('sik,sjk->kij', left.astype(jnp.float32), right.astype(jnp.float32), precision=lax.Precision.HIGHEST)

def cross_spectra(own_spectra, far_spectra):
    half_bins = own_spectra.shape[-1] // 2
    own_real, own_imag = (own_spectra[..., :half_bins], own_spectra[..., half_bins:])
    far_real, far_imag = (far_spectra[..., :half_bins], far_spectra[..., half_bins:])
    cross_real = contract(own_real, far_real) + contract(own_imag, far_imag)
    cross_imag = contract(own_real, far_imag) - contract(own_imag, far_real)
    return (cross_real, cross_imag)

def lag_block(cross_real, cross_imag, first_slot, second_slot, own_count, far_count, cos_part, sin_part, stack_scale):
    events = cross_real.shape[1]
    flat_index = first_slot * events + second_slot
    picked_real = jnp.take(cross_real.reshape(cross_real.shape[0], -1), flat_index, axis=1)
    picked_imag = jnp.take(cross_imag.reshape(cross_imag.shape[0], -1), flat_index, axis=1)
    lag_values = jnp.einsum('kp,kt->pt', picked_real, cos_part, precision=lax.Precision.HIGHEST)
    lag_values = lag_values + jnp.einsum('kp,kt->pt', picked_imag, sin_part, precision=lax.Precision.HIGHEST)
    live_pair = (first_slot < own_count) & (second_slot < far_count)
    return jnp.where(live_pair[:, None], lag_values * stack_scale, 0.0)

def round_bit(step_round, levels, rounds):
    return step_round * (levels - 1) // max(rounds - 1, 1)

def reference(windows, counts, pairs):
    samples = windows.shape[-1]
    forward = forward_matrix(samples)
    cos_part, sin_part = inverse_matrices(samples)
    stack_scale = math.sqrt(samples / (3.0 * STATIONS))

    def cell_spectra(cell):
        block = lax.dynamic_slice_in_dim(windows, cell * EV_DEV, EV_DEV, 2)
        return spectra_of(block, forward).reshape(3 * STATIONS, EV_DEV, samples)
    cell_ids = jnp.arange(CELLS, dtype=jnp.int32)
    all_spectra = lax.map(cell_spectra, cell_ids)
    levels = N_CELL.bit_length() - 1
    results = []
    for step_round in range(ROUNDS):
        partner_mask = 1 << round_bit(step_round, levels, ROUNDS)

        def cell_lags(cell):
            partner = jnp.bitwise_xor(cell, partner_mask)
            cross_real, cross_imag = cross_spectra(all_spectra[cell], all_spectra[partner])
            first_slot = lax.dynamic_slice_in_dim(pairs[step_round, 0], cell * PAIRS, PAIRS)
            second_slot = lax.dynamic_slice_in_dim(pairs[step_round, 1], cell * PAIRS, PAIRS)
            return lag_block(cross_real, cross_imag, first_slot, second_slot, counts[cell], counts[partner], cos_part, sin_part, stack_scale)
        results.append(lax.map(cell_lags, cell_ids).reshape(CELLS * PAIRS, samples))
    return jnp.stack(results)
```

```python
import math

import jax
import jax.numpy as jnp
import numpy as np
from jax import lax
from jax.experimental import pallas as pl
from jax.experimental.pallas import tpu as pltpu
from jax.sharding import PartitionSpec as P

EPSILON = 1e-06
SLOTS = 32
NT = (((1,), (1,)), ((), ()))
TN = (((0,), (0,)), ((), ()))
VMEM_LIMIT = 40 * 1024 * 1024


def tables(samples, stations):
    bins = samples // 2
    quarter = bins // 4
    turn = np.arange(bins)[:, None] * np.arange(samples)[None, :] % samples
    angle = turn * (2.0 * math.pi / samples)
    weight = np.where(np.arange(bins) == 0, 1.0, 2.0)[:, None] / samples
    weight = weight * math.sqrt(samples / (3.0 * stations))

    def by_quarter(real, imag):
        rows = [real.reshape(4, quarter, samples), imag.reshape(4, quarter, samples)]
        return np.concatenate(rows, axis=1).reshape(4 * 2 * quarter, samples)

    forward = by_quarter(np.cos(angle), -np.sin(angle)).astype(np.float32)
    inverse = by_quarter(weight * np.cos(angle), -weight * np.sin(angle)).astype(np.float32)
    return forward.astype(jnp.bfloat16), inverse


def spectra_kernel(place_ref, windows_ref, forward_ref, *piece_refs):
    groups = windows_ref.shape[2]
    rows = forward_ref.shape[0] // 4
    quarter, group = place_ref[0], place_ref[1]
    table = jnp.concatenate(
        [forward_ref[pl.ds(pl.multiple_of((quarter ^ m) * rows, rows), rows), :] for m in range(4)]
    )
    ones = jnp.ones((16, table.shape[1]), jnp.bfloat16)
    for mg in range(groups):
        parts = []
        for comp in range(windows_ref.shape[0]):
            low = windows_ref[comp, 0, group ^ mg]
            high = windows_ref[comp, 1, group ^ mg]
            parts += [low[:SLOTS], high[SLOTS:], low[SLOTS:], high[:SLOTS]]
        traces = jnp.concatenate(parts)
        square = jnp.square(traces.astype(jnp.float32))
        square_hi = square.astype(jnp.bfloat16)
        square_lo = (square - square_hi.astype(jnp.float32)).astype(jnp.bfloat16)
        energy = lax.dot_general(ones, square_hi, NT, preferred_element_type=jnp.float32)
        energy += lax.dot_general(ones, square_lo, NT, preferred_element_type=jnp.float32)
        scale = lax.rsqrt(energy[:1] + EPSILON)
        raw = lax.dot_general(table, traces, NT, preferred_element_type=jnp.float32)
        spectra = (raw * scale).astype(jnp.bfloat16)
        lanes = 4 * SLOTS
        for mq in range(4):
            piece = piece_refs[(mq // 2) * 2 * groups + mg * 2 + mq % 2]
            for comp in range(windows_ref.shape[0]):
                piece[comp] = spectra[mq * rows : (mq + 1) * rows, comp * lanes : (comp + 1) * lanes]


def pick_kernel(place_ref, *refs):
    index_refs, refs = refs[:4], refs[4:]
    piece_refs, refs = refs[:-7], refs[-7:]
    picked_refs, (trace_ref, cross_ref, flat_ref) = refs[:4], refs[4:]
    quarter = place_ref[0]
    comps, rows, lanes = piece_refs[0].shape
    bins = rows // 2
    traces = comps * len(piece_refs)
    for s, piece in enumerate(piece_refs):
        for comp in range(comps):
            start = (s * comps + comp) * rows
            trace_ref[start : start + rows] = piece[comp].astype(jnp.float32)
    half = 2 * SLOTS
    for k in range(bins):
        real = trace_ref[pl.ds(k, traces, stride=rows), :].astype(jnp.bfloat16)
        imag = trace_ref[pl.ds(bins + k, traces, stride=rows), :].astype(jnp.bfloat16)
        left = jnp.concatenate([real, imag], axis=0)
        right = jnp.concatenate(
            [jnp.concatenate([real, imag], axis=1), jnp.concatenate([imag, -real], axis=1)], axis=0
        )
        cross = lax.dot_general(left, right, TN, preferred_element_type=jnp.float32)
        cross_ref[k * half : (k + 1) * half] = cross[:half, :lanes]
        cross_ref[(bins + k) * half : (bins + k + 1) * half] = cross[:half, lanes:]
    for i in range(half):
        turned = cross_ref[pl.ds(i, rows, stride=half), :].T.astype(jnp.bfloat16)
        own, slot = i // SLOTS, i % SLOTS
        for far in range(2):
            start = half + far * SLOTS
            flat_ref[own, far, slot * SLOTS : (slot + 1) * SLOTS] = turned[start : start + SLOTS]
    pairs = index_refs[0].shape[1]
    columns = jnp.concatenate([ref[...] for ref in index_refs], axis=0).T
    lane = lax.broadcasted_iota(jnp.int32, (pairs, lanes), 1)
    for mq in range(4):
        cell = quarter ^ mq
        high, low = cell // 2, cell % 2
        sides = ((high, high), (low, 1 - low))
        found = []
        for step_round in range(2):
            at = mq * 2 + step_round
            offset = columns[:, at : at + 1] - lane
            hot = jnp.concatenate(
                [
                    jnp.where(offset == lanes * t, 1.0, 0.0).astype(jnp.bfloat16)
                    for t in range(SLOTS * SLOTS // lanes)
                ],
                axis=1,
            )
            block = flat_ref[sides[step_round][0], sides[step_round][1]]
            found.append(jnp.dot(hot, block, preferred_element_type=jnp.float32))
        picked_refs[mq][...] = jnp.concatenate(found, axis=1).astype(jnp.bfloat16)


def lag_kernel(place_ref, inverse_ref, *refs):
    picked_refs, lags_ref = refs[:4], refs[4]
    quarter = place_ref[0]
    rows = inverse_ref.shape[0] // 4
    sign = jnp.where(quarter // 2 == quarter % 2, 1.0, -1.0)
    row = lax.broadcasted_iota(jnp.int32, (rows, inverse_ref.shape[1]), 0)
    factor = jnp.where(row < rows // 2, 1.0, sign)
    table = jnp.concatenate(
        [
            inverse_ref[pl.ds(pl.multiple_of((quarter ^ m) * rows, rows), rows), :] * factor
            for m in range(4)
        ]
    )
    table_hi = table.astype(jnp.bfloat16)
    table_lo = (table - table_hi.astype(jnp.float32)).astype(jnp.bfloat16)
    picked = [ref[...] for ref in picked_refs]
    for step_round in range(2):
        cross = jnp.concatenate([p[:, step_round * rows : (step_round + 1) * rows] for p in picked], axis=1)
        lags_ref[step_round] = jnp.dot(
            cross, table_hi, preferred_element_type=jnp.float32
        ) + jnp.dot(cross, table_lo, preferred_element_type=jnp.float32)


def on_device(windows, counts, pairs):
    comps, _, events, samples = windows.shape
    cells = lax.axis_size("cell")
    half, groups = cells // 2, cells // 4
    count = pairs.shape[2]
    rows = samples // 4
    lanes = 4 * SLOTS
    forward, inverse = tables(samples, cells)
    position = lax.axis_index("cell")
    high, low = position // half, position % 2
    place = jnp.stack([high * 2 + low, (position % half) // 2]).astype(jnp.int32)

    def swap(x, mask):
        return lax.ppermute(x, "cell", [(i, i ^ mask) for i in range(cells)])

    vmem = pl.BlockSpec(memory_space=pltpu.VMEM)
    smem = pl.BlockSpec(memory_space=pltpu.SMEM)
    params = pltpu.CompilerParams(vmem_limit_bytes=VMEM_LIMIT)

    first, second = pairs[:, 0], pairs[:, 1]
    far_counts = jnp.stack([counts[position ^ 1], counts[position ^ half]])
    live = (first < counts[position]) & (second < far_counts[:, None])
    flat = jnp.where(high == low, first * SLOTS + second, second * SLOTS + first)
    index = jnp.where(live, flat, -1)
    masks = [(m // 2) * half + m % 2 for m in range(4)]
    indices = [index] + [swap(index, m) for m in masks[1:]]

    pieces = pl.pallas_call(
        spectra_kernel,
        out_shape=[jax.ShapeDtypeStruct((comps, rows, lanes), jnp.bfloat16)] * cells,
        in_specs=[smem, vmem, vmem],
        out_specs=[vmem] * cells,
        compiler_params=params,
        name="spectra",
    )(place, windows.reshape(comps, 2, groups, 2 * SLOTS, samples), jnp.asarray(forward))
    pieces = [pieces[0]] + [swap(pieces[m], m) for m in range(1, cells)]

    picked = pl.pallas_call(
        pick_kernel,
        out_shape=[jax.ShapeDtypeStruct((count, 2 * rows), jnp.bfloat16)] * 4,
        in_specs=[smem] + [vmem] * (4 + cells),
        out_specs=[vmem] * 4,
        scratch_shapes=[
            pltpu.VMEM((comps * cells * rows, lanes), jnp.float32),
            pltpu.VMEM((rows * 2 * SLOTS, lanes), jnp.float32),
            pltpu.VMEM((2, 2, SLOTS * SLOTS, rows), jnp.bfloat16),
        ],
        compiler_params=params,
        name="picks",
    )(place, *indices, *pieces)
    picked = [picked[0]] + [swap(p, m) for p, m in zip(picked[1:], masks[1:])]

    return pl.pallas_call(
        lag_kernel,
        out_shape=jax.ShapeDtypeStruct((2, count, samples), jnp.float32),
        in_specs=[smem] + [vmem] * 5,
        out_specs=vmem,
        compiler_params=params,
        name="lags",
    )(place, jnp.asarray(inverse), *picked)


def solution(mesh):
    in_specs = (P(None, "cell", "grp", None), P("grp"), P(None, None, ("grp", "cell")))
    out_specs = P(None, ("grp", "cell"), None)
    return jax.shard_map(
        on_device, mesh=mesh, in_specs=in_specs, out_specs=out_specs, check_vma=False
    )
```

```python
import functools
import math

import jax
import jax.numpy as jnp
import numpy as np
from jax import lax
from jax.experimental import pallas as pl
from jax.experimental.pallas import tpu as pltpu
from jax.sharding import PartitionSpec as P

EPSILON = 1e-06
SLOTS = 32
NT = (((1,), (1,)), ((), ()))
TN = (((0,), (0,)), ((), ()))
VMEM_LIMIT = 40 * 1024 * 1024


def tables(samples, stations):
    bins = samples // 2
    quarter = bins // 4
    turn = np.arange(bins)[:, None] * np.arange(samples)[None, :] % samples
    angle = turn * (2.0 * math.pi / samples)
    weight = np.where(np.arange(bins) == 0, 1.0, 2.0)[:, None] / samples
    weight = weight * math.sqrt(samples / (3.0 * stations))

    def by_quarter(real, imag):
        rows = [real.reshape(4, quarter, samples), imag.reshape(4, quarter, samples)]
        return np.concatenate(rows, axis=1).reshape(4 * 2 * quarter, samples)

    forward = by_quarter(np.cos(angle), -np.sin(angle)).astype(np.float32)
    inverse = by_quarter(weight * np.cos(angle), -weight * np.sin(angle)).astype(np.float32)
    return forward.astype(jnp.bfloat16), inverse


def place_of(place_ref, groups):
    position = place_ref[0]
    high, inner = position // (2 * groups), position % (2 * groups)
    return high * 2 + inner % 2, inner // 2


def spectra_kernel(place_ref, windows_ref, pairs_ref, forward_ref, *piece_refs):
    comps, _, groups, _, samples = windows_ref.shape
    rows = forward_ref.shape[0] // 4
    lanes = 4 * SLOTS
    quarter, group = place_of(place_ref, groups)
    table = jnp.concatenate(
        [forward_ref[pl.ds(pl.multiple_of((quarter ^ m) * rows, rows), rows), :] for m in range(4)]
    )
    ones = jnp.ones((16, samples), jnp.bfloat16)
    listed = jnp.concatenate([pairs_ref[0], pairs_ref[1]]).astype(jnp.float32)
    listed = jnp.concatenate(
        [listed[:, at : at + lanes] for at in range(0, listed.shape[1], lanes)]
    ).astype(jnp.bfloat16)
    for mg in range(groups):
        parts = []
        for comp in range(comps):
            low = windows_ref[comp, 0, group ^ mg]
            high = windows_ref[comp, 1, group ^ mg]
            parts += [low[:SLOTS], high[SLOTS:], low[SLOTS:], high[:SLOTS]]
        traces = jnp.concatenate(parts)
        square = jnp.square(traces.astype(jnp.float32))
        square_hi = square.astype(jnp.bfloat16)
        square_lo = (square - square_hi.astype(jnp.float32)).astype(jnp.bfloat16)
        energy = lax.dot_general(ones, square_hi, NT, preferred_element_type=jnp.float32)
        energy += lax.dot_general(ones, square_lo, NT, preferred_element_type=jnp.float32)
        scale = lax.rsqrt(energy[:1] + EPSILON)
        raw = lax.dot_general(table, traces, NT, preferred_element_type=jnp.float32)
        spectra = (raw * scale).astype(jnp.bfloat16)
        for mq in range(4):
            piece = piece_refs[(mq // 2) * 2 * groups + mg * 2 + mq % 2]
            for comp in range(comps):
                piece[comp * rows : (comp + 1) * rows] = spectra[
                    mq * rows : (mq + 1) * rows, comp * lanes : (comp + 1) * lanes
                ]
            if mg == 0:
                piece[comps * rows :] = listed


def pick(place_ref, counts_ref, listed, flat_ref, mq, *picked_refs):
    cells = counts_ref.shape[0]
    quarter, group = place_of(place_ref, cells // 4)
    own = quarter ^ mq
    high, low = own // 2, own % 2
    cell = high * (cells // 2) + group * 2 + low
    lanes = listed.shape[1]
    turned = listed.astype(jnp.float32).T
    lane = lax.broadcasted_iota(jnp.int32, (lanes, lanes), 1)
    sides = ((high, high), (low, 1 - low))
    found = []
    for step_round in range(2):
        own_count = counts_ref[cell].astype(jnp.float32)
        far_count = counts_ref[cell ^ (cells // 2 if step_round else 1)].astype(jnp.float32)
        hot = []
        for chunk in range(listed.shape[0] // 4):
            at = chunk * 4 + step_round * 2
            first, second = turned[:, at : at + 1], turned[:, at + 1 : at + 2]
            live = (first < own_count) & (second < far_count)
            place = jnp.where(high == low, first * SLOTS + second, second * SLOTS + first)
            offset = jnp.where(live, place, -1.0).astype(jnp.int32) - lane
            hot.append(
                jnp.concatenate(
                    [
                        jnp.where(offset == lanes * t, 1.0, 0.0).astype(jnp.bfloat16)
                        for t in range(SLOTS * SLOTS // lanes)
                    ],
                    axis=1,
                )
            )
        block = flat_ref[sides[step_round][0], sides[step_round][1]]
        found.append(jnp.dot(jnp.concatenate(hot), block, preferred_element_type=jnp.float32))
    found = jnp.concatenate(found, axis=1).astype(jnp.bfloat16)
    each = found.shape[0] // len(picked_refs)
    for at, ref in enumerate(picked_refs):
        ref[...] = found[at * each : (at + 1) * each]


def cross_kernel(place_ref, counts_ref, *refs):
    piece_refs, (flat_ref, picked_0, picked_1, trace_ref, cross_ref) = refs[:-5], refs[-5:]
    rows = flat_ref.shape[3]
    bins = rows // 2
    lanes = piece_refs[0].shape[1]
    each = piece_refs[-1].shape[0]
    traces = len(piece_refs) * each // rows
    for s, piece in enumerate(piece_refs):
        trace_ref[s * each : (s + 1) * each] = piece[:each].astype(jnp.float32)
    half = 2 * SLOTS
    for k in range(bins):
        real = trace_ref[pl.ds(k, traces, stride=rows), :].astype(jnp.bfloat16)
        imag = trace_ref[pl.ds(bins + k, traces, stride=rows), :].astype(jnp.bfloat16)
        left = jnp.concatenate([real, imag], axis=0)
        right = jnp.concatenate(
            [jnp.concatenate([real, imag], axis=1), jnp.concatenate([imag, -real], axis=1)], axis=0
        )
        cross = lax.dot_general(left, right, TN, preferred_element_type=jnp.float32)
        cross_ref[k * half : (k + 1) * half] = cross[:half, :lanes]
        cross_ref[(bins + k) * half : (bins + k + 1) * half] = cross[:half, lanes:]
    for i in range(half):
        turned = cross_ref[pl.ds(i, rows, stride=half), :].T.astype(jnp.bfloat16)
        own, slot = i // SLOTS, i % SLOTS
        for far in range(2):
            start = half + far * SLOTS
            flat_ref[own, far, slot * SLOTS : (slot + 1) * SLOTS] = turned[start : start + SLOTS]
    pick(place_ref, counts_ref, piece_refs[2][each:], flat_ref, 2, picked_0)
    pick(place_ref, counts_ref, piece_refs[3][each:], flat_ref, 3, picked_1)


def near_kernel(place_ref, counts_ref, listed_0, listed_1, flat_ref, picked_0, *picked_1):
    listing = picked_0.shape[0] * 4 // listed_0.shape[1]
    pick(place_ref, counts_ref, listed_1[listed_1.shape[0] - listing :], flat_ref, 1, *picked_1)
    pick(place_ref, counts_ref, listed_0[listed_0.shape[0] - listing :], flat_ref, 0, picked_0)


def lag_kernel(groups, place_ref, inverse_ref, *refs):
    picked_refs, lags_ref = refs[:-1], refs[-1]
    quarter, _ = place_of(place_ref, groups)
    rows = inverse_ref.shape[0] // 4
    sign = jnp.where(quarter // 2 == quarter % 2, 1.0, -1.0)
    row = lax.broadcasted_iota(jnp.int32, (rows, inverse_ref.shape[1]), 0)
    factor = jnp.where(row < rows // 2, 1.0, sign)
    table = jnp.concatenate(
        [
            inverse_ref[pl.ds(pl.multiple_of((quarter ^ m) * rows, rows), rows), :] * factor
            for m in (0, 2, 3, 1)
        ]
    )
    table_hi = table.astype(jnp.bfloat16)
    table_lo = (table - table_hi.astype(jnp.float32)).astype(jnp.bfloat16)
    picked = [ref[...] for ref in picked_refs]
    picked[3:] = [jnp.concatenate(picked[3:])]
    for step_round in range(2):
        cross = jnp.concatenate([p[:, step_round * rows : (step_round + 1) * rows] for p in picked], axis=1)
        lags_ref[step_round] = jnp.dot(
            cross, table_hi, preferred_element_type=jnp.float32
        ) + jnp.dot(cross, table_lo, preferred_element_type=jnp.float32)


def on_device(windows, counts, pairs):
    comps, _, events, samples = windows.shape
    cells = lax.axis_size("cell")
    half, groups = cells // 2, cells // 4
    count = pairs.shape[2]
    rows = samples // 4
    lanes = 4 * SLOTS
    forward, inverse = tables(samples, cells)
    place = lax.axis_index("cell").astype(jnp.int32).reshape(1)

    def swap(x, mask):
        return lax.ppermute(x, "cell", [(i, i ^ mask) for i in range(cells)])

    vmem = pl.BlockSpec(memory_space=pltpu.VMEM)
    smem = pl.BlockSpec(memory_space=pltpu.SMEM)
    params = pltpu.CompilerParams(vmem_limit_bytes=VMEM_LIMIT)

    near = [0, 1, half, half + 1]
    listing = pairs.size // lanes
    pieces = pl.pallas_call(
        spectra_kernel,
        out_shape=[
            jax.ShapeDtypeStruct((comps * rows + listing * (m in near), lanes), jnp.bfloat16)
            for m in range(cells)
        ],
        in_specs=[smem, vmem, vmem, vmem],
        out_specs=[vmem] * cells,
        compiler_params=params,
        name="spectra",
    )(place, windows.reshape(comps, 2, groups, 2 * SLOTS, samples), pairs, jnp.asarray(forward))
    order = [half, 1]
    for m in range(1, half):
        order += [half + m] + [m + 1] * (m + 1 < half)
    arrived = {m: swap(pieces[m], m) for m in order}
    arrived[0] = pieces[0]
    pieces = [arrived[m] for m in near + [m for m in order if m not in near]]

    picked_shape = jax.ShapeDtypeStruct((count, 2 * rows), jnp.bfloat16)
    flat, picked_2, picked_3 = pl.pallas_call(
        cross_kernel,
        out_shape=[
            jax.ShapeDtypeStruct((2, 2, SLOTS * SLOTS, rows), jnp.bfloat16),
            picked_shape,
            picked_shape,
        ],
        in_specs=[smem, smem] + [vmem] * cells,
        out_specs=[vmem] * 3,
        scratch_shapes=[
            pltpu.VMEM((comps * cells * rows, lanes), jnp.float32),
            pltpu.VMEM((rows * 2 * SLOTS, lanes), jnp.float32),
        ],
        compiler_params=params,
        name="cross",
    )(place, counts, *pieces)
    picked_2, picked_3 = swap(picked_2, near[2]), swap(picked_3, near[3])
    picked_0, *picked_1 = pl.pallas_call(
        near_kernel,
        out_shape=[picked_shape] + [jax.ShapeDtypeStruct((count // 2, 2 * rows), jnp.bfloat16)] * 2,
        in_specs=[smem, smem] + [vmem] * 3,
        out_specs=[vmem] * 3,
        compiler_params=params,
        cost_estimate=pl.CostEstimate(
            flops=128 * count * SLOTS * SLOTS * rows, bytes_accessed=2**21, transcendentals=0
        ),
        name="near",
    )(place, counts, pieces[0], pieces[1], flat)
    picked_1 = [swap(p, near[1]) for p in picked_1]

    return pl.pallas_call(
        functools.partial(lag_kernel, groups),
        out_shape=jax.ShapeDtypeStruct((2, count, samples), jnp.float32),
        in_specs=[smem] + [vmem] * 6,
        out_specs=vmem,
        compiler_params=params,
        name="lags",
    )(place, jnp.asarray(inverse), picked_0, picked_2, picked_3, *picked_1)


def solution(mesh):
    in_specs = (P(None, "cell", "grp", None), P("grp"), P(None, None, ("grp", "cell")))
    out_specs = P(None, ("grp", "cell"), None)
    return jax.shard_map(
        on_device, mesh=mesh, in_specs=in_specs, out_specs=out_specs, check_vma=False
    )
```

```python
import functools
import math

import jax
import jax.numpy as jnp
import numpy as np
from jax import lax
from jax.experimental import pallas as pl
from jax.experimental.pallas import tpu as pltpu
from jax.sharding import PartitionSpec as P

EPSILON = 1e-06
SLOTS = 32
NT = (((1,), (1,)), ((), ()))
TN = (((0,), (0,)), ((), ()))
VMEM_LIMIT = 40 * 1024 * 1024


def tables(samples, stations):
    bins = samples // 2
    quarter = bins // 4
    turn = np.arange(bins)[:, None] * np.arange(samples)[None, :] % samples
    angle = turn * (2.0 * math.pi / samples)
    weight = np.where(np.arange(bins) == 0, 1.0, 2.0)[:, None] / samples
    weight = weight * math.sqrt(samples / (3.0 * stations))

    def by_quarter(real, imag):
        rows = [real.reshape(4, quarter, samples), imag.reshape(4, quarter, samples)]
        return np.concatenate(rows, axis=1).reshape(4 * 2 * quarter, samples)

    forward = by_quarter(np.cos(angle), -np.sin(angle)).astype(np.float32)
    inverse = by_quarter(weight * np.cos(angle), -weight * np.sin(angle)).astype(np.float32)
    return forward.astype(jnp.bfloat16), inverse


def place_of(place_ref, groups):
    position = place_ref[0]
    high, inner = position // (2 * groups), position % (2 * groups)
    return high * 2 + inner % 2, inner // 2


def listing_of(pairs_ref, lanes):
    listed = jnp.concatenate([pairs_ref[0], pairs_ref[1]]).astype(jnp.float32)
    return jnp.concatenate([listed[:, at : at + lanes] for at in range(0, listed.shape[1], lanes)])


def spectra_kernel(place_ref, own_ref, near_ref, own_pairs_ref, near_pairs_ref, forward_ref, *piece_refs):
    comps, _, groups, _, samples = own_ref.shape
    rows = forward_ref.shape[0] // 4
    lanes = 4 * SLOTS
    quarter, group = place_of(place_ref, groups)
    table = jnp.concatenate(
        [forward_ref[pl.ds(pl.multiple_of((quarter ^ m) * rows, rows), rows), :] for m in (0, 2)]
    )
    ones = jnp.ones((16, samples), jnp.bfloat16)
    piece_refs[groups][2 * comps * rows :] = jnp.concatenate(
        [listing_of(own_pairs_ref, lanes), listing_of(near_pairs_ref, lanes)]
    ).astype(jnp.bfloat16)
    for mg in range(groups):
        for station, windows_ref in enumerate((own_ref, near_ref)):
            parts = []
            for comp in range(comps):
                low = windows_ref[comp, 0, group ^ mg]
                high = windows_ref[comp, 1, group ^ mg]
                parts += [low[:SLOTS], high[SLOTS:], low[SLOTS:], high[:SLOTS]]
            traces = jnp.concatenate(parts)
            square = jnp.square(traces.astype(jnp.float32))
            square_hi = square.astype(jnp.bfloat16)
            square_lo = (square - square_hi.astype(jnp.float32)).astype(jnp.bfloat16)
            energy = lax.dot_general(ones, square_hi, NT, preferred_element_type=jnp.float32)
            energy += lax.dot_general(ones, square_lo, NT, preferred_element_type=jnp.float32)
            scale = lax.rsqrt(energy[:1] + EPSILON)
            raw = lax.dot_general(table, traces, NT, preferred_element_type=jnp.float32)
            spectra = (raw * scale).astype(jnp.bfloat16)
            for far in range(2):
                piece = piece_refs[far * groups + mg]
                for comp in range(comps):
                    start = (station * comps + comp) * rows
                    piece[start : start + rows] = spectra[
                        far * rows : (far + 1) * rows, comp * lanes : (comp + 1) * lanes
                    ]


def pick(place_ref, counts_ref, listed, flat_ref, mq, *picked_refs):
    cells = counts_ref.shape[0]
    quarter, group = place_of(place_ref, cells // 4)
    own = quarter ^ mq
    high, low = own // 2, own % 2
    cell = high * (cells // 2) + group * 2 + low
    lanes = listed.shape[1]
    turned = listed.T
    lane = lax.broadcasted_iota(jnp.int32, (lanes, lanes), 1)
    sides = ((high, high), (low, 1 - low))
    found = []
    for step_round in range(2):
        own_count = counts_ref[cell].astype(jnp.float32)
        far_count = counts_ref[cell ^ (cells // 2 if step_round else 1)].astype(jnp.float32)
        hot = []
        for chunk in range(listed.shape[0] // 4):
            at = chunk * 4 + step_round * 2
            first, second = turned[:, at : at + 1], turned[:, at + 1 : at + 2]
            live = (first < own_count) & (second < far_count)
            place = jnp.where(high == low, first * SLOTS + second, second * SLOTS + first)
            offset = jnp.where(live, place, -1.0).astype(jnp.int32) - lane
            hot.append(
                jnp.concatenate(
                    [
                        jnp.where(offset == lanes * t, 1.0, 0.0).astype(jnp.bfloat16)
                        for t in range(SLOTS * SLOTS // lanes)
                    ],
                    axis=1,
                )
            )
        block = flat_ref[sides[step_round][0], sides[step_round][1]]
        found.append(jnp.dot(jnp.concatenate(hot), block, preferred_element_type=jnp.float32))
    found = jnp.concatenate(found, axis=1).astype(jnp.bfloat16)
    each = found.shape[0] // len(picked_refs)
    for at, ref in enumerate(picked_refs):
        ref[...] = found[at * each : (at + 1) * each]


def cross_kernel(place_ref, counts_ref, *refs):
    piece_refs, (flat_ref, picked_0, picked_1, trace_ref, cross_ref) = refs[:-5], refs[-5:]
    rows = flat_ref.shape[3]
    bins = rows // 2
    each, lanes = piece_refs[0].shape
    traces = len(piece_refs) * each // rows
    for s, piece in enumerate(piece_refs):
        trace_ref[s * each : (s + 1) * each] = piece[:each].astype(jnp.float32)
    half = 2 * SLOTS
    for k in range(bins):
        real = trace_ref[pl.ds(k, traces, stride=rows), :].astype(jnp.bfloat16)
        imag = trace_ref[pl.ds(bins + k, traces, stride=rows), :].astype(jnp.bfloat16)
        left = jnp.concatenate([real, imag], axis=0)
        right = jnp.concatenate(
            [jnp.concatenate([real, imag], axis=1), jnp.concatenate([imag, -real], axis=1)], axis=0
        )
        cross = lax.dot_general(left, right, TN, preferred_element_type=jnp.float32)
        cross_ref[k * half : (k + 1) * half] = cross[:half, :lanes]
        cross_ref[(bins + k) * half : (bins + k + 1) * half] = cross[:half, lanes:]
    for i in range(half):
        turned = cross_ref[pl.ds(i, rows, stride=half), :].T.astype(jnp.bfloat16)
        own, slot = i // SLOTS, i % SLOTS
        for far in range(2):
            start = half + far * SLOTS
            flat_ref[own, far, slot * SLOTS : (slot + 1) * SLOTS] = turned[start : start + SLOTS]
    listed = piece_refs[1][each:].astype(jnp.float32)
    listing = listed.shape[0] // 2
    pick(place_ref, counts_ref, listed[:listing], flat_ref, 2, picked_0)
    pick(place_ref, counts_ref, listed[listing:], flat_ref, 3, picked_1)


def near_kernel(place_ref, counts_ref, own_pairs_ref, near_pairs_ref, flat_ref, picked_0, *picked_1):
    lanes = 4 * SLOTS
    pick(place_ref, counts_ref, listing_of(near_pairs_ref, lanes), flat_ref, 1, *picked_1)
    pick(place_ref, counts_ref, listing_of(own_pairs_ref, lanes), flat_ref, 0, picked_0)


def lag_kernel(groups, place_ref, inverse_ref, *refs):
    picked_refs, lags_ref = refs[:-1], refs[-1]
    quarter, _ = place_of(place_ref, groups)
    rows = inverse_ref.shape[0] // 4
    sign = jnp.where(quarter // 2 == quarter % 2, 1.0, -1.0)
    row = lax.broadcasted_iota(jnp.int32, (rows, inverse_ref.shape[1]), 0)
    factor = jnp.where(row < rows // 2, 1.0, sign)
    table = jnp.concatenate(
        [
            inverse_ref[pl.ds(pl.multiple_of((quarter ^ m) * rows, rows), rows), :] * factor
            for m in (0, 2, 3, 1)
        ]
    )
    table_hi = table.astype(jnp.bfloat16)
    table_lo = (table - table_hi.astype(jnp.float32)).astype(jnp.bfloat16)
    picked = [ref[...] for ref in picked_refs]
    picked[3:] = [jnp.concatenate(picked[3:])]
    for step_round in range(2):
        cross = jnp.concatenate([p[:, step_round * rows : (step_round + 1) * rows] for p in picked], axis=1)
        lags_ref[step_round] = jnp.dot(
            cross, table_hi, preferred_element_type=jnp.float32
        ) + jnp.dot(cross, table_lo, preferred_element_type=jnp.float32)


def on_device(windows, counts, pairs):
    comps, _, events, samples = windows.shape
    cells = lax.axis_size("cell")
    half, groups = cells // 2, cells // 4
    count = pairs.shape[2]
    rows = samples // 4
    lanes = 4 * SLOTS
    forward, inverse = tables(samples, cells)
    place = lax.axis_index("cell").astype(jnp.int32).reshape(1)

    def swap(x, mask):
        return lax.ppermute(x, "cell", [(i, i ^ mask) for i in range(cells)])

    vmem = pl.BlockSpec(memory_space=pltpu.VMEM)
    smem = pl.BlockSpec(memory_space=pltpu.SMEM)
    params = pltpu.CompilerParams(vmem_limit_bytes=VMEM_LIMIT)

    windows = windows.reshape(comps, 2, groups, 2 * SLOTS, samples)
    near_windows, near_pairs = swap(windows, 1), swap(pairs, 1)
    listing = 2 * pairs.size // lanes
    pieces = pl.pallas_call(
        spectra_kernel,
        out_shape=[
            jax.ShapeDtypeStruct((2 * comps * rows + listing * (m == groups), lanes), jnp.bfloat16)
            for m in range(2 * groups)
        ],
        in_specs=[smem] + [vmem] * 5,
        out_specs=[vmem] * (2 * groups),
        compiler_params=params,
        name="spectra",
    )(place, windows, near_windows, pairs, near_pairs, jnp.asarray(forward))
    order = [m for pair in zip(range(groups, 2 * groups), range(groups)) for m in pair if m]
    arrived = {m: swap(pieces[m], 2 * m) for m in order}
    pieces = [pieces[0]] + [arrived[m] for m in order]

    picked_shape = jax.ShapeDtypeStruct((count, 2 * rows), jnp.bfloat16)
    flat, picked_2, picked_3 = pl.pallas_call(
        cross_kernel,
        out_shape=[
            jax.ShapeDtypeStruct((2, 2, SLOTS * SLOTS, rows), jnp.bfloat16),
            picked_shape,
            picked_shape,
        ],
        in_specs=[smem, smem] + [vmem] * (2 * groups),
        out_specs=[vmem] * 3,
        scratch_shapes=[
            pltpu.VMEM((comps * cells * rows, lanes), jnp.float32),
            pltpu.VMEM((rows * 2 * SLOTS, lanes), jnp.float32),
        ],
        compiler_params=params,
        name="cross",
    )(place, counts, *pieces)
    picked_2, picked_3 = swap(picked_2, half), swap(picked_3, half + 1)
    picked_0, *picked_1 = pl.pallas_call(
        near_kernel,
        out_shape=[picked_shape] + [jax.ShapeDtypeStruct((count // 2, 2 * rows), jnp.bfloat16)] * 2,
        in_specs=[smem, smem] + [vmem] * 3,
        out_specs=[vmem] * 3,
        compiler_params=params,
        cost_estimate=pl.CostEstimate(
            flops=128 * count * SLOTS * SLOTS * rows, bytes_accessed=2**21, transcendentals=0
        ),
        name="near",
    )(place, counts, pairs, near_pairs, flat)
    picked_1 = [swap(p, 1) for p in picked_1]

    return pl.pallas_call(
        functools.partial(lag_kernel, groups),
        out_shape=jax.ShapeDtypeStruct((2, count, samples), jnp.float32),
        in_specs=[smem] + [vmem] * 6,
        out_specs=vmem,
        compiler_params=params,
        name="lags",
    )(place, jnp.asarray(inverse), picked_0, picked_2, picked_3, *picked_1)


def solution(mesh):
    in_specs = (P(None, "cell", "grp", None), P("grp"), P(None, None, ("grp", "cell")))
    out_specs = P(None, ("grp", "cell"), None)
    return jax.shard_map(
        on_device, mesh=mesh, in_specs=in_specs, out_specs=out_specs, check_vma=False
    )
```

```python
import functools
import math

import jax
import jax.numpy as jnp
import numpy as np
from jax import lax
from jax.experimental import pallas as pl
from jax.experimental.pallas import tpu as pltpu
from jax.sharding import PartitionSpec as P

EPSILON = 1e-06
SLOTS = 32
NT = (((1,), (1,)), ((), ()))
TN = (((0,), (0,)), ((), ()))
VMEM_LIMIT = 40 * 1024 * 1024


def tables(samples, stations):
    bins = samples // 2
    quarter = bins // 4
    turn = np.arange(bins)[:, None] * np.arange(samples)[None, :] % samples
    angle = turn * (2.0 * math.pi / samples)
    weight = np.where(np.arange(bins) == 0, 1.0, 2.0)[:, None] / samples
    weight = weight * math.sqrt(samples / (3.0 * stations))

    def by_quarter(real, imag):
        rows = [real.reshape(4, quarter, samples), imag.reshape(4, quarter, samples)]
        return np.concatenate(rows, axis=1).reshape(4 * 2 * quarter, samples)

    forward = by_quarter(np.cos(angle), -np.sin(angle)).astype(np.float32)
    inverse = by_quarter(weight * np.cos(angle), -weight * np.sin(angle)).astype(np.float32)
    return forward.astype(jnp.bfloat16), inverse


def place_of(place_ref, groups):
    position = place_ref[0]
    high, inner = position // (2 * groups), position % (2 * groups)
    return high * 2 + inner % 2, inner // 2


def listing_of(pairs_ref, lanes):
    listed = jnp.concatenate([pairs_ref[0], pairs_ref[1]]).astype(jnp.float32)
    return jnp.concatenate([listed[:, at : at + lanes] for at in range(0, listed.shape[1], lanes)])


def station_spectra(windows_ref, at, table):
    parts = []
    for comp in range(windows_ref.shape[0]):
        low = windows_ref[comp, 0, at]
        high = windows_ref[comp, 1, at]
        parts += [low[:SLOTS], high[SLOTS:], low[SLOTS:], high[:SLOTS]]
    traces = jnp.concatenate(parts)
    square = jnp.square(traces.astype(jnp.float32))
    square_hi = square.astype(jnp.bfloat16)
    square_lo = (square - square_hi.astype(jnp.float32)).astype(jnp.bfloat16)
    ones = jnp.ones((16, traces.shape[1]), jnp.bfloat16)
    energy = lax.dot_general(ones, square_hi, NT, preferred_element_type=jnp.float32)
    energy += lax.dot_general(ones, square_lo, NT, preferred_element_type=jnp.float32)
    scale = lax.rsqrt(energy[:1] + EPSILON)
    raw = lax.dot_general(table, traces, NT, preferred_element_type=jnp.float32)
    return (raw * scale).astype(jnp.bfloat16)


def own_kernel(place_ref, windows_ref, forward_ref, spectra_ref, table_ref, held_ref, whole_ref, sems):
    comps, _, groups, _, _ = windows_ref.shape
    rows = forward_ref.shape[0] // 4
    lanes = 4 * SLOTS
    quarter, group = place_of(place_ref, groups)
    copies = [pltpu.make_async_copy(forward_ref, whole_ref, sems.at[groups])]
    for mg in range(groups):
        copies.append(
            pltpu.make_async_copy(windows_ref.at[:, :, group ^ mg], held_ref.at[:, :, mg], sems.at[mg])
        )
    for copy in copies:
        copy.start()
    copies[0].wait()
    for far in range(2):
        start = pl.multiple_of((quarter ^ (2 * far)) * rows, rows)
        table_ref[far * rows : (far + 1) * rows] = whole_ref[pl.ds(start, rows), :]
    table = table_ref[...]
    for mg in range(groups):
        copies[1 + mg].wait()
        spectra = station_spectra(held_ref, mg, table)
        for far in range(2):
            for comp in range(comps):
                spectra_ref[far * groups + mg, comp * rows : (comp + 1) * rows] = spectra[
                    far * rows : (far + 1) * rows, comp * lanes : (comp + 1) * lanes
                ]


def near_spectra_kernel(
    place_ref, own_pairs_ref, near_pairs_ref, table_ref, own_ref, windows_ref, *piece_refs
):
    comps, _, groups, _, _ = windows_ref.shape
    rows = table_ref.shape[0] // 2
    lanes = 4 * SLOTS
    _, group = place_of(place_ref, groups)
    table = table_ref[...]
    piece_refs[groups][2 * comps * rows :] = jnp.concatenate(
        [listing_of(own_pairs_ref, lanes), listing_of(near_pairs_ref, lanes)]
    ).astype(jnp.bfloat16)
    for mg in range(groups):
        spectra = station_spectra(windows_ref, group ^ mg, table)
        for far in range(2):
            piece = piece_refs[far * groups + mg]
            piece[: comps * rows] = own_ref[far * groups + mg]
            for comp in range(comps):
                start = (comps + comp) * rows
                piece[start : start + rows] = spectra[
                    far * rows : (far + 1) * rows, comp * lanes : (comp + 1) * lanes
                ]


def pick(place_ref, counts_ref, listed, flat_ref, mq, *picked_refs):
    cells = counts_ref.shape[0]
    quarter, group = place_of(place_ref, cells // 4)
    own = quarter ^ mq
    high, low = own // 2, own % 2
    cell = high * (cells // 2) + group * 2 + low
    lanes = listed.shape[1]
    turned = listed.T
    lane = lax.broadcasted_iota(jnp.int32, (lanes, lanes), 1)
    sides = ((high, high), (low, 1 - low))
    found = []
    for step_round in range(2):
        own_count = counts_ref[cell].astype(jnp.float32)
        far_count = counts_ref[cell ^ (cells // 2 if step_round else 1)].astype(jnp.float32)
        hot = []
        for chunk in range(listed.shape[0] // 4):
            at = chunk * 4 + step_round * 2
            first, second = turned[:, at : at + 1], turned[:, at + 1 : at + 2]
            live = (first < own_count) & (second < far_count)
            place = jnp.where(high == low, first * SLOTS + second, second * SLOTS + first)
            offset = jnp.where(live, place, -1.0).astype(jnp.int32) - lane
            hot.append(
                jnp.concatenate(
                    [
                        jnp.where(offset == lanes * t, 1.0, 0.0).astype(jnp.bfloat16)
                        for t in range(SLOTS * SLOTS // lanes)
                    ],
                    axis=1,
                )
            )
        block = flat_ref[sides[step_round][0], sides[step_round][1]]
        found.append(jnp.dot(jnp.concatenate(hot), block, preferred_element_type=jnp.float32))
    found = jnp.concatenate(found, axis=1).astype(jnp.bfloat16)
    each = found.shape[0] // len(picked_refs)
    for at, ref in enumerate(picked_refs):
        ref[...] = found[at * each : (at + 1) * each]


def cross_kernel(place_ref, counts_ref, *refs):
    piece_refs, (flat_ref, picked_0, picked_1, trace_ref, cross_ref) = refs[:-5], refs[-5:]
    rows = flat_ref.shape[3]
    bins = rows // 2
    each, lanes = piece_refs[1].shape
    traces = len(piece_refs) * each // rows
    for s, piece in enumerate(piece_refs):
        trace_ref[s * each : (s + 1) * each] = piece[:each].astype(jnp.float32)
    half = 2 * SLOTS
    for k in range(bins):
        real = trace_ref[pl.ds(k, traces, stride=rows), :].astype(jnp.bfloat16)
        imag = trace_ref[pl.ds(bins + k, traces, stride=rows), :].astype(jnp.bfloat16)
        left = jnp.concatenate([real, imag], axis=0)
        right = jnp.concatenate(
            [jnp.concatenate([real, imag], axis=1), jnp.concatenate([imag, -real], axis=1)], axis=0
        )
        cross = lax.dot_general(left, right, TN, preferred_element_type=jnp.float32)
        cross_ref[k * half : (k + 1) * half] = cross[:half, :lanes]
        cross_ref[(bins + k) * half : (bins + k + 1) * half] = cross[:half, lanes:]
    for i in range(half):
        turned = cross_ref[pl.ds(i, rows, stride=half), :].T.astype(jnp.bfloat16)
        own, slot = i // SLOTS, i % SLOTS
        for far in range(2):
            start = half + far * SLOTS
            flat_ref[own, far, slot * SLOTS : (slot + 1) * SLOTS] = turned[start : start + SLOTS]
    listed = piece_refs[0][each:].astype(jnp.float32)
    listing = listed.shape[0] // 2
    pick(place_ref, counts_ref, listed[:listing], flat_ref, 2, picked_0)
    pick(place_ref, counts_ref, listed[listing:], flat_ref, 3, picked_1)


def near_kernel(place_ref, counts_ref, own_pairs_ref, near_pairs_ref, flat_ref, picked_0, *picked_1):
    lanes = 4 * SLOTS
    pick(place_ref, counts_ref, listing_of(near_pairs_ref, lanes), flat_ref, 1, *picked_1)
    pick(place_ref, counts_ref, listing_of(own_pairs_ref, lanes), flat_ref, 0, picked_0)


def lag_kernel(groups, place_ref, inverse_ref, *refs):
    picked_refs, lags_ref = refs[:-1], refs[-1]
    quarter, _ = place_of(place_ref, groups)
    rows = inverse_ref.shape[0] // 4
    sign = jnp.where(quarter // 2 == quarter % 2, 1.0, -1.0)
    row = lax.broadcasted_iota(jnp.int32, (rows, inverse_ref.shape[1]), 0)
    factor = jnp.where(row < rows // 2, 1.0, sign)
    table = jnp.concatenate(
        [
            inverse_ref[pl.ds(pl.multiple_of((quarter ^ m) * rows, rows), rows), :] * factor
            for m in (0, 2, 3, 1)
        ]
    )
    table_hi = table.astype(jnp.bfloat16)
    table_lo = (table - table_hi.astype(jnp.float32)).astype(jnp.bfloat16)
    picked = [ref[...] for ref in picked_refs]
    picked[3:] = [jnp.concatenate(picked[3:])]
    for step_round in range(2):
        cross = jnp.concatenate([p[:, step_round * rows : (step_round + 1) * rows] for p in picked], axis=1)
        lags_ref[step_round] = jnp.dot(
            cross, table_hi, preferred_element_type=jnp.float32
        ) + jnp.dot(cross, table_lo, preferred_element_type=jnp.float32)


def on_device(windows, counts, pairs):
    comps, _, events, samples = windows.shape
    cells = lax.axis_size("cell")
    half, groups = cells // 2, cells // 4
    count = pairs.shape[2]
    rows = samples // 4
    lanes = 4 * SLOTS
    forward, inverse = tables(samples, cells)
    place = lax.axis_index("cell").astype(jnp.int32).reshape(1)

    def swap(x, mask):
        return lax.ppermute(x, "cell", [(i, i ^ mask) for i in range(cells)])

    vmem = pl.BlockSpec(memory_space=pltpu.VMEM)
    smem = pl.BlockSpec(memory_space=pltpu.SMEM)
    params = pltpu.CompilerParams(vmem_limit_bytes=VMEM_LIMIT)

    windows = windows.reshape(comps, 2, groups, 2 * SLOTS, samples)
    near_windows, near_pairs = swap(windows, 1), swap(pairs, 1)
    listing = 2 * pairs.size // lanes
    hbm = pl.BlockSpec(memory_space=pltpu.HBM)
    own_spectra, table = pl.pallas_call(
        own_kernel,
        out_shape=[
            jax.ShapeDtypeStruct((2 * groups, comps * rows, lanes), jnp.bfloat16),
            jax.ShapeDtypeStruct((2 * rows, samples), jnp.bfloat16),
        ],
        in_specs=[smem, hbm, hbm],
        out_specs=[vmem, vmem],
        scratch_shapes=[
            pltpu.VMEM(windows.shape, jnp.bfloat16),
            pltpu.VMEM(forward.shape, jnp.bfloat16),
            pltpu.SemaphoreType.DMA((groups + 1,)),
        ],
        compiler_params=params,
        cost_estimate=pl.CostEstimate(
            flops=4 * windows.size * samples, bytes_accessed=4 * windows.size, transcendentals=0
        ),
        name="own_spectra",
    )(place, windows, jnp.asarray(forward))
    pieces = pl.pallas_call(
        near_spectra_kernel,
        out_shape=[
            jax.ShapeDtypeStruct((2 * comps * rows + listing * (m == groups), lanes), jnp.bfloat16)
            for m in range(2 * groups)
        ],
        in_specs=[smem] + [vmem] * 5,
        out_specs=[vmem] * (2 * groups),
        compiler_params=params,
        name="near_spectra",
    )(place, pairs, near_pairs, table, own_spectra, near_windows)
    order = [*range(1, groups - 1), *range(groups, 2 * groups), groups - 1]
    arrived = {m: swap(pieces[m], 2 * m) for m in order}
    pieces = [arrived.pop(groups), pieces[0]] + list(arrived.values())

    picked_shape = jax.ShapeDtypeStruct((count, 2 * rows), jnp.bfloat16)
    flat, picked_2, picked_3 = pl.pallas_call(
        cross_kernel,
        out_shape=[
            jax.ShapeDtypeStruct((2, 2, SLOTS * SLOTS, rows), jnp.bfloat16),
            picked_shape,
            picked_shape,
        ],
        in_specs=[smem, smem] + [vmem] * (2 * groups),
        out_specs=[vmem] * 3,
        scratch_shapes=[
            pltpu.VMEM((comps * cells * rows, lanes), jnp.float32),
            pltpu.VMEM((rows * 2 * SLOTS, lanes), jnp.float32),
        ],
        compiler_params=params,
        name="cross",
    )(place, counts, *pieces)
    picked_2, picked_3 = swap(picked_2, half), swap(picked_3, half + 1)
    picked_0, *picked_1 = pl.pallas_call(
        near_kernel,
        out_shape=[picked_shape] + [jax.ShapeDtypeStruct((count // 2, 2 * rows), jnp.bfloat16)] * 2,
        in_specs=[smem, smem] + [vmem] * 3,
        out_specs=[vmem] * 3,
        compiler_params=params,
        cost_estimate=pl.CostEstimate(
            flops=128 * count * SLOTS * SLOTS * rows, bytes_accessed=2**21, transcendentals=0
        ),
        name="near",
    )(place, counts, pairs, near_pairs, flat)
    picked_1 = [swap(p, 1) for p in picked_1]

    return pl.pallas_call(
        functools.partial(lag_kernel, groups),
        out_shape=jax.ShapeDtypeStruct((2, count, samples), jnp.float32),
        in_specs=[smem] + [vmem] * 6,
        out_specs=vmem,
        compiler_params=params,
        name="lags",
    )(place, jnp.asarray(inverse), picked_0, picked_2, picked_3, *picked_1)


def solution(mesh):
    in_specs = (P(None, "cell", "grp", None), P("grp"), P(None, None, ("grp", "cell")))
    out_specs = P(None, ("grp", "cell"), None)
    return jax.shard_map(
        on_device, mesh=mesh, in_specs=in_specs, out_specs=out_specs, check_vma=False
    )
```

```python
import functools
import math

import jax
import jax.numpy as jnp
import numpy as np
from jax import lax
from jax.experimental import pallas as pl
from jax.experimental.pallas import tpu as pltpu
from jax.sharding import PartitionSpec as P

EPSILON = 1e-06
SLOTS = 32
NT = (((1,), (1,)), ((), ()))
TN = (((0,), (0,)), ((), ()))
VMEM_LIMIT = 40 * 1024 * 1024


def tables(samples, stations):
    bins = samples // 2
    quarter = bins // 4
    turn = np.arange(bins)[:, None] * np.arange(samples)[None, :] % samples
    angle = turn * (2.0 * math.pi / samples)
    weight = np.where(np.arange(bins) == 0, 1.0, 2.0)[:, None] / samples
    weight = weight * math.sqrt(samples / (3.0 * stations))

    def by_quarter(real, imag):
        rows = [real.reshape(4, quarter, samples), imag.reshape(4, quarter, samples)]
        return np.concatenate(rows, axis=1).reshape(4 * 2 * quarter, samples)

    forward = by_quarter(np.cos(angle), -np.sin(angle)).astype(np.float32)
    inverse = by_quarter(weight * np.cos(angle), -weight * np.sin(angle)).astype(np.float32)
    return forward.astype(jnp.bfloat16), inverse


def place_of(place_ref, groups):
    position = place_ref[0]
    high, inner = position // (2 * groups), position % (2 * groups)
    return high * 2 + inner % 2, inner // 2


def listing_of(pairs_ref, lanes):
    ends = []
    for end in range(2):
        slots = pairs_ref[:, end, :].astype(jnp.float32)
        ends += [slots[:, at : at + lanes] for at in range(0, slots.shape[1], lanes)]
    return jnp.concatenate(ends)


def station_spectra(windows_ref, at, table):
    parts = []
    for comp in range(windows_ref.shape[0]):
        low = windows_ref[comp, 0, at]
        high = windows_ref[comp, 1, at]
        parts += [low[:SLOTS], high[SLOTS:], low[SLOTS:], high[:SLOTS]]
    traces = jnp.concatenate(parts)
    square = jnp.square(traces.astype(jnp.float32))
    square_hi = square.astype(jnp.bfloat16)
    square_lo = (square - square_hi.astype(jnp.float32)).astype(jnp.bfloat16)
    ones = jnp.ones((16, traces.shape[1]), jnp.bfloat16)
    energy = lax.dot_general(ones, square_hi, NT, preferred_element_type=jnp.float32)
    energy += lax.dot_general(ones, square_lo, NT, preferred_element_type=jnp.float32)
    scale = lax.rsqrt(energy[:1] + EPSILON)
    raw = lax.dot_general(table, traces, NT, preferred_element_type=jnp.float32)
    return (raw * scale).astype(jnp.bfloat16)


def own_kernel(place_ref, windows_ref, forward_ref, spectra_ref, table_ref):
    comps, _, groups, _, _ = windows_ref.shape
    rows = forward_ref.shape[0] // 4
    lanes = 4 * SLOTS
    quarter, group = place_of(place_ref, groups)
    for far in range(2):
        start = pl.multiple_of((quarter ^ (2 * far)) * rows, rows)
        table_ref[far * rows : (far + 1) * rows] = forward_ref[pl.ds(start, rows), :]
    table = table_ref[...]
    for mg in range(groups):
        spectra = station_spectra(windows_ref, group ^ mg, table)
        for far in range(2):
            for comp in range(comps):
                spectra_ref[far * groups + mg, comp * rows : (comp + 1) * rows] = spectra[
                    far * rows : (far + 1) * rows, comp * lanes : (comp + 1) * lanes
                ]


def near_spectra_kernel(
    place_ref, own_pairs_ref, near_pairs_ref, table_ref, own_ref, windows_ref, *piece_refs
):
    comps, _, groups, _, _ = windows_ref.shape
    rows = table_ref.shape[0] // 2
    lanes = 4 * SLOTS
    _, group = place_of(place_ref, groups)
    table = table_ref[...]
    piece_refs[groups][2 * comps * rows :] = jnp.concatenate(
        [listing_of(own_pairs_ref, lanes), listing_of(near_pairs_ref, lanes)]
    ).astype(jnp.bfloat16)
    for mg in range(groups):
        spectra = station_spectra(windows_ref, group ^ mg, table)
        for far in range(2):
            piece = piece_refs[far * groups + mg]
            piece[: comps * rows] = own_ref[far * groups + mg]
            for comp in range(comps):
                start = (comps + comp) * rows
                piece[start : start + rows] = spectra[
                    far * rows : (far + 1) * rows, comp * lanes : (comp + 1) * lanes
                ]


def pick(place_ref, counts_ref, listed, flat_ref, mq, *picked_refs):
    cells = counts_ref.shape[0]
    quarter, group = place_of(place_ref, cells // 4)
    own = quarter ^ mq
    high, low = own // 2, own % 2
    cell = high * (cells // 2) + group * 2 + low
    lanes = listed.shape[1]
    count = listed.shape[0] // 2
    first, second = listed[:count].astype(jnp.int32), listed[count:].astype(jnp.int32)
    far_counts = [counts_ref[cell ^ 1], counts_ref[cell ^ (cells // 2)]]
    odd = lax.broadcasted_iota(jnp.int32, (count, lanes), 0) % 2
    live = (first < counts_ref[cell]) & (second < jnp.where(odd == 1, far_counts[1], far_counts[0]))
    left, right = jnp.where(high == low, first, second), jnp.where(high == low, second, first)
    spot = jnp.where(live, (left // 4) * SLOTS + right, -1)
    turned = jnp.concatenate([spot, left % 4]).T
    lane = lax.broadcasted_iota(jnp.int32, (lanes, lanes), 1)
    run = lane // SLOTS
    spread = lax.broadcasted_iota(jnp.int32, (2 * lanes, lanes), 0)
    kept = lax.broadcasted_iota(jnp.int32, (2 * lanes, lanes), 1)
    sides = ((high, high), (low, 1 - low))
    found = []
    folds = []
    for step_round in range(2):
        hot = []
        for at in range(step_round, count, 2):
            offset = turned[:, at : at + 1] - lane
            hot.append(
                jnp.concatenate(
                    [jnp.where(offset == start, 1.0, 0.0).astype(jnp.bfloat16) for start in (0, lanes)],
                    axis=1,
                )
            )
        block = flat_ref[sides[step_round][0], sides[step_round][1]]
        wide = jnp.dot(jnp.concatenate(hot), block, preferred_element_type=jnp.float32)
        masked = []
        for chunk, at in enumerate(range(step_round, count, 2)):
            here = run == turned[:, count + at : count + at + 1]
            part = wide[chunk * lanes : (chunk + 1) * lanes]
            masked.append(
                jnp.concatenate(
                    [
                        jnp.where(here, part[:, :lanes], 0.0).astype(jnp.bfloat16),
                        jnp.where(here, part[:, lanes:], 0.0).astype(jnp.bfloat16),
                    ],
                    axis=1,
                )
            )
        found.append(jnp.concatenate(masked))
        place = (step_round * 2 + spread // lanes) * SLOTS + spread % SLOTS
        folds.append(jnp.where(kept == place, 1.0, 0.0).astype(jnp.bfloat16))
    picked = jnp.dot(
        jnp.concatenate(found, axis=1),
        jnp.concatenate(folds),
        preferred_element_type=jnp.float32,
    ).astype(jnp.bfloat16)
    each = picked.shape[0] // len(picked_refs)
    for at, ref in enumerate(picked_refs):
        ref[...] = picked[at * each : (at + 1) * each]


def padded(traces):
    return -(-traces // 16) * 16


def add_cross(piece_refs, trace_ref, rows, sums_ref, before_ref=None):
    bins = rows // 2
    slots, lanes = 2 * SLOTS, 4 * SLOTS
    traces = trace_ref.shape[0] // rows
    each = traces * rows
    start = 0
    for piece in piece_refs:
        held = piece.shape[0] // rows * rows
        trace_ref[start : start + held] = piece[:held].astype(jnp.float32)
        start += held
    if start < each:
        trace_ref[start:] = jnp.zeros((each - start, lanes), jnp.float32)
    for k in range(bins):
        real = trace_ref[pl.ds(k, traces, stride=rows), :].astype(jnp.bfloat16)
        imag = trace_ref[pl.ds(bins + k, traces, stride=rows), :].astype(jnp.bfloat16)
        left = jnp.concatenate([real, imag], axis=0)[:, :slots]
        right = jnp.concatenate(
            [jnp.concatenate([real, imag], axis=1), jnp.concatenate([imag, -real], axis=1)], axis=0
        )
        cross = lax.dot_general(left, right, TN, preferred_element_type=jnp.float32)
        for part in range(2):
            at = (part * bins + k) * slots
            value = cross[:, part * lanes : (part + 1) * lanes]
            if before_ref is not None:
                value += before_ref[at : at + slots]
            sums_ref[at : at + slots] = value


def early_kernel(*refs):
    piece_refs, (sums_ref, trace_ref) = refs[:-2], refs[-2:]
    add_cross(piece_refs, trace_ref, sums_ref.shape[0] // (2 * SLOTS), sums_ref)


def cross_kernel(place_ref, counts_ref, listed_ref, before_ref, *refs):
    piece_refs, (flat_ref, picked_0, picked_1, trace_ref, cross_ref) = refs[:-5], refs[-5:]
    slots, lanes = 2 * SLOTS, 4 * SLOTS
    rows = before_ref.shape[0] // slots
    bins = rows // 2
    add_cross(piece_refs, trace_ref, rows, cross_ref, before_ref)
    for own in range(2):
        for four in range(SLOTS // 4):
            for part in range(2):
                first = part * bins * slots + own * SLOTS + four * 4
                block = jnp.concatenate(
                    [cross_ref[pl.ds(first + i, bins, stride=slots), :] for i in range(4)]
                ).T.astype(jnp.bfloat16)
                for far in range(2):
                    flat_ref[
                        own, far, four * SLOTS : (four + 1) * SLOTS, part * lanes : (part + 1) * lanes
                    ] = block[slots + far * SLOTS : slots + (far + 1) * SLOTS]
    listed = listed_ref[listed_ref.shape[0] // rows * rows :].astype(jnp.float32)
    listing = listed.shape[0] // 2
    pick(place_ref, counts_ref, listed[:listing], flat_ref, 2, picked_0)
    pick(place_ref, counts_ref, listed[listing:], flat_ref, 3, picked_1)


def near_kernel(place_ref, counts_ref, own_pairs_ref, near_pairs_ref, flat_ref, picked_0, *picked_1):
    lanes = 4 * SLOTS
    pick(place_ref, counts_ref, listing_of(near_pairs_ref, lanes), flat_ref, 1, *picked_1)
    pick(place_ref, counts_ref, listing_of(own_pairs_ref, lanes), flat_ref, 0, picked_0)


def lag_kernel(groups, place_ref, inverse_ref, *refs):
    picked_refs, lags_ref = refs[:-1], refs[-1]
    quarter, _ = place_of(place_ref, groups)
    rows = inverse_ref.shape[0] // 4
    sign = jnp.where(quarter // 2 == quarter % 2, 1.0, -1.0)
    row = lax.broadcasted_iota(jnp.int32, (rows, inverse_ref.shape[1]), 0)
    factor = jnp.where(row < rows // 2, 1.0, sign)
    table = jnp.concatenate(
        [
            inverse_ref[pl.ds(pl.multiple_of((quarter ^ m) * rows, rows), rows), :] * factor
            for m in (0, 2, 3, 1)
        ]
    )
    table_hi = table.astype(jnp.bfloat16)
    table_lo = (table - table_hi.astype(jnp.float32)).astype(jnp.bfloat16)
    picked = [ref[...] for ref in picked_refs]
    picked[3:] = [jnp.concatenate(picked[3:])]
    for step_round in range(2):
        cross = jnp.concatenate([p[:, step_round * rows : (step_round + 1) * rows] for p in picked], axis=1)
        lags_ref[step_round] = jnp.dot(
            cross, table_hi, preferred_element_type=jnp.float32
        ) + jnp.dot(cross, table_lo, preferred_element_type=jnp.float32)


def on_device(windows, counts, pairs):
    comps, _, events, samples = windows.shape
    cells = lax.axis_size("cell")
    half, groups = cells // 2, cells // 4
    count = pairs.shape[2]
    rows = samples // 4
    lanes = 4 * SLOTS
    forward, inverse = tables(samples, cells)
    place = lax.axis_index("cell").astype(jnp.int32).reshape(1)

    def swap(x, mask):
        return lax.ppermute(x, "cell", [(i, i ^ mask) for i in range(cells)])

    vmem = pl.BlockSpec(memory_space=pltpu.VMEM)
    smem = pl.BlockSpec(memory_space=pltpu.SMEM)
    params = pltpu.CompilerParams(vmem_limit_bytes=VMEM_LIMIT)

    windows = windows.reshape(comps, 2, groups, 2 * SLOTS, samples)
    near_windows, near_pairs = swap(windows, 1), swap(pairs, 1)
    listing = 2 * pairs.size // lanes
    own_spectra, table = pl.pallas_call(
        own_kernel,
        out_shape=[
            jax.ShapeDtypeStruct((2 * groups, comps * rows, lanes), jnp.bfloat16),
            jax.ShapeDtypeStruct((2 * rows, samples), jnp.bfloat16),
        ],
        in_specs=[smem, vmem, vmem],
        out_specs=[vmem, vmem],
        compiler_params=params,
        cost_estimate=pl.CostEstimate(
            flops=4 * windows.size * samples, bytes_accessed=4 * windows.size, transcendentals=0
        ),
        name="own_spectra",
    )(place, windows, jnp.asarray(forward))
    pieces = pl.pallas_call(
        near_spectra_kernel,
        out_shape=[
            jax.ShapeDtypeStruct((2 * comps * rows + listing * (m == groups), lanes), jnp.bfloat16)
            for m in range(2 * groups)
        ],
        in_specs=[smem] + [vmem] * 5,
        out_specs=[vmem] * (2 * groups),
        compiler_params=params,
        name="near_spectra",
    )(place, pairs, near_pairs, table, own_spectra, near_windows)
    order = [*range(1, groups - 1), *range(groups, 2 * groups), groups - 1]
    arrived = {m: swap(pieces[m], 2 * m) for m in order}
    late = [2 * groups - 2, 2 * groups - 1]
    early = [pieces[0]] + [arrived[m] for m in order if m not in late]

    sums = pl.pallas_call(
        early_kernel,
        out_shape=jax.ShapeDtypeStruct((2 * SLOTS * rows, lanes), jnp.float32),
        in_specs=[vmem] * len(early),
        out_specs=vmem,
        scratch_shapes=[pltpu.VMEM((padded(len(early) * 2 * comps) * rows, lanes), jnp.float32)],
        compiler_params=params,
        cost_estimate=pl.CostEstimate(flops=2**31, bytes_accessed=2**22, transcendentals=0),
        name="early",
    )(*early)
    picked_shape = jax.ShapeDtypeStruct((count, 2 * rows), jnp.bfloat16)
    flat, picked_2, picked_3 = pl.pallas_call(
        cross_kernel,
        out_shape=[
            jax.ShapeDtypeStruct((2, 2, SLOTS * SLOTS // 4, 2 * lanes), jnp.bfloat16),
            picked_shape,
            picked_shape,
        ],
        in_specs=[smem, smem] + [vmem] * (2 + len(late)),
        out_specs=[vmem] * 3,
        scratch_shapes=[
            pltpu.VMEM((padded(len(late) * 2 * comps) * rows, lanes), jnp.float32),
            pltpu.VMEM((2 * SLOTS * rows, lanes), jnp.float32),
        ],
        compiler_params=params,
        name="cross",
    )(place, counts, arrived[groups], sums, *[arrived[m] for m in late])
    picked_2, picked_3 = swap(picked_2, half), swap(picked_3, half + 1)
    picked_0, *picked_1 = pl.pallas_call(
        near_kernel,
        out_shape=[picked_shape] + [jax.ShapeDtypeStruct((count // 2, 2 * rows), jnp.bfloat16)] * 2,
        in_specs=[smem, smem] + [vmem] * 3,
        out_specs=[vmem] * 3,
        compiler_params=params,
        cost_estimate=pl.CostEstimate(
            flops=128 * count * SLOTS * SLOTS * rows, bytes_accessed=2**21, transcendentals=0
        ),
        name="near",
    )(place, counts, pairs, near_pairs, flat)
    picked_1 = [swap(p, 1) for p in picked_1]

    return pl.pallas_call(
        functools.partial(lag_kernel, groups),
        out_shape=jax.ShapeDtypeStruct((2, count, samples), jnp.float32),
        in_specs=[smem] + [vmem] * 6,
        out_specs=vmem,
        compiler_params=params,
        name="lags",
    )(place, jnp.asarray(inverse), picked_0, picked_2, picked_3, *picked_1)


def solution(mesh):
    in_specs = (P(None, "cell", "grp", None), P("grp"), P(None, None, ("grp", "cell")))
    out_specs = P(None, ("grp", "cell"), None)
    return jax.shard_map(
        on_device, mesh=mesh, in_specs=in_specs, out_specs=out_specs, check_vma=False
    )
```

```python
import functools
import math

import jax
import jax.numpy as jnp
import numpy as np
from jax import lax
from jax.experimental import pallas as pl
from jax.experimental.pallas import tpu as pltpu
from jax.sharding import PartitionSpec as P

EPSILON = 1e-06
COSINE = (
    0.9999999999993376,
    -4.934802200431432,
    4.058712123240781,
    -1.3352627346923478,
    0.23533044681677665,
    -0.02580633847975355,
    0.0019285963125396874,
    -0.00010362767792380447,
    3.734915399663344e-06,
)
SLOTS = 32
NT = (((1,), (1,)), ((), ()))
TN = (((0,), (0,)), ((), ()))
VMEM_LIMIT = 40 * 1024 * 1024


def inverse_table(samples, stations):
    bins = samples // 2
    quarter = bins // 4
    turn = np.arange(bins)[:, None] * np.arange(samples)[None, :] % samples
    angle = turn * (2.0 * math.pi / samples)
    weight = np.where(np.arange(bins) == 0, 1.0, 2.0)[:, None] / samples
    weight = weight * math.sqrt(samples / (3.0 * stations))
    parts = [weight * np.cos(angle), -weight * np.sin(angle)]
    rows = [part.reshape(4, quarter, samples) for part in parts]
    return np.concatenate(rows, axis=1).reshape(2 * bins, samples).astype(np.float32)


def forward_rows(bins, samples):
    count = bins.shape[0]
    sample = lax.broadcasted_iota(jnp.int32, (2 * count, samples), 1)
    turn = jnp.concatenate([bins * sample[:count], bins * sample[:count] + samples // 4]) % samples
    x = jnp.where(turn > samples // 2, turn - samples, turn).astype(jnp.float32) * (2.0 / samples)
    square = x * x
    value = jnp.full(square.shape, COSINE[-1], jnp.float32)
    for factor in COSINE[-2::-1]:
        value = value * square + factor
    return value.astype(jnp.bfloat16)


def place_of(place_ref, groups):
    position = place_ref[0]
    high, inner = position // (2 * groups), position % (2 * groups)
    return high * 2 + inner % 2, inner // 2


def listing_of(pairs_ref, lanes):
    ends = []
    for end in range(2):
        slots = pairs_ref[:, end, :].astype(jnp.float32)
        ends += [slots[:, at : at + lanes] for at in range(0, slots.shape[1], lanes)]
    return jnp.concatenate(ends)


def station_spectra(windows_ref, at, table):
    parts = []
    for comp in range(windows_ref.shape[0]):
        low = windows_ref[comp, 0, at]
        high = windows_ref[comp, 1, at]
        parts += [low[:SLOTS], high[SLOTS:], low[SLOTS:], high[:SLOTS]]
    traces = jnp.concatenate(parts)
    square = jnp.square(traces.astype(jnp.float32))
    square_hi = square.astype(jnp.bfloat16)
    square_lo = (square - square_hi.astype(jnp.float32)).astype(jnp.bfloat16)
    ones = jnp.ones((16, traces.shape[1]), jnp.bfloat16)
    energy = lax.dot_general(ones, square_hi, NT, preferred_element_type=jnp.float32)
    energy += lax.dot_general(ones, square_lo, NT, preferred_element_type=jnp.float32)
    scale = lax.rsqrt(energy[:1] + EPSILON)
    raw = lax.dot_general(table, traces, NT, preferred_element_type=jnp.float32)
    return (raw * scale).astype(jnp.bfloat16)


def own_kernel(place_ref, windows_ref, spectra_ref, table_ref):
    comps, _, groups, _, samples = windows_ref.shape
    rows = table_ref.shape[0] // 2
    lanes = 4 * SLOTS
    quarter, group = place_of(place_ref, groups)
    for far in range(2):
        bins = lax.broadcasted_iota(jnp.int32, (rows // 2, samples), 0)
        table_ref[far * rows : (far + 1) * rows] = forward_rows(
            bins + (quarter ^ (2 * far)) * (rows // 2), samples
        )
    table = table_ref[...]
    for mg in range(groups):
        spectra = station_spectra(windows_ref, group ^ mg, table)
        for far in range(2):
            for comp in range(comps):
                spectra_ref[far * groups + mg, comp * rows : (comp + 1) * rows] = spectra[
                    far * rows : (far + 1) * rows, comp * lanes : (comp + 1) * lanes
                ]


def near_spectra_kernel(place_ref, table_ref, own_ref, windows_ref, *refs):
    pairs_refs, listed_ref, piece_refs = refs[:3], refs[3], refs[4:]
    comps, _, groups, _, _ = windows_ref.shape
    rows = table_ref.shape[0] // 2
    lanes = 4 * SLOTS
    _, group = place_of(place_ref, groups)
    table = table_ref[...]
    for at, pairs_ref in enumerate(pairs_refs):
        listed_ref[at] = listing_of(pairs_ref, lanes)
    for mg in range(groups):
        spectra = station_spectra(windows_ref, group ^ mg, table)
        for far in range(2):
            piece = piece_refs[far * groups + mg]
            piece[: comps * rows] = own_ref[far * groups + mg]
            for comp in range(comps):
                start = (comps + comp) * rows
                piece[start : start + rows] = spectra[
                    far * rows : (far + 1) * rows, comp * lanes : (comp + 1) * lanes
                ]


def pick(place_ref, counts_ref, listed, flat_ref, mq, *picked_refs):
    cells = counts_ref.shape[0]
    quarter, group = place_of(place_ref, cells // 4)
    own = quarter ^ mq
    high, low = own // 2, own % 2
    cell = high * (cells // 2) + group * 2 + low
    lanes = listed.shape[1]
    count = listed.shape[0] // 2
    first, second = listed[:count].astype(jnp.int32), listed[count:].astype(jnp.int32)
    far_counts = [counts_ref[cell ^ 1], counts_ref[cell ^ (cells // 2)]]
    odd = lax.broadcasted_iota(jnp.int32, (count, lanes), 0) % 2
    live = (first < counts_ref[cell]) & (second < jnp.where(odd == 1, far_counts[1], far_counts[0]))
    left, right = jnp.where(high == low, first, second), jnp.where(high == low, second, first)
    spot = jnp.where(live, (left // 4) * SLOTS + right, -1)
    turned = jnp.concatenate([spot, left % 4]).T
    lane = lax.broadcasted_iota(jnp.int32, (lanes, lanes), 1)
    run = lane // SLOTS
    spread = lax.broadcasted_iota(jnp.int32, (2 * lanes, lanes), 0)
    kept = lax.broadcasted_iota(jnp.int32, (2 * lanes, lanes), 1)
    sides = ((high, high), (low, 1 - low))
    found = []
    folds = []
    for step_round in range(2):
        hot = []
        for at in range(step_round, count, 2):
            offset = turned[:, at : at + 1] - lane
            hot.append(
                jnp.concatenate(
                    [jnp.where(offset == start, 1.0, 0.0).astype(jnp.bfloat16) for start in (0, lanes)],
                    axis=1,
                )
            )
        block = flat_ref[sides[step_round][0], sides[step_round][1]]
        wide = jnp.dot(jnp.concatenate(hot), block, preferred_element_type=jnp.float32)
        masked = []
        for chunk, at in enumerate(range(step_round, count, 2)):
            here = run == turned[:, count + at : count + at + 1]
            part = wide[chunk * lanes : (chunk + 1) * lanes]
            masked.append(
                jnp.concatenate(
                    [
                        jnp.where(here, part[:, :lanes], 0.0).astype(jnp.bfloat16),
                        jnp.where(here, part[:, lanes:], 0.0).astype(jnp.bfloat16),
                    ],
                    axis=1,
                )
            )
        found.append(jnp.concatenate(masked))
        place = (step_round * 2 + spread // lanes) * SLOTS + spread % SLOTS
        folds.append(jnp.where(kept == place, 1.0, 0.0).astype(jnp.bfloat16))
    picked = jnp.dot(
        jnp.concatenate(found, axis=1),
        jnp.concatenate(folds),
        preferred_element_type=jnp.float32,
    ).astype(jnp.bfloat16)
    each = picked.shape[0] // len(picked_refs)
    for at, ref in enumerate(picked_refs):
        ref[...] = picked[at * each : (at + 1) * each]


def padded(traces):
    return -(-traces // 16) * 16


def add_cross(piece_refs, trace_ref, rows, sums_ref, before_ref=None):
    bins = rows // 2
    slots, lanes = 2 * SLOTS, 4 * SLOTS
    traces = trace_ref.shape[0] // rows
    each = traces * rows
    start = 0
    for piece in piece_refs:
        held = piece.shape[0]
        trace_ref[start : start + held] = piece[...].astype(jnp.float32)
        start += held
    if start < each:
        trace_ref[start:] = jnp.zeros((each - start, lanes), jnp.float32)
    for k in range(bins):
        real = trace_ref[pl.ds(k, traces, stride=rows), :].astype(jnp.bfloat16)
        imag = trace_ref[pl.ds(bins + k, traces, stride=rows), :].astype(jnp.bfloat16)
        left = jnp.concatenate([real, imag], axis=0)[:, :slots]
        right = jnp.concatenate(
            [jnp.concatenate([real, imag], axis=1), jnp.concatenate([imag, -real], axis=1)], axis=0
        )
        cross = lax.dot_general(left, right, TN, preferred_element_type=jnp.float32)
        for part in range(2):
            at = (part * bins + k) * slots
            value = cross[:, part * lanes : (part + 1) * lanes]
            if before_ref is not None:
                value += before_ref[at : at + slots]
            sums_ref[at : at + slots] = value


def early_kernel(*refs):
    piece_refs, (sums_ref, trace_ref) = refs[:-2], refs[-2:]
    add_cross(piece_refs, trace_ref, sums_ref.shape[0] // (2 * SLOTS), sums_ref)


def cross_kernel(place_ref, counts_ref, listed_ref, before_ref, *refs):
    piece_refs, (flat_ref, picked_0, picked_1, trace_ref, cross_ref) = refs[:-5], refs[-5:]
    slots, lanes = 2 * SLOTS, 4 * SLOTS
    rows = before_ref.shape[0] // slots
    bins = rows // 2
    add_cross(piece_refs, trace_ref, rows, cross_ref, before_ref)
    for own in range(2):
        for four in range(SLOTS // 4):
            for part in range(2):
                first = part * bins * slots + own * SLOTS + four * 4
                block = jnp.concatenate(
                    [cross_ref[pl.ds(first + i, bins, stride=slots), :] for i in range(4)]
                ).T.astype(jnp.bfloat16)
                for far in range(2):
                    flat_ref[
                        own, far, four * SLOTS : (four + 1) * SLOTS, part * lanes : (part + 1) * lanes
                    ] = block[slots + far * SLOTS : slots + (far + 1) * SLOTS]
    pick(place_ref, counts_ref, listed_ref[1], flat_ref, 2, picked_0)
    pick(place_ref, counts_ref, listed_ref[2], flat_ref, 3, picked_1)


def near_kernel(place_ref, counts_ref, own_pairs_ref, listed_ref, flat_ref, picked_0, *picked_1):
    lanes = 4 * SLOTS
    pick(place_ref, counts_ref, listed_ref[0], flat_ref, 1, *picked_1)
    pick(place_ref, counts_ref, listing_of(own_pairs_ref, lanes), flat_ref, 0, picked_0)


def lag_kernel(groups, place_ref, inverse_ref, *refs):
    picked_refs, lags_ref = refs[:-1], refs[-1]
    quarter, _ = place_of(place_ref, groups)
    rows = inverse_ref.shape[0] // 4
    sign = jnp.where(quarter // 2 == quarter % 2, 1.0, -1.0)
    row = lax.broadcasted_iota(jnp.int32, (rows, inverse_ref.shape[1]), 0)
    factor = jnp.where(row < rows // 2, 1.0, sign)
    table = jnp.concatenate(
        [
            inverse_ref[pl.ds(pl.multiple_of((quarter ^ m) * rows, rows), rows), :] * factor
            for m in (0, 2, 3, 1)
        ]
    )
    table_hi = table.astype(jnp.bfloat16)
    table_lo = (table - table_hi.astype(jnp.float32)).astype(jnp.bfloat16)
    picked = [ref[...] for ref in picked_refs]
    picked[3:] = [jnp.concatenate(picked[3:])]
    for step_round in range(2):
        cross = jnp.concatenate([p[:, step_round * rows : (step_round + 1) * rows] for p in picked], axis=1)
        lags_ref[step_round] = jnp.dot(
            cross, table_hi, preferred_element_type=jnp.float32
        ) + jnp.dot(cross, table_lo, preferred_element_type=jnp.float32)


def on_device(windows, counts, pairs):
    comps, _, events, samples = windows.shape
    cells = lax.axis_size("cell")
    half, groups = cells // 2, cells // 4
    count = pairs.shape[2]
    rows = samples // 4
    lanes = 4 * SLOTS
    inverse = inverse_table(samples, cells)
    place = lax.axis_index("cell").astype(jnp.int32).reshape(1)

    def swap(x, mask):
        return lax.ppermute(x, "cell", [(i, i ^ mask) for i in range(cells)])

    vmem = pl.BlockSpec(memory_space=pltpu.VMEM)
    smem = pl.BlockSpec(memory_space=pltpu.SMEM)
    params = pltpu.CompilerParams(vmem_limit_bytes=VMEM_LIMIT)

    windows = windows.reshape(comps, 2, groups, 2 * SLOTS, samples)
    near_windows = swap(windows, 1)
    other_pairs = [swap(pairs, m) for m in (1, half, half + 1)]
    listing = pairs.size // lanes
    own_spectra, table = pl.pallas_call(
        own_kernel,
        out_shape=[
            jax.ShapeDtypeStruct((2 * groups, comps * rows, lanes), jnp.bfloat16),
            jax.ShapeDtypeStruct((2 * rows, samples), jnp.bfloat16),
        ],
        in_specs=[smem, vmem],
        out_specs=[vmem, vmem],
        compiler_params=params,
        cost_estimate=pl.CostEstimate(
            flops=4 * windows.size * samples, bytes_accessed=4 * windows.size, transcendentals=0
        ),
        name="own_spectra",
    )(place, windows)
    listed, *pieces = pl.pallas_call(
        near_spectra_kernel,
        out_shape=[jax.ShapeDtypeStruct((3, listing, lanes), jnp.float32)]
        + [jax.ShapeDtypeStruct((2 * comps * rows, lanes), jnp.bfloat16)] * (2 * groups),
        in_specs=[smem] + [vmem] * 6,
        out_specs=[vmem] * (1 + 2 * groups),
        compiler_params=params,
        name="near_spectra",
    )(place, table, own_spectra, near_windows, *other_pairs)
    order = [*range(1, groups - 1), *range(groups, 2 * groups), groups - 1]
    arrived = {m: swap(pieces[m], 2 * m) for m in order}
    late = [2 * groups - 2, 2 * groups - 1]
    early = [pieces[0]] + [arrived[m] for m in order if m not in late]

    sums = pl.pallas_call(
        early_kernel,
        out_shape=jax.ShapeDtypeStruct((2 * SLOTS * rows, lanes), jnp.float32),
        in_specs=[vmem] * len(early),
        out_specs=vmem,
        scratch_shapes=[pltpu.VMEM((padded(len(early) * 2 * comps) * rows, lanes), jnp.float32)],
        compiler_params=params,
        cost_estimate=pl.CostEstimate(flops=2**31, bytes_accessed=2**22, transcendentals=0),
        name="early",
    )(*early)
    picked_shape = jax.ShapeDtypeStruct((count, 2 * rows), jnp.bfloat16)
    flat, picked_2, picked_3 = pl.pallas_call(
        cross_kernel,
        out_shape=[
            jax.ShapeDtypeStruct((2, 2, SLOTS * SLOTS // 4, 2 * lanes), jnp.bfloat16),
            picked_shape,
            picked_shape,
        ],
        in_specs=[smem, smem] + [vmem] * (2 + len(late)),
        out_specs=[vmem] * 3,
        scratch_shapes=[
            pltpu.VMEM((padded(len(late) * 2 * comps) * rows, lanes), jnp.float32),
            pltpu.VMEM((2 * SLOTS * rows, lanes), jnp.float32),
        ],
        compiler_params=params,
        name="cross",
    )(place, counts, listed, sums, *[arrived[m] for m in late])
    picked_2, picked_3 = swap(picked_2, half), swap(picked_3, half + 1)
    picked_0, *picked_1 = pl.pallas_call(
        near_kernel,
        out_shape=[picked_shape] + [jax.ShapeDtypeStruct((count // 2, 2 * rows), jnp.bfloat16)] * 2,
        in_specs=[smem, smem] + [vmem] * 3,
        out_specs=[vmem] * 3,
        compiler_params=params,
        cost_estimate=pl.CostEstimate(
            flops=128 * count * SLOTS * SLOTS * rows, bytes_accessed=2**21, transcendentals=0
        ),
        name="near",
    )(place, counts, pairs, listed, flat)
    picked_1 = [swap(p, 1) for p in picked_1]

    return pl.pallas_call(
        functools.partial(lag_kernel, groups),
        out_shape=jax.ShapeDtypeStruct((2, count, samples), jnp.float32),
        in_specs=[smem] + [vmem] * 6,
        out_specs=vmem,
        compiler_params=params,
        name="lags",
    )(place, jnp.asarray(inverse), picked_0, picked_2, picked_3, *picked_1)


def solution(mesh):
    in_specs = (P(None, "cell", "grp", None), P("grp"), P(None, None, ("grp", "cell")))
    out_specs = P(None, ("grp", "cell"), None)
    return jax.shard_map(
        on_device, mesh=mesh, in_specs=in_specs, out_specs=out_specs, check_vma=False
    )
```

```python
import functools
import math

import jax
import jax.numpy as jnp
import numpy as np
from jax import lax
from jax.experimental import pallas as pl
from jax.experimental.pallas import tpu as pltpu
from jax.sharding import PartitionSpec as P

EPSILON = 1e-06
COSINE = (
    0.9999999999993376,
    -4.934802200431432,
    4.058712123240781,
    -1.3352627346923478,
    0.23533044681677665,
    -0.02580633847975355,
    0.0019285963125396874,
    -0.00010362767792380447,
    3.734915399663344e-06,
)
SLOTS = 32
LANES = 4 * SLOTS
COMPS = 3
NT = (((1,), (1,)), ((), ()))
TN = (((0,), (0,)), ((), ()))
VMEM_LIMIT = 40 * 1024 * 1024

PART = 32
FULL = 16


def inverse_table(samples, stations):
    bins = samples // 2
    turn = np.arange(bins)[:, None] * np.arange(samples)[None, :] % samples
    angle = turn * (2.0 * math.pi / samples)
    weight = np.where(np.arange(bins) == 0, 1.0, 2.0)[:, None] / samples
    weight = weight * math.sqrt(samples / (3.0 * stations))
    real, imag = weight * np.cos(angle), -weight * np.sin(angle)
    runs = [(at, PART) for at in range(0, bins // 2, PART)]
    runs += [(at, FULL) for at in range(bins // 2, bins, FULL)]
    rows = [part[at : at + run] for at, run in runs for part in (real, imag)]
    return np.concatenate(rows).astype(np.float32)


def forward_rows(bins, samples):
    count = bins.shape[0]
    sample = lax.broadcasted_iota(jnp.int32, (2 * count, samples), 1)
    turn = jnp.concatenate([bins * sample[:count], bins * sample[:count] + samples // 4]) % samples
    x = jnp.where(turn > samples // 2, turn - samples, turn).astype(jnp.float32) * (2.0 / samples)
    square = x * x
    value = jnp.full(square.shape, COSINE[-1], jnp.float32)
    for factor in COSINE[-2::-1]:
        value = value * square + factor
    return value.astype(jnp.bfloat16)


def place_of(place_ref, groups):
    position = place_ref[0]
    high, inner = position // (2 * groups), position % (2 * groups)
    return high * 2 + inner % 2, inner // 2


def listing_of(pairs_ref, lanes):
    ends = []
    for end in range(2):
        slots = pairs_ref[:, end, :].astype(jnp.float32)
        ends += [slots[:, at : at + lanes] for at in range(0, slots.shape[1], lanes)]
    return jnp.concatenate(ends)


def station_spectra(windows_ref, at, table):
    parts = []
    for comp in range(windows_ref.shape[0]):
        low = windows_ref[comp, 0, at]
        high = windows_ref[comp, 1, at]
        parts += [low[:SLOTS], high[SLOTS:], low[SLOTS:], high[:SLOTS]]
    traces = jnp.concatenate(parts)
    square = jnp.square(traces.astype(jnp.float32))
    square_hi = square.astype(jnp.bfloat16)
    square_lo = (square - square_hi.astype(jnp.float32)).astype(jnp.bfloat16)
    ones = jnp.ones((16, traces.shape[1]), jnp.bfloat16)
    energy = lax.dot_general(ones, square_hi, NT, preferred_element_type=jnp.float32)
    energy += lax.dot_general(ones, square_lo, NT, preferred_element_type=jnp.float32)
    scale = lax.rsqrt(energy[:1] + EPSILON)
    raw = lax.dot_general(table, traces, NT, preferred_element_type=jnp.float32)
    return (raw * scale).astype(jnp.bfloat16)


def own_kernel(place_ref, windows_ref, part_ref, full_ref, table_ref):
    groups, samples = windows_ref.shape[2], windows_ref.shape[4]
    quarter, group = place_of(place_ref, groups)
    bins = lax.broadcasted_iota(jnp.int32, (PART, samples), 0) + (quarter % 2) * PART
    table_ref[: 2 * PART] = forward_rows(bins, samples)
    for far in range(2):
        start = samples // 4 + (quarter ^ (2 * far)) * FULL
        bins = lax.broadcasted_iota(jnp.int32, (FULL, samples), 0) + start
        at = 2 * PART + 2 * FULL * far
        table_ref[at : at + 2 * FULL] = forward_rows(bins, samples)
    table = table_ref[...]
    for mg in range(groups):
        spectra = station_spectra(windows_ref, group ^ mg, table)
        for comp in range(COMPS):
            lanes = spectra[:, comp * LANES : (comp + 1) * LANES]
            part_ref[mg, comp * 2 * PART : (comp + 1) * 2 * PART] = lanes[: 2 * PART]
            for far in range(2):
                at = 2 * PART + 2 * FULL * far
                full_ref[far * groups + mg, comp * 2 * FULL : (comp + 1) * 2 * FULL] = lanes[at : at + 2 * FULL]


def near_spectra_kernel(
    place_ref, own_pairs_ref, near_pairs_ref, table_ref, part_ref, full_ref, windows_ref, *piece_refs
):
    groups = windows_ref.shape[2]
    _, group = place_of(place_ref, groups)
    table = table_ref[...]
    part_rows, full_rows = COMPS * 2 * PART, COMPS * 2 * FULL
    piece_refs[groups][2 * full_rows :] = jnp.concatenate(
        [listing_of(own_pairs_ref, LANES), listing_of(near_pairs_ref, LANES)]
    ).astype(jnp.bfloat16)
    for mg in range(groups):
        spectra = station_spectra(windows_ref, group ^ mg, table)
        side, cross = piece_refs[mg], piece_refs[groups + mg]
        side[:part_rows] = part_ref[mg]
        side[2 * part_rows : 2 * part_rows + full_rows] = full_ref[mg]
        cross[:full_rows] = full_ref[groups + mg]
        for comp in range(COMPS):
            lanes = spectra[:, comp * LANES : (comp + 1) * LANES]
            at = part_rows + comp * 2 * PART
            side[at : at + 2 * PART] = lanes[: 2 * PART]
            at = 2 * part_rows + full_rows + comp * 2 * FULL
            side[at : at + 2 * FULL] = lanes[2 * PART : 2 * PART + 2 * FULL]
            at = full_rows + comp * 2 * FULL
            cross[at : at + 2 * FULL] = lanes[2 * PART + 2 * FULL :]


def pick(place_ref, counts_ref, listed, flat_ref, bins, mq, *picked_refs):
    cells = counts_ref.shape[0]
    quarter, group = place_of(place_ref, cells // 4)
    own = quarter ^ mq
    high, low = own // 2, own % 2
    cell = high * (cells // 2) + group * 2 + low
    count = listed.shape[0] // 2
    runs = LANES // bins
    first, second = listed[:count].astype(jnp.int32), listed[count:].astype(jnp.int32)
    far_counts = [counts_ref[cell ^ 1], counts_ref[cell ^ (cells // 2)]]
    odd = lax.broadcasted_iota(jnp.int32, (count, LANES), 0) % 2
    live = (first < counts_ref[cell]) & (second < jnp.where(odd == 1, far_counts[1], far_counts[0]))
    left, right = jnp.where(high == low, first, second), jnp.where(high == low, second, first)
    spot = jnp.where(live, (left // runs) * SLOTS + right, -1)
    turned = jnp.concatenate([spot, left % runs]).T
    lane = lax.broadcasted_iota(jnp.int32, (LANES, LANES), 1)
    run = lane // bins
    spread = lax.broadcasted_iota(jnp.int32, (2 * LANES, LANES), 0)
    kept = lax.broadcasted_iota(jnp.int32, (2 * LANES, LANES), 1)
    sides = ((high, high), (low, 1 - low))
    found = []
    for step_round in range(2):
        hot = []
        for at in range(step_round, count, 2):
            offset = turned[:, at : at + 1] - lane
            hot.append(
                jnp.concatenate(
                    [
                        jnp.where(offset == start, 1.0, 0.0).astype(jnp.bfloat16)
                        for start in range(0, flat_ref.shape[2], LANES)
                    ],
                    axis=1,
                )
            )
        block = flat_ref[sides[step_round][0], sides[step_round][1]]
        wide = jnp.dot(jnp.concatenate(hot), block, preferred_element_type=jnp.float32)
        masked = []
        for chunk, at in enumerate(range(step_round, count, 2)):
            here = run == turned[:, count + at : count + at + 1]
            part = wide[chunk * LANES : (chunk + 1) * LANES]
            masked.append(
                jnp.concatenate(
                    [
                        jnp.where(here, part[:, :LANES], 0.0).astype(jnp.bfloat16),
                        jnp.where(here, part[:, LANES:], 0.0).astype(jnp.bfloat16),
                    ],
                    axis=1,
                )
            )
        found.append(jnp.concatenate(masked))
    found = jnp.concatenate(found, axis=1)
    packs = LANES // (4 * bins)
    held = found.shape[0] // packs
    picked = 0.0
    for pack in range(packs):
        folds = []
        for step_round in range(2):
            place = (pack * 4 + step_round * 2 + spread // LANES) * bins + spread % bins
            folds.append(jnp.where(kept == place, 1.0, 0.0).astype(jnp.bfloat16))
        picked += jnp.dot(
            found[pack * held : (pack + 1) * held],
            jnp.concatenate(folds),
            preferred_element_type=jnp.float32,
        )
    picked = picked.astype(jnp.bfloat16)
    each = held // len(picked_refs)
    for at, ref in enumerate(picked_refs):
        ref[...] = picked[at * each : (at + 1) * each]


def padded(traces):
    return -(-traces // 16) * 16


def add_cross(pieces, trace_ref, bins, sums_ref, before_ref=None):
    slots, rows = 2 * SLOTS, 2 * bins
    traces = trace_ref.shape[0] // rows
    start = 0
    for piece, at, size in pieces:
        trace_ref[start : start + size] = piece[at : at + size].astype(jnp.float32)
        start += size
    if start < traces * rows:
        trace_ref[start:] = jnp.zeros((traces * rows - start, LANES), jnp.float32)
    for k in range(bins):
        real = trace_ref[pl.ds(k, traces, stride=rows), :].astype(jnp.bfloat16)
        imag = trace_ref[pl.ds(bins + k, traces, stride=rows), :].astype(jnp.bfloat16)
        left = jnp.concatenate([real, imag], axis=0)[:, :slots]
        right = jnp.concatenate(
            [jnp.concatenate([real, imag], axis=1), jnp.concatenate([imag, -real], axis=1)], axis=0
        )
        cross = lax.dot_general(left, right, TN, preferred_element_type=jnp.float32)
        for part in range(2):
            at = (part * bins + k) * slots
            value = cross[:, part * LANES : (part + 1) * LANES]
            if before_ref is not None:
                value += before_ref[at : at + slots]
            sums_ref[at : at + slots] = value


def turn_blocks(cross_ref, bins, flat_ref):
    slots, runs = 2 * SLOTS, LANES // bins
    for own in range(2):
        for at in range(SLOTS // runs):
            for part in range(2):
                first = part * bins * slots + own * SLOTS + at * runs
                block = jnp.concatenate(
                    [cross_ref[pl.ds(first + i, bins, stride=slots), :] for i in range(runs)]
                ).T.astype(jnp.bfloat16)
                for far in range(2):
                    flat_ref[
                        own, far, at * SLOTS : (at + 1) * SLOTS, part * LANES : (part + 1) * LANES
                    ] = block[slots + far * SLOTS : slots + (far + 1) * SLOTS]


def side_part(ref):
    return (ref, 0, 2 * COMPS * 2 * PART)


def side_full(ref):
    return (ref, 2 * COMPS * 2 * PART, 2 * COMPS * 2 * FULL)


def cross_full(ref):
    return (ref, 0, 2 * COMPS * 2 * FULL)


def part_kernel(place_ref, counts_ref, listed_ref, *refs):
    piece_refs, (flat_ref, picked_0, picked_1, trace_ref, cross_ref) = refs[:-5], refs[-5:]
    add_cross([side_part(ref) for ref in piece_refs], trace_ref, PART, cross_ref)
    turn_blocks(cross_ref, PART, flat_ref)
    listed = listed_ref[cross_full(listed_ref)[2] :].astype(jnp.float32)
    listing = listed.shape[0] // 2
    pick(place_ref, counts_ref, listed[:listing], flat_ref, PART, 2, picked_0)
    pick(place_ref, counts_ref, listed[listing:], flat_ref, PART, 3, picked_1)


def early_kernel(sides, after_ref, *refs):
    piece_refs, (sums_ref, trace_ref) = refs[:-2], refs[-2:]
    pieces = [side_full(ref) for ref in piece_refs[:sides]] + [cross_full(ref) for ref in piece_refs[sides:]]
    add_cross(pieces, trace_ref, FULL, sums_ref)


def full_kernel(before_ref, *refs):
    piece_refs, (flat_ref, trace_ref, cross_ref) = refs[:-3], refs[-3:]
    add_cross([cross_full(ref) for ref in piece_refs], trace_ref, FULL, cross_ref, before_ref)
    turn_blocks(cross_ref, FULL, flat_ref)


def far_kernel(mq, place_ref, counts_ref, listed_ref, flat_ref, after_ref, picked_ref):
    listed = listed_ref[cross_full(listed_ref)[2] :].astype(jnp.float32)
    listing = listed.shape[0] // 2
    listed = listed[(mq % 2) * listing : (mq % 2 + 1) * listing]
    pick(place_ref, counts_ref, listed, flat_ref, FULL, mq, picked_ref)


def near_kernel(
    place_ref, counts_ref, own_pairs_ref, near_pairs_ref, part_ref, full_ref, part_0, full_0, full_1, *part_1
):
    listed = listing_of(near_pairs_ref, LANES)
    pick(place_ref, counts_ref, listed, part_ref, PART, 1, *part_1)
    pick(place_ref, counts_ref, listed, full_ref, FULL, 1, full_1)
    listed = listing_of(own_pairs_ref, LANES)
    pick(place_ref, counts_ref, listed, part_ref, PART, 0, part_0)
    pick(place_ref, counts_ref, listed, full_ref, FULL, 0, full_0)


def both_rounds(rows, sign):
    row = lax.broadcasted_iota(jnp.int32, rows.shape, 0)
    rows = rows * jnp.where(row < rows.shape[0] // 2, 1.0, sign)
    empty = jnp.zeros_like(rows)
    return jnp.concatenate(
        [jnp.concatenate([rows, empty], axis=1), jnp.concatenate([empty, rows], axis=1)]
    )


def halves(table):
    high = table.astype(jnp.bfloat16)
    return high, (table - high.astype(jnp.float32)).astype(jnp.bfloat16)


def first_lags_kernel(groups, place_ref, inverse_ref, *refs):
    part_0, part_2, part_3, full_0, full_1, *part_1, lags_ref, table_ref = refs
    count, held = part_0.shape[0], full_0.shape[0]
    part_1 = jnp.concatenate([ref[...] for ref in part_1])
    parts = [part_0[...], part_2[...], part_1, part_3[...]]
    full_refs = [full_0, full_1]
    samples = inverse_ref.shape[1]
    quarter, _ = place_of(place_ref, groups)
    low = quarter % 2
    sign = jnp.where(quarter // 2 == low, 1.0, -1.0)

    def part_table(which):
        start = pl.multiple_of((low ^ which) * 2 * PART, 2 * PART)
        return both_rounds(inverse_ref[pl.ds(start, 2 * PART), :], sign)

    def full_table(mq):
        start = pl.multiple_of(samples // 2 + (quarter ^ mq) * 2 * FULL, 2 * FULL)
        return both_rounds(inverse_ref[pl.ds(start, 2 * FULL), :], sign)

    near, other = halves(part_table(0)), halves(part_table(1))
    picked = jnp.concatenate(parts, axis=1)
    lags = 0.0
    for which in range(2):
        table = jnp.concatenate([near[which], near[which], other[which], other[which]])
        lags += jnp.dot(picked, table, preferred_element_type=jnp.float32)
    packs = count // held
    here = [halves(full_table(m)) for m in (0, 1)]
    away = [halves(full_table(m)) for m in (2, 3)]
    picked = jnp.concatenate([ref[...] for ref in full_refs], axis=1)
    for pack in range(packs):
        more = 0.0
        for which in range(2):
            def placed(table):
                empty = jnp.zeros_like(table)
                return jnp.concatenate([table if at == pack else empty for at in range(packs)])

            more += jnp.dot(
                picked,
                jnp.concatenate([placed(table[which]) for table in here]),
                preferred_element_type=jnp.float32,
            )
            table_ref[pack, which] = jnp.concatenate([placed(table[which]) for table in away])
        total = lags[pack * held : (pack + 1) * held] + more
        for step_round in range(2):
            lags_ref[step_round, pack * held : (pack + 1) * held] = total[
                :, step_round * samples : (step_round + 1) * samples
            ]


def lag_kernel(first_ref, table_ref, *refs):
    picked_refs, lags_ref = refs[:-1], refs[-1]
    samples = lags_ref.shape[2]
    held = picked_refs[0].shape[0]
    picked = jnp.concatenate([ref[...] for ref in picked_refs], axis=1)
    for pack in range(table_ref.shape[0]):
        more = jnp.dot(picked, table_ref[pack, 0], preferred_element_type=jnp.float32)
        more += jnp.dot(picked, table_ref[pack, 1], preferred_element_type=jnp.float32)
        for step_round in range(2):
            lags_ref[step_round, pack * held : (pack + 1) * held] = (
                first_ref[step_round, pack * held : (pack + 1) * held]
                + more[:, step_round * samples : (step_round + 1) * samples]
            )


def on_device(windows, counts, pairs):
    comps, _, events, samples = windows.shape
    cells = lax.axis_size("cell")
    half, groups = cells // 2, cells // 4
    count = pairs.shape[2]
    inverse = jnp.asarray(inverse_table(samples, cells))
    place = lax.axis_index("cell").astype(jnp.int32).reshape(1)

    def swap(x, mask):
        return lax.ppermute(x, "cell", [(i, i ^ mask) for i in range(cells)])

    def shape(*dims, dtype=jnp.bfloat16):
        return jax.ShapeDtypeStruct(dims, dtype)

    vmem = pl.BlockSpec(memory_space=pltpu.VMEM)
    smem = pl.BlockSpec(memory_space=pltpu.SMEM)
    params = pltpu.CompilerParams(vmem_limit_bytes=VMEM_LIMIT)

    def cost(microseconds):
        return pl.CostEstimate(
            flops=int(microseconds * 1e9), bytes_accessed=2**20, transcendentals=0
        )

    windows = windows.reshape(comps, 2, groups, 2 * SLOTS, samples)
    near_windows, near_pairs = swap(windows, 1), swap(pairs, 1)
    part_rows, full_rows = comps * 2 * PART, comps * 2 * FULL
    part_spectra, full_spectra, table = pl.pallas_call(
        own_kernel,
        out_shape=[
            shape(groups, part_rows, LANES),
            shape(2 * groups, full_rows, LANES),
            shape(2 * PART + 4 * FULL, samples),
        ],
        in_specs=[smem, vmem],
        out_specs=[vmem] * 3,
        compiler_params=params,
        cost_estimate=cost(1),
        name="own_spectra",
    )(place, windows)
    listing = 2 * pairs.size // LANES
    pieces = pl.pallas_call(
        near_spectra_kernel,
        out_shape=[shape(2 * (part_rows + full_rows), LANES)] * groups
        + [shape(2 * full_rows + listing * (mg == 0), LANES) for mg in range(groups)],
        in_specs=[smem] + [vmem] * 6,
        out_specs=[vmem] * (2 * groups),
        compiler_params=params,
        cost_estimate=cost(1),
        name="near_spectra",
    )(place, pairs, near_pairs, table, part_spectra, full_spectra, near_windows)
    arrived = [pieces[0]] + [swap(pieces[m], 2 * m) for m in range(1, 2 * groups)]
    sides, far = arrived[:groups], arrived[groups:]

    part_flat, part_2, part_3 = pl.pallas_call(
        part_kernel,
        out_shape=[shape(2, 2, SLOTS * SLOTS * PART // LANES, 2 * LANES)] + [shape(count, 4 * PART)] * 2,
        in_specs=[smem, smem] + [vmem] * (1 + groups),
        out_specs=[vmem] * 3,
        scratch_shapes=[
            pltpu.VMEM((padded(groups * 2 * comps) * 2 * PART, LANES), jnp.float32),
            pltpu.VMEM((2 * SLOTS * 2 * PART, LANES), jnp.float32),
        ],
        compiler_params=params,
        cost_estimate=cost(4),
        name="part",
    )(place, counts, far[0], *sides)
    part_2, part_3 = swap(part_2, half), swap(part_3, half + 1)
    packed = count * 4 * FULL // LANES
    early, late = far[: groups - 2], far[groups - 2 :]
    sums = pl.pallas_call(
        functools.partial(early_kernel, groups),
        out_shape=shape(2 * SLOTS * 2 * FULL, LANES, dtype=jnp.float32),
        in_specs=[pl.BlockSpec(memory_space=pl.ANY)] + [vmem] * (groups + len(early)),
        out_specs=vmem,
        scratch_shapes=[
            pltpu.VMEM((padded((groups + len(early)) * 2 * comps) * 2 * FULL, LANES), jnp.float32)
        ],
        compiler_params=params,
        cost_estimate=cost(0.001),
        name="early",
    )(part_flat, *sides, *early)
    full_flat = pl.pallas_call(
        full_kernel,
        out_shape=shape(2, 2, SLOTS * SLOTS * FULL // LANES, 2 * LANES),
        in_specs=[vmem] * (1 + len(late)),
        out_specs=vmem,
        scratch_shapes=[
            pltpu.VMEM((padded(len(late) * 2 * comps) * 2 * FULL, LANES), jnp.float32),
            pltpu.VMEM((2 * SLOTS * 2 * FULL, LANES), jnp.float32),
        ],
        compiler_params=params,
        cost_estimate=cost(10),
        name="full",
    )(sums, *late)
    part_0, full_0, *near = pl.pallas_call(
        near_kernel,
        out_shape=[shape(count, LANES)] + [shape(packed, LANES)] * 2 + [shape(count // 2, LANES)] * 2,
        in_specs=[smem, smem] + [vmem] * 4,
        out_specs=[vmem] * 5,
        compiler_params=params,
        cost_estimate=cost(0.001),
        name="near",
    )(place, counts, pairs, near_pairs, part_flat, full_flat)
    near = [swap(x, 1) for x in near]

    def far_full(mq, after):
        picked = pl.pallas_call(
            functools.partial(far_kernel, mq),
            out_shape=shape(packed, LANES),
            in_specs=[smem, smem, vmem, vmem, pl.BlockSpec(memory_space=pl.ANY)],
            out_specs=vmem,
            compiler_params=params,
            cost_estimate=cost(0.001),
            name=f"far_{mq}",
        )(place, counts, far[0], full_flat, after)
        return swap(picked, half + mq % 2)

    full_2, full_3 = far_full(2, part_2), far_full(3, part_3)

    first, tables = pl.pallas_call(
        functools.partial(first_lags_kernel, groups),
        out_shape=[
            shape(2, count, samples, dtype=jnp.float32),
            shape(count // packed, 2, 2 * LANES, 2 * samples),
        ],
        in_specs=[smem] + [vmem] * 8,
        out_specs=[vmem] * 2,
        compiler_params=params,
        cost_estimate=cost(0.001),
        name="first_lags",
    )(place, inverse, part_0, part_2, part_3, full_0, *near)
    return pl.pallas_call(
        lag_kernel,
        out_shape=shape(2, count, samples, dtype=jnp.float32),
        in_specs=[vmem] * 4,
        out_specs=vmem,
        compiler_params=params,
        cost_estimate=cost(1),
        name="lags",
    )(first, tables, full_2, full_3)


def solution(mesh):
    in_specs = (P(None, "cell", "grp", None), P("grp"), P(None, None, ("grp", "cell")))
    out_specs = P(None, ("grp", "cell"), None)
    return jax.shard_map(
        on_device, mesh=mesh, in_specs=in_specs, out_specs=out_specs, check_vma=False
    )
```

```python
import functools
import math

import jax
import jax.numpy as jnp
import numpy as np
from jax import lax
from jax.experimental import pallas as pl
from jax.experimental.pallas import tpu as pltpu
from jax.sharding import PartitionSpec as P

EPSILON = 1e-06
COSINE = (
    0.9999999999993376,
    -4.934802200431432,
    4.058712123240781,
    -1.3352627346923478,
    0.23533044681677665,
    -0.02580633847975355,
    0.0019285963125396874,
    -0.00010362767792380447,
    3.734915399663344e-06,
)
SLOTS = 32
LANES = 4 * SLOTS
COMPS = 3
NT = (((1,), (1,)), ((), ()))
TN = (((0,), (0,)), ((), ()))
VMEM_LIMIT = 40 * 1024 * 1024

PART = 32
FULL = 16


def inverse_table(samples, stations):
    bins = samples // 2
    turn = np.arange(bins)[:, None] * np.arange(samples)[None, :] % samples
    angle = turn * (2.0 * math.pi / samples)
    weight = np.where(np.arange(bins) == 0, 1.0, 2.0)[:, None] / samples
    weight = weight * math.sqrt(samples / (3.0 * stations))
    real, imag = weight * np.cos(angle), -weight * np.sin(angle)
    runs = [(at, PART) for at in range(0, bins // 2, PART)]
    runs += [(at, FULL) for at in range(bins // 2, bins, FULL)]
    rows = [part[at : at + run] for at, run in runs for part in (real, imag)]
    return np.concatenate(rows).astype(np.float32)


def forward_rows(bins, samples):
    count = bins.shape[0]
    sample = lax.broadcasted_iota(jnp.int32, (2 * count, samples), 1)
    turn = jnp.concatenate([bins * sample[:count], bins * sample[:count] + samples // 4])
    turn &= samples - 1
    x = jnp.where(turn > samples // 2, turn - samples, turn).astype(jnp.float32) * (2.0 / samples)
    square = x * x
    value = jnp.full(square.shape, COSINE[-1], jnp.float32)
    for factor in COSINE[-2::-1]:
        value = value * square + factor
    return value.astype(jnp.bfloat16)


def place_of(place_ref, groups):
    position = place_ref[0]
    high, inner = position // (2 * groups), position % (2 * groups)
    return high * 2 + inner % 2, inner // 2


def listing_of(pairs_ref, lanes):
    ends = []
    for end in range(2):
        slots = pairs_ref[:, end, :].astype(jnp.float32)
        ends += [slots[:, at : at + lanes] for at in range(0, slots.shape[1], lanes)]
    return jnp.concatenate(ends)


def station_spectra(windows_ref, at, table):
    parts = []
    for comp in range(windows_ref.shape[0]):
        low = windows_ref[comp, 0, at]
        high = windows_ref[comp, 1, at]
        parts += [low[:SLOTS], high[SLOTS:], low[SLOTS:], high[:SLOTS]]
    traces = jnp.concatenate(parts)
    square = jnp.square(traces.astype(jnp.float32))
    square_hi = square.astype(jnp.bfloat16)
    square_lo = (square - square_hi.astype(jnp.float32)).astype(jnp.bfloat16)
    ones = jnp.ones((16, traces.shape[1]), jnp.bfloat16)
    energy = lax.dot_general(ones, square_hi, NT, preferred_element_type=jnp.float32)
    energy += lax.dot_general(ones, square_lo, NT, preferred_element_type=jnp.float32)
    scale = lax.rsqrt(energy[:1] + EPSILON)
    raw = lax.dot_general(table, traces, NT, preferred_element_type=jnp.float32)
    return (raw * scale).astype(jnp.bfloat16)


def own_kernel(place_ref, windows_ref, part_ref, full_ref, table_ref):
    groups, samples = windows_ref.shape[2], windows_ref.shape[4]
    quarter, group = place_of(place_ref, groups)
    bins = lax.broadcasted_iota(jnp.int32, (PART, samples), 0) + (quarter % 2) * PART
    table_ref[: 2 * PART] = forward_rows(bins, samples)
    for far in range(2):
        start = samples // 4 + (quarter ^ (2 * far)) * FULL
        bins = lax.broadcasted_iota(jnp.int32, (FULL, samples), 0) + start
        at = 2 * PART + 2 * FULL * far
        table_ref[at : at + 2 * FULL] = forward_rows(bins, samples)
    table = table_ref[...]
    for mg in range(groups):
        spectra = station_spectra(windows_ref, group ^ mg, table)
        for comp in range(COMPS):
            lanes = spectra[:, comp * LANES : (comp + 1) * LANES]
            part_ref[mg, comp * 2 * PART : (comp + 1) * 2 * PART] = lanes[: 2 * PART]
            for far in range(2):
                at = 2 * PART + 2 * FULL * far
                full_ref[far * groups + mg, comp * 2 * FULL : (comp + 1) * 2 * FULL] = lanes[at : at + 2 * FULL]


def near_spectra_kernel(
    place_ref, own_pairs_ref, near_pairs_ref, table_ref, part_ref, full_ref, windows_ref, *piece_refs
):
    groups = windows_ref.shape[2]
    _, group = place_of(place_ref, groups)
    table = table_ref[...]
    part_rows, full_rows = COMPS * 2 * PART, COMPS * 2 * FULL
    piece_refs[groups][2 * full_rows :] = jnp.concatenate(
        [listing_of(own_pairs_ref, LANES), listing_of(near_pairs_ref, LANES)]
    ).astype(jnp.bfloat16)
    for mg in range(groups):
        spectra = station_spectra(windows_ref, group ^ mg, table)
        side, cross = piece_refs[mg], piece_refs[groups + mg]
        side[:part_rows] = part_ref[mg]
        side[2 * part_rows : 2 * part_rows + full_rows] = full_ref[mg]
        cross[:full_rows] = full_ref[groups + mg]
        for comp in range(COMPS):
            lanes = spectra[:, comp * LANES : (comp + 1) * LANES]
            at = part_rows + comp * 2 * PART
            side[at : at + 2 * PART] = lanes[: 2 * PART]
            at = 2 * part_rows + full_rows + comp * 2 * FULL
            side[at : at + 2 * FULL] = lanes[2 * PART : 2 * PART + 2 * FULL]
            at = full_rows + comp * 2 * FULL
            cross[at : at + 2 * FULL] = lanes[2 * PART + 2 * FULL :]


def pick(place_ref, counts_ref, listed, flat_ref, bins, mq, *picked_refs):
    cells = counts_ref.shape[0]
    quarter, group = place_of(place_ref, cells // 4)
    own = quarter ^ mq
    high, low = own // 2, own % 2
    cell = high * (cells // 2) + group * 2 + low
    count = listed.shape[0] // 2
    runs = LANES // bins
    run_bits, bin_bits, lane_bits = (n.bit_length() - 1 for n in (runs, bins, LANES))
    first, second = listed[:count].astype(jnp.int32), listed[count:].astype(jnp.int32)
    far_counts = [counts_ref[cell ^ 1], counts_ref[cell ^ (cells // 2)]]
    odd = lax.broadcasted_iota(jnp.int32, (count, LANES), 0) & 1
    live = (first < counts_ref[cell]) & (second < jnp.where(odd == 1, far_counts[1], far_counts[0]))
    left, right = jnp.where(high == low, first, second), jnp.where(high == low, second, first)
    spot = jnp.where(live, (left >> run_bits) * SLOTS + right, -1)
    turned = jnp.concatenate([spot, left & (runs - 1)]).T
    lane = lax.broadcasted_iota(jnp.int32, (LANES, LANES), 1)
    run = lane >> bin_bits
    spread = lax.broadcasted_iota(jnp.int32, (2 * LANES, LANES), 0)
    kept = lax.broadcasted_iota(jnp.int32, (2 * LANES, LANES), 1)
    sides = ((high, high), (low, 1 - low))
    found = []
    for step_round in range(2):
        hot = []
        for at in range(step_round, count, 2):
            offset = turned[:, at : at + 1] - lane
            hot.append(
                jnp.concatenate(
                    [
                        jnp.where(offset == start, 1.0, 0.0).astype(jnp.bfloat16)
                        for start in range(0, flat_ref.shape[2], LANES)
                    ],
                    axis=1,
                )
            )
        block = flat_ref[sides[step_round][0], sides[step_round][1]]
        wide = jnp.dot(jnp.concatenate(hot), block, preferred_element_type=jnp.float32)
        masked = []
        for chunk, at in enumerate(range(step_round, count, 2)):
            here = run == turned[:, count + at : count + at + 1]
            part = wide[chunk * LANES : (chunk + 1) * LANES]
            masked.append(
                jnp.concatenate(
                    [
                        jnp.where(here, part[:, :LANES], 0.0).astype(jnp.bfloat16),
                        jnp.where(here, part[:, LANES:], 0.0).astype(jnp.bfloat16),
                    ],
                    axis=1,
                )
            )
        found.append(jnp.concatenate(masked))
    found = jnp.concatenate(found, axis=1)
    packs = LANES // (4 * bins)
    held = found.shape[0] // packs
    picked = 0.0
    for pack in range(packs):
        folds = []
        for step_round in range(2):
            place = (pack * 4 + step_round * 2 + (spread >> lane_bits)) * bins + (spread & (bins - 1))
            folds.append(jnp.where(kept == place, 1.0, 0.0).astype(jnp.bfloat16))
        picked += jnp.dot(
            found[pack * held : (pack + 1) * held],
            jnp.concatenate(folds),
            preferred_element_type=jnp.float32,
        )
    picked = picked.astype(jnp.bfloat16)
    each = held // len(picked_refs)
    for at, ref in enumerate(picked_refs):
        ref[...] = picked[at * each : (at + 1) * each]


def padded(traces):
    return -(-traces // 16) * 16


def add_cross(pieces, trace_ref, bins, sums_ref, before_ref=None):
    slots, rows = 2 * SLOTS, 2 * bins
    traces = trace_ref.shape[0] // rows
    start = 0
    for piece, at, size in pieces:
        trace_ref[start : start + size] = piece[at : at + size].astype(jnp.float32)
        start += size
    if start < traces * rows:
        trace_ref[start:] = jnp.zeros((traces * rows - start, LANES), jnp.float32)
    for k in range(bins):
        real = trace_ref[pl.ds(k, traces, stride=rows), :].astype(jnp.bfloat16)
        imag = trace_ref[pl.ds(bins + k, traces, stride=rows), :].astype(jnp.bfloat16)
        left = jnp.concatenate([real, imag], axis=0)[:, :slots]
        right = jnp.concatenate(
            [jnp.concatenate([real, imag], axis=1), jnp.concatenate([imag, -real], axis=1)], axis=0
        )
        cross = lax.dot_general(left, right, TN, preferred_element_type=jnp.float32)
        for part in range(2):
            at = (part * bins + k) * slots
            value = cross[:, part * LANES : (part + 1) * LANES]
            if before_ref is not None:
                value += before_ref[at : at + slots]
            sums_ref[at : at + slots] = value


def turn_blocks(cross_ref, bins, flat_ref):
    slots, runs = 2 * SLOTS, LANES // bins
    for own in range(2):
        for at in range(SLOTS // runs):
            for part in range(2):
                first = part * bins * slots + own * SLOTS + at * runs
                block = jnp.concatenate(
                    [cross_ref[pl.ds(first + i, bins, stride=slots), :] for i in range(runs)]
                ).T.astype(jnp.bfloat16)
                for far in range(2):
                    flat_ref[
                        own, far, at * SLOTS : (at + 1) * SLOTS, part * LANES : (part + 1) * LANES
                    ] = block[slots + far * SLOTS : slots + (far + 1) * SLOTS]


def side_part(ref):
    return (ref, 0, 2 * COMPS * 2 * PART)


def side_full(ref):
    return (ref, 2 * COMPS * 2 * PART, 2 * COMPS * 2 * FULL)


def cross_full(ref):
    return (ref, 0, 2 * COMPS * 2 * FULL)


def part_kernel(place_ref, counts_ref, listed_ref, *refs):
    piece_refs, (flat_ref, picked_0, picked_1, trace_ref, cross_ref) = refs[:-5], refs[-5:]
    add_cross([side_part(ref) for ref in piece_refs], trace_ref, PART, cross_ref)
    turn_blocks(cross_ref, PART, flat_ref)
    listed = listed_ref[cross_full(listed_ref)[2] :].astype(jnp.float32)
    listing = listed.shape[0] // 2
    pick(place_ref, counts_ref, listed[:listing], flat_ref, PART, 2, picked_0)
    pick(place_ref, counts_ref, listed[listing:], flat_ref, PART, 3, picked_1)


def early_kernel(sides, after_ref, *refs):
    piece_refs, (sums_ref, trace_ref) = refs[:-2], refs[-2:]
    pieces = [side_full(ref) for ref in piece_refs[:sides]] + [cross_full(ref) for ref in piece_refs[sides:]]
    add_cross(pieces, trace_ref, FULL, sums_ref)


def full_kernel(place_ref, counts_ref, listed_ref, before_ref, *refs):
    piece_refs, (flat_ref, picked_0, picked_1, trace_ref, cross_ref) = refs[:-5], refs[-5:]
    add_cross([cross_full(ref) for ref in piece_refs], trace_ref, FULL, cross_ref, before_ref)
    turn_blocks(cross_ref, FULL, flat_ref)
    listed = listed_ref[cross_full(listed_ref)[2] :].astype(jnp.float32)
    listing = listed.shape[0] // 2
    pick(place_ref, counts_ref, listed[:listing], flat_ref, FULL, 2, picked_0)
    pick(place_ref, counts_ref, listed[listing:], flat_ref, FULL, 3, picked_1)


def near_kernel(
    place_ref, counts_ref, own_pairs_ref, near_pairs_ref, part_ref, full_ref, part_0, full_0, full_1, *part_1
):
    listed = listing_of(near_pairs_ref, LANES)
    pick(place_ref, counts_ref, listed, part_ref, PART, 1, *part_1)
    pick(place_ref, counts_ref, listed, full_ref, FULL, 1, full_1)
    listed = listing_of(own_pairs_ref, LANES)
    pick(place_ref, counts_ref, listed, part_ref, PART, 0, part_0)
    pick(place_ref, counts_ref, listed, full_ref, FULL, 0, full_0)


def both_rounds(rows, sign):
    row = lax.broadcasted_iota(jnp.int32, rows.shape, 0)
    rows = rows * jnp.where(row < rows.shape[0] // 2, 1.0, sign)
    empty = jnp.zeros_like(rows)
    return jnp.concatenate(
        [jnp.concatenate([rows, empty], axis=1), jnp.concatenate([empty, rows], axis=1)]
    )


def halves(table):
    high = table.astype(jnp.bfloat16)
    return high, (table - high.astype(jnp.float32)).astype(jnp.bfloat16)


def first_lags_kernel(groups, place_ref, inverse_ref, *refs):
    part_0, part_2, part_3, full_0, full_1, *part_1, lags_ref, table_ref = refs
    count, held = part_0.shape[0], full_0.shape[0]
    part_1 = jnp.concatenate([ref[...] for ref in part_1])
    parts = [part_0[...], part_2[...], part_1, part_3[...]]
    full_refs = [full_0, full_1]
    samples = inverse_ref.shape[1]
    quarter, _ = place_of(place_ref, groups)
    low = quarter % 2
    sign = jnp.where(quarter // 2 == low, 1.0, -1.0)

    def part_table(which):
        start = pl.multiple_of((low ^ which) * 2 * PART, 2 * PART)
        return both_rounds(inverse_ref[pl.ds(start, 2 * PART), :], sign)

    def full_table(mq):
        start = pl.multiple_of(samples // 2 + (quarter ^ mq) * 2 * FULL, 2 * FULL)
        return both_rounds(inverse_ref[pl.ds(start, 2 * FULL), :], sign)

    near, other = halves(part_table(0)), halves(part_table(1))
    picked = jnp.concatenate(parts, axis=1)
    lags = 0.0
    for which in range(2):
        table = jnp.concatenate([near[which], near[which], other[which], other[which]])
        lags += jnp.dot(picked, table, preferred_element_type=jnp.float32)
    packs = count // held
    here = [halves(full_table(m)) for m in (0, 1)]
    away = [halves(full_table(m)) for m in (2, 3)]
    picked = jnp.concatenate([ref[...] for ref in full_refs], axis=1)
    for pack in range(packs):
        more = 0.0
        for which in range(2):
            def placed(table):
                empty = jnp.zeros_like(table)
                return jnp.concatenate([table if at == pack else empty for at in range(packs)])

            more += jnp.dot(
                picked,
                jnp.concatenate([placed(table[which]) for table in here]),
                preferred_element_type=jnp.float32,
            )
            table_ref[pack, which] = jnp.concatenate([placed(table[which]) for table in away])
        total = lags[pack * held : (pack + 1) * held] + more
        for step_round in range(2):
            lags_ref[step_round, pack * held : (pack + 1) * held] = total[
                :, step_round * samples : (step_round + 1) * samples
            ]


def lag_kernel(first_ref, table_ref, *refs):
    picked_refs, lags_ref = refs[:-1], refs[-1]
    samples = lags_ref.shape[2]
    held = picked_refs[0].shape[0]
    picked = jnp.concatenate([ref[...] for ref in picked_refs], axis=1)
    for pack in range(table_ref.shape[0]):
        more = jnp.dot(picked, table_ref[pack, 0], preferred_element_type=jnp.float32)
        more += jnp.dot(picked, table_ref[pack, 1], preferred_element_type=jnp.float32)
        for step_round in range(2):
            lags_ref[step_round, pack * held : (pack + 1) * held] = (
                first_ref[step_round, pack * held : (pack + 1) * held]
                + more[:, step_round * samples : (step_round + 1) * samples]
            )


def on_device(windows, counts, pairs):
    comps, _, events, samples = windows.shape
    cells = lax.axis_size("cell")
    half, groups = cells // 2, cells // 4
    count = pairs.shape[2]
    inverse = jnp.asarray(inverse_table(samples, cells))
    place = lax.axis_index("cell").astype(jnp.int32).reshape(1)

    def swap(x, mask):
        return lax.ppermute(x, "cell", [(i, i ^ mask) for i in range(cells)])

    def shape(*dims, dtype=jnp.bfloat16):
        return jax.ShapeDtypeStruct(dims, dtype)

    vmem = pl.BlockSpec(memory_space=pltpu.VMEM)
    smem = pl.BlockSpec(memory_space=pltpu.SMEM)
    params = pltpu.CompilerParams(vmem_limit_bytes=VMEM_LIMIT)

    def cost(microseconds):
        return pl.CostEstimate(
            flops=int(microseconds * 1e9), bytes_accessed=2**20, transcendentals=0
        )

    windows = windows.reshape(comps, 2, groups, 2 * SLOTS, samples)
    near_windows, near_pairs = swap(windows, 1), swap(pairs, 1)
    part_rows, full_rows = comps * 2 * PART, comps * 2 * FULL
    part_spectra, full_spectra, table = pl.pallas_call(
        own_kernel,
        out_shape=[
            shape(groups, part_rows, LANES),
            shape(2 * groups, full_rows, LANES),
            shape(2 * PART + 4 * FULL, samples),
        ],
        in_specs=[smem, vmem],
        out_specs=[vmem] * 3,
        compiler_params=params,
        cost_estimate=cost(1),
        name="own_spectra",
    )(place, windows)
    listing = 2 * pairs.size // LANES
    pieces = pl.pallas_call(
        near_spectra_kernel,
        out_shape=[shape(2 * (part_rows + full_rows), LANES)] * groups
        + [shape(2 * full_rows + listing * (mg == 0), LANES) for mg in range(groups)],
        in_specs=[smem] + [vmem] * 6,
        out_specs=[vmem] * (2 * groups),
        compiler_params=params,
        cost_estimate=cost(1),
        name="near_spectra",
    )(place, pairs, near_pairs, table, part_spectra, full_spectra, near_windows)
    arrived = [pieces[0]] + [swap(pieces[m], 2 * m) for m in range(1, 2 * groups)]
    sides, far = arrived[:groups], arrived[groups:]

    part_flat, part_2, part_3 = pl.pallas_call(
        part_kernel,
        out_shape=[shape(2, 2, SLOTS * SLOTS * PART // LANES, 2 * LANES)] + [shape(count, 4 * PART)] * 2,
        in_specs=[smem, smem] + [vmem] * (1 + groups),
        out_specs=[vmem] * 3,
        scratch_shapes=[
            pltpu.VMEM((padded(groups * 2 * comps) * 2 * PART, LANES), jnp.float32),
            pltpu.VMEM((2 * SLOTS * 2 * PART, LANES), jnp.float32),
        ],
        compiler_params=params,
        cost_estimate=cost(4),
        name="part",
    )(place, counts, far[0], *sides)
    part_2, part_3 = swap(part_2, half), swap(part_3, half + 1)
    packed = count * 4 * FULL // LANES
    early, late = far[: groups - 2], far[groups - 2 :]
    sums = pl.pallas_call(
        functools.partial(early_kernel, groups),
        out_shape=shape(2 * SLOTS * 2 * FULL, LANES, dtype=jnp.float32),
        in_specs=[pl.BlockSpec(memory_space=pl.ANY)] + [vmem] * (groups + len(early)),
        out_specs=vmem,
        scratch_shapes=[
            pltpu.VMEM((padded((groups + len(early)) * 2 * comps) * 2 * FULL, LANES), jnp.float32)
        ],
        compiler_params=params,
        cost_estimate=cost(0.001),
        name="early",
    )(part_flat, *sides, *early)
    full_flat, full_2, full_3 = pl.pallas_call(
        full_kernel,
        out_shape=[shape(2, 2, SLOTS * SLOTS * FULL // LANES, 2 * LANES)] + [shape(packed, LANES)] * 2,
        in_specs=[smem, smem] + [vmem] * (2 + len(late)),
        out_specs=[vmem] * 3,
        scratch_shapes=[
            pltpu.VMEM((padded(len(late) * 2 * comps) * 2 * FULL, LANES), jnp.float32),
            pltpu.VMEM((2 * SLOTS * 2 * FULL, LANES), jnp.float32),
        ],
        compiler_params=params,
        cost_estimate=cost(10),
        name="full",
    )(place, counts, far[0], sums, *late)
    full_2, full_3 = swap(full_2, half), swap(full_3, half + 1)
    part_0, full_0, *near = pl.pallas_call(
        near_kernel,
        out_shape=[shape(count, LANES)] + [shape(packed, LANES)] * 2 + [shape(count // 2, LANES)] * 2,
        in_specs=[smem, smem] + [vmem] * 4,
        out_specs=[vmem] * 5,
        compiler_params=params,
        cost_estimate=cost(0.5),
        name="near",
    )(place, counts, pairs, near_pairs, part_flat, full_flat)
    near = [swap(x, 1) for x in near]

    first, tables = pl.pallas_call(
        functools.partial(first_lags_kernel, groups),
        out_shape=[
            shape(2, count, samples, dtype=jnp.float32),
            shape(count // packed, 2, 2 * LANES, 2 * samples),
        ],
        in_specs=[smem] + [vmem] * 8,
        out_specs=[vmem] * 2,
        compiler_params=params,
        cost_estimate=cost(0.001),
        name="first_lags",
    )(place, inverse, part_0, part_2, part_3, full_0, *near)
    return pl.pallas_call(
        lag_kernel,
        out_shape=shape(2, count, samples, dtype=jnp.float32),
        in_specs=[vmem] * 4,
        out_specs=vmem,
        compiler_params=params,
        cost_estimate=cost(1),
        name="lags",
    )(first, tables, full_2, full_3)


def solution(mesh):
    in_specs = (P(None, "cell", "grp", None), P("grp"), P(None, None, ("grp", "cell")))
    out_specs = P(None, ("grp", "cell"), None)
    return jax.shard_map(
        on_device, mesh=mesh, in_specs=in_specs, out_specs=out_specs, check_vma=False
    )
```

```python
import functools
import math

import jax
import jax.numpy as jnp
import numpy as np
from jax import lax
from jax.experimental import pallas as pl
from jax.experimental.pallas import tpu as pltpu
from jax.sharding import PartitionSpec as P

EPSILON = 1e-06
COSINE = (
    0.9999999999993376,
    -4.934802200431432,
    4.058712123240781,
    -1.3352627346923478,
    0.23533044681677665,
    -0.02580633847975355,
    0.0019285963125396874,
    -0.00010362767792380447,
    3.734915399663344e-06,
)
SLOTS = 32
LANES = 4 * SLOTS
COMPS = 3
NT = (((1,), (1,)), ((), ()))
TN = (((0,), (0,)), ((), ()))
VMEM_LIMIT = 40 * 1024 * 1024

PART = 16
FULL = 24


def inverse_table(samples, stations):
    bins = samples // 2
    turn = np.arange(bins)[:, None] * np.arange(samples)[None, :] % samples
    angle = turn * (2.0 * math.pi / samples)
    weight = np.where(np.arange(bins) == 0, 1.0, 2.0)[:, None] / samples
    weight = weight * math.sqrt(samples / (3.0 * stations))
    real, imag = weight * np.cos(angle), -weight * np.sin(angle)
    runs = [(at, PART) for at in range(0, 2 * PART, PART)]
    runs += [(at, FULL) for at in range(2 * PART, bins, FULL)]
    rows = [part[at : at + run] for at, run in runs for part in (real, imag)]
    return np.concatenate(rows).astype(np.float32)


def forward_rows(bins, samples):
    count = bins.shape[0]
    sample = lax.broadcasted_iota(jnp.int32, (2 * count, samples), 1)
    turn = jnp.concatenate([bins * sample[:count], bins * sample[:count] + samples // 4])
    turn &= samples - 1
    x = jnp.where(turn > samples // 2, turn - samples, turn).astype(jnp.float32) * (2.0 / samples)
    square = x * x
    value = jnp.full(square.shape, COSINE[-1], jnp.float32)
    for factor in COSINE[-2::-1]:
        value = value * square + factor
    return value.astype(jnp.bfloat16)


def place_of(place_ref, groups):
    position = place_ref[0]
    high, inner = position // (2 * groups), position % (2 * groups)
    return high * 2 + inner % 2, inner // 2


def listing_of(pairs_ref, lanes):
    ends = []
    for end in range(2):
        slots = pairs_ref[:, end, :].astype(jnp.float32)
        ends += [slots[:, at : at + lanes] for at in range(0, slots.shape[1], lanes)]
    return jnp.concatenate(ends)


def station_spectra(windows_ref, at, table):
    parts = []
    for comp in range(windows_ref.shape[0]):
        low = windows_ref[comp, 0, at]
        high = windows_ref[comp, 1, at]
        parts += [low[:SLOTS], high[SLOTS:], low[SLOTS:], high[:SLOTS]]
    traces = jnp.concatenate(parts)
    square = jnp.square(traces.astype(jnp.float32))
    square_hi = square.astype(jnp.bfloat16)
    square_lo = (square - square_hi.astype(jnp.float32)).astype(jnp.bfloat16)
    ones = jnp.ones((16, traces.shape[1]), jnp.bfloat16)
    energy = lax.dot_general(ones, square_hi, NT, preferred_element_type=jnp.float32)
    energy += lax.dot_general(ones, square_lo, NT, preferred_element_type=jnp.float32)
    scale = lax.rsqrt(energy[:1] + EPSILON)
    raw = lax.dot_general(table, traces, NT, preferred_element_type=jnp.float32)
    return (raw * scale).astype(jnp.bfloat16)


def own_kernel(place_ref, windows_ref, part_ref, full_ref, table_ref):
    groups, samples = windows_ref.shape[2], windows_ref.shape[4]
    quarter, group = place_of(place_ref, groups)
    bins = lax.broadcasted_iota(jnp.int32, (PART, samples), 0) + (quarter % 2) * PART
    table_ref[: 2 * PART] = forward_rows(bins, samples)
    for far in range(2):
        start = 2 * PART + (quarter ^ (2 * far)) * FULL
        bins = lax.broadcasted_iota(jnp.int32, (FULL, samples), 0) + start
        at = 2 * PART + 2 * FULL * far
        table_ref[at : at + 2 * FULL] = forward_rows(bins, samples)
    table = table_ref[...]
    for mg in range(groups):
        spectra = station_spectra(windows_ref, group ^ mg, table)
        for comp in range(COMPS):
            lanes = spectra[:, comp * LANES : (comp + 1) * LANES]
            part_ref[mg, comp * 2 * PART : (comp + 1) * 2 * PART] = lanes[: 2 * PART]
            for far in range(2):
                at = 2 * PART + 2 * FULL * far
                full_ref[far * groups + mg, comp * 2 * FULL : (comp + 1) * 2 * FULL] = lanes[at : at + 2 * FULL]


def near_spectra_kernel(
    place_ref, own_pairs_ref, near_pairs_ref, table_ref, part_ref, full_ref, windows_ref, *piece_refs
):
    groups = windows_ref.shape[2]
    _, group = place_of(place_ref, groups)
    table = table_ref[...]
    part_rows, full_rows = COMPS * 2 * PART, COMPS * 2 * FULL
    piece_refs[groups][2 * full_rows :] = jnp.concatenate(
        [listing_of(own_pairs_ref, LANES), listing_of(near_pairs_ref, LANES)]
    ).astype(jnp.bfloat16)
    for mg in range(groups):
        spectra = station_spectra(windows_ref, group ^ mg, table)
        side, cross = piece_refs[mg], piece_refs[groups + mg]
        side[:part_rows] = part_ref[mg]
        side[2 * part_rows : 2 * part_rows + full_rows] = full_ref[mg]
        cross[:full_rows] = full_ref[groups + mg]
        for comp in range(COMPS):
            lanes = spectra[:, comp * LANES : (comp + 1) * LANES]
            at = part_rows + comp * 2 * PART
            side[at : at + 2 * PART] = lanes[: 2 * PART]
            at = 2 * part_rows + full_rows + comp * 2 * FULL
            side[at : at + 2 * FULL] = lanes[2 * PART : 2 * PART + 2 * FULL]
            at = full_rows + comp * 2 * FULL
            cross[at : at + 2 * FULL] = lanes[2 * PART + 2 * FULL :]


def width(bins):
    return 1 << (bins - 1).bit_length()


def packing(count, bins):
    used = 4 * bins
    spare = LANES - used
    if not spare:
        return count, [[(0, 0, 0, used)]]
    runs = used // spare
    rows = count // (runs + 1)
    return rows, [
        [(at * rows, 0, 0, used), (runs * rows, used, at * spare, (at + 1) * spare)] for at in range(runs)
    ]


def packed_rows(count, bins):
    rows, parts = packing(count, bins)
    return rows * len(parts)


def unpack(picked, bins):
    used = 4 * bins
    spare = LANES - used
    if not spare:
        return picked
    runs = used // spare
    rows = picked.shape[0] // runs
    rest = [picked[at * rows : (at + 1) * rows, used:] for at in range(runs)]
    return jnp.concatenate([picked[:, :used], jnp.concatenate(rest, axis=1)])


def pick(place_ref, counts_ref, listed, flat_ref, bins, mq, *picked_refs):
    cells = counts_ref.shape[0]
    quarter, group = place_of(place_ref, cells // 4)
    own = quarter ^ mq
    high, low = own // 2, own % 2
    cell = high * (cells // 2) + group * 2 + low
    count = listed.shape[0] // 2
    runs = LANES // width(bins)
    run_bits, bin_bits, lane_bits = (n.bit_length() - 1 for n in (runs, width(bins), LANES))
    first, second = listed[:count].astype(jnp.int32), listed[count:].astype(jnp.int32)
    far_counts = [counts_ref[cell ^ 1], counts_ref[cell ^ (cells // 2)]]
    odd = lax.broadcasted_iota(jnp.int32, (count, LANES), 0) & 1
    live = (first < counts_ref[cell]) & (second < jnp.where(odd == 1, far_counts[1], far_counts[0]))
    left, right = jnp.where(high == low, first, second), jnp.where(high == low, second, first)
    spot = jnp.where(live, (left >> run_bits) * SLOTS + right, -1)
    turned = (spot * runs + (left & (runs - 1))).T
    lane = lax.broadcasted_iota(jnp.int32, (LANES, LANES), 1)
    run = lane >> bin_bits
    sides = ((high, high), (low, 1 - low))
    found = []
    for step_round in range(2):
        hot, here = [], []
        for at in range(step_round, count, 2):
            both = jnp.broadcast_to(turned[:, at : at + 1], (LANES, LANES))
            here.append((both & (runs - 1)) == run)
            offset = (both >> run_bits) - lane
            hot.append(
                jnp.concatenate(
                    [
                        jnp.where(offset == start, 1.0, 0.0).astype(jnp.bfloat16)
                        for start in range(0, flat_ref.shape[2], LANES)
                    ],
                    axis=1,
                )
            )
        block = flat_ref[sides[step_round][0], sides[step_round][1]]
        wide = jnp.dot(jnp.concatenate(hot), block, preferred_element_type=jnp.float32)
        masked = []
        for chunk, mask in enumerate(here):
            part = wide[chunk * LANES : (chunk + 1) * LANES]
            masked.append(
                jnp.concatenate(
                    [
                        jnp.where(mask, part[:, :LANES], 0.0).astype(jnp.bfloat16),
                        jnp.where(mask, part[:, LANES:], 0.0).astype(jnp.bfloat16),
                    ],
                    axis=1,
                )
            )
        found.append(jnp.concatenate(masked))
    found = jnp.concatenate(found, axis=1)
    spread = lax.broadcasted_iota(jnp.int32, (4 * LANES, LANES), 0)
    kept = lax.broadcasted_iota(jnp.int32, (4 * LANES, LANES), 1)
    bin_of = spread & (width(bins) - 1)
    value = jnp.where(bin_of < bins, (spread >> lane_bits) * bins + bin_of, -1)
    rows, parts = packing(found.shape[0], bins)
    picked = []
    for entries in parts:
        total = 0.0
        for start, at, least, end in entries:
            fold = (value >= least) & (value < end) & (kept == value + (at - least))
            total += jnp.dot(
                found[start : start + rows],
                jnp.where(fold, 1.0, 0.0).astype(jnp.bfloat16),
                preferred_element_type=jnp.float32,
            )
        picked.append(total.astype(jnp.bfloat16))
    picked = jnp.concatenate(picked)
    each = picked.shape[0] // len(picked_refs)
    for at, ref in enumerate(picked_refs):
        ref[...] = picked[at * each : (at + 1) * each]


def padded(traces):
    return -(-traces // 16) * 16


def add_cross(pieces, trace_ref, bins, sums_ref, before_ref=None):
    slots, rows = 2 * SLOTS, 2 * bins
    traces = trace_ref.shape[0] // rows
    start = 0
    for piece, at, size in pieces:
        trace_ref[start : start + size] = piece[at : at + size].astype(jnp.float32)
        start += size
    if start < traces * rows:
        trace_ref[start:] = jnp.zeros((traces * rows - start, LANES), jnp.float32)
    for k in range(bins):
        real = trace_ref[pl.ds(k, traces, stride=rows), :].astype(jnp.bfloat16)
        imag = trace_ref[pl.ds(bins + k, traces, stride=rows), :].astype(jnp.bfloat16)
        left = jnp.concatenate([real, imag], axis=0)[:, :slots]
        right = jnp.concatenate(
            [jnp.concatenate([real, imag], axis=1), jnp.concatenate([imag, -real], axis=1)], axis=0
        )
        cross = lax.dot_general(left, right, TN, preferred_element_type=jnp.float32)
        for part in range(2):
            at = (part * bins + k) * slots
            value = cross[:, part * LANES : (part + 1) * LANES]
            if before_ref is not None:
                value += before_ref[at : at + slots]
            sums_ref[at : at + slots] = value


def turn_blocks(cross_ref, bins, flat_ref):
    slots, runs = 2 * SLOTS, LANES // width(bins)
    empty = jnp.zeros((width(bins) - bins, LANES), jnp.float32)
    for own in range(2):
        for at in range(SLOTS // runs):
            for part in range(2):
                first = part * bins * slots + own * SLOTS + at * runs
                block = []
                for i in range(runs):
                    block.append(cross_ref[pl.ds(first + i, bins, stride=slots), :])
                    block += [empty] * (bins < width(bins))
                block = jnp.concatenate(block).T.astype(jnp.bfloat16)
                for far in range(2):
                    flat_ref[
                        own, far, at * SLOTS : (at + 1) * SLOTS, part * LANES : (part + 1) * LANES
                    ] = block[slots + far * SLOTS : slots + (far + 1) * SLOTS]


def side_part(ref):
    return (ref, 0, 2 * COMPS * 2 * PART)


def side_full(ref):
    return (ref, 2 * COMPS * 2 * PART, 2 * COMPS * 2 * FULL)


def cross_full(ref):
    return (ref, 0, 2 * COMPS * 2 * FULL)


def part_kernel(*refs):
    piece_refs, (flat_ref, trace_ref, cross_ref) = refs[:-3], refs[-3:]
    add_cross([side_part(ref) for ref in piece_refs], trace_ref, PART, cross_ref)
    turn_blocks(cross_ref, PART, flat_ref)


def far_kernel(bins, place_ref, counts_ref, listed_ref, flat_ref, picked_0, picked_1):
    listed = listed_ref[cross_full(listed_ref)[2] :].astype(jnp.float32)
    listing = listed.shape[0] // 2
    pick(place_ref, counts_ref, listed[:listing], flat_ref, bins, 2, picked_0)
    pick(place_ref, counts_ref, listed[listing:], flat_ref, bins, 3, picked_1)


def early_kernel(sides, after_ref, *refs):
    piece_refs, (sums_ref, trace_ref) = refs[:-2], refs[-2:]
    pieces = [side_full(ref) for ref in piece_refs[:sides]] + [cross_full(ref) for ref in piece_refs[sides:]]
    add_cross(pieces, trace_ref, FULL, sums_ref)


def full_kernel(place_ref, counts_ref, listed_ref, before_ref, *refs):
    piece_refs, (flat_ref, picked_0, picked_1, trace_ref, cross_ref) = refs[:-5], refs[-5:]
    add_cross([cross_full(ref) for ref in piece_refs], trace_ref, FULL, cross_ref, before_ref)
    turn_blocks(cross_ref, FULL, flat_ref)
    listed = listed_ref[cross_full(listed_ref)[2] :].astype(jnp.float32)
    listing = listed.shape[0] // 2
    pick(place_ref, counts_ref, listed[:listing], flat_ref, FULL, 2, picked_0)
    pick(place_ref, counts_ref, listed[listing:], flat_ref, FULL, 3, picked_1)


def near_kernel(
    place_ref,
    counts_ref,
    own_pairs_ref,
    near_pairs_ref,
    part_ref,
    full_ref,
    after_2,
    after_3,
    part_0,
    full_0,
    part_1,
    *full_1,
):
    listed = listing_of(near_pairs_ref, LANES)
    pick(place_ref, counts_ref, listed, part_ref, PART, 1, part_1)
    pick(place_ref, counts_ref, listed, full_ref, FULL, 1, *full_1)
    listed = listing_of(own_pairs_ref, LANES)
    pick(place_ref, counts_ref, listed, part_ref, PART, 0, part_0)
    pick(place_ref, counts_ref, listed, full_ref, FULL, 0, full_0)


def both_rounds(rows, sign):
    row = lax.broadcasted_iota(jnp.int32, rows.shape, 0)
    rows = rows * jnp.where(row < rows.shape[0] // 2, 1.0, sign)
    empty = jnp.zeros_like(rows)
    return jnp.concatenate(
        [jnp.concatenate([rows, empty], axis=1), jnp.concatenate([empty, rows], axis=1)]
    )


def halves(table):
    high = table.astype(jnp.bfloat16)
    return high, (table - high.astype(jnp.float32)).astype(jnp.bfloat16)


def first_lags_kernel(groups, place_ref, inverse_ref, *refs):
    part_0, part_2, part_3, full_0, part_1, *full_1, lags_ref, table_ref = refs
    samples = inverse_ref.shape[1]
    quarter, _ = place_of(place_ref, groups)
    low = quarter % 2
    sign = jnp.where(quarter // 2 == low, 1.0, -1.0)

    def part_table(which):
        start = pl.multiple_of((low ^ which) * 2 * PART, 2 * PART)
        return halves(both_rounds(inverse_ref[pl.ds(start, 2 * PART), :], sign))

    def full_table(mq):
        start = pl.multiple_of(4 * PART + (quarter ^ mq) * 2 * FULL, 2 * FULL)
        return halves(both_rounds(inverse_ref[pl.ds(start, 2 * FULL), :], sign))

    near, other = part_table(0), part_table(1)
    lags = 0.0
    full_1 = jnp.concatenate([ref[...] for ref in full_1])
    for picked, bins, table in (
        (part_0[...], PART, near),
        (part_2[...], PART, near),
        (part_1[...], PART, other),
        (part_3[...], PART, other),
        (full_0[...], FULL, full_table(0)),
        (full_1, FULL, full_table(1)),
    ):
        picked = unpack(picked, bins)
        for half in table:
            lags += jnp.dot(picked, half, preferred_element_type=jnp.float32)
    for step_round in range(2):
        lags_ref[step_round] = lags[:, step_round * samples : (step_round + 1) * samples]
    for at in range(2):
        for which, half in enumerate(full_table(2 + at)):
            table_ref[at, which] = half


def lag_kernel(first_ref, table_ref, *refs):
    picked_refs, lags_ref = refs[:-1], refs[-1]
    samples = lags_ref.shape[2]
    more = 0.0
    for at, ref in enumerate(picked_refs):
        picked = unpack(ref[...], FULL)
        for which in range(2):
            more += jnp.dot(picked, table_ref[at, which], preferred_element_type=jnp.float32)
    for step_round in range(2):
        lags_ref[step_round] = (
            first_ref[step_round] + more[:, step_round * samples : (step_round + 1) * samples]
        )


def on_device(windows, counts, pairs):
    comps, _, events, samples = windows.shape
    cells = lax.axis_size("cell")
    half, groups = cells // 2, cells // 4
    count = pairs.shape[2]
    inverse = jnp.asarray(inverse_table(samples, cells))
    place = lax.axis_index("cell").astype(jnp.int32).reshape(1)

    def swap(x, mask):
        return lax.ppermute(x, "cell", [(i, i ^ mask) for i in range(cells)])

    def shape(*dims, dtype=jnp.bfloat16):
        return jax.ShapeDtypeStruct(dims, dtype)

    vmem = pl.BlockSpec(memory_space=pltpu.VMEM)
    smem = pl.BlockSpec(memory_space=pltpu.SMEM)
    params = pltpu.CompilerParams(vmem_limit_bytes=VMEM_LIMIT)

    def cost(microseconds):
        return pl.CostEstimate(
            flops=int(microseconds * 1e9), bytes_accessed=2**20, transcendentals=0
        )

    windows = windows.reshape(comps, 2, groups, 2 * SLOTS, samples)
    near_windows, near_pairs = swap(windows, 1), swap(pairs, 1)
    part_rows, full_rows = comps * 2 * PART, comps * 2 * FULL
    part_spectra, full_spectra, table = pl.pallas_call(
        own_kernel,
        out_shape=[
            shape(groups, part_rows, LANES),
            shape(2 * groups, full_rows, LANES),
            shape(2 * PART + 4 * FULL, samples),
        ],
        in_specs=[smem, vmem],
        out_specs=[vmem] * 3,
        compiler_params=params,
        cost_estimate=cost(1),
        name="own_spectra",
    )(place, windows)
    listing = 2 * pairs.size // LANES
    pieces = pl.pallas_call(
        near_spectra_kernel,
        out_shape=[shape(2 * (part_rows + full_rows), LANES)] * groups
        + [shape(2 * full_rows + listing * (mg == 0), LANES) for mg in range(groups)],
        in_specs=[smem] + [vmem] * 6,
        out_specs=[vmem] * (2 * groups),
        compiler_params=params,
        cost_estimate=cost(1),
        name="near_spectra",
    )(place, pairs, near_pairs, table, part_spectra, full_spectra, near_windows)
    arrived = [pieces[0]] + [swap(pieces[m], 2 * m) for m in range(1, 2 * groups)]
    sides, far = arrived[:groups], arrived[groups:]

    part_packed = shape(packed_rows(count, PART), LANES)
    full_packed = shape(packed_rows(count, FULL), LANES)
    half_packed = shape(packed_rows(count, FULL) // 2, LANES)
    part_blocks = shape(2, 2, SLOTS * SLOTS * width(PART) // LANES, 2 * LANES)
    full_blocks = shape(2, 2, SLOTS * SLOTS * width(FULL) // LANES, 2 * LANES)
    part_flat = pl.pallas_call(
        part_kernel,
        out_shape=part_blocks,
        in_specs=[vmem] * groups,
        out_specs=vmem,
        scratch_shapes=[
            pltpu.VMEM((padded(groups * 2 * comps) * 2 * PART, LANES), jnp.float32),
            pltpu.VMEM((2 * SLOTS * 2 * PART, LANES), jnp.float32),
        ],
        compiler_params=params,
        cost_estimate=cost(2),
        name="part",
    )(*sides)
    part_2, part_3 = pl.pallas_call(
        functools.partial(far_kernel, PART),
        out_shape=[part_packed, part_packed],
        in_specs=[smem, smem, vmem, vmem],
        out_specs=[vmem, vmem],
        compiler_params=params,
        cost_estimate=cost(1),
        name="part_far",
    )(place, counts, far[0], part_flat)
    part_2, part_3 = swap(part_2, half), swap(part_3, half + 1)
    early, late = far[: groups - 2], far[groups - 2 :]
    sums = pl.pallas_call(
        functools.partial(early_kernel, groups),
        out_shape=shape(2 * SLOTS * 2 * FULL, LANES, dtype=jnp.float32),
        in_specs=[pl.BlockSpec(memory_space=pl.ANY)] + [vmem] * (groups + len(early)),
        out_specs=vmem,
        scratch_shapes=[
            pltpu.VMEM((padded((groups + len(early)) * 2 * comps) * 2 * FULL, LANES), jnp.float32)
        ],
        compiler_params=params,
        cost_estimate=cost(0.001),
        name="early",
    )(part_flat, *sides, *early)
    full_flat, full_2, full_3 = pl.pallas_call(
        full_kernel,
        out_shape=[full_blocks, full_packed, full_packed],
        in_specs=[smem, smem] + [vmem] * (2 + len(late)),
        out_specs=[vmem] * 3,
        scratch_shapes=[
            pltpu.VMEM((padded(len(late) * 2 * comps) * 2 * FULL, LANES), jnp.float32),
            pltpu.VMEM((2 * SLOTS * 2 * FULL, LANES), jnp.float32),
        ],
        compiler_params=params,
        cost_estimate=cost(10),
        name="full",
    )(place, counts, far[0], sums, *late)
    full_2, full_3 = swap(full_2, half), swap(full_3, half + 1)
    part_0, full_0, *near = pl.pallas_call(
        near_kernel,
        out_shape=[part_packed, full_packed, part_packed] + [half_packed] * 2,
        in_specs=[smem, smem] + [vmem] * 4 + [pl.BlockSpec(memory_space=pl.ANY)] * 2,
        out_specs=[vmem] * 5,
        compiler_params=params,
        cost_estimate=cost(0.5),
        name="near",
    )(place, counts, pairs, near_pairs, part_flat, full_flat, part_2, part_3)
    near = [swap(x, 1) for x in near]

    first, tables = pl.pallas_call(
        functools.partial(first_lags_kernel, groups),
        out_shape=[
            shape(2, count, samples, dtype=jnp.float32),
            shape(2, 2, 4 * FULL, 2 * samples),
        ],
        in_specs=[smem] + [vmem] * 8,
        out_specs=[vmem] * 2,
        compiler_params=params,
        cost_estimate=cost(0.001),
        name="first_lags",
    )(place, inverse, part_0, part_2, part_3, full_0, *near)
    return pl.pallas_call(
        lag_kernel,
        out_shape=shape(2, count, samples, dtype=jnp.float32),
        in_specs=[vmem] * 4,
        out_specs=vmem,
        compiler_params=params,
        cost_estimate=cost(1),
        name="lags",
    )(first, tables, full_2, full_3)


def solution(mesh):
    in_specs = (P(None, "cell", "grp", None), P("grp"), P(None, None, ("grp", "cell")))
    out_specs = P(None, ("grp", "cell"), None)
    return jax.shard_map(
        on_device, mesh=mesh, in_specs=in_specs, out_specs=out_specs, check_vma=False
    )
```

```python
import functools
import math

import jax
import jax.numpy as jnp
import numpy as np
from jax import lax
from jax.experimental import pallas as pl
from jax.experimental.pallas import tpu as pltpu
from jax.sharding import PartitionSpec as P

EPSILON = 1e-06
COSINE = (
    0.9999999999993376,
    -4.934802200431432,
    4.058712123240781,
    -1.3352627346923478,
    0.23533044681677665,
    -0.02580633847975355,
    0.0019285963125396874,
    -0.00010362767792380447,
    3.734915399663344e-06,
)
SLOTS = 32
LANES = 4 * SLOTS
COMPS = 3
NT = (((1,), (1,)), ((), ()))
TN = (((0,), (0,)), ((), ()))
VMEM_LIMIT = 40 * 1024 * 1024

PART = 16
FULL = 24


def inverse_table(samples, stations):
    bins = samples // 2
    turn = np.arange(bins)[:, None] * np.arange(samples)[None, :] % samples
    angle = turn * (2.0 * math.pi / samples)
    weight = np.where(np.arange(bins) == 0, 1.0, 2.0)[:, None] / samples
    weight = weight * math.sqrt(samples / (3.0 * stations))
    real, imag = weight * np.cos(angle), -weight * np.sin(angle)
    runs = [(at, PART) for at in range(0, 2 * PART, PART)]
    runs += [(at, FULL) for at in range(2 * PART, bins, FULL)]
    rows = [part[at : at + run] for at, run in runs for part in (real, imag)]
    return np.concatenate(rows).astype(np.float32)


def forward_rows(bins, samples):
    count = bins.shape[0]
    sample = lax.broadcasted_iota(jnp.int32, (2 * count, samples), 1)
    turn = jnp.concatenate([bins * sample[:count], bins * sample[:count] + samples // 4])
    turn &= samples - 1
    x = jnp.where(turn > samples // 2, turn - samples, turn).astype(jnp.float32) * (2.0 / samples)
    square = x * x
    value = jnp.full(square.shape, COSINE[-1], jnp.float32)
    for factor in COSINE[-2::-1]:
        value = value * square + factor
    return value.astype(jnp.bfloat16)


def place_of(place_ref, groups):
    position = place_ref[0]
    high, inner = position // (2 * groups), position % (2 * groups)
    return high * 2 + inner % 2, inner // 2


def listing_of(pairs_ref, lanes):
    ends = []
    for end in range(2):
        slots = pairs_ref[:, end, :].astype(jnp.float32)
        ends += [slots[:, at : at + lanes] for at in range(0, slots.shape[1], lanes)]
    return jnp.concatenate(ends)


def station_spectra(windows_ref, at, table):
    parts = []
    for comp in range(windows_ref.shape[0]):
        low = windows_ref[comp, 0, at]
        high = windows_ref[comp, 1, at]
        parts += [low[:SLOTS], high[SLOTS:], low[SLOTS:], high[:SLOTS]]
    traces = jnp.concatenate(parts)
    square = jnp.square(traces.astype(jnp.float32))
    square_hi = square.astype(jnp.bfloat16)
    square_lo = (square - square_hi.astype(jnp.float32)).astype(jnp.bfloat16)
    ones = jnp.ones((16, traces.shape[1]), jnp.bfloat16)
    energy = lax.dot_general(ones, square_hi, NT, preferred_element_type=jnp.float32)
    energy += lax.dot_general(ones, square_lo, NT, preferred_element_type=jnp.float32)
    scale = lax.rsqrt(energy[:1] + EPSILON)
    raw = lax.dot_general(table, traces, NT, preferred_element_type=jnp.float32)
    return (raw * scale).astype(jnp.bfloat16)


def own_kernel(place_ref, windows_ref, part_ref, full_ref, table_ref):
    groups, samples = windows_ref.shape[2], windows_ref.shape[4]
    quarter, group = place_of(place_ref, groups)
    bins = lax.broadcasted_iota(jnp.int32, (PART, samples), 0) + (quarter % 2) * PART
    table_ref[: 2 * PART] = forward_rows(bins, samples)
    for far in range(2):
        start = 2 * PART + (quarter ^ (2 * far)) * FULL
        bins = lax.broadcasted_iota(jnp.int32, (FULL, samples), 0) + start
        at = 2 * PART + 2 * FULL * far
        table_ref[at : at + 2 * FULL] = forward_rows(bins, samples)
    table = table_ref[...]
    for mg in range(groups):
        spectra = station_spectra(windows_ref, group ^ mg, table)
        for comp in range(COMPS):
            lanes = spectra[:, comp * LANES : (comp + 1) * LANES]
            part_ref[mg, comp * 2 * PART : (comp + 1) * 2 * PART] = lanes[: 2 * PART]
            for far in range(2):
                at = 2 * PART + 2 * FULL * far
                full_ref[far * groups + mg, comp * 2 * FULL : (comp + 1) * 2 * FULL] = lanes[at : at + 2 * FULL]


def near_spectra_kernel(
    place_ref, own_pairs_ref, near_pairs_ref, table_ref, part_ref, full_ref, windows_ref, *piece_refs
):
    groups = windows_ref.shape[2]
    _, group = place_of(place_ref, groups)
    table = table_ref[...]
    part_rows, full_rows = COMPS * 2 * PART, COMPS * 2 * FULL
    piece_refs[groups][2 * full_rows :] = jnp.concatenate(
        [listing_of(own_pairs_ref, LANES), listing_of(near_pairs_ref, LANES)]
    ).astype(jnp.bfloat16)
    for mg in range(groups):
        spectra = station_spectra(windows_ref, group ^ mg, table)
        side, cross = piece_refs[mg], piece_refs[groups + mg]
        side[:part_rows] = part_ref[mg]
        side[2 * part_rows : 2 * part_rows + full_rows] = full_ref[mg]
        cross[:full_rows] = full_ref[groups + mg]
        for comp in range(COMPS):
            lanes = spectra[:, comp * LANES : (comp + 1) * LANES]
            at = part_rows + comp * 2 * PART
            side[at : at + 2 * PART] = lanes[: 2 * PART]
            at = 2 * part_rows + full_rows + comp * 2 * FULL
            side[at : at + 2 * FULL] = lanes[2 * PART : 2 * PART + 2 * FULL]
            at = full_rows + comp * 2 * FULL
            cross[at : at + 2 * FULL] = lanes[2 * PART + 2 * FULL :]


def width(bins):
    return 1 << (bins - 1).bit_length()


def packing(count, bins):
    used = 4 * bins
    spare = LANES - used
    if not spare:
        return count, [[(0, 0, 0, used)]]
    runs = used // spare
    rows = count // (runs + 1)
    return rows, [
        [(at * rows, 0, 0, used), (runs * rows, used, at * spare, (at + 1) * spare)] for at in range(runs)
    ]


def packed_rows(count, bins):
    rows, parts = packing(count, bins)
    return rows * len(parts)


def unpack(picked, bins):
    used = 4 * bins
    spare = LANES - used
    if not spare:
        return picked
    runs = used // spare
    rows = picked.shape[0] // runs
    rest = [picked[at * rows : (at + 1) * rows, used:] for at in range(runs)]
    return jnp.concatenate([picked[:, :used], jnp.concatenate(rest, axis=1)])


def pick(place_ref, counts_ref, listed, flat_ref, bins, mq, *picked_refs):
    cells = counts_ref.shape[0]
    quarter, group = place_of(place_ref, cells // 4)
    own = quarter ^ mq
    high, low = own // 2, own % 2
    cell = high * (cells // 2) + group * 2 + low
    count = listed.shape[0] // 2
    runs = LANES // width(bins)
    run_bits, bin_bits, lane_bits = (n.bit_length() - 1 for n in (runs, width(bins), LANES))
    first, second = listed[:count].astype(jnp.int32), listed[count:].astype(jnp.int32)
    far_counts = [counts_ref[cell ^ 1], counts_ref[cell ^ (cells // 2)]]
    odd = lax.broadcasted_iota(jnp.int32, (count, LANES), 0) & 1
    live = (first < counts_ref[cell]) & (second < jnp.where(odd == 1, far_counts[1], far_counts[0]))
    left, right = jnp.where(high == low, first, second), jnp.where(high == low, second, first)
    spot = jnp.where(live, (left >> run_bits) * SLOTS + right, -1)
    turned = (spot * runs + (left & (runs - 1))).T
    lane = lax.broadcasted_iota(jnp.int32, (LANES, LANES), 1)
    run = lane >> bin_bits
    sides = ((high, high), (low, 1 - low))
    found = []
    for step_round in range(2):
        hot, here = [], []
        for at in range(step_round, count, 2):
            both = jnp.broadcast_to(turned[:, at : at + 1], (LANES, LANES))
            here.append((both & (runs - 1)) == run)
            offset = (both >> run_bits) - lane
            hot.append(
                jnp.concatenate(
                    [
                        jnp.where(offset == start, 1.0, 0.0).astype(jnp.bfloat16)
                        for start in range(0, flat_ref.shape[2], LANES)
                    ],
                    axis=1,
                )
            )
        block = flat_ref[sides[step_round][0], sides[step_round][1]]
        wide = jnp.dot(jnp.concatenate(hot), block, preferred_element_type=jnp.float32)
        masked = []
        for chunk, mask in enumerate(here):
            part = wide[chunk * LANES : (chunk + 1) * LANES]
            masked.append(
                jnp.concatenate(
                    [
                        jnp.where(mask, part[:, :LANES], 0.0).astype(jnp.bfloat16),
                        jnp.where(mask, part[:, LANES:], 0.0).astype(jnp.bfloat16),
                    ],
                    axis=1,
                )
            )
        found.append(jnp.concatenate(masked))
    found = jnp.concatenate(found, axis=1)
    spread = lax.broadcasted_iota(jnp.int32, (4 * LANES, LANES), 0)
    kept = lax.broadcasted_iota(jnp.int32, (4 * LANES, LANES), 1)
    bin_of = spread & (width(bins) - 1)
    value = jnp.where(bin_of < bins, (spread >> lane_bits) * bins + bin_of, -1)
    rows, parts = packing(found.shape[0], bins)
    picked = []
    for entries in parts:
        total = 0.0
        for start, at, least, end in entries:
            fold = (value >= least) & (value < end) & (kept == value + (at - least))
            total += jnp.dot(
                found[start : start + rows],
                jnp.where(fold, 1.0, 0.0).astype(jnp.bfloat16),
                preferred_element_type=jnp.float32,
            )
        picked.append(total.astype(jnp.bfloat16))
    picked = jnp.concatenate(picked)
    each = picked.shape[0] // len(picked_refs)
    for at, ref in enumerate(picked_refs):
        ref[...] = picked[at * each : (at + 1) * each]


def padded(traces):
    return -(-traces // 16) * 16


def add_cross(pieces, trace_ref, bins, sums_ref, before_ref=None):
    slots, rows = 2 * SLOTS, 2 * bins
    traces = trace_ref.shape[0] // rows
    start = 0
    for piece, at, size in pieces:
        trace_ref[start : start + size] = piece[at : at + size].astype(jnp.float32)
        start += size
    if start < traces * rows:
        trace_ref[start:] = jnp.zeros((traces * rows - start, LANES), jnp.float32)
    for k in range(bins):
        real = trace_ref[pl.ds(k, traces, stride=rows), :].astype(jnp.bfloat16)
        imag = trace_ref[pl.ds(bins + k, traces, stride=rows), :].astype(jnp.bfloat16)
        left = jnp.concatenate([real, imag], axis=0)[:, :slots]
        right = jnp.concatenate(
            [jnp.concatenate([real, imag], axis=1), jnp.concatenate([imag, -real], axis=1)], axis=0
        )
        cross = lax.dot_general(left, right, TN, preferred_element_type=jnp.float32)
        for part in range(2):
            at = (part * bins + k) * slots
            value = cross[:, part * LANES : (part + 1) * LANES]
            if before_ref is not None:
                value += before_ref[at : at + slots]
            sums_ref[at : at + slots] = value


def turn_blocks(cross_ref, bins, flat_ref):
    slots, runs = 2 * SLOTS, LANES // width(bins)
    empty = jnp.zeros((width(bins) - bins, LANES), jnp.float32)
    for own in range(2):
        for at in range(SLOTS // runs):
            for part in range(2):
                first = part * bins * slots + own * SLOTS + at * runs
                block = []
                for i in range(runs):
                    block.append(cross_ref[pl.ds(first + i, bins, stride=slots), :])
                    block += [empty] * (bins < width(bins))
                block = jnp.concatenate(block).T.astype(jnp.bfloat16)
                for far in range(2):
                    flat_ref[
                        own, far, at * SLOTS : (at + 1) * SLOTS, part * LANES : (part + 1) * LANES
                    ] = block[slots + far * SLOTS : slots + (far + 1) * SLOTS]


def side_part(ref):
    return (ref, 0, 2 * COMPS * 2 * PART)


def side_full(ref):
    return (ref, 2 * COMPS * 2 * PART, 2 * COMPS * 2 * FULL)


def cross_full(ref):
    return (ref, 0, 2 * COMPS * 2 * FULL)


def part_kernel(*refs):
    piece_refs, (flat_ref, trace_ref, cross_ref) = refs[:-3], refs[-3:]
    add_cross([side_part(ref) for ref in piece_refs], trace_ref, PART, cross_ref)
    turn_blocks(cross_ref, PART, flat_ref)


def far_kernel(bins, place_ref, counts_ref, listed_ref, flat_ref, after_ref, picked_0, picked_1):
    listed = listed_ref[cross_full(listed_ref)[2] :].astype(jnp.float32)
    listing = listed.shape[0] // 2
    pick(place_ref, counts_ref, listed[:listing], flat_ref, bins, 2, picked_0)
    pick(place_ref, counts_ref, listed[listing:], flat_ref, bins, 3, picked_1)


def early_kernel(sides, after_ref, *refs):
    piece_refs, (sums_ref, trace_ref) = refs[:-2], refs[-2:]
    pieces = [side_full(ref) for ref in piece_refs[:sides]] + [cross_full(ref) for ref in piece_refs[sides:]]
    add_cross(pieces, trace_ref, FULL, sums_ref)


def full_kernel(place_ref, counts_ref, listed_ref, after_0, after_2, before_ref, *refs):
    piece_refs, (flat_ref, picked_0, picked_1, trace_ref, cross_ref) = refs[:-5], refs[-5:]
    add_cross([cross_full(ref) for ref in piece_refs], trace_ref, FULL, cross_ref, before_ref)
    turn_blocks(cross_ref, FULL, flat_ref)
    listed = listed_ref[cross_full(listed_ref)[2] :].astype(jnp.float32)
    listing = listed.shape[0] // 2
    pick(place_ref, counts_ref, listed[:listing], flat_ref, FULL, 2, picked_0)
    pick(place_ref, counts_ref, listed[listing:], flat_ref, FULL, 3, picked_1)


def near_kernel(bins, sent, place_ref, counts_ref, own_pairs_ref, near_pairs_ref, flat_ref, *refs):
    picked_0, *picked_1 = refs[-1 - sent :]
    pick(place_ref, counts_ref, listing_of(near_pairs_ref, LANES), flat_ref, bins, 1, *picked_1)
    pick(place_ref, counts_ref, listing_of(own_pairs_ref, LANES), flat_ref, bins, 0, picked_0)


def both_rounds(rows, sign):
    row = lax.broadcasted_iota(jnp.int32, rows.shape, 0)
    rows = rows * jnp.where(row < rows.shape[0] // 2, 1.0, sign)
    empty = jnp.zeros_like(rows)
    return jnp.concatenate(
        [jnp.concatenate([rows, empty], axis=1), jnp.concatenate([empty, rows], axis=1)]
    )


def halves(table):
    high = table.astype(jnp.bfloat16)
    return high, (table - high.astype(jnp.float32)).astype(jnp.bfloat16)


def first_lags_kernel(groups, place_ref, inverse_ref, *refs):
    part_0, part_2, part_3, full_0, part_1, *full_1, lags_ref, table_ref = refs
    samples = inverse_ref.shape[1]
    quarter, _ = place_of(place_ref, groups)
    low = quarter % 2
    sign = jnp.where(quarter // 2 == low, 1.0, -1.0)

    def part_table(which):
        start = pl.multiple_of((low ^ which) * 2 * PART, 2 * PART)
        return halves(both_rounds(inverse_ref[pl.ds(start, 2 * PART), :], sign))

    def full_table(mq):
        start = pl.multiple_of(4 * PART + (quarter ^ mq) * 2 * FULL, 2 * FULL)
        return halves(both_rounds(inverse_ref[pl.ds(start, 2 * FULL), :], sign))

    near, other = part_table(0), part_table(1)
    lags = 0.0
    full_1 = jnp.concatenate([ref[...] for ref in full_1])
    for picked, bins, table in (
        (part_0[...], PART, near),
        (part_2[...], PART, near),
        (part_1[...], PART, other),
        (part_3[...], PART, other),
        (full_0[...], FULL, full_table(0)),
        (full_1, FULL, full_table(1)),
    ):
        picked = unpack(picked, bins)
        for half in table:
            lags += jnp.dot(picked, half, preferred_element_type=jnp.float32)
    for step_round in range(2):
        lags_ref[step_round] = lags[:, step_round * samples : (step_round + 1) * samples]
    for at in range(2):
        for which, half in enumerate(full_table(2 + at)):
            table_ref[at, which] = half


def lag_kernel(first_ref, table_ref, *refs):
    picked_refs, lags_ref = refs[:-1], refs[-1]
    samples = lags_ref.shape[2]
    more = 0.0
    for at, ref in enumerate(picked_refs):
        picked = unpack(ref[...], FULL)
        for which in range(2):
            more += jnp.dot(picked, table_ref[at, which], preferred_element_type=jnp.float32)
    for step_round in range(2):
        lags_ref[step_round] = (
            first_ref[step_round] + more[:, step_round * samples : (step_round + 1) * samples]
        )


def on_device(windows, counts, pairs):
    comps, _, events, samples = windows.shape
    cells = lax.axis_size("cell")
    half, groups = cells // 2, cells // 4
    count = pairs.shape[2]
    inverse = jnp.asarray(inverse_table(samples, cells))
    place = lax.axis_index("cell").astype(jnp.int32).reshape(1)

    def swap(x, mask):
        return lax.ppermute(x, "cell", [(i, i ^ mask) for i in range(cells)])

    def shape(*dims, dtype=jnp.bfloat16):
        return jax.ShapeDtypeStruct(dims, dtype)

    vmem = pl.BlockSpec(memory_space=pltpu.VMEM)
    smem = pl.BlockSpec(memory_space=pltpu.SMEM)
    params = pltpu.CompilerParams(vmem_limit_bytes=VMEM_LIMIT)

    def cost(microseconds):
        return pl.CostEstimate(
            flops=int(microseconds * 1e9), bytes_accessed=2**20, transcendentals=0
        )

    windows = windows.reshape(comps, 2, groups, 2 * SLOTS, samples)
    near_windows, near_pairs = swap(windows, 1), swap(pairs, 1)
    part_rows, full_rows = comps * 2 * PART, comps * 2 * FULL
    part_spectra, full_spectra, table = pl.pallas_call(
        own_kernel,
        out_shape=[
            shape(groups, part_rows, LANES),
            shape(2 * groups, full_rows, LANES),
            shape(2 * PART + 4 * FULL, samples),
        ],
        in_specs=[smem, vmem],
        out_specs=[vmem] * 3,
        compiler_params=params,
        cost_estimate=cost(1),
        name="own_spectra",
    )(place, windows)
    listing = 2 * pairs.size // LANES
    pieces = pl.pallas_call(
        near_spectra_kernel,
        out_shape=[shape(2 * (part_rows + full_rows), LANES)] * groups
        + [shape(2 * full_rows + listing * (mg == 0), LANES) for mg in range(groups)],
        in_specs=[smem] + [vmem] * 6,
        out_specs=[vmem] * (2 * groups),
        compiler_params=params,
        cost_estimate=cost(1),
        name="near_spectra",
    )(place, pairs, near_pairs, table, part_spectra, full_spectra, near_windows)
    arrived = [pieces[0]] + [swap(pieces[m], 2 * m) for m in range(1, 2 * groups)]
    sides, far = arrived[:groups], arrived[groups:]

    early, late = far[: groups - 2], far[groups - 2 :]
    part_packed = shape(packed_rows(count, PART), LANES)
    full_packed = shape(packed_rows(count, FULL), LANES)
    half_packed = shape(packed_rows(count, FULL) // 2, LANES)
    part_blocks = shape(2, 2, SLOTS * SLOTS * width(PART) // LANES, 2 * LANES)
    full_blocks = shape(2, 2, SLOTS * SLOTS * width(FULL) // LANES, 2 * LANES)
    part_flat = pl.pallas_call(
        part_kernel,
        out_shape=part_blocks,
        in_specs=[vmem] * groups,
        out_specs=vmem,
        scratch_shapes=[
            pltpu.VMEM((padded(groups * 2 * comps) * 2 * PART, LANES), jnp.float32),
            pltpu.VMEM((2 * SLOTS * 2 * PART, LANES), jnp.float32),
        ],
        compiler_params=params,
        cost_estimate=cost(2),
        name="part",
    )(*sides)
    part_2, part_3 = pl.pallas_call(
        functools.partial(far_kernel, PART),
        out_shape=[part_packed, part_packed],
        in_specs=[smem, smem, vmem, vmem, pl.BlockSpec(memory_space=pl.ANY)],
        out_specs=[vmem, vmem],
        compiler_params=params,
        cost_estimate=cost(1),
        name="part_far",
    )(place, counts, far[0], part_flat, late[0])
    sent, part_2, part_3 = part_2, swap(part_2, half), swap(part_3, half + 1)
    part_0, part_1 = pl.pallas_call(
        functools.partial(near_kernel, PART, 1),
        out_shape=[part_packed, part_packed],
        in_specs=[smem, smem] + [vmem] * 3,
        out_specs=[vmem] * 2,
        compiler_params=params,
        cost_estimate=cost(1),
        name="part_near",
    )(place, counts, pairs, near_pairs, part_flat)
    part_1 = swap(part_1, 1)
    sums = pl.pallas_call(
        functools.partial(early_kernel, groups),
        out_shape=shape(2 * SLOTS * 2 * FULL, LANES, dtype=jnp.float32),
        in_specs=[pl.BlockSpec(memory_space=pl.ANY)] + [vmem] * (groups + len(early)),
        out_specs=vmem,
        scratch_shapes=[
            pltpu.VMEM((padded((groups + len(early)) * 2 * comps) * 2 * FULL, LANES), jnp.float32)
        ],
        compiler_params=params,
        cost_estimate=cost(0.001),
        name="early",
    )(part_flat, *sides, *early)
    full_flat, full_2, full_3 = pl.pallas_call(
        full_kernel,
        out_shape=[full_blocks, full_packed, full_packed],
        in_specs=[smem, smem, vmem] + [pl.BlockSpec(memory_space=pl.ANY)] * 2 + [vmem] * (1 + len(late)),
        out_specs=[vmem] * 3,
        scratch_shapes=[
            pltpu.VMEM((padded(len(late) * 2 * comps) * 2 * FULL, LANES), jnp.float32),
            pltpu.VMEM((2 * SLOTS * 2 * FULL, LANES), jnp.float32),
        ],
        compiler_params=params,
        cost_estimate=cost(10),
        name="full",
    )(place, counts, far[0], part_0, sent, sums, *late)
    full_2, full_3 = swap(full_2, half), swap(full_3, half + 1)
    full_0, *full_1 = pl.pallas_call(
        functools.partial(near_kernel, FULL, 2),
        out_shape=[full_packed, half_packed, half_packed],
        in_specs=[smem, smem] + [vmem] * 3 + [pl.BlockSpec(memory_space=pl.ANY)] * 3,
        out_specs=[vmem] * 3,
        compiler_params=params,
        cost_estimate=cost(0.5),
        name="full_near",
    )(place, counts, pairs, near_pairs, full_flat, part_1, part_2, part_3)
    full_1 = [swap(x, 1) for x in full_1]

    first, tables = pl.pallas_call(
        functools.partial(first_lags_kernel, groups),
        out_shape=[
            shape(2, count, samples, dtype=jnp.float32),
            shape(2, 2, 4 * FULL, 2 * samples),
        ],
        in_specs=[smem] + [vmem] * 8,
        out_specs=[vmem] * 2,
        compiler_params=params,
        cost_estimate=cost(0.001),
        name="first_lags",
    )(place, inverse, part_0, part_2, part_3, full_0, part_1, *full_1)
    return pl.pallas_call(
        lag_kernel,
        out_shape=shape(2, count, samples, dtype=jnp.float32),
        in_specs=[vmem] * 4,
        out_specs=vmem,
        compiler_params=params,
        cost_estimate=cost(1),
        name="lags",
    )(first, tables, full_2, full_3)


def solution(mesh):
    in_specs = (P(None, "cell", "grp", None), P("grp"), P(None, None, ("grp", "cell")))
    out_specs = P(None, ("grp", "cell"), None)
    return jax.shard_map(
        on_device, mesh=mesh, in_specs=in_specs, out_specs=out_specs, check_vma=False
    )
```

```python
import functools
import math

import jax
import jax.numpy as jnp
import numpy as np
from jax import lax
from jax.experimental import pallas as pl
from jax.experimental.pallas import tpu as pltpu
from jax.sharding import PartitionSpec as P

EPSILON = 1e-06
COSINE = (
    0.9999999999993376,
    -4.934802200431432,
    4.058712123240781,
    -1.3352627346923478,
    0.23533044681677665,
    -0.02580633847975355,
    0.0019285963125396874,
    -0.00010362767792380447,
    3.734915399663344e-06,
)
SLOTS = 32
LANES = 4 * SLOTS
COMPS = 3
NT = (((1,), (1,)), ((), ()))
TN = (((0,), (0,)), ((), ()))
VMEM_LIMIT = 40 * 1024 * 1024

PART = 16
FULL = 24


def inverse_table(samples, stations):
    bins = samples // 2
    turn = np.arange(bins)[:, None] * np.arange(samples)[None, :] % samples
    angle = turn * (2.0 * math.pi / samples)
    weight = np.where(np.arange(bins) == 0, 1.0, 2.0)[:, None] / samples
    weight = weight * math.sqrt(samples / (3.0 * stations))
    real, imag = weight * np.cos(angle), -weight * np.sin(angle)
    runs = [(at, PART) for at in range(0, 2 * PART, PART)]
    runs += [(at, FULL) for at in range(2 * PART, bins, FULL)]
    rows = [part[at : at + run] for at, run in runs for part in (real, imag)]
    return np.concatenate(rows).astype(np.float32)


def forward_rows(bins, samples):
    count = bins.shape[0]
    sample = lax.broadcasted_iota(jnp.int32, (2 * count, samples), 1)
    turn = jnp.concatenate([bins * sample[:count], bins * sample[:count] + samples // 4])
    turn &= samples - 1
    x = jnp.where(turn > samples // 2, turn - samples, turn).astype(jnp.float32) * (2.0 / samples)
    square = x * x
    value = jnp.full(square.shape, COSINE[-1], jnp.float32)
    for factor in COSINE[-2::-1]:
        value = value * square + factor
    return value.astype(jnp.bfloat16)


def place_of(place_ref, groups):
    position = place_ref[0]
    high, inner = position // (2 * groups), position % (2 * groups)
    return high * 2 + inner % 2, inner // 2


def listing_of(pairs_ref, lanes):
    ends = []
    for end in range(2):
        slots = pairs_ref[:, end, :].astype(jnp.float32)
        ends += [slots[:, at : at + lanes] for at in range(0, slots.shape[1], lanes)]
    return jnp.concatenate(ends)


def station_spectra(windows_ref, at, table):
    parts = []
    for comp in range(windows_ref.shape[0]):
        low = windows_ref[comp, 0, at]
        high = windows_ref[comp, 1, at]
        parts += [low[:SLOTS], high[SLOTS:], low[SLOTS:], high[:SLOTS]]
    traces = jnp.concatenate(parts)
    square = jnp.square(traces.astype(jnp.float32))
    square_hi = square.astype(jnp.bfloat16)
    square_lo = (square - square_hi.astype(jnp.float32)).astype(jnp.bfloat16)
    ones = jnp.ones((16, traces.shape[1]), jnp.bfloat16)
    energy = lax.dot_general(ones, square_hi, NT, preferred_element_type=jnp.float32)
    energy += lax.dot_general(ones, square_lo, NT, preferred_element_type=jnp.float32)
    scale = lax.rsqrt(energy[:1] + EPSILON)
    raw = lax.dot_general(table, traces, NT, preferred_element_type=jnp.float32)
    return (raw * scale).astype(jnp.bfloat16)


def own_kernel(place_ref, windows_ref, part_ref, full_ref, table_ref):
    groups, samples = windows_ref.shape[2], windows_ref.shape[4]
    quarter, group = place_of(place_ref, groups)
    bins = lax.broadcasted_iota(jnp.int32, (PART, samples), 0) + (quarter % 2) * PART
    table_ref[: 2 * PART] = forward_rows(bins, samples)
    for far in range(2):
        start = 2 * PART + (quarter ^ (2 * far)) * FULL
        bins = lax.broadcasted_iota(jnp.int32, (FULL, samples), 0) + start
        at = 2 * PART + 2 * FULL * far
        table_ref[at : at + 2 * FULL] = forward_rows(bins, samples)
    table = table_ref[...]
    for mg in range(groups):
        spectra = station_spectra(windows_ref, group ^ mg, table)
        for comp in range(COMPS):
            lanes = spectra[:, comp * LANES : (comp + 1) * LANES]
            part_ref[mg, comp * 2 * PART : (comp + 1) * 2 * PART] = lanes[: 2 * PART]
            for far in range(2):
                at = 2 * PART + 2 * FULL * far
                full_ref[far * groups + mg, comp * 2 * FULL : (comp + 1) * 2 * FULL] = lanes[at : at + 2 * FULL]


def near_spectra_kernel(
    place_ref, own_pairs_ref, near_pairs_ref, table_ref, part_ref, full_ref, windows_ref, *piece_refs
):
    groups = windows_ref.shape[2]
    _, group = place_of(place_ref, groups)
    table = table_ref[...]
    part_rows, full_rows = COMPS * 2 * PART, COMPS * 2 * FULL
    piece_refs[groups][2 * full_rows :] = jnp.concatenate(
        [listing_of(own_pairs_ref, LANES), listing_of(near_pairs_ref, LANES)]
    ).astype(jnp.bfloat16)
    for mg in range(groups):
        spectra = station_spectra(windows_ref, group ^ mg, table)
        side, cross = piece_refs[mg], piece_refs[groups + mg]
        side[:part_rows] = part_ref[mg]
        side[2 * part_rows : 2 * part_rows + full_rows] = full_ref[mg]
        cross[:full_rows] = full_ref[groups + mg]
        for comp in range(COMPS):
            lanes = spectra[:, comp * LANES : (comp + 1) * LANES]
            at = part_rows + comp * 2 * PART
            side[at : at + 2 * PART] = lanes[: 2 * PART]
            at = 2 * part_rows + full_rows + comp * 2 * FULL
            side[at : at + 2 * FULL] = lanes[2 * PART : 2 * PART + 2 * FULL]
            at = full_rows + comp * 2 * FULL
            cross[at : at + 2 * FULL] = lanes[2 * PART + 2 * FULL :]


def width(bins):
    return 1 << (bins - 1).bit_length()


def packing(count, bins):
    used = 4 * bins
    spare = LANES - used
    if not spare:
        return count, [[(0, 0, 0, used)]]
    runs = used // spare
    rows = count // (runs + 1)
    return rows, [
        [(at * rows, 0, 0, used), (runs * rows, used, at * spare, (at + 1) * spare)] for at in range(runs)
    ]


def packed_rows(count, bins):
    rows, parts = packing(count, bins)
    return rows * len(parts)


def unpack(picked, bins):
    used = 4 * bins
    spare = LANES - used
    if not spare:
        return picked
    runs = used // spare
    rows = picked.shape[0] // runs
    rest = [picked[at * rows : (at + 1) * rows, used:] for at in range(runs)]
    return jnp.concatenate([picked[:, :used], jnp.concatenate(rest, axis=1)])


def pick(place_ref, counts_ref, listed, flat_ref, bins, mq, *picked_refs):
    cells = counts_ref.shape[0]
    quarter, group = place_of(place_ref, cells // 4)
    own = quarter ^ mq
    high, low = own // 2, own % 2
    cell = high * (cells // 2) + group * 2 + low
    count = listed.shape[0] // 2
    runs = LANES // width(bins)
    run_bits, bin_bits, lane_bits = (n.bit_length() - 1 for n in (runs, width(bins), LANES))
    first, second = listed[:count].astype(jnp.int32), listed[count:].astype(jnp.int32)
    far_counts = [counts_ref[cell ^ 1], counts_ref[cell ^ (cells // 2)]]
    odd = lax.broadcasted_iota(jnp.int32, (count, LANES), 0) & 1
    live = (first < counts_ref[cell]) & (second < jnp.where(odd == 1, far_counts[1], far_counts[0]))
    left, right = jnp.where(high == low, first, second), jnp.where(high == low, second, first)
    spot = jnp.where(live, (left >> run_bits) * SLOTS + right, -1)
    turned = (spot * runs + (left & (runs - 1))).T
    lane = lax.broadcasted_iota(jnp.int32, (LANES, LANES), 1)
    run = lane >> bin_bits
    sides = ((high, high), (low, 1 - low))
    found = []
    for step_round in range(2):
        hot, here = [], []
        for at in range(step_round, count, 2):
            both = jnp.broadcast_to(turned[:, at : at + 1], (LANES, LANES))
            here.append((both & (runs - 1)) == run)
            offset = (both >> run_bits) - lane
            hot.append(
                jnp.concatenate(
                    [
                        jnp.where(offset == start, 1.0, 0.0).astype(jnp.bfloat16)
                        for start in range(0, flat_ref.shape[2], LANES)
                    ],
                    axis=1,
                )
            )
        block = flat_ref[sides[step_round][0], sides[step_round][1]]
        wide = jnp.dot(jnp.concatenate(hot), block, preferred_element_type=jnp.float32)
        masked = []
        for chunk, mask in enumerate(here):
            part = wide[chunk * LANES : (chunk + 1) * LANES]
            masked.append(
                jnp.concatenate(
                    [
                        jnp.where(mask, part[:, :LANES], 0.0).astype(jnp.bfloat16),
                        jnp.where(mask, part[:, LANES:], 0.0).astype(jnp.bfloat16),
                    ],
                    axis=1,
                )
            )
        found.append(jnp.concatenate(masked))
    found = jnp.concatenate(found, axis=1)
    spread = lax.broadcasted_iota(jnp.int32, (4 * LANES, LANES), 0)
    kept = lax.broadcasted_iota(jnp.int32, (4 * LANES, LANES), 1)
    bin_of = spread & (width(bins) - 1)
    value = jnp.where(bin_of < bins, (spread >> lane_bits) * bins + bin_of, -1)
    rows, parts = packing(found.shape[0], bins)
    picked = []
    for entries in parts:
        total = 0.0
        for start, at, least, end in entries:
            fold = (value >= least) & (value < end) & (kept == value + (at - least))
            total += jnp.dot(
                found[start : start + rows],
                jnp.where(fold, 1.0, 0.0).astype(jnp.bfloat16),
                preferred_element_type=jnp.float32,
            )
        picked.append(total.astype(jnp.bfloat16))
    picked = jnp.concatenate(picked)
    each = picked.shape[0] // len(picked_refs)
    for at, ref in enumerate(picked_refs):
        ref[...] = picked[at * each : (at + 1) * each]


def padded(traces):
    return -(-traces // 16) * 16


def add_cross(pieces, trace_ref, bins, sums_ref, before_ref=None):
    slots, rows = 2 * SLOTS, 2 * bins
    traces = trace_ref.shape[0] // rows
    start = 0
    for piece, at, size in pieces:
        trace_ref[start : start + size] = piece[at : at + size].astype(jnp.float32)
        start += size
    if start < traces * rows:
        trace_ref[start:] = jnp.zeros((traces * rows - start, LANES), jnp.float32)
    for k in range(bins):
        real = trace_ref[pl.ds(k, traces, stride=rows), :].astype(jnp.bfloat16)
        imag = trace_ref[pl.ds(bins + k, traces, stride=rows), :].astype(jnp.bfloat16)
        left = jnp.concatenate([real, imag], axis=0)[:, :slots]
        right = jnp.concatenate(
            [jnp.concatenate([real, imag], axis=1), jnp.concatenate([imag, -real], axis=1)], axis=0
        )
        cross = lax.dot_general(left, right, TN, preferred_element_type=jnp.float32)
        for part in range(2):
            at = (part * bins + k) * slots
            value = cross[:, part * LANES : (part + 1) * LANES]
            if before_ref is not None:
                value += before_ref[at : at + slots]
            sums_ref[at : at + slots] = value


def turn_blocks(cross_ref, bins, flat_ref):
    slots, runs = 2 * SLOTS, LANES // width(bins)
    empty = jnp.zeros((width(bins) - bins, LANES), jnp.float32)
    for own in range(2):
        for at in range(SLOTS // runs):
            for part in range(2):
                first = part * bins * slots + own * SLOTS + at * runs
                block = []
                for i in range(runs):
                    block.append(cross_ref[pl.ds(first + i, bins, stride=slots), :])
                    block += [empty] * (bins < width(bins))
                block = jnp.concatenate(block).T.astype(jnp.bfloat16)
                for far in range(2):
                    flat_ref[
                        own, far, at * SLOTS : (at + 1) * SLOTS, part * LANES : (part + 1) * LANES
                    ] = block[slots + far * SLOTS : slots + (far + 1) * SLOTS]


def side_part(ref):
    return (ref, 0, 2 * COMPS * 2 * PART)


def side_full(ref):
    return (ref, 2 * COMPS * 2 * PART, 2 * COMPS * 2 * FULL)


def cross_full(ref):
    return (ref, 0, 2 * COMPS * 2 * FULL)


def part_kernel(*refs):
    piece_refs, (flat_ref, trace_ref, cross_ref) = refs[:-3], refs[-3:]
    add_cross([side_part(ref) for ref in piece_refs], trace_ref, PART, cross_ref)
    turn_blocks(cross_ref, PART, flat_ref)


def far_kernel(bins, place_ref, counts_ref, listed_ref, flat_ref, picked_0, picked_1):
    listed = listed_ref[cross_full(listed_ref)[2] :].astype(jnp.float32)
    listing = listed.shape[0] // 2
    pick(place_ref, counts_ref, listed[:listing], flat_ref, bins, 2, picked_0)
    pick(place_ref, counts_ref, listed[listing:], flat_ref, bins, 3, picked_1)


def hold_kernel(picked_0, picked_1, after_0, after_1, after_2, held_0, held_1):
    held_0[...] = picked_0[...]
    held_1[...] = picked_1[...]


def early_kernel(sides, after_ref, *refs):
    piece_refs, (sums_ref, trace_ref) = refs[:-2], refs[-2:]
    pieces = [side_full(ref) for ref in piece_refs[:sides]] + [cross_full(ref) for ref in piece_refs[sides:]]
    add_cross(pieces, trace_ref, FULL, sums_ref)


def full_kernel(place_ref, counts_ref, listed_ref, after_0, after_2, before_ref, *refs):
    piece_refs, (flat_ref, picked_0, picked_1, trace_ref, cross_ref) = refs[:-5], refs[-5:]
    add_cross([cross_full(ref) for ref in piece_refs], trace_ref, FULL, cross_ref, before_ref)
    turn_blocks(cross_ref, FULL, flat_ref)
    listed = listed_ref[cross_full(listed_ref)[2] :].astype(jnp.float32)
    listing = listed.shape[0] // 2
    pick(place_ref, counts_ref, listed[:listing], flat_ref, FULL, 2, picked_0)
    pick(place_ref, counts_ref, listed[listing:], flat_ref, FULL, 3, picked_1)


def near_kernel(bins, sent, place_ref, counts_ref, own_pairs_ref, near_pairs_ref, flat_ref, *refs):
    picked_0, *picked_1 = refs[-1 - sent :]
    pick(place_ref, counts_ref, listing_of(near_pairs_ref, LANES), flat_ref, bins, 1, *picked_1)
    pick(place_ref, counts_ref, listing_of(own_pairs_ref, LANES), flat_ref, bins, 0, picked_0)


def both_rounds(rows, sign):
    row = lax.broadcasted_iota(jnp.int32, rows.shape, 0)
    rows = rows * jnp.where(row < rows.shape[0] // 2, 1.0, sign)
    empty = jnp.zeros_like(rows)
    return jnp.concatenate(
        [jnp.concatenate([rows, empty], axis=1), jnp.concatenate([empty, rows], axis=1)]
    )


def halves(table):
    high = table.astype(jnp.bfloat16)
    return high, (table - high.astype(jnp.float32)).astype(jnp.bfloat16)


def first_lags_kernel(groups, place_ref, inverse_ref, *refs):
    part_0, part_2, part_3, full_0, part_1, *full_1, lags_ref, table_ref = refs
    samples = inverse_ref.shape[1]
    quarter, _ = place_of(place_ref, groups)
    low = quarter % 2
    sign = jnp.where(quarter // 2 == low, 1.0, -1.0)

    def part_table(which):
        start = pl.multiple_of((low ^ which) * 2 * PART, 2 * PART)
        return halves(both_rounds(inverse_ref[pl.ds(start, 2 * PART), :], sign))

    def full_table(mq):
        start = pl.multiple_of(4 * PART + (quarter ^ mq) * 2 * FULL, 2 * FULL)
        return halves(both_rounds(inverse_ref[pl.ds(start, 2 * FULL), :], sign))

    near, other = part_table(0), part_table(1)
    lags = 0.0
    full_1 = jnp.concatenate([ref[...] for ref in full_1])
    for picked, bins, table in (
        (part_0[...], PART, near),
        (part_2[...], PART, near),
        (part_1[...], PART, other),
        (part_3[...], PART, other),
        (full_0[...], FULL, full_table(0)),
        (full_1, FULL, full_table(1)),
    ):
        picked = unpack(picked, bins)
        for half in table:
            lags += jnp.dot(picked, half, preferred_element_type=jnp.float32)
    for step_round in range(2):
        lags_ref[step_round] = lags[:, step_round * samples : (step_round + 1) * samples]
    for at in range(2):
        for which, half in enumerate(full_table(2 + at)):
            table_ref[at, which] = half


def lag_kernel(first_ref, table_ref, *refs):
    picked_refs, lags_ref = refs[:-1], refs[-1]
    samples = lags_ref.shape[2]
    more = 0.0
    for at, ref in enumerate(picked_refs):
        picked = unpack(ref[...], FULL)
        for which in range(2):
            more += jnp.dot(picked, table_ref[at, which], preferred_element_type=jnp.float32)
    for step_round in range(2):
        lags_ref[step_round] = (
            first_ref[step_round] + more[:, step_round * samples : (step_round + 1) * samples]
        )


def on_device(windows, counts, pairs):
    comps, _, events, samples = windows.shape
    cells = lax.axis_size("cell")
    half, groups = cells // 2, cells // 4
    count = pairs.shape[2]
    inverse = jnp.asarray(inverse_table(samples, cells))
    place = lax.axis_index("cell").astype(jnp.int32).reshape(1)

    def swap(x, mask):
        return lax.ppermute(x, "cell", [(i, i ^ mask) for i in range(cells)])

    def shape(*dims, dtype=jnp.bfloat16):
        return jax.ShapeDtypeStruct(dims, dtype)

    vmem = pl.BlockSpec(memory_space=pltpu.VMEM)
    smem = pl.BlockSpec(memory_space=pltpu.SMEM)
    params = pltpu.CompilerParams(vmem_limit_bytes=VMEM_LIMIT)

    def cost(microseconds):
        return pl.CostEstimate(
            flops=int(microseconds * 1e9), bytes_accessed=2**20, transcendentals=0
        )

    windows = windows.reshape(comps, 2, groups, 2 * SLOTS, samples)
    near_windows, near_pairs = swap(windows, 1), swap(pairs, 1)
    part_rows, full_rows = comps * 2 * PART, comps * 2 * FULL
    part_spectra, full_spectra, table = pl.pallas_call(
        own_kernel,
        out_shape=[
            shape(groups, part_rows, LANES),
            shape(2 * groups, full_rows, LANES),
            shape(2 * PART + 4 * FULL, samples),
        ],
        in_specs=[smem, vmem],
        out_specs=[vmem] * 3,
        compiler_params=params,
        cost_estimate=cost(1),
        name="own_spectra",
    )(place, windows)
    listing = 2 * pairs.size // LANES
    pieces = pl.pallas_call(
        near_spectra_kernel,
        out_shape=[shape(2 * (part_rows + full_rows), LANES)] * groups
        + [shape(2 * full_rows + listing * (mg == 0), LANES) for mg in range(groups)],
        in_specs=[smem] + [vmem] * 6,
        out_specs=[vmem] * (2 * groups),
        compiler_params=params,
        cost_estimate=cost(1),
        name="near_spectra",
    )(place, pairs, near_pairs, table, part_spectra, full_spectra, near_windows)
    arrived = [pieces[0]] + [swap(pieces[m], 2 * m) for m in range(1, 2 * groups)]
    sides, far = arrived[:groups], arrived[groups:]

    early, late = far[: groups - 2], far[groups - 2 :]
    part_packed = shape(packed_rows(count, PART), LANES)
    full_packed = shape(packed_rows(count, FULL), LANES)
    half_packed = shape(packed_rows(count, FULL) // 2, LANES)
    part_blocks = shape(2, 2, SLOTS * SLOTS * width(PART) // LANES, 2 * LANES)
    full_blocks = shape(2, 2, SLOTS * SLOTS * width(FULL) // LANES, 2 * LANES)
    part_flat = pl.pallas_call(
        part_kernel,
        out_shape=part_blocks,
        in_specs=[vmem] * groups,
        out_specs=vmem,
        scratch_shapes=[
            pltpu.VMEM((padded(groups * 2 * comps) * 2 * PART, LANES), jnp.float32),
            pltpu.VMEM((2 * SLOTS * 2 * PART, LANES), jnp.float32),
        ],
        compiler_params=params,
        cost_estimate=cost(2),
        name="part",
    )(*sides)
    part_2, part_3 = pl.pallas_call(
        functools.partial(far_kernel, PART),
        out_shape=[part_packed, part_packed],
        in_specs=[smem, smem, vmem, vmem],
        out_specs=[vmem, vmem],
        compiler_params=params,
        cost_estimate=cost(1),
        name="part_far",
    )(place, counts, far[0], part_flat)
    part_0, part_1 = pl.pallas_call(
        functools.partial(near_kernel, PART, 1),
        out_shape=[part_packed, part_packed],
        in_specs=[smem, smem] + [vmem] * 3,
        out_specs=[vmem] * 2,
        compiler_params=params,
        cost_estimate=cost(1),
        name="part_near",
    )(place, counts, pairs, near_pairs, part_flat)
    part_1 = swap(part_1, 1)
    sums = pl.pallas_call(
        functools.partial(early_kernel, groups),
        out_shape=shape(2 * SLOTS * 2 * FULL, LANES, dtype=jnp.float32),
        in_specs=[pl.BlockSpec(memory_space=pl.ANY)] + [vmem] * (groups + len(early)),
        out_specs=vmem,
        scratch_shapes=[
            pltpu.VMEM((padded((groups + len(early)) * 2 * comps) * 2 * FULL, LANES), jnp.float32)
        ],
        compiler_params=params,
        cost_estimate=cost(0.001),
        name="early",
    )(part_flat, *sides, *early)
    sent, part_3 = pl.pallas_call(
        hold_kernel,
        out_shape=[part_packed, part_packed],
        in_specs=[vmem] * 2 + [pl.BlockSpec(memory_space=pl.ANY)] * 3,
        out_specs=[vmem] * 2,
        compiler_params=params,
        cost_estimate=cost(0.1),
        name="hold",
    )(part_2, part_3, part_0, sums, late[0])
    part_2, part_3 = swap(sent, half), swap(part_3, half + 1)
    full_flat, full_2, full_3 = pl.pallas_call(
        full_kernel,
        out_shape=[full_blocks, full_packed, full_packed],
        in_specs=[smem, smem, vmem] + [pl.BlockSpec(memory_space=pl.ANY)] * 2 + [vmem] * (1 + len(late)),
        out_specs=[vmem] * 3,
        scratch_shapes=[
            pltpu.VMEM((padded(len(late) * 2 * comps) * 2 * FULL, LANES), jnp.float32),
            pltpu.VMEM((2 * SLOTS * 2 * FULL, LANES), jnp.float32),
        ],
        compiler_params=params,
        cost_estimate=cost(10),
        name="full",
    )(place, counts, far[0], part_0, sent, sums, *late)
    full_2, full_3 = swap(full_2, half), swap(full_3, half + 1)
    full_0, *full_1 = pl.pallas_call(
        functools.partial(near_kernel, FULL, 2),
        out_shape=[full_packed, half_packed, half_packed],
        in_specs=[smem, smem] + [vmem] * 3 + [pl.BlockSpec(memory_space=pl.ANY)] * 2,
        out_specs=[vmem] * 3,
        compiler_params=params,
        cost_estimate=cost(0.5),
        name="full_near",
    )(place, counts, pairs, near_pairs, full_flat, part_2, part_3)
    full_1 = [swap(x, 1) for x in full_1]

    first, tables = pl.pallas_call(
        functools.partial(first_lags_kernel, groups),
        out_shape=[
            shape(2, count, samples, dtype=jnp.float32),
            shape(2, 2, 4 * FULL, 2 * samples),
        ],
        in_specs=[smem] + [vmem] * 8,
        out_specs=[vmem] * 2,
        compiler_params=params,
        cost_estimate=cost(0.001),
        name="first_lags",
    )(place, inverse, part_0, part_2, part_3, full_0, part_1, *full_1)
    return pl.pallas_call(
        lag_kernel,
        out_shape=shape(2, count, samples, dtype=jnp.float32),
        in_specs=[vmem] * 4,
        out_specs=vmem,
        compiler_params=params,
        cost_estimate=cost(1),
        name="lags",
    )(first, tables, full_2, full_3)


def solution(mesh):
    in_specs = (P(None, "cell", "grp", None), P("grp"), P(None, None, ("grp", "cell")))
    out_specs = P(None, ("grp", "cell"), None)
    return jax.shard_map(
        on_device, mesh=mesh, in_specs=in_specs, out_specs=out_specs, check_vma=False
    )
```

```python
import functools
import math

import jax
import jax.numpy as jnp
import numpy as np
from jax import lax
from jax.experimental import pallas as pl
from jax.experimental.pallas import tpu as pltpu
from jax.sharding import PartitionSpec as P

EPSILON = 1e-06
COSINE = (
    0.9999999999993376,
    -4.934802200431432,
    4.058712123240781,
    -1.3352627346923478,
    0.23533044681677665,
    -0.02580633847975355,
    0.0019285963125396874,
    -0.00010362767792380447,
    3.734915399663344e-06,
)
SLOTS = 32
LANES = 4 * SLOTS
COMPS = 3
NT = (((1,), (1,)), ((), ()))
TN = (((0,), (0,)), ((), ()))
VMEM_LIMIT = 40 * 1024 * 1024

PART = 16
FULL = 24


def inverse_table(samples, stations):
    bins = samples // 2
    turn = np.arange(bins)[:, None] * np.arange(samples)[None, :] % samples
    angle = turn * (2.0 * math.pi / samples)
    weight = np.where(np.arange(bins) == 0, 1.0, 2.0)[:, None] / samples
    weight = weight * math.sqrt(samples / (3.0 * stations))
    real, imag = weight * np.cos(angle), -weight * np.sin(angle)
    runs = [(at, PART) for at in range(0, 2 * PART, PART)]
    runs += [(at, FULL) for at in range(2 * PART, bins, FULL)]
    rows = [part[at : at + run] for at, run in runs for part in (real, imag)]
    return np.concatenate(rows).astype(np.float32)


def forward_rows(bins, samples):
    count = bins.shape[0]
    sample = lax.broadcasted_iota(jnp.int32, (2 * count, samples), 1)
    turn = jnp.concatenate([bins * sample[:count], bins * sample[:count] + samples // 4])
    turn &= samples - 1
    x = jnp.where(turn > samples // 2, turn - samples, turn).astype(jnp.float32) * (2.0 / samples)
    square = x * x
    value = jnp.full(square.shape, COSINE[-1], jnp.float32)
    for factor in COSINE[-2::-1]:
        value = value * square + factor
    return value.astype(jnp.bfloat16)


def place_of(place_ref, groups):
    position = place_ref[0]
    high, inner = position // (2 * groups), position % (2 * groups)
    return high * 2 + inner % 2, inner // 2


def listing_of(pairs_ref, lanes):
    ends = []
    for end in range(2):
        slots = pairs_ref[:, end, :].astype(jnp.float32)
        ends += [slots[:, at : at + lanes] for at in range(0, slots.shape[1], lanes)]
    return jnp.concatenate(ends)


def station_spectra(windows_ref, at, table):
    parts = []
    for comp in range(windows_ref.shape[0]):
        low = windows_ref[comp, 0, at]
        high = windows_ref[comp, 1, at]
        parts += [low[:SLOTS], high[SLOTS:], low[SLOTS:], high[:SLOTS]]
    traces = jnp.concatenate(parts)
    square = jnp.square(traces.astype(jnp.float32))
    square_hi = square.astype(jnp.bfloat16)
    square_lo = (square - square_hi.astype(jnp.float32)).astype(jnp.bfloat16)
    ones = jnp.ones((16, traces.shape[1]), jnp.bfloat16)
    energy = lax.dot_general(ones, square_hi, NT, preferred_element_type=jnp.float32)
    energy += lax.dot_general(ones, square_lo, NT, preferred_element_type=jnp.float32)
    scale = lax.rsqrt(energy[:1] + EPSILON)
    raw = lax.dot_general(table, traces, NT, preferred_element_type=jnp.float32)
    return (raw * scale).astype(jnp.bfloat16)


def own_kernel(place_ref, windows_ref, part_ref, full_ref, table_ref):
    groups, samples = windows_ref.shape[2], windows_ref.shape[4]
    quarter, group = place_of(place_ref, groups)
    bins = lax.broadcasted_iota(jnp.int32, (PART, samples), 0) + (quarter % 2) * PART
    table_ref[: 2 * PART] = forward_rows(bins, samples)
    for far in range(2):
        start = 2 * PART + (quarter ^ (2 * far)) * FULL
        bins = lax.broadcasted_iota(jnp.int32, (FULL, samples), 0) + start
        at = 2 * PART + 2 * FULL * far
        table_ref[at : at + 2 * FULL] = forward_rows(bins, samples)
    table = table_ref[...]
    for mg in range(groups):
        spectra = station_spectra(windows_ref, group ^ mg, table)
        for comp in range(COMPS):
            lanes = spectra[:, comp * LANES : (comp + 1) * LANES]
            part_ref[mg, comp * 2 * PART : (comp + 1) * 2 * PART] = lanes[: 2 * PART]
            for far in range(2):
                at = 2 * PART + 2 * FULL * far
                full_ref[far * groups + mg, comp * 2 * FULL : (comp + 1) * 2 * FULL] = lanes[at : at + 2 * FULL]


def near_spectra_kernel(
    place_ref, own_pairs_ref, near_pairs_ref, table_ref, part_ref, full_ref, windows_ref, *piece_refs
):
    groups = windows_ref.shape[2]
    _, group = place_of(place_ref, groups)
    table = table_ref[...]
    part_rows, full_rows = COMPS * 2 * PART, COMPS * 2 * FULL
    piece_refs[groups][2 * full_rows :] = jnp.concatenate(
        [listing_of(own_pairs_ref, LANES), listing_of(near_pairs_ref, LANES)]
    ).astype(jnp.bfloat16)
    for mg in range(groups):
        spectra = station_spectra(windows_ref, group ^ mg, table)
        side, cross = piece_refs[mg], piece_refs[groups + mg]
        side[:part_rows] = part_ref[mg]
        side[2 * part_rows : 2 * part_rows + full_rows] = full_ref[mg]
        cross[:full_rows] = full_ref[groups + mg]
        for comp in range(COMPS):
            lanes = spectra[:, comp * LANES : (comp + 1) * LANES]
            at = part_rows + comp * 2 * PART
            side[at : at + 2 * PART] = lanes[: 2 * PART]
            at = 2 * part_rows + full_rows + comp * 2 * FULL
            side[at : at + 2 * FULL] = lanes[2 * PART : 2 * PART + 2 * FULL]
            at = full_rows + comp * 2 * FULL
            cross[at : at + 2 * FULL] = lanes[2 * PART + 2 * FULL :]


def width(bins):
    return 1 << (bins - 1).bit_length()


def packing(count, bins):
    used = 4 * bins
    spare = LANES - used
    if not spare:
        return count, [[(0, 0, 0, used)]]
    runs = used // spare
    rows = count // (runs + 1)
    return rows, [
        [(at * rows, 0, 0, used), (runs * rows, used, at * spare, (at + 1) * spare)] for at in range(runs)
    ]


def packed_rows(count, bins):
    rows, parts = packing(count, bins)
    return rows * len(parts)


def unpack(picked, bins):
    used = 4 * bins
    spare = LANES - used
    if not spare:
        return picked
    runs = used // spare
    rows = picked.shape[0] // runs
    rest = [picked[at * rows : (at + 1) * rows, used:] for at in range(runs)]
    return jnp.concatenate([picked[:, :used], jnp.concatenate(rest, axis=1)])


def pick(place_ref, counts_ref, listed, flat_ref, bins, mq, *picked_refs):
    cells = counts_ref.shape[0]
    quarter, group = place_of(place_ref, cells // 4)
    own = quarter ^ mq
    high, low = own // 2, own % 2
    cell = high * (cells // 2) + group * 2 + low
    count = listed.shape[0] // 2
    runs = LANES // width(bins)
    run_bits, bin_bits, lane_bits = (n.bit_length() - 1 for n in (runs, width(bins), LANES))
    first, second = listed[:count].astype(jnp.int32), listed[count:].astype(jnp.int32)
    far_counts = [counts_ref[cell ^ 1], counts_ref[cell ^ (cells // 2)]]
    odd = lax.broadcasted_iota(jnp.int32, (count, LANES), 0) & 1
    live = (first < counts_ref[cell]) & (second < jnp.where(odd == 1, far_counts[1], far_counts[0]))
    left, right = jnp.where(high == low, first, second), jnp.where(high == low, second, first)
    spot = jnp.where(live, (left >> run_bits) * SLOTS + right, -1)
    turned = (spot * runs + (left & (runs - 1))).T
    lane = lax.broadcasted_iota(jnp.int32, (LANES, LANES), 1)
    run = lane >> bin_bits
    sides = ((high, high), (low, 1 - low))
    found = []
    for step_round in range(2):
        hot, here = [], []
        for at in range(step_round, count, 2):
            both = jnp.broadcast_to(turned[:, at : at + 1], (LANES, LANES))
            here.append((both & (runs - 1)) == run)
            offset = (both >> run_bits) - lane
            hot.append(
                jnp.concatenate(
                    [
                        jnp.where(offset == start, 1.0, 0.0).astype(jnp.bfloat16)
                        for start in range(0, flat_ref.shape[2], LANES)
                    ],
                    axis=1,
                )
            )
        block = flat_ref[sides[step_round][0], sides[step_round][1]]
        wide = jnp.dot(jnp.concatenate(hot), block, preferred_element_type=jnp.float32)
        masked = []
        for chunk, mask in enumerate(here):
            part = wide[chunk * LANES : (chunk + 1) * LANES]
            masked.append(
                jnp.concatenate(
                    [
                        jnp.where(mask, part[:, :LANES], 0.0).astype(jnp.bfloat16),
                        jnp.where(mask, part[:, LANES:], 0.0).astype(jnp.bfloat16),
                    ],
                    axis=1,
                )
            )
        found.append(jnp.concatenate(masked))
    found = jnp.concatenate(found, axis=1)
    spread = lax.broadcasted_iota(jnp.int32, (4 * LANES, LANES), 0)
    kept = lax.broadcasted_iota(jnp.int32, (4 * LANES, LANES), 1)
    bin_of = spread & (width(bins) - 1)
    value = jnp.where(bin_of < bins, (spread >> lane_bits) * bins + bin_of, -1)
    rows, parts = packing(found.shape[0], bins)
    picked = []
    for entries in parts:
        total = 0.0
        for start, at, least, end in entries:
            fold = (value >= least) & (value < end) & (kept == value + (at - least))
            total += jnp.dot(
                found[start : start + rows],
                jnp.where(fold, 1.0, 0.0).astype(jnp.bfloat16),
                preferred_element_type=jnp.float32,
            )
        picked.append(total.astype(jnp.bfloat16))
    picked = jnp.concatenate(picked)
    each = picked.shape[0] // len(picked_refs)
    for at, ref in enumerate(picked_refs):
        ref[...] = picked[at * each : (at + 1) * each]


def padded(traces):
    return -(-traces // 16) * 16


def add_cross(pieces, trace_ref, bins, sums_ref, before_ref=None):
    slots, rows = 2 * SLOTS, 2 * bins
    traces = trace_ref.shape[0] // rows
    start = 0
    for piece, at, size in pieces:
        trace_ref[start : start + size] = piece[at : at + size].astype(jnp.float32)
        start += size
    if start < traces * rows:
        trace_ref[start:] = jnp.zeros((traces * rows - start, LANES), jnp.float32)
    lower = lax.broadcasted_iota(jnp.int32, (traces, LANES), 1) < slots
    for k in range(bins):
        real = trace_ref[pl.ds(k, traces, stride=rows), :]
        imag = trace_ref[pl.ds(bins + k, traces, stride=rows), :]
        left = jnp.concatenate([real, imag]).astype(jnp.bfloat16)[:, :slots]
        right = jnp.concatenate(
            [
                jnp.where(lower, pltpu.roll(real, slots, 1), imag),
                jnp.where(lower, pltpu.roll(imag, slots, 1), -real),
            ]
        ).astype(jnp.bfloat16)
        cross = lax.dot_general(left, right, TN, preferred_element_type=jnp.float32)
        if before_ref is not None:
            cross += before_ref[k * slots : (k + 1) * slots]
        sums_ref[k * slots : (k + 1) * slots] = cross


def turn_blocks(cross_ref, bins, flat_ref):
    slots, runs = 2 * SLOTS, LANES // width(bins)
    empty = jnp.zeros((width(bins) - bins, LANES), jnp.float32)
    for own in range(2):
        for at in range(SLOTS // runs):
            block = []
            for i in range(runs):
                block.append(cross_ref[pl.ds(own * SLOTS + at * runs + i, bins, stride=slots), :])
                block += [empty] * (bins < width(bins))
            block = jnp.concatenate(block).T.astype(jnp.bfloat16)
            for part in range(2):
                for far in range(2):
                    start = (part * 2 + far) * SLOTS
                    flat_ref[
                        own, far, at * SLOTS : (at + 1) * SLOTS, part * LANES : (part + 1) * LANES
                    ] = block[start : start + SLOTS]


def side_part(ref):
    return (ref, 0, 2 * COMPS * 2 * PART)


def side_full(ref):
    return (ref, 2 * COMPS * 2 * PART, 2 * COMPS * 2 * FULL)


def cross_full(ref):
    return (ref, 0, 2 * COMPS * 2 * FULL)


def part_kernel(*refs):
    piece_refs, (flat_ref, trace_ref, cross_ref) = refs[:-3], refs[-3:]
    add_cross([side_part(ref) for ref in piece_refs], trace_ref, PART, cross_ref)
    turn_blocks(cross_ref, PART, flat_ref)


def far_kernel(bins, place_ref, counts_ref, listed_ref, flat_ref, picked_0, picked_1):
    listed = listed_ref[cross_full(listed_ref)[2] :].astype(jnp.float32)
    listing = listed.shape[0] // 2
    pick(place_ref, counts_ref, listed[:listing], flat_ref, bins, 2, picked_0)
    pick(place_ref, counts_ref, listed[listing:], flat_ref, bins, 3, picked_1)


def hold_kernel(picked_ref, after_0, after_1, held_ref):
    held_ref[...] = picked_ref[...]


def early_kernel(sides, after_0, after_1, *refs):
    piece_refs, (sums_ref, trace_ref) = refs[:-2], refs[-2:]
    pieces = [side_full(ref) for ref in piece_refs[:sides]] + [cross_full(ref) for ref in piece_refs[sides:]]
    add_cross(pieces, trace_ref, FULL, sums_ref)


def full_kernel(place_ref, counts_ref, listed_ref, after_0, after_2, before_ref, *refs):
    piece_refs, (flat_ref, picked_0, picked_1, trace_ref, cross_ref) = refs[:-5], refs[-5:]
    add_cross([cross_full(ref) for ref in piece_refs], trace_ref, FULL, cross_ref, before_ref)
    turn_blocks(cross_ref, FULL, flat_ref)
    listed = listed_ref[cross_full(listed_ref)[2] :].astype(jnp.float32)
    listing = listed.shape[0] // 2
    pick(place_ref, counts_ref, listed[:listing], flat_ref, FULL, 2, picked_0)
    pick(place_ref, counts_ref, listed[listing:], flat_ref, FULL, 3, picked_1)


def near_kernel(bins, sent, place_ref, counts_ref, own_pairs_ref, near_pairs_ref, flat_ref, *refs):
    picked_0, *picked_1 = refs[-1 - sent :]
    pick(place_ref, counts_ref, listing_of(near_pairs_ref, LANES), flat_ref, bins, 1, *picked_1)
    pick(place_ref, counts_ref, listing_of(own_pairs_ref, LANES), flat_ref, bins, 0, picked_0)


def both_rounds(rows, sign):
    row = lax.broadcasted_iota(jnp.int32, rows.shape, 0)
    rows = rows * jnp.where(row < rows.shape[0] // 2, 1.0, sign)
    empty = jnp.zeros_like(rows)
    return jnp.concatenate(
        [jnp.concatenate([rows, empty], axis=1), jnp.concatenate([empty, rows], axis=1)]
    )


def halves(table):
    high = table.astype(jnp.bfloat16)
    return high, (table - high.astype(jnp.float32)).astype(jnp.bfloat16)


def first_lags_kernel(groups, place_ref, inverse_ref, *refs):
    part_0, part_2, part_3, full_0, part_1, *full_1, lags_ref, table_ref = refs
    samples = inverse_ref.shape[1]
    quarter, _ = place_of(place_ref, groups)
    low = quarter % 2
    sign = jnp.where(quarter // 2 == low, 1.0, -1.0)

    def part_table(which):
        start = pl.multiple_of((low ^ which) * 2 * PART, 2 * PART)
        return halves(both_rounds(inverse_ref[pl.ds(start, 2 * PART), :], sign))

    def full_table(mq):
        start = pl.multiple_of(4 * PART + (quarter ^ mq) * 2 * FULL, 2 * FULL)
        return halves(both_rounds(inverse_ref[pl.ds(start, 2 * FULL), :], sign))

    near, other = part_table(0), part_table(1)
    lags = 0.0
    full_1 = jnp.concatenate([ref[...] for ref in full_1])
    for picked, bins, table in (
        (part_0[...], PART, near),
        (part_2[...], PART, near),
        (part_1[...], PART, other),
        (part_3[...], PART, other),
        (full_0[...], FULL, full_table(0)),
        (full_1, FULL, full_table(1)),
    ):
        picked = unpack(picked, bins)
        for half in table:
            lags += jnp.dot(picked, half, preferred_element_type=jnp.float32)
    for step_round in range(2):
        lags_ref[step_round] = lags[:, step_round * samples : (step_round + 1) * samples]
    for at in range(2):
        table_ref[at] = full_table(2 + at)[0]


def lag_kernel(first_ref, table_ref, *refs):
    picked_refs, lags_ref = refs[:-1], refs[-1]
    samples = lags_ref.shape[2]
    more = 0.0
    for at, ref in enumerate(picked_refs):
        more += jnp.dot(unpack(ref[...], FULL), table_ref[at], preferred_element_type=jnp.float32)
    for step_round in range(2):
        lags_ref[step_round] = (
            first_ref[step_round] + more[:, step_round * samples : (step_round + 1) * samples]
        )


def on_device(windows, counts, pairs):
    comps, _, events, samples = windows.shape
    cells = lax.axis_size("cell")
    half, groups = cells // 2, cells // 4
    count = pairs.shape[2]
    inverse = jnp.asarray(inverse_table(samples, cells))
    place = lax.axis_index("cell").astype(jnp.int32).reshape(1)

    def swap(x, mask):
        return lax.ppermute(x, "cell", [(i, i ^ mask) for i in range(cells)])

    def shape(*dims, dtype=jnp.bfloat16):
        return jax.ShapeDtypeStruct(dims, dtype)

    vmem = pl.BlockSpec(memory_space=pltpu.VMEM)
    smem = pl.BlockSpec(memory_space=pltpu.SMEM)
    params = pltpu.CompilerParams(vmem_limit_bytes=VMEM_LIMIT)

    def cost(microseconds):
        return pl.CostEstimate(
            flops=int(microseconds * 1e9), bytes_accessed=2**20, transcendentals=0
        )

    windows = windows.reshape(comps, 2, groups, 2 * SLOTS, samples)
    near_windows, near_pairs = swap(windows, 1), swap(pairs, 1)
    part_rows, full_rows = comps * 2 * PART, comps * 2 * FULL
    part_spectra, full_spectra, table = pl.pallas_call(
        own_kernel,
        out_shape=[
            shape(groups, part_rows, LANES),
            shape(2 * groups, full_rows, LANES),
            shape(2 * PART + 4 * FULL, samples),
        ],
        in_specs=[smem, vmem],
        out_specs=[vmem] * 3,
        compiler_params=params,
        cost_estimate=cost(1),
        name="own_spectra",
    )(place, windows)
    listing = 2 * pairs.size // LANES
    pieces = pl.pallas_call(
        near_spectra_kernel,
        out_shape=[shape(2 * (part_rows + full_rows), LANES)] * groups
        + [shape(2 * full_rows + listing * (mg == 0), LANES) for mg in range(groups)],
        in_specs=[smem] + [vmem] * 6,
        out_specs=[vmem] * (2 * groups),
        compiler_params=params,
        cost_estimate=cost(1),
        name="near_spectra",
    )(place, pairs, near_pairs, table, part_spectra, full_spectra, near_windows)
    arrived = [pieces[0]] + [swap(pieces[m], 2 * m) for m in range(1, 2 * groups)]
    sides, far = arrived[:groups], arrived[groups:]

    early, late = far[: groups - 2], far[groups - 2 :]
    part_packed = shape(packed_rows(count, PART), LANES)
    full_packed = shape(packed_rows(count, FULL), LANES)
    half_packed = shape(packed_rows(count, FULL) // 2, LANES)
    part_blocks = shape(2, 2, SLOTS * SLOTS * width(PART) // LANES, 2 * LANES)
    full_blocks = shape(2, 2, SLOTS * SLOTS * width(FULL) // LANES, 2 * LANES)
    part_flat = pl.pallas_call(
        part_kernel,
        out_shape=part_blocks,
        in_specs=[vmem] * groups,
        out_specs=vmem,
        scratch_shapes=[
            pltpu.VMEM((padded(groups * 2 * comps) * 2 * PART, LANES), jnp.float32),
            pltpu.VMEM((2 * SLOTS * PART, LANES), jnp.float32),
        ],
        compiler_params=params,
        cost_estimate=cost(0.001),
        name="part",
    )(*sides)
    part_2, part_3 = pl.pallas_call(
        functools.partial(far_kernel, PART),
        out_shape=[part_packed, part_packed],
        in_specs=[smem, smem, vmem, vmem],
        out_specs=[vmem, vmem],
        compiler_params=params,
        cost_estimate=cost(1),
        name="part_far",
    )(place, counts, far[0], part_flat)
    part_0, part_1 = pl.pallas_call(
        functools.partial(near_kernel, PART, 1),
        out_shape=[part_packed, part_packed],
        in_specs=[smem, smem] + [vmem] * 3,
        out_specs=[vmem] * 2,
        compiler_params=params,
        cost_estimate=cost(0.001),
        name="part_near",
    )(place, counts, pairs, near_pairs, part_flat)
    part_1 = swap(part_1, 1)
    sums = pl.pallas_call(
        functools.partial(early_kernel, groups),
        out_shape=shape(2 * SLOTS * FULL, LANES, dtype=jnp.float32),
        in_specs=[pl.BlockSpec(memory_space=pl.ANY)] * 2 + [vmem] * (groups + len(early)),
        out_specs=vmem,
        scratch_shapes=[
            pltpu.VMEM((padded((groups + len(early)) * 2 * comps) * 2 * FULL, LANES), jnp.float32)
        ],
        compiler_params=params,
        cost_estimate=cost(0.001),
        name="early",
    )(part_0, part_2, *sides, *early)
    held = pl.pallas_call(
        hold_kernel,
        out_shape=part_packed,
        in_specs=[vmem] + [pl.BlockSpec(memory_space=pl.ANY)] * 2,
        out_specs=vmem,
        compiler_params=params,
        cost_estimate=cost(0.1),
        name="hold",
    )(part_3, sums, late[0])
    part_2, part_3 = swap(part_2, half), swap(held, half + 1)
    full_flat, full_2, full_3 = pl.pallas_call(
        full_kernel,
        out_shape=[full_blocks, full_packed, full_packed],
        in_specs=[smem, smem, vmem] + [pl.BlockSpec(memory_space=pl.ANY)] * 2 + [vmem] * (1 + len(late)),
        out_specs=[vmem] * 3,
        scratch_shapes=[
            pltpu.VMEM((padded(len(late) * 2 * comps) * 2 * FULL, LANES), jnp.float32),
            pltpu.VMEM((2 * SLOTS * FULL, LANES), jnp.float32),
        ],
        compiler_params=params,
        cost_estimate=cost(10),
        name="full",
    )(place, counts, far[0], part_0, held, sums, *late)
    full_2, full_3 = swap(full_2, half), swap(full_3, half + 1)
    full_0, *full_1 = pl.pallas_call(
        functools.partial(near_kernel, FULL, 2),
        out_shape=[full_packed, half_packed, half_packed],
        in_specs=[smem, smem] + [vmem] * 3 + [pl.BlockSpec(memory_space=pl.ANY)] * 2,
        out_specs=[vmem] * 3,
        compiler_params=params,
        cost_estimate=cost(0.5),
        name="full_near",
    )(place, counts, pairs, near_pairs, full_flat, part_2, part_3)
    full_1 = [swap(x, 1) for x in full_1]

    first, tables = pl.pallas_call(
        functools.partial(first_lags_kernel, groups),
        out_shape=[
            shape(2, count, samples, dtype=jnp.float32),
            shape(2, 4 * FULL, 2 * samples),
        ],
        in_specs=[smem] + [vmem] * 8,
        out_specs=[vmem] * 2,
        compiler_params=params,
        cost_estimate=cost(0.001),
        name="first_lags",
    )(place, inverse, part_0, part_2, part_3, full_0, part_1, *full_1)
    return pl.pallas_call(
        lag_kernel,
        out_shape=shape(2, count, samples, dtype=jnp.float32),
        in_specs=[vmem] * 4,
        out_specs=vmem,
        compiler_params=params,
        cost_estimate=cost(1),
        name="lags",
    )(first, tables, full_2, full_3)


def solution(mesh):
    in_specs = (P(None, "cell", "grp", None), P("grp"), P(None, None, ("grp", "cell")))
    out_specs = P(None, ("grp", "cell"), None)
    return jax.shard_map(
        on_device, mesh=mesh, in_specs=in_specs, out_specs=out_specs, check_vma=False
    )
```

```python
import functools
import math

import jax
import jax.numpy as jnp
import numpy as np
from jax import lax
from jax.experimental import pallas as pl
from jax.experimental.pallas import tpu as pltpu
from jax.sharding import PartitionSpec as P

EPSILON = 1e-06
COSINE = (
    0.9999999999993376,
    -4.934802200431432,
    4.058712123240781,
    -1.3352627346923478,
    0.23533044681677665,
    -0.02580633847975355,
    0.0019285963125396874,
    -0.00010362767792380447,
    3.734915399663344e-06,
)
SLOTS = 32
LANES = 4 * SLOTS
COMPS = 3
NT = (((1,), (1,)), ((), ()))
TN = (((0,), (0,)), ((), ()))
VMEM_LIMIT = 40 * 1024 * 1024

PART = 16
FULL = 24


def inverse_table(samples, stations):
    bins = samples // 2
    turn = np.arange(bins)[:, None] * np.arange(samples)[None, :] % samples
    angle = turn * (2.0 * math.pi / samples)
    weight = np.where(np.arange(bins) == 0, 1.0, 2.0)[:, None] / samples
    weight = weight * math.sqrt(samples / (3.0 * stations))
    real, imag = weight * np.cos(angle), -weight * np.sin(angle)
    runs = [(at, PART) for at in range(0, 2 * PART, PART)]
    runs += [(at, FULL) for at in range(2 * PART, bins, FULL)]
    rows = [part[at : at + run] for at, run in runs for part in (real, imag)]
    return np.concatenate(rows).astype(np.float32)


def forward_rows(bins, samples):
    count = bins.shape[0]
    sample = lax.broadcasted_iota(jnp.int32, (2 * count, samples), 1)
    turn = jnp.concatenate([bins * sample[:count], bins * sample[:count] + samples // 4])
    turn &= samples - 1
    x = jnp.where(turn > samples // 2, turn - samples, turn).astype(jnp.float32) * (2.0 / samples)
    square = x * x
    value = jnp.full(square.shape, COSINE[-1], jnp.float32)
    for factor in COSINE[-2::-1]:
        value = value * square + factor
    return value.astype(jnp.bfloat16)


def place_of(place_ref, groups):
    position = place_ref[0]
    high, inner = position // (2 * groups), position % (2 * groups)
    return high * 2 + inner % 2, inner // 2


def listing_of(pairs_ref, lanes):
    ends = []
    for end in range(2):
        slots = pairs_ref[:, end, :].astype(jnp.float32)
        ends += [slots[:, at : at + lanes] for at in range(0, slots.shape[1], lanes)]
    return jnp.concatenate(ends)


def station_spectra(windows_ref, at, table):
    parts = []
    for comp in range(windows_ref.shape[0]):
        low = windows_ref[comp, 0, at]
        high = windows_ref[comp, 1, at]
        parts += [low[:SLOTS], high[SLOTS:], low[SLOTS:], high[:SLOTS]]
    traces = jnp.concatenate(parts)
    square = jnp.square(traces.astype(jnp.float32))
    square_hi = square.astype(jnp.bfloat16)
    square_lo = (square - square_hi.astype(jnp.float32)).astype(jnp.bfloat16)
    ones = jnp.ones((16, traces.shape[1]), jnp.bfloat16)
    energy = lax.dot_general(ones, square_hi, NT, preferred_element_type=jnp.float32)
    energy += lax.dot_general(ones, square_lo, NT, preferred_element_type=jnp.float32)
    scale = lax.rsqrt(energy[:1] + EPSILON)
    raw = lax.dot_general(table, traces, NT, preferred_element_type=jnp.float32)
    return (raw * scale).astype(jnp.bfloat16)


def own_kernel(place_ref, windows_ref, part_ref, full_ref, table_ref):
    groups, samples = windows_ref.shape[2], windows_ref.shape[4]
    quarter, group = place_of(place_ref, groups)
    bins = lax.broadcasted_iota(jnp.int32, (PART, samples), 0) + (quarter % 2) * PART
    table_ref[: 2 * PART] = forward_rows(bins, samples)
    for far in range(2):
        start = 2 * PART + (quarter ^ (2 * far)) * FULL
        bins = lax.broadcasted_iota(jnp.int32, (FULL, samples), 0) + start
        at = 2 * PART + 2 * FULL * far
        table_ref[at : at + 2 * FULL] = forward_rows(bins, samples)
    table = table_ref[...]
    for mg in range(groups):
        spectra = station_spectra(windows_ref, group ^ mg, table)
        for comp in range(COMPS):
            lanes = spectra[:, comp * LANES : (comp + 1) * LANES]
            part_ref[mg, comp * 2 * PART : (comp + 1) * 2 * PART] = lanes[: 2 * PART]
            for far in range(2):
                at = 2 * PART + 2 * FULL * far
                full_ref[far * groups + mg, comp * 2 * FULL : (comp + 1) * 2 * FULL] = lanes[at : at + 2 * FULL]


def near_spectra_kernel(
    place_ref, own_pairs_ref, near_pairs_ref, table_ref, part_ref, full_ref, windows_ref, *piece_refs
):
    groups = windows_ref.shape[2]
    _, group = place_of(place_ref, groups)
    table = table_ref[...]
    part_rows, full_rows = COMPS * 2 * PART, COMPS * 2 * FULL
    piece_refs[groups][2 * full_rows :] = jnp.concatenate(
        [listing_of(own_pairs_ref, LANES), listing_of(near_pairs_ref, LANES)]
    ).astype(jnp.bfloat16)
    for mg in range(groups):
        spectra = station_spectra(windows_ref, group ^ mg, table)
        side, cross = piece_refs[mg], piece_refs[groups + mg]
        side[:part_rows] = part_ref[mg]
        side[2 * part_rows : 2 * part_rows + full_rows] = full_ref[mg]
        cross[:full_rows] = full_ref[groups + mg]
        for comp in range(COMPS):
            lanes = spectra[:, comp * LANES : (comp + 1) * LANES]
            at = part_rows + comp * 2 * PART
            side[at : at + 2 * PART] = lanes[: 2 * PART]
            at = 2 * part_rows + full_rows + comp * 2 * FULL
            side[at : at + 2 * FULL] = lanes[2 * PART : 2 * PART + 2 * FULL]
            at = full_rows + comp * 2 * FULL
            cross[at : at + 2 * FULL] = lanes[2 * PART + 2 * FULL :]


def width(bins):
    return 1 << (bins - 1).bit_length()


def packing(count, bins):
    used = 4 * bins
    spare = LANES - used
    if not spare:
        return count, [[(0, 0, 0, used)]]
    runs = used // spare
    rows = count // (runs + 1)
    return rows, [
        [(at * rows, 0, 0, used), (runs * rows, used, at * spare, (at + 1) * spare)] for at in range(runs)
    ]


def packed_rows(count, bins):
    rows, parts = packing(count, bins)
    return rows * len(parts)


def unpack(picked, bins):
    used = 4 * bins
    spare = LANES - used
    if not spare:
        return picked
    runs = used // spare
    rows = picked.shape[0] // runs
    rest = [picked[at * rows : (at + 1) * rows, used:] for at in range(runs)]
    return jnp.concatenate([picked[:, :used], jnp.concatenate(rest, axis=1)])


def pick(place_ref, counts_ref, listed, flat_ref, bins, mq, *picked_refs):
    cells = counts_ref.shape[0]
    quarter, group = place_of(place_ref, cells // 4)
    own = quarter ^ mq
    high, low = own // 2, own % 2
    cell = high * (cells // 2) + group * 2 + low
    count = listed.shape[0] // 2
    runs = LANES // width(bins)
    run_bits, bin_bits, lane_bits = (n.bit_length() - 1 for n in (runs, width(bins), LANES))
    first, second = listed[:count].astype(jnp.int32), listed[count:].astype(jnp.int32)
    far_counts = [counts_ref[cell ^ 1], counts_ref[cell ^ (cells // 2)]]
    odd = lax.broadcasted_iota(jnp.int32, (count, LANES), 0) & 1
    live = (first < counts_ref[cell]) & (second < jnp.where(odd == 1, far_counts[1], far_counts[0]))
    left, right = jnp.where(high == low, first, second), jnp.where(high == low, second, first)
    spot = jnp.where(live, (left >> run_bits) * SLOTS + right, -1)
    turned = (spot * runs + (left & (runs - 1))).T
    lane = lax.broadcasted_iota(jnp.int32, (LANES, LANES), 1)
    run = lane >> bin_bits
    sides = ((high, high), (low, 1 - low))
    found = []
    for step_round in range(2):
        hot, here = [], []
        for at in range(step_round, count, 2):
            both = jnp.broadcast_to(turned[:, at : at + 1], (LANES, LANES))
            here.append((both & (runs - 1)) == run)
            offset = (both >> run_bits) - lane
            hot.append(
                jnp.concatenate(
                    [
                        jnp.where(offset == start, 1.0, 0.0).astype(jnp.bfloat16)
                        for start in range(0, flat_ref.shape[2], LANES)
                    ],
                    axis=1,
                )
            )
        block = flat_ref[sides[step_round][0], sides[step_round][1]]
        wide = jnp.dot(jnp.concatenate(hot), block, preferred_element_type=jnp.float32)
        masked = []
        for chunk, mask in enumerate(here):
            part = wide[chunk * LANES : (chunk + 1) * LANES]
            masked.append(
                jnp.concatenate(
                    [
                        jnp.where(mask, part[:, :LANES], 0.0).astype(jnp.bfloat16),
                        jnp.where(mask, part[:, LANES:], 0.0).astype(jnp.bfloat16),
                    ],
                    axis=1,
                )
            )
        found.append(jnp.concatenate(masked))
    found = jnp.concatenate(found, axis=1)
    spread = lax.broadcasted_iota(jnp.int32, (4 * LANES, LANES), 0)
    kept = lax.broadcasted_iota(jnp.int32, (4 * LANES, LANES), 1)
    bin_of = spread & (width(bins) - 1)
    value = jnp.where(bin_of < bins, (spread >> lane_bits) * bins + bin_of, -1)
    rows, parts = packing(found.shape[0], bins)
    picked = []
    for entries in parts:
        total = 0.0
        for start, at, least, end in entries:
            fold = (value >= least) & (value < end) & (kept == value + (at - least))
            total += jnp.dot(
                found[start : start + rows],
                jnp.where(fold, 1.0, 0.0).astype(jnp.bfloat16),
                preferred_element_type=jnp.float32,
            )
        picked.append(total.astype(jnp.bfloat16))
    picked = jnp.concatenate(picked)
    each = picked.shape[0] // len(picked_refs)
    for at, ref in enumerate(picked_refs):
        ref[...] = picked[at * each : (at + 1) * each]


def padded(traces):
    return -(-traces // 16) * 16


def add_cross(pieces, trace_ref, bins, sums_ref, before_ref=None):
    slots, rows = 2 * SLOTS, 2 * bins
    traces = trace_ref.shape[0] // rows
    start = 0
    for piece, at, size in pieces:
        trace_ref[start : start + size] = piece[at : at + size].astype(jnp.float32)
        start += size
    if start < traces * rows:
        trace_ref[start:] = jnp.zeros((traces * rows - start, LANES), jnp.float32)
    lower = lax.broadcasted_iota(jnp.int32, (traces, LANES), 1) < slots
    for k in range(bins):
        real = trace_ref[pl.ds(k, traces, stride=rows), :]
        imag = trace_ref[pl.ds(bins + k, traces, stride=rows), :]
        left = jnp.concatenate([real, imag]).astype(jnp.bfloat16)[:, :slots]
        right = jnp.concatenate(
            [
                jnp.where(lower, pltpu.roll(real, slots, 1), imag),
                jnp.where(lower, pltpu.roll(imag, slots, 1), -real),
            ]
        ).astype(jnp.bfloat16)
        cross = lax.dot_general(left, right, TN, preferred_element_type=jnp.float32)
        if before_ref is not None:
            cross += before_ref[k * slots : (k + 1) * slots]
        sums_ref[k * slots : (k + 1) * slots] = cross


def turn_blocks(cross_ref, bins, flat_ref):
    slots, runs = 2 * SLOTS, LANES // width(bins)
    empty = jnp.zeros((width(bins) - bins, LANES), jnp.float32)
    for own in range(2):
        for at in range(SLOTS // runs):
            block = []
            for i in range(runs):
                block.append(cross_ref[pl.ds(own * SLOTS + at * runs + i, bins, stride=slots), :])
                block += [empty] * (bins < width(bins))
            block = jnp.concatenate(block).T.astype(jnp.bfloat16)
            for part in range(2):
                for far in range(2):
                    start = (part * 2 + far) * SLOTS
                    flat_ref[
                        own, far, at * SLOTS : (at + 1) * SLOTS, part * LANES : (part + 1) * LANES
                    ] = block[start : start + SLOTS]


def side_part(ref):
    return (ref, 0, 2 * COMPS * 2 * PART)


def side_full(ref):
    return (ref, 2 * COMPS * 2 * PART, 2 * COMPS * 2 * FULL)


def cross_full(ref):
    return (ref, 0, 2 * COMPS * 2 * FULL)


def part_kernel(*refs):
    piece_refs, (flat_ref, trace_ref, cross_ref) = refs[:-3], refs[-3:]
    add_cross([side_part(ref) for ref in piece_refs], trace_ref, PART, cross_ref)
    turn_blocks(cross_ref, PART, flat_ref)


def far_kernel(bins, place_ref, counts_ref, listed_ref, flat_ref, after_ref, picked_0, picked_1):
    listed = listed_ref[cross_full(listed_ref)[2] :].astype(jnp.float32)
    listing = listed.shape[0] // 2
    pick(place_ref, counts_ref, listed[:listing], flat_ref, bins, 2, picked_0)
    pick(place_ref, counts_ref, listed[listing:], flat_ref, bins, 3, picked_1)


def early_kernel(sides, after_0, after_1, *refs):
    piece_refs, (sums_ref, trace_ref) = refs[:-2], refs[-2:]
    pieces = [side_full(ref) for ref in piece_refs[:sides]] + [cross_full(ref) for ref in piece_refs[sides:]]
    add_cross(pieces, trace_ref, FULL, sums_ref)


def full_kernel(place_ref, counts_ref, listed_ref, after_0, after_2, before_ref, *refs):
    piece_refs, (flat_ref, picked_0, picked_1, trace_ref, cross_ref) = refs[:-5], refs[-5:]
    add_cross([cross_full(ref) for ref in piece_refs], trace_ref, FULL, cross_ref, before_ref)
    turn_blocks(cross_ref, FULL, flat_ref)
    listed = listed_ref[cross_full(listed_ref)[2] :].astype(jnp.float32)
    listing = listed.shape[0] // 2
    pick(place_ref, counts_ref, listed[:listing], flat_ref, FULL, 2, picked_0)
    pick(place_ref, counts_ref, listed[listing:], flat_ref, FULL, 3, picked_1)


def near_kernel(bins, sent, place_ref, counts_ref, own_pairs_ref, near_pairs_ref, flat_ref, *refs):
    picked_0, *picked_1 = refs[-1 - sent :]
    pick(place_ref, counts_ref, listing_of(near_pairs_ref, LANES), flat_ref, bins, 1, *picked_1)
    pick(place_ref, counts_ref, listing_of(own_pairs_ref, LANES), flat_ref, bins, 0, picked_0)


def both_rounds(rows, sign):
    row = lax.broadcasted_iota(jnp.int32, rows.shape, 0)
    rows = rows * jnp.where(row < rows.shape[0] // 2, 1.0, sign)
    empty = jnp.zeros_like(rows)
    return jnp.concatenate(
        [jnp.concatenate([rows, empty], axis=1), jnp.concatenate([empty, rows], axis=1)]
    )


def halves(table):
    high = table.astype(jnp.bfloat16)
    return high, (table - high.astype(jnp.float32)).astype(jnp.bfloat16)


def first_lags_kernel(groups, place_ref, inverse_ref, *refs):
    part_0, part_2, part_3, full_0, part_1, *full_1, lags_ref, table_ref = refs
    samples = inverse_ref.shape[1]
    quarter, _ = place_of(place_ref, groups)
    low = quarter % 2
    sign = jnp.where(quarter // 2 == low, 1.0, -1.0)

    def part_table(which):
        start = pl.multiple_of((low ^ which) * 2 * PART, 2 * PART)
        return halves(both_rounds(inverse_ref[pl.ds(start, 2 * PART), :], sign))

    def full_table(mq):
        start = pl.multiple_of(4 * PART + (quarter ^ mq) * 2 * FULL, 2 * FULL)
        return halves(both_rounds(inverse_ref[pl.ds(start, 2 * FULL), :], sign))

    near, other = part_table(0), part_table(1)
    lags = 0.0
    full_1 = jnp.concatenate([ref[...] for ref in full_1])
    for picked, bins, table in (
        (part_0[...], PART, near),
        (part_2[...], PART, near),
        (part_1[...], PART, other),
        (part_3[...], PART, other),
        (full_0[...], FULL, full_table(0)),
        (full_1, FULL, full_table(1)),
    ):
        picked = unpack(picked, bins)
        for half in table:
            lags += jnp.dot(picked, half, preferred_element_type=jnp.float32)
    for step_round in range(2):
        lags_ref[step_round] = lags[:, step_round * samples : (step_round + 1) * samples]
    for at in range(2):
        table_ref[at] = full_table(2 + at)[0]


def lag_kernel(first_ref, table_ref, *refs):
    picked_refs, lags_ref = refs[:-1], refs[-1]
    samples = lags_ref.shape[2]
    more = 0.0
    for at, ref in enumerate(picked_refs):
        more += jnp.dot(unpack(ref[...], FULL), table_ref[at], preferred_element_type=jnp.float32)
    for step_round in range(2):
        lags_ref[step_round] = (
            first_ref[step_round] + more[:, step_round * samples : (step_round + 1) * samples]
        )


def on_device(windows, counts, pairs):
    comps, _, events, samples = windows.shape
    cells = lax.axis_size("cell")
    half, groups = cells // 2, cells // 4
    count = pairs.shape[2]
    inverse = jnp.asarray(inverse_table(samples, cells))
    place = lax.axis_index("cell").astype(jnp.int32).reshape(1)

    def swap(x, mask):
        return lax.ppermute(x, "cell", [(i, i ^ mask) for i in range(cells)])

    def shape(*dims, dtype=jnp.bfloat16):
        return jax.ShapeDtypeStruct(dims, dtype)

    vmem = pl.BlockSpec(memory_space=pltpu.VMEM)
    smem = pl.BlockSpec(memory_space=pltpu.SMEM)
    params = pltpu.CompilerParams(vmem_limit_bytes=VMEM_LIMIT)

    def cost(microseconds):
        return pl.CostEstimate(
            flops=int(microseconds * 1e9), bytes_accessed=2**20, transcendentals=0
        )

    windows = windows.reshape(comps, 2, groups, 2 * SLOTS, samples)
    near_windows, near_pairs = swap(windows, 1), swap(pairs, 1)
    part_rows, full_rows = comps * 2 * PART, comps * 2 * FULL
    part_spectra, full_spectra, table = pl.pallas_call(
        own_kernel,
        out_shape=[
            shape(groups, part_rows, LANES),
            shape(2 * groups, full_rows, LANES),
            shape(2 * PART + 4 * FULL, samples),
        ],
        in_specs=[smem, vmem],
        out_specs=[vmem] * 3,
        compiler_params=params,
        cost_estimate=cost(1),
        name="own_spectra",
    )(place, windows)
    listing = 2 * pairs.size // LANES
    pieces = pl.pallas_call(
        near_spectra_kernel,
        out_shape=[shape(2 * (part_rows + full_rows), LANES)] * groups
        + [shape(2 * full_rows + listing * (mg == 0), LANES) for mg in range(groups)],
        in_specs=[smem] + [vmem] * 6,
        out_specs=[vmem] * (2 * groups),
        compiler_params=params,
        cost_estimate=cost(1),
        name="near_spectra",
    )(place, pairs, near_pairs, table, part_spectra, full_spectra, near_windows)
    arrived = [pieces[0]] + [swap(pieces[m], 2 * m) for m in range(1, 2 * groups)]
    sides, far = arrived[:groups], arrived[groups:]

    early, late = far[: groups - 2], far[groups - 2 :]
    part_packed = shape(packed_rows(count, PART), LANES)
    full_packed = shape(packed_rows(count, FULL), LANES)
    half_packed = shape(packed_rows(count, FULL) // 2, LANES)
    part_blocks = shape(2, 2, SLOTS * SLOTS * width(PART) // LANES, 2 * LANES)
    full_blocks = shape(2, 2, SLOTS * SLOTS * width(FULL) // LANES, 2 * LANES)
    part_flat = pl.pallas_call(
        part_kernel,
        out_shape=part_blocks,
        in_specs=[vmem] * groups,
        out_specs=vmem,
        scratch_shapes=[
            pltpu.VMEM((padded(groups * 2 * comps) * 2 * PART, LANES), jnp.float32),
            pltpu.VMEM((2 * SLOTS * PART, LANES), jnp.float32),
        ],
        compiler_params=params,
        cost_estimate=cost(0.001),
        name="part",
    )(*sides)
    part_0, part_1 = pl.pallas_call(
        functools.partial(near_kernel, PART, 1),
        out_shape=[part_packed, part_packed],
        in_specs=[smem, smem] + [vmem] * 3,
        out_specs=[vmem] * 2,
        compiler_params=params,
        cost_estimate=cost(0.001),
        name="part_near",
    )(place, counts, pairs, near_pairs, part_flat)
    part_2, part_3 = pl.pallas_call(
        functools.partial(far_kernel, PART),
        out_shape=[part_packed, part_packed],
        in_specs=[smem, smem, vmem, vmem, pl.BlockSpec(memory_space=pl.ANY)],
        out_specs=[vmem, vmem],
        compiler_params=params,
        cost_estimate=cost(1),
        name="part_far",
    )(place, counts, far[0], part_flat, part_0)
    part_1 = swap(part_1, 1)
    sums = pl.pallas_call(
        functools.partial(early_kernel, groups),
        out_shape=shape(2 * SLOTS * FULL, LANES, dtype=jnp.float32),
        in_specs=[pl.BlockSpec(memory_space=pl.ANY)] * 2 + [vmem] * (groups + len(early)),
        out_specs=vmem,
        scratch_shapes=[
            pltpu.VMEM((padded((groups + len(early)) * 2 * comps) * 2 * FULL, LANES), jnp.float32)
        ],
        compiler_params=params,
        cost_estimate=cost(0.001),
        name="early",
    )(part_0, part_2, *sides, *early)
    sent, part_2, part_3 = part_2, swap(part_2, half), swap(part_3, half + 1)
    full_flat, full_2, full_3 = pl.pallas_call(
        full_kernel,
        out_shape=[full_blocks, full_packed, full_packed],
        in_specs=[smem, smem, vmem] + [pl.BlockSpec(memory_space=pl.ANY)] * 2 + [vmem] * (1 + len(late)),
        out_specs=[vmem] * 3,
        scratch_shapes=[
            pltpu.VMEM((padded(len(late) * 2 * comps) * 2 * FULL, LANES), jnp.float32),
            pltpu.VMEM((2 * SLOTS * FULL, LANES), jnp.float32),
        ],
        compiler_params=params,
        cost_estimate=cost(10),
        name="full",
    )(place, counts, far[0], part_0, sent, sums, *late)
    full_2, full_3 = swap(full_2, half), swap(full_3, half + 1)
    full_0, *full_1 = pl.pallas_call(
        functools.partial(near_kernel, FULL, 2),
        out_shape=[full_packed, half_packed, half_packed],
        in_specs=[smem, smem] + [vmem] * 3 + [pl.BlockSpec(memory_space=pl.ANY)] * 2,
        out_specs=[vmem] * 3,
        compiler_params=params,
        cost_estimate=cost(0.5),
        name="full_near",
    )(place, counts, pairs, near_pairs, full_flat, part_2, part_3)
    full_1 = [swap(x, 1) for x in full_1]

    first, tables = pl.pallas_call(
        functools.partial(first_lags_kernel, groups),
        out_shape=[
            shape(2, count, samples, dtype=jnp.float32),
            shape(2, 4 * FULL, 2 * samples),
        ],
        in_specs=[smem] + [vmem] * 8,
        out_specs=[vmem] * 2,
        compiler_params=params,
        cost_estimate=cost(0.001),
        name="first_lags",
    )(place, inverse, part_0, part_2, part_3, full_0, part_1, *full_1)
    return pl.pallas_call(
        lag_kernel,
        out_shape=shape(2, count, samples, dtype=jnp.float32),
        in_specs=[vmem] * 4,
        out_specs=vmem,
        compiler_params=params,
        cost_estimate=cost(1),
        name="lags",
    )(first, tables, full_2, full_3)


def solution(mesh):
    in_specs = (P(None, "cell", "grp", None), P("grp"), P(None, None, ("grp", "cell")))
    out_specs = P(None, ("grp", "cell"), None)
    return jax.shard_map(
        on_device, mesh=mesh, in_specs=in_specs, out_specs=out_specs, check_vma=False
    )
```

```python
import functools
import math

import jax
import jax.numpy as jnp
import numpy as np
from jax import lax
from jax.experimental import pallas as pl
from jax.experimental.pallas import tpu as pltpu
from jax.sharding import PartitionSpec as P

EPSILON = 1e-06
COSINE = (
    0.9999999999993376,
    -4.934802200431432,
    4.058712123240781,
    -1.3352627346923478,
    0.23533044681677665,
    -0.02580633847975355,
    0.0019285963125396874,
    -0.00010362767792380447,
    3.734915399663344e-06,
)
SLOTS = 32
LANES = 4 * SLOTS
COMPS = 3
NT = (((1,), (1,)), ((), ()))
TN = (((0,), (0,)), ((), ()))
VMEM_LIMIT = 40 * 1024 * 1024

PART = 16
FULL = 24


def inverse_table(samples, stations):
    bins = samples // 2
    turn = np.arange(bins)[:, None] * np.arange(samples)[None, :] % samples
    angle = turn * (2.0 * math.pi / samples)
    weight = np.where(np.arange(bins) == 0, 1.0, 2.0)[:, None] / samples
    weight = weight * math.sqrt(samples / (3.0 * stations))
    real, imag = weight * np.cos(angle), -weight * np.sin(angle)
    runs = [(at, PART) for at in range(0, 2 * PART, PART)]
    runs += [(at, FULL) for at in range(2 * PART, bins, FULL)]
    rows = [part[at : at + run] for at, run in runs for part in (real, imag)]
    return np.concatenate(rows).astype(np.float32)


def forward_rows(bins, samples):
    count = bins.shape[0]
    sample = lax.broadcasted_iota(jnp.int32, (2 * count, samples), 1)
    turn = jnp.concatenate([bins * sample[:count], bins * sample[:count] + samples // 4])
    turn &= samples - 1
    x = jnp.where(turn > samples // 2, turn - samples, turn).astype(jnp.float32) * (2.0 / samples)
    square = x * x
    value = jnp.full(square.shape, COSINE[-1], jnp.float32)
    for factor in COSINE[-2::-1]:
        value = value * square + factor
    return value.astype(jnp.bfloat16)


def place_of(place_ref, groups):
    position = place_ref[0]
    high, inner = position // (2 * groups), position % (2 * groups)
    return high * 2 + inner % 2, inner // 2


def listing_of(pairs_ref, lanes):
    ends = []
    for end in range(2):
        slots = pairs_ref[:, end, :].astype(jnp.float32)
        ends += [slots[:, at : at + lanes] for at in range(0, slots.shape[1], lanes)]
    return jnp.concatenate(ends)


def station_spectra(windows_ref, at, table):
    parts = []
    for comp in range(windows_ref.shape[0]):
        low = windows_ref[comp, 0, at]
        high = windows_ref[comp, 1, at]
        parts += [low[:SLOTS], high[SLOTS:], low[SLOTS:], high[:SLOTS]]
    traces = jnp.concatenate(parts)
    square = jnp.square(traces.astype(jnp.float32))
    square_hi = square.astype(jnp.bfloat16)
    square_lo = (square - square_hi.astype(jnp.float32)).astype(jnp.bfloat16)
    ones = jnp.ones((16, traces.shape[1]), jnp.bfloat16)
    energy = lax.dot_general(ones, square_hi, NT, preferred_element_type=jnp.float32)
    energy += lax.dot_general(ones, square_lo, NT, preferred_element_type=jnp.float32)
    scale = lax.rsqrt(energy[:1] + EPSILON)
    raw = lax.dot_general(table, traces, NT, preferred_element_type=jnp.float32)
    return (raw * scale).astype(jnp.bfloat16)


def own_kernel(place_ref, windows_ref, part_ref, full_ref, table_ref):
    groups, samples = windows_ref.shape[2], windows_ref.shape[4]
    quarter, group = place_of(place_ref, groups)
    bins = lax.broadcasted_iota(jnp.int32, (PART, samples), 0) + (quarter % 2) * PART
    table_ref[: 2 * PART] = forward_rows(bins, samples)
    for far in range(2):
        start = 2 * PART + (quarter ^ (2 * far)) * FULL
        bins = lax.broadcasted_iota(jnp.int32, (FULL, samples), 0) + start
        at = 2 * PART + 2 * FULL * far
        table_ref[at : at + 2 * FULL] = forward_rows(bins, samples)
    table = table_ref[...]
    for mg in range(groups):
        spectra = station_spectra(windows_ref, group ^ mg, table)
        for comp in range(COMPS):
            lanes = spectra[:, comp * LANES : (comp + 1) * LANES]
            part_ref[mg, comp * 2 * PART : (comp + 1) * 2 * PART] = lanes[: 2 * PART]
            for far in range(2):
                at = 2 * PART + 2 * FULL * far
                full_ref[far * groups + mg, comp * 2 * FULL : (comp + 1) * 2 * FULL] = lanes[at : at + 2 * FULL]


def near_spectra_kernel(
    place_ref, own_pairs_ref, near_pairs_ref, table_ref, part_ref, full_ref, windows_ref, *refs
):
    groups = windows_ref.shape[2]
    side_refs, full_refs = refs[:groups], refs[groups:]
    _, group = place_of(place_ref, groups)
    table = table_ref[...]
    part_rows, full_rows = COMPS * 2 * PART, COMPS * 2 * FULL
    full_refs[groups][2 * full_rows :] = jnp.concatenate(
        [listing_of(own_pairs_ref, LANES), listing_of(near_pairs_ref, LANES)]
    ).astype(jnp.bfloat16)
    for mg in range(groups):
        spectra = station_spectra(windows_ref, group ^ mg, table)
        side_refs[mg][:part_rows] = part_ref[mg]
        for far in range(2):
            full_refs[far * groups + mg][:full_rows] = full_ref[far * groups + mg]
        for comp in range(COMPS):
            lanes = spectra[:, comp * LANES : (comp + 1) * LANES]
            at = part_rows + comp * 2 * PART
            side_refs[mg][at : at + 2 * PART] = lanes[: 2 * PART]
            for far in range(2):
                at = full_rows + comp * 2 * FULL
                start = 2 * PART + 2 * FULL * far
                full_refs[far * groups + mg][at : at + 2 * FULL] = lanes[start : start + 2 * FULL]


def width(bins):
    return 1 << (bins - 1).bit_length()


def packing(count, bins):
    used = 4 * bins
    spare = LANES - used
    if not spare:
        return count, [[(0, 0, 0, used)]]
    runs = used // spare
    rows = count // (runs + 1)
    return rows, [
        [(at * rows, 0, 0, used), (runs * rows, used, at * spare, (at + 1) * spare)] for at in range(runs)
    ]


def packed_rows(count, bins):
    rows, parts = packing(count, bins)
    return rows * len(parts)


def unpack(picked, bins):
    used = 4 * bins
    spare = LANES - used
    if not spare:
        return picked
    runs = used // spare
    rows = picked.shape[0] // runs
    rest = [picked[at * rows : (at + 1) * rows, used:] for at in range(runs)]
    return jnp.concatenate([picked[:, :used], jnp.concatenate(rest, axis=1)])


def pick(place_ref, counts_ref, listed, flat_ref, bins, mq, *picked_refs):
    cells = counts_ref.shape[0]
    quarter, group = place_of(place_ref, cells // 4)
    own = quarter ^ mq
    high, low = own // 2, own % 2
    cell = high * (cells // 2) + group * 2 + low
    count = listed.shape[0] // 2
    runs = LANES // width(bins)
    run_bits, bin_bits, lane_bits = (n.bit_length() - 1 for n in (runs, width(bins), LANES))
    first, second = listed[:count].astype(jnp.int32), listed[count:].astype(jnp.int32)
    far_counts = [counts_ref[cell ^ 1], counts_ref[cell ^ (cells // 2)]]
    odd = lax.broadcasted_iota(jnp.int32, (count, LANES), 0) & 1
    live = (first < counts_ref[cell]) & (second < jnp.where(odd == 1, far_counts[1], far_counts[0]))
    left, right = jnp.where(high == low, first, second), jnp.where(high == low, second, first)
    spot = jnp.where(live, (left >> run_bits) * SLOTS + right, -1)
    turned = (spot * runs + (left & (runs - 1))).T
    lane = lax.broadcasted_iota(jnp.int32, (LANES, LANES), 1)
    run = lane >> bin_bits
    sides = ((high, high), (low, 1 - low))
    found = []
    for step_round in range(2):
        hot, here = [], []
        for at in range(step_round, count, 2):
            both = jnp.broadcast_to(turned[:, at : at + 1], (LANES, LANES))
            here.append((both & (runs - 1)) == run)
            offset = (both >> run_bits) - lane
            hot.append(
                jnp.concatenate(
                    [
                        jnp.where(offset == start, 1.0, 0.0).astype(jnp.bfloat16)
                        for start in range(0, flat_ref.shape[2], LANES)
                    ],
                    axis=1,
                )
            )
        block = flat_ref[sides[step_round][0], sides[step_round][1]]
        wide = jnp.dot(jnp.concatenate(hot), block, preferred_element_type=jnp.float32)
        masked = []
        for chunk, mask in enumerate(here):
            part = wide[chunk * LANES : (chunk + 1) * LANES]
            masked.append(
                jnp.concatenate(
                    [
                        jnp.where(mask, part[:, :LANES], 0.0).astype(jnp.bfloat16),
                        jnp.where(mask, part[:, LANES:], 0.0).astype(jnp.bfloat16),
                    ],
                    axis=1,
                )
            )
        found.append(jnp.concatenate(masked))
    found = jnp.concatenate(found, axis=1)
    spread = lax.broadcasted_iota(jnp.int32, (4 * LANES, LANES), 0)
    kept = lax.broadcasted_iota(jnp.int32, (4 * LANES, LANES), 1)
    bin_of = spread & (width(bins) - 1)
    value = jnp.where(bin_of < bins, (spread >> lane_bits) * bins + bin_of, -1)
    rows, parts = packing(found.shape[0], bins)
    picked = []
    for entries in parts:
        total = 0.0
        for start, at, least, end in entries:
            fold = (value >= least) & (value < end) & (kept == value + (at - least))
            total += jnp.dot(
                found[start : start + rows],
                jnp.where(fold, 1.0, 0.0).astype(jnp.bfloat16),
                preferred_element_type=jnp.float32,
            )
        picked.append(total.astype(jnp.bfloat16))
    picked = jnp.concatenate(picked)
    each = picked.shape[0] // len(picked_refs)
    for at, ref in enumerate(picked_refs):
        ref[...] = picked[at * each : (at + 1) * each]


def padded(traces):
    return -(-traces // 16) * 16


def add_cross(pieces, trace_ref, bins, sums_ref, before_ref=None):
    slots, rows = 2 * SLOTS, 2 * bins
    traces = trace_ref.shape[0] // rows
    start = 0
    for piece, at, size in pieces:
        trace_ref[start : start + size] = piece[at : at + size].astype(jnp.float32)
        start += size
    if start < traces * rows:
        trace_ref[start:] = jnp.zeros((traces * rows - start, LANES), jnp.float32)
    lower = lax.broadcasted_iota(jnp.int32, (traces, LANES), 1) < slots
    for k in range(bins):
        real = trace_ref[pl.ds(k, traces, stride=rows), :]
        imag = trace_ref[pl.ds(bins + k, traces, stride=rows), :]
        left = jnp.concatenate([real, imag]).astype(jnp.bfloat16)[:, :slots]
        right = jnp.concatenate(
            [
                jnp.where(lower, pltpu.roll(real, slots, 1), imag),
                jnp.where(lower, pltpu.roll(imag, slots, 1), -real),
            ]
        ).astype(jnp.bfloat16)
        cross = lax.dot_general(left, right, TN, preferred_element_type=jnp.float32)
        if before_ref is not None:
            cross += before_ref[k * slots : (k + 1) * slots]
        sums_ref[k * slots : (k + 1) * slots] = cross


def turn_blocks(cross_ref, bins, flat_ref):
    slots, runs = 2 * SLOTS, LANES // width(bins)
    empty = jnp.zeros((width(bins) - bins, LANES), jnp.float32)
    for own in range(2):
        for at in range(SLOTS // runs):
            block = []
            for i in range(runs):
                block.append(cross_ref[pl.ds(own * SLOTS + at * runs + i, bins, stride=slots), :])
                block += [empty] * (bins < width(bins))
            block = jnp.concatenate(block).T.astype(jnp.bfloat16)
            for part in range(2):
                for far in range(2):
                    start = (part * 2 + far) * SLOTS
                    flat_ref[
                        own, far, at * SLOTS : (at + 1) * SLOTS, part * LANES : (part + 1) * LANES
                    ] = block[start : start + SLOTS]


def full_part(ref):
    return (ref, 0, 2 * COMPS * 2 * FULL)


def part_kernel(*refs):
    piece_refs, (flat_ref, trace_ref, cross_ref) = refs[:-3], refs[-3:]
    add_cross([(ref, 0, ref.shape[0]) for ref in piece_refs], trace_ref, PART, cross_ref)
    turn_blocks(cross_ref, PART, flat_ref)


def far_kernel(bins, place_ref, counts_ref, listed_ref, flat_ref, after_ref, picked_0, picked_1):
    listed = listed_ref[full_part(listed_ref)[2] :].astype(jnp.float32)
    listing = listed.shape[0] // 2
    pick(place_ref, counts_ref, listed[:listing], flat_ref, bins, 2, picked_0)
    pick(place_ref, counts_ref, listed[listing:], flat_ref, bins, 3, picked_1)


def early_kernel(after_0, after_1, *refs):
    piece_refs, (sums_ref, trace_ref) = refs[:-2], refs[-2:]
    add_cross([full_part(ref) for ref in piece_refs], trace_ref, FULL, sums_ref)


def full_kernel(place_ref, counts_ref, listed_ref, after_0, after_2, before_ref, *refs):
    piece_refs, (flat_ref, picked_0, picked_1, trace_ref, cross_ref) = refs[:-5], refs[-5:]
    add_cross([full_part(ref) for ref in piece_refs], trace_ref, FULL, cross_ref, before_ref)
    turn_blocks(cross_ref, FULL, flat_ref)
    listed = listed_ref[full_part(listed_ref)[2] :].astype(jnp.float32)
    listing = listed.shape[0] // 2
    pick(place_ref, counts_ref, listed[:listing], flat_ref, FULL, 2, picked_0)
    pick(place_ref, counts_ref, listed[listing:], flat_ref, FULL, 3, picked_1)


def near_kernel(bins, sent, place_ref, counts_ref, own_pairs_ref, near_pairs_ref, flat_ref, *refs):
    picked_0, *picked_1 = refs[-1 - sent :]
    pick(place_ref, counts_ref, listing_of(near_pairs_ref, LANES), flat_ref, bins, 1, *picked_1)
    pick(place_ref, counts_ref, listing_of(own_pairs_ref, LANES), flat_ref, bins, 0, picked_0)


def both_rounds(rows, sign):
    row = lax.broadcasted_iota(jnp.int32, rows.shape, 0)
    rows = rows * jnp.where(row < rows.shape[0] // 2, 1.0, sign)
    empty = jnp.zeros_like(rows)
    return jnp.concatenate(
        [jnp.concatenate([rows, empty], axis=1), jnp.concatenate([empty, rows], axis=1)]
    )


def halves(table):
    high = table.astype(jnp.bfloat16)
    return high, (table - high.astype(jnp.float32)).astype(jnp.bfloat16)


def first_lags_kernel(groups, place_ref, inverse_ref, *refs):
    part_0, part_2, part_3, full_0, part_1, *full_1, lags_ref, table_ref = refs
    samples = inverse_ref.shape[1]
    quarter, _ = place_of(place_ref, groups)
    low = quarter % 2
    sign = jnp.where(quarter // 2 == low, 1.0, -1.0)

    def part_table(which):
        start = pl.multiple_of((low ^ which) * 2 * PART, 2 * PART)
        return halves(both_rounds(inverse_ref[pl.ds(start, 2 * PART), :], sign))

    def full_table(mq):
        start = pl.multiple_of(4 * PART + (quarter ^ mq) * 2 * FULL, 2 * FULL)
        return halves(both_rounds(inverse_ref[pl.ds(start, 2 * FULL), :], sign))

    near, other = part_table(0), part_table(1)
    lags = 0.0
    full_1 = jnp.concatenate([ref[...] for ref in full_1])
    for picked, bins, table in (
        (part_0[...], PART, near),
        (part_2[...], PART, near),
        (part_1[...], PART, other),
        (part_3[...], PART, other),
        (full_0[...], FULL, full_table(0)),
        (full_1, FULL, full_table(1)),
    ):
        picked = unpack(picked, bins)
        for half in table:
            lags += jnp.dot(picked, half, preferred_element_type=jnp.float32)
    for step_round in range(2):
        lags_ref[step_round] = lags[:, step_round * samples : (step_round + 1) * samples]
    for at in range(2):
        table_ref[at] = full_table(2 + at)[0]


def lag_kernel(first_ref, table_ref, *refs):
    picked_refs, lags_ref = refs[:-1], refs[-1]
    samples = lags_ref.shape[2]
    more = 0.0
    for at, ref in enumerate(picked_refs):
        more += jnp.dot(unpack(ref[...], FULL), table_ref[at], preferred_element_type=jnp.float32)
    for step_round in range(2):
        lags_ref[step_round] = (
            first_ref[step_round] + more[:, step_round * samples : (step_round + 1) * samples]
        )


def on_device(windows, counts, pairs):
    comps, _, events, samples = windows.shape
    cells = lax.axis_size("cell")
    half, groups = cells // 2, cells // 4
    count = pairs.shape[2]
    inverse = jnp.asarray(inverse_table(samples, cells))
    place = lax.axis_index("cell").astype(jnp.int32).reshape(1)

    def swap(x, mask):
        return lax.ppermute(x, "cell", [(i, i ^ mask) for i in range(cells)])

    def shape(*dims, dtype=jnp.bfloat16):
        return jax.ShapeDtypeStruct(dims, dtype)

    vmem = pl.BlockSpec(memory_space=pltpu.VMEM)
    smem = pl.BlockSpec(memory_space=pltpu.SMEM)
    params = pltpu.CompilerParams(vmem_limit_bytes=VMEM_LIMIT)

    def cost(microseconds):
        return pl.CostEstimate(
            flops=int(microseconds * 1e9), bytes_accessed=2**20, transcendentals=0
        )

    windows = windows.reshape(comps, 2, groups, 2 * SLOTS, samples)
    near_windows, near_pairs = swap(windows, 1), swap(pairs, 1)
    part_rows, full_rows = comps * 2 * PART, comps * 2 * FULL
    part_spectra, full_spectra, table = pl.pallas_call(
        own_kernel,
        out_shape=[
            shape(groups, part_rows, LANES),
            shape(2 * groups, full_rows, LANES),
            shape(2 * PART + 4 * FULL, samples),
        ],
        in_specs=[smem, vmem],
        out_specs=[vmem] * 3,
        compiler_params=params,
        cost_estimate=cost(1),
        name="own_spectra",
    )(place, windows)
    listing = 2 * pairs.size // LANES
    pieces = pl.pallas_call(
        near_spectra_kernel,
        out_shape=[shape(2 * part_rows, LANES)] * groups
        + [shape(2 * full_rows + listing * (m == groups), LANES) for m in range(2 * groups)],
        in_specs=[smem] + [vmem] * 6,
        out_specs=[vmem] * (3 * groups),
        compiler_params=params,
        cost_estimate=cost(1),
        name="near_spectra",
    )(place, pairs, near_pairs, table, part_spectra, full_spectra, near_windows)
    parts, fulls = pieces[:groups], pieces[groups:]
    parts = [parts[0]] + [swap(parts[m], 2 * m) for m in range(1, groups)]
    fulls = [fulls[0]] + [swap(fulls[m], 2 * m) for m in range(1, 2 * groups)]
    sides, far = fulls[:groups], fulls[groups:]

    early, late = [sides[0], *far[: groups - 2]], [*far[groups - 2 :], *sides[1:]]
    part_packed = shape(packed_rows(count, PART), LANES)
    full_packed = shape(packed_rows(count, FULL), LANES)
    half_packed = shape(packed_rows(count, FULL) // 2, LANES)
    part_blocks = shape(2, 2, SLOTS * SLOTS * width(PART) // LANES, 2 * LANES)
    full_blocks = shape(2, 2, SLOTS * SLOTS * width(FULL) // LANES, 2 * LANES)
    part_flat = pl.pallas_call(
        part_kernel,
        out_shape=part_blocks,
        in_specs=[vmem] * groups,
        out_specs=vmem,
        scratch_shapes=[
            pltpu.VMEM((padded(groups * 2 * comps) * 2 * PART, LANES), jnp.float32),
            pltpu.VMEM((2 * SLOTS * PART, LANES), jnp.float32),
        ],
        compiler_params=params,
        cost_estimate=cost(0.001),
        name="part",
    )(*parts)
    part_0, part_1 = pl.pallas_call(
        functools.partial(near_kernel, PART, 1),
        out_shape=[part_packed, part_packed],
        in_specs=[smem, smem] + [vmem] * 3,
        out_specs=[vmem] * 2,
        compiler_params=params,
        cost_estimate=cost(0.001),
        name="part_near",
    )(place, counts, pairs, near_pairs, part_flat)
    part_2, part_3 = pl.pallas_call(
        functools.partial(far_kernel, PART),
        out_shape=[part_packed, part_packed],
        in_specs=[smem, smem, vmem, vmem, pl.BlockSpec(memory_space=pl.ANY)],
        out_specs=[vmem, vmem],
        compiler_params=params,
        cost_estimate=cost(1),
        name="part_far",
    )(place, counts, far[0], part_flat, part_0)
    part_1 = swap(part_1, 1)
    sums = pl.pallas_call(
        early_kernel,
        out_shape=shape(2 * SLOTS * FULL, LANES, dtype=jnp.float32),
        in_specs=[pl.BlockSpec(memory_space=pl.ANY)] * 2 + [vmem] * len(early),
        out_specs=vmem,
        scratch_shapes=[
            pltpu.VMEM((padded(len(early) * 2 * comps) * 2 * FULL, LANES), jnp.float32)
        ],
        compiler_params=params,
        cost_estimate=cost(0.001),
        name="early",
    )(part_0, part_2, *early)
    sent, part_2, part_3 = part_2, swap(part_2, half), swap(part_3, half + 1)
    full_flat, full_2, full_3 = pl.pallas_call(
        full_kernel,
        out_shape=[full_blocks, full_packed, full_packed],
        in_specs=[smem, smem, vmem] + [pl.BlockSpec(memory_space=pl.ANY)] * 2 + [vmem] * (1 + len(late)),
        out_specs=[vmem] * 3,
        scratch_shapes=[
            pltpu.VMEM((padded(len(late) * 2 * comps) * 2 * FULL, LANES), jnp.float32),
            pltpu.VMEM((2 * SLOTS * FULL, LANES), jnp.float32),
        ],
        compiler_params=params,
        cost_estimate=cost(10),
        name="full",
    )(place, counts, far[0], part_0, sent, sums, *late)
    full_2, full_3 = swap(full_2, half), swap(full_3, half + 1)
    full_0, *full_1 = pl.pallas_call(
        functools.partial(near_kernel, FULL, 2),
        out_shape=[full_packed, half_packed, half_packed],
        in_specs=[smem, smem] + [vmem] * 3 + [pl.BlockSpec(memory_space=pl.ANY)] * 2,
        out_specs=[vmem] * 3,
        compiler_params=params,
        cost_estimate=cost(0.5),
        name="full_near",
    )(place, counts, pairs, near_pairs, full_flat, part_2, part_3)
    full_1 = [swap(x, 1) for x in full_1]

    first, tables = pl.pallas_call(
        functools.partial(first_lags_kernel, groups),
        out_shape=[
            shape(2, count, samples, dtype=jnp.float32),
            shape(2, 4 * FULL, 2 * samples),
        ],
        in_specs=[smem] + [vmem] * 8,
        out_specs=[vmem] * 2,
        compiler_params=params,
        cost_estimate=cost(0.001),
        name="first_lags",
    )(place, inverse, part_0, part_2, part_3, full_0, part_1, *full_1)
    return pl.pallas_call(
        lag_kernel,
        out_shape=shape(2, count, samples, dtype=jnp.float32),
        in_specs=[vmem] * 4,
        out_specs=vmem,
        compiler_params=params,
        cost_estimate=cost(1),
        name="lags",
    )(first, tables, full_2, full_3)


def solution(mesh):
    in_specs = (P(None, "cell", "grp", None), P("grp"), P(None, None, ("grp", "cell")))
    out_specs = P(None, ("grp", "cell"), None)
    return jax.shard_map(
        on_device, mesh=mesh, in_specs=in_specs, out_specs=out_specs, check_vma=False
    )
```

```python
import functools
import math

import jax
import jax.numpy as jnp
import numpy as np
from jax import lax
from jax.experimental import pallas as pl
from jax.experimental.pallas import tpu as pltpu
from jax.sharding import PartitionSpec as P

EPSILON = 1e-06
COSINE = (
    0.9999999999993376,
    -4.934802200431432,
    4.058712123240781,
    -1.3352627346923478,
    0.23533044681677665,
    -0.02580633847975355,
    0.0019285963125396874,
    -0.00010362767792380447,
    3.734915399663344e-06,
)
SLOTS = 32
LANES = 4 * SLOTS
COMPS = 3
NT = (((1,), (1,)), ((), ()))
TN = (((0,), (0,)), ((), ()))
VMEM_LIMIT = 40 * 1024 * 1024

PART = 32
FULL = 16


def inverse_table(samples, stations):
    bins = samples // 2
    turn = np.arange(bins)[:, None] * np.arange(samples)[None, :] % samples
    angle = turn * (2.0 * math.pi / samples)
    weight = np.where(np.arange(bins) == 0, 1.0, 2.0)[:, None] / samples
    weight = weight * math.sqrt(samples / (3.0 * stations))
    real, imag = weight * np.cos(angle), -weight * np.sin(angle)
    runs = [(at, PART) for at in range(0, 2 * PART, PART)]
    runs += [(at, FULL) for at in range(2 * PART, bins, FULL)]
    rows = [part[at : at + run] for at, run in runs for part in (real, imag)]
    return np.concatenate(rows).astype(np.float32)


def forward_rows(bins, samples):
    count = bins.shape[0]
    sample = lax.broadcasted_iota(jnp.int32, (2 * count, samples), 1)
    turn = jnp.concatenate([bins * sample[:count], bins * sample[:count] + samples // 4])
    turn &= samples - 1
    x = jnp.where(turn > samples // 2, turn - samples, turn).astype(jnp.float32) * (2.0 / samples)
    square = x * x
    value = jnp.full(square.shape, COSINE[-1], jnp.float32)
    for factor in COSINE[-2::-1]:
        value = value * square + factor
    return value.astype(jnp.bfloat16)


def place_of(place_ref, groups):
    position = place_ref[0]
    high, inner = position // (2 * groups), position % (2 * groups)
    return high * 2 + inner % 2, inner // 2


def listing_of(pairs_ref, lanes):
    ends = []
    for end in range(2):
        slots = pairs_ref[:, end, :].astype(jnp.float32)
        ends += [slots[:, at : at + lanes] for at in range(0, slots.shape[1], lanes)]
    return jnp.concatenate(ends)


def station_spectra(windows_ref, at, table):
    parts = []
    for comp in range(windows_ref.shape[0]):
        low = windows_ref[comp, 0, at]
        high = windows_ref[comp, 1, at]
        parts += [low[:SLOTS], high[SLOTS:], low[SLOTS:], high[:SLOTS]]
    traces = jnp.concatenate(parts)
    square = jnp.square(traces.astype(jnp.float32))
    square_hi = square.astype(jnp.bfloat16)
    square_lo = (square - square_hi.astype(jnp.float32)).astype(jnp.bfloat16)
    ones = jnp.ones((16, traces.shape[1]), jnp.bfloat16)
    energy = lax.dot_general(ones, square_hi, NT, preferred_element_type=jnp.float32)
    energy += lax.dot_general(ones, square_lo, NT, preferred_element_type=jnp.float32)
    scale = lax.rsqrt(energy[:1] + EPSILON)
    raw = lax.dot_general(table, traces, NT, preferred_element_type=jnp.float32)
    return (raw * scale).astype(jnp.bfloat16)


def own_kernel(place_ref, windows_ref, part_ref, full_ref, table_ref):
    groups, samples = windows_ref.shape[2], windows_ref.shape[4]
    quarter, group = place_of(place_ref, groups)
    bins = lax.broadcasted_iota(jnp.int32, (PART, samples), 0) + (quarter % 2) * PART
    table_ref[: 2 * PART] = forward_rows(bins, samples)
    for far in range(2):
        start = 2 * PART + (quarter ^ (2 * far)) * FULL
        bins = lax.broadcasted_iota(jnp.int32, (FULL, samples), 0) + start
        at = 2 * PART + 2 * FULL * far
        table_ref[at : at + 2 * FULL] = forward_rows(bins, samples)
    table = table_ref[...]
    for mg in range(groups):
        spectra = station_spectra(windows_ref, group ^ mg, table)
        for comp in range(COMPS):
            lanes = spectra[:, comp * LANES : (comp + 1) * LANES]
            part_ref[mg, comp * 2 * PART : (comp + 1) * 2 * PART] = lanes[: 2 * PART]
            for far in range(2):
                at = 2 * PART + 2 * FULL * far
                full_ref[far * groups + mg, comp * 2 * FULL : (comp + 1) * 2 * FULL] = lanes[at : at + 2 * FULL]


def near_spectra_kernel(
    place_ref, own_pairs_ref, near_pairs_ref, table_ref, part_ref, full_ref, windows_ref, *piece_refs
):
    groups = windows_ref.shape[2]
    _, group = place_of(place_ref, groups)
    table = table_ref[...]
    part_rows, full_rows = COMPS * 2 * PART, COMPS * 2 * FULL
    piece_refs[groups][2 * full_rows :] = jnp.concatenate(
        [listing_of(own_pairs_ref, LANES), listing_of(near_pairs_ref, LANES)]
    ).astype(jnp.bfloat16)
    for mg in range(groups):
        spectra = station_spectra(windows_ref, group ^ mg, table)
        side, cross = piece_refs[mg], piece_refs[groups + mg]
        side[:part_rows] = part_ref[mg]
        side[2 * part_rows : 2 * part_rows + full_rows] = full_ref[mg]
        cross[:full_rows] = full_ref[groups + mg]
        for comp in range(COMPS):
            lanes = spectra[:, comp * LANES : (comp + 1) * LANES]
            at = part_rows + comp * 2 * PART
            side[at : at + 2 * PART] = lanes[: 2 * PART]
            at = 2 * part_rows + full_rows + comp * 2 * FULL
            side[at : at + 2 * FULL] = lanes[2 * PART : 2 * PART + 2 * FULL]
            at = full_rows + comp * 2 * FULL
            cross[at : at + 2 * FULL] = lanes[2 * PART + 2 * FULL :]


def width(bins):
    return 1 << (bins - 1).bit_length()


def packing(count, bins):
    used = 4 * bins
    spare = LANES - used
    if not spare:
        return count, [[(0, 0, 0, used)]]
    runs = used // spare
    rows = count // (runs + 1)
    return rows, [
        [(at * rows, 0, 0, used), (runs * rows, used, at * spare, (at + 1) * spare)] for at in range(runs)
    ]


def packed_rows(count, bins):
    rows, parts = packing(count, bins)
    return rows * len(parts)


def unpack(picked, bins):
    used = 4 * bins
    spare = LANES - used
    if not spare:
        return picked
    runs = used // spare
    rows = picked.shape[0] // runs
    rest = [picked[at * rows : (at + 1) * rows, used:] for at in range(runs)]
    return jnp.concatenate([picked[:, :used], jnp.concatenate(rest, axis=1)])


def pick(place_ref, counts_ref, listed, flat_ref, bins, mq, *picked_refs):
    cells = counts_ref.shape[0]
    quarter, group = place_of(place_ref, cells // 4)
    own = quarter ^ mq
    high, low = own // 2, own % 2
    cell = high * (cells // 2) + group * 2 + low
    count = listed.shape[0] // 2
    runs = LANES // width(bins)
    run_bits, bin_bits, lane_bits = (n.bit_length() - 1 for n in (runs, width(bins), LANES))
    first, second = listed[:count].astype(jnp.int32), listed[count:].astype(jnp.int32)
    far_counts = [counts_ref[cell ^ 1], counts_ref[cell ^ (cells // 2)]]
    odd = lax.broadcasted_iota(jnp.int32, (count, LANES), 0) & 1
    live = (first < counts_ref[cell]) & (second < jnp.where(odd == 1, far_counts[1], far_counts[0]))
    left, right = jnp.where(high == low, first, second), jnp.where(high == low, second, first)
    spot = jnp.where(live, (left >> run_bits) * SLOTS + right, -1)
    turned = (spot * runs + (left & (runs - 1))).T
    lane = lax.broadcasted_iota(jnp.int32, (LANES, LANES), 1)
    run = lane >> bin_bits
    sides = ((high, high), (low, 1 - low))
    found = []
    for step_round in range(2):
        hot, here = [], []
        for at in range(step_round, count, 2):
            both = jnp.broadcast_to(turned[:, at : at + 1], (LANES, LANES))
            here.append((both & (runs - 1)) == run)
            offset = (both >> run_bits) - lane
            hot.append(
                jnp.concatenate(
                    [
                        jnp.where(offset == start, 1.0, 0.0).astype(jnp.bfloat16)
                        for start in range(0, flat_ref.shape[2], LANES)
                    ],
                    axis=1,
                )
            )
        block = flat_ref[sides[step_round][0], sides[step_round][1]]
        wide = jnp.dot(jnp.concatenate(hot), block, preferred_element_type=jnp.float32)
        masked = []
        for chunk, mask in enumerate(here):
            part = wide[chunk * LANES : (chunk + 1) * LANES]
            masked.append(
                jnp.concatenate(
                    [
                        jnp.where(mask, part[:, :LANES], 0.0).astype(jnp.bfloat16),
                        jnp.where(mask, part[:, LANES:], 0.0).astype(jnp.bfloat16),
                    ],
                    axis=1,
                )
            )
        found.append(jnp.concatenate(masked))
    found = jnp.concatenate(found, axis=1)
    spread = lax.broadcasted_iota(jnp.int32, (4 * LANES, LANES), 0)
    kept = lax.broadcasted_iota(jnp.int32, (4 * LANES, LANES), 1)
    bin_of = spread & (width(bins) - 1)
    value = jnp.where(bin_of < bins, (spread >> lane_bits) * bins + bin_of, -1)
    rows, parts = packing(found.shape[0], bins)
    picked = []
    for entries in parts:
        total = 0.0
        for start, at, least, end in entries:
            fold = (value >= least) & (value < end) & (kept == value + (at - least))
            total += jnp.dot(
                found[start : start + rows],
                jnp.where(fold, 1.0, 0.0).astype(jnp.bfloat16),
                preferred_element_type=jnp.float32,
            )
        picked.append(total.astype(jnp.bfloat16))
    picked = jnp.concatenate(picked)
    each = picked.shape[0] // len(picked_refs)
    for at, ref in enumerate(picked_refs):
        ref[...] = picked[at * each : (at + 1) * each]


def padded(traces):
    return -(-traces // 16) * 16


def add_cross(pieces, trace_ref, bins, sums_ref, before_ref=None):
    slots, rows = 2 * SLOTS, 2 * bins
    traces = trace_ref.shape[0] // rows
    start = 0
    for piece, at, size in pieces:
        trace_ref[start : start + size] = piece[at : at + size].astype(jnp.float32)
        start += size
    if start < traces * rows:
        trace_ref[start:] = jnp.zeros((traces * rows - start, LANES), jnp.float32)
    lower = lax.broadcasted_iota(jnp.int32, (traces, LANES), 1) < slots
    for k in range(bins):
        real = trace_ref[pl.ds(k, traces, stride=rows), :]
        imag = trace_ref[pl.ds(bins + k, traces, stride=rows), :]
        left = jnp.concatenate([real, imag]).astype(jnp.bfloat16)[:, :slots]
        right = jnp.concatenate(
            [
                jnp.where(lower, pltpu.roll(real, slots, 1), imag),
                jnp.where(lower, pltpu.roll(imag, slots, 1), -real),
            ]
        ).astype(jnp.bfloat16)
        cross = lax.dot_general(left, right, TN, preferred_element_type=jnp.float32)
        if before_ref is not None:
            cross += before_ref[k * slots : (k + 1) * slots]
        sums_ref[k * slots : (k + 1) * slots] = cross


def turn_blocks(cross_ref, bins, flat_ref):
    slots, runs = 2 * SLOTS, LANES // width(bins)
    empty = jnp.zeros((width(bins) - bins, LANES), jnp.float32)
    for own in range(2):
        for at in range(SLOTS // runs):
            block = []
            for i in range(runs):
                block.append(cross_ref[pl.ds(own * SLOTS + at * runs + i, bins, stride=slots), :])
                block += [empty] * (bins < width(bins))
            block = jnp.concatenate(block).T.astype(jnp.bfloat16)
            for part in range(2):
                for far in range(2):
                    start = (part * 2 + far) * SLOTS
                    flat_ref[
                        own, far, at * SLOTS : (at + 1) * SLOTS, part * LANES : (part + 1) * LANES
                    ] = block[start : start + SLOTS]


def side_part(ref):
    return (ref, 0, 2 * COMPS * 2 * PART)


def side_full(ref):
    return (ref, 2 * COMPS * 2 * PART, 2 * COMPS * 2 * FULL)


def cross_full(ref):
    return (ref, 0, 2 * COMPS * 2 * FULL)


def part_kernel(*refs):
    piece_refs, (flat_ref, trace_ref, cross_ref) = refs[:-3], refs[-3:]
    add_cross([side_part(ref) for ref in piece_refs], trace_ref, PART, cross_ref)
    turn_blocks(cross_ref, PART, flat_ref)


def far_kernel(bins, place_ref, counts_ref, listed_ref, flat_ref, after_ref, picked_0, picked_1):
    listed = listed_ref[cross_full(listed_ref)[2] :].astype(jnp.float32)
    listing = listed.shape[0] // 2
    pick(place_ref, counts_ref, listed[:listing], flat_ref, bins, 2, picked_0)
    pick(place_ref, counts_ref, listed[listing:], flat_ref, bins, 3, picked_1)


def early_kernel(sides, after_0, after_1, *refs):
    piece_refs, (sums_ref, trace_ref) = refs[:-2], refs[-2:]
    pieces = [side_full(ref) for ref in piece_refs[:sides]] + [cross_full(ref) for ref in piece_refs[sides:]]
    add_cross(pieces, trace_ref, FULL, sums_ref)


def full_kernel(place_ref, counts_ref, listed_ref, after_0, after_2, before_ref, *refs):
    piece_refs, (flat_ref, picked_0, picked_1, trace_ref, cross_ref) = refs[:-5], refs[-5:]
    add_cross([cross_full(ref) for ref in piece_refs], trace_ref, FULL, cross_ref, before_ref)
    turn_blocks(cross_ref, FULL, flat_ref)
    listed = listed_ref[cross_full(listed_ref)[2] :].astype(jnp.float32)
    listing = listed.shape[0] // 2
    pick(place_ref, counts_ref, listed[:listing], flat_ref, FULL, 2, picked_0)
    pick(place_ref, counts_ref, listed[listing:], flat_ref, FULL, 3, picked_1)


def near_kernel(bins, sent, place_ref, counts_ref, own_pairs_ref, near_pairs_ref, flat_ref, *refs):
    picked_0, *picked_1 = refs[-1 - sent :]
    pick(place_ref, counts_ref, listing_of(near_pairs_ref, LANES), flat_ref, bins, 1, *picked_1)
    pick(place_ref, counts_ref, listing_of(own_pairs_ref, LANES), flat_ref, bins, 0, picked_0)


def both_rounds(rows, sign):
    row = lax.broadcasted_iota(jnp.int32, rows.shape, 0)
    rows = rows * jnp.where(row < rows.shape[0] // 2, 1.0, sign)
    empty = jnp.zeros_like(rows)
    return jnp.concatenate(
        [jnp.concatenate([rows, empty], axis=1), jnp.concatenate([empty, rows], axis=1)]
    )


def halves(table):
    high = table.astype(jnp.bfloat16)
    return high, (table - high.astype(jnp.float32)).astype(jnp.bfloat16)


def first_lags_kernel(groups, place_ref, inverse_ref, *refs):
    part_0, part_2, part_3, full_0, part_1, *full_1, lags_ref, table_ref = refs
    samples = inverse_ref.shape[1]
    quarter, _ = place_of(place_ref, groups)
    low = quarter % 2
    sign = jnp.where(quarter // 2 == low, 1.0, -1.0)

    def part_table(which):
        start = pl.multiple_of((low ^ which) * 2 * PART, 2 * PART)
        return halves(both_rounds(inverse_ref[pl.ds(start, 2 * PART), :], sign))

    def full_table(mq):
        start = pl.multiple_of(4 * PART + (quarter ^ mq) * 2 * FULL, 2 * FULL)
        return halves(both_rounds(inverse_ref[pl.ds(start, 2 * FULL), :], sign))

    near, other = part_table(0), part_table(1)
    lags = 0.0
    full_1 = jnp.concatenate([ref[...] for ref in full_1])
    for picked, bins, table in (
        (part_0[...], PART, near),
        (part_2[...], PART, near),
        (part_1[...], PART, other),
        (part_3[...], PART, other),
        (full_0[...], FULL, full_table(0)),
        (full_1, FULL, full_table(1)),
    ):
        picked = unpack(picked, bins)
        for half in table:
            lags += jnp.dot(picked, half, preferred_element_type=jnp.float32)
    for step_round in range(2):
        lags_ref[step_round] = lags[:, step_round * samples : (step_round + 1) * samples]
    for at in range(2):
        table_ref[at] = full_table(2 + at)[0]


def lag_kernel(first_ref, table_ref, *refs):
    picked_refs, lags_ref = refs[:-1], refs[-1]
    samples = lags_ref.shape[2]
    more = 0.0
    for at, ref in enumerate(picked_refs):
        more += jnp.dot(unpack(ref[...], FULL), table_ref[at], preferred_element_type=jnp.float32)
    for step_round in range(2):
        lags_ref[step_round] = (
            first_ref[step_round] + more[:, step_round * samples : (step_round + 1) * samples]
        )


def on_device(windows, counts, pairs):
    comps, _, events, samples = windows.shape
    cells = lax.axis_size("cell")
    half, groups = cells // 2, cells // 4
    count = pairs.shape[2]
    inverse = jnp.asarray(inverse_table(samples, cells))
    place = lax.axis_index("cell").astype(jnp.int32).reshape(1)

    def swap(x, mask):
        return lax.ppermute(x, "cell", [(i, i ^ mask) for i in range(cells)])

    def shape(*dims, dtype=jnp.bfloat16):
        return jax.ShapeDtypeStruct(dims, dtype)

    vmem = pl.BlockSpec(memory_space=pltpu.VMEM)
    smem = pl.BlockSpec(memory_space=pltpu.SMEM)
    params = pltpu.CompilerParams(vmem_limit_bytes=VMEM_LIMIT)

    def cost(microseconds):
        return pl.CostEstimate(
            flops=int(microseconds * 1e9), bytes_accessed=2**20, transcendentals=0
        )

    windows = windows.reshape(comps, 2, groups, 2 * SLOTS, samples)
    near_windows, near_pairs = swap(windows, 1), swap(pairs, 1)
    part_rows, full_rows = comps * 2 * PART, comps * 2 * FULL
    part_spectra, full_spectra, table = pl.pallas_call(
        own_kernel,
        out_shape=[
            shape(groups, part_rows, LANES),
            shape(2 * groups, full_rows, LANES),
            shape(2 * PART + 4 * FULL, samples),
        ],
        in_specs=[smem, vmem],
        out_specs=[vmem] * 3,
        compiler_params=params,
        cost_estimate=cost(1),
        name="own_spectra",
    )(place, windows)
    listing = 2 * pairs.size // LANES
    pieces = pl.pallas_call(
        near_spectra_kernel,
        out_shape=[shape(2 * (part_rows + full_rows), LANES)] * groups
        + [shape(2 * full_rows + listing * (mg == 0), LANES) for mg in range(groups)],
        in_specs=[smem] + [vmem] * 6,
        out_specs=[vmem] * (2 * groups),
        compiler_params=params,
        cost_estimate=cost(1),
        name="near_spectra",
    )(place, pairs, near_pairs, table, part_spectra, full_spectra, near_windows)
    arrived = [pieces[0]] + [swap(pieces[m], 2 * m) for m in range(1, 2 * groups)]
    sides, far = arrived[:groups], arrived[groups:]

    early, late = far[: groups - 2], far[groups - 2 :]
    part_packed = shape(packed_rows(count, PART), LANES)
    full_packed = shape(packed_rows(count, FULL), LANES)
    half_packed = shape(packed_rows(count, FULL) // 2, LANES)
    part_blocks = shape(2, 2, SLOTS * SLOTS * width(PART) // LANES, 2 * LANES)
    full_blocks = shape(2, 2, SLOTS * SLOTS * width(FULL) // LANES, 2 * LANES)
    part_flat = pl.pallas_call(
        part_kernel,
        out_shape=part_blocks,
        in_specs=[vmem] * groups,
        out_specs=vmem,
        scratch_shapes=[
            pltpu.VMEM((padded(groups * 2 * comps) * 2 * PART, LANES), jnp.float32),
            pltpu.VMEM((2 * SLOTS * PART, LANES), jnp.float32),
        ],
        compiler_params=params,
        cost_estimate=cost(0.001),
        name="part",
    )(*sides)
    part_0, part_1 = pl.pallas_call(
        functools.partial(near_kernel, PART, 1),
        out_shape=[part_packed, part_packed],
        in_specs=[smem, smem] + [vmem] * 3,
        out_specs=[vmem] * 2,
        compiler_params=params,
        cost_estimate=cost(0.001),
        name="part_near",
    )(place, counts, pairs, near_pairs, part_flat)
    part_2, part_3 = pl.pallas_call(
        functools.partial(far_kernel, PART),
        out_shape=[part_packed, part_packed],
        in_specs=[smem, smem, vmem, vmem, pl.BlockSpec(memory_space=pl.ANY)],
        out_specs=[vmem, vmem],
        compiler_params=params,
        cost_estimate=cost(1),
        name="part_far",
    )(place, counts, far[0], part_flat, part_0)
    part_1 = swap(part_1, 1)
    sums = pl.pallas_call(
        functools.partial(early_kernel, groups),
        out_shape=shape(2 * SLOTS * FULL, LANES, dtype=jnp.float32),
        in_specs=[pl.BlockSpec(memory_space=pl.ANY)] * 2 + [vmem] * (groups + len(early)),
        out_specs=vmem,
        scratch_shapes=[
            pltpu.VMEM((padded((groups + len(early)) * 2 * comps) * 2 * FULL, LANES), jnp.float32)
        ],
        compiler_params=params,
        cost_estimate=cost(0.001),
        name="early",
    )(part_0, part_2, *sides, *early)
    sent, part_2, part_3 = part_2, swap(part_2, half), swap(part_3, half + 1)
    full_flat, full_2, full_3 = pl.pallas_call(
        full_kernel,
        out_shape=[full_blocks, full_packed, full_packed],
        in_specs=[smem, smem, vmem] + [pl.BlockSpec(memory_space=pl.ANY)] * 2 + [vmem] * (1 + len(late)),
        out_specs=[vmem] * 3,
        scratch_shapes=[
            pltpu.VMEM((padded(len(late) * 2 * comps) * 2 * FULL, LANES), jnp.float32),
            pltpu.VMEM((2 * SLOTS * FULL, LANES), jnp.float32),
        ],
        compiler_params=params,
        cost_estimate=cost(10),
        name="full",
    )(place, counts, far[0], part_0, sent, sums, *late)
    full_2, full_3 = swap(full_2, half), swap(full_3, half + 1)
    full_0, *full_1 = pl.pallas_call(
        functools.partial(near_kernel, FULL, 2),
        out_shape=[full_packed, half_packed, half_packed],
        in_specs=[smem, smem] + [vmem] * 3 + [pl.BlockSpec(memory_space=pl.ANY)] * 2,
        out_specs=[vmem] * 3,
        compiler_params=params,
        cost_estimate=cost(0.5),
        name="full_near",
    )(place, counts, pairs, near_pairs, full_flat, part_2, part_3)
    full_1 = [swap(x, 1) for x in full_1]

    first, tables = pl.pallas_call(
        functools.partial(first_lags_kernel, groups),
        out_shape=[
            shape(2, count, samples, dtype=jnp.float32),
            shape(2, 4 * FULL, 2 * samples),
        ],
        in_specs=[smem] + [vmem] * 8,
        out_specs=[vmem] * 2,
        compiler_params=params,
        cost_estimate=cost(0.001),
        name="first_lags",
    )(place, inverse, part_0, part_2, part_3, full_0, part_1, *full_1)
    return pl.pallas_call(
        lag_kernel,
        out_shape=shape(2, count, samples, dtype=jnp.float32),
        in_specs=[vmem] * 4,
        out_specs=vmem,
        compiler_params=params,
        cost_estimate=cost(1),
        name="lags",
    )(first, tables, full_2, full_3)


def solution(mesh):
    in_specs = (P(None, "cell", "grp", None), P("grp"), P(None, None, ("grp", "cell")))
    out_specs = P(None, ("grp", "cell"), None)
    return jax.shard_map(
        on_device, mesh=mesh, in_specs=in_specs, out_specs=out_specs, check_vma=False
    )
```

```python
import functools
import math

import jax
import jax.numpy as jnp
import numpy as np
from jax import lax
from jax.experimental import pallas as pl
from jax.experimental.pallas import tpu as pltpu
from jax.sharding import PartitionSpec as P

EPSILON = 1e-06
COSINE = (
    0.9999999999993376,
    -4.934802200431432,
    4.058712123240781,
    -1.3352627346923478,
    0.23533044681677665,
    -0.02580633847975355,
    0.0019285963125396874,
    -0.00010362767792380447,
    3.734915399663344e-06,
)
SLOTS = 32
LANES = 4 * SLOTS
COMPS = 3
NT = (((1,), (1,)), ((), ()))
TN = (((0,), (0,)), ((), ()))
VMEM_LIMIT = 40 * 1024 * 1024

PART = 16
FULL = 24


def inverse_table(samples, stations):
    bins = samples // 2
    turn = np.arange(bins)[:, None] * np.arange(samples)[None, :] % samples
    angle = turn * (2.0 * math.pi / samples)
    weight = np.where(np.arange(bins) == 0, 1.0, 2.0)[:, None] / samples
    weight = weight * math.sqrt(samples / (3.0 * stations))
    real, imag = weight * np.cos(angle), -weight * np.sin(angle)
    runs = [(at, PART) for at in range(0, 2 * PART, PART)]
    runs += [(at, FULL) for at in range(2 * PART, bins, FULL)]
    rows = [part[at : at + run] for at, run in runs for part in (real, imag)]
    return np.concatenate(rows).astype(np.float32)


def forward_rows(bins, samples):
    count = bins.shape[0]
    sample = lax.broadcasted_iota(jnp.int32, (2 * count, samples), 1)
    turn = jnp.concatenate([bins * sample[:count], bins * sample[:count] + samples // 4])
    turn &= samples - 1
    x = jnp.where(turn > samples // 2, turn - samples, turn).astype(jnp.float32) * (2.0 / samples)
    square = x * x
    value = jnp.full(square.shape, COSINE[-1], jnp.float32)
    for factor in COSINE[-2::-1]:
        value = value * square + factor
    return value.astype(jnp.bfloat16)


def place_of(place_ref, groups):
    position = place_ref[0]
    high, inner = position // (2 * groups), position % (2 * groups)
    return high * 2 + inner % 2, inner // 2


def listing_of(pairs_ref, lanes):
    ends = []
    for end in range(2):
        slots = pairs_ref[:, end, :].astype(jnp.float32)
        ends += [slots[:, at : at + lanes] for at in range(0, slots.shape[1], lanes)]
    return jnp.concatenate(ends)


def station_spectra(windows_ref, at, table):
    parts = []
    for comp in range(windows_ref.shape[0]):
        low = windows_ref[comp, 0, at]
        high = windows_ref[comp, 1, at]
        parts += [low[:SLOTS], high[SLOTS:], low[SLOTS:], high[:SLOTS]]
    traces = jnp.concatenate(parts)
    square = jnp.square(traces.astype(jnp.float32))
    square_hi = square.astype(jnp.bfloat16)
    square_lo = (square - square_hi.astype(jnp.float32)).astype(jnp.bfloat16)
    ones = jnp.ones((16, traces.shape[1]), jnp.bfloat16)
    energy = lax.dot_general(ones, square_hi, NT, preferred_element_type=jnp.float32)
    energy += lax.dot_general(ones, square_lo, NT, preferred_element_type=jnp.float32)
    scale = lax.rsqrt(energy[:1] + EPSILON)
    raw = lax.dot_general(table, traces, NT, preferred_element_type=jnp.float32)
    return (raw * scale).astype(jnp.bfloat16)


def own_kernel(place_ref, windows_ref, part_ref, full_ref, table_ref):
    groups, samples = windows_ref.shape[2], windows_ref.shape[4]
    quarter, group = place_of(place_ref, groups)
    bins = lax.broadcasted_iota(jnp.int32, (PART, samples), 0) + (quarter % 2) * PART
    table_ref[: 2 * PART] = forward_rows(bins, samples)
    for far in range(2):
        start = 2 * PART + (quarter ^ (2 * far)) * FULL
        bins = lax.broadcasted_iota(jnp.int32, (FULL, samples), 0) + start
        at = 2 * PART + 2 * FULL * far
        table_ref[at : at + 2 * FULL] = forward_rows(bins, samples)
    table = table_ref[...]
    for mg in range(groups):
        spectra = station_spectra(windows_ref, group ^ mg, table)
        for comp in range(COMPS):
            lanes = spectra[:, comp * LANES : (comp + 1) * LANES]
            part_ref[mg, comp * 2 * PART : (comp + 1) * 2 * PART] = lanes[: 2 * PART]
            for far in range(2):
                at = 2 * PART + 2 * FULL * far
                full_ref[far * groups + mg, comp * 2 * FULL : (comp + 1) * 2 * FULL] = lanes[at : at + 2 * FULL]


def near_spectra_kernel(
    place_ref, own_pairs_ref, near_pairs_ref, table_ref, part_ref, full_ref, windows_ref, *piece_refs
):
    groups = windows_ref.shape[2]
    _, group = place_of(place_ref, groups)
    table = table_ref[...]
    part_rows, full_rows = COMPS * 2 * PART, COMPS * 2 * FULL
    listed = jnp.concatenate([listing_of(own_pairs_ref, LANES), listing_of(near_pairs_ref, LANES)])
    for m in (groups, groups + 1):
        piece_refs[m][2 * full_rows :] = listed.astype(jnp.bfloat16)
    for mg in range(groups):
        spectra = station_spectra(windows_ref, group ^ mg, table)
        side, cross = piece_refs[mg], piece_refs[groups + mg]
        side[:part_rows] = part_ref[mg]
        side[2 * part_rows : 2 * part_rows + full_rows] = full_ref[mg]
        cross[:full_rows] = full_ref[groups + mg]
        for comp in range(COMPS):
            lanes = spectra[:, comp * LANES : (comp + 1) * LANES]
            at = part_rows + comp * 2 * PART
            side[at : at + 2 * PART] = lanes[: 2 * PART]
            at = 2 * part_rows + full_rows + comp * 2 * FULL
            side[at : at + 2 * FULL] = lanes[2 * PART : 2 * PART + 2 * FULL]
            at = full_rows + comp * 2 * FULL
            cross[at : at + 2 * FULL] = lanes[2 * PART + 2 * FULL :]


def width(bins):
    return 1 << (bins - 1).bit_length()


def packing(count, bins):
    used = 4 * bins
    spare = LANES - used
    if not spare:
        return count, [[(0, 0, 0, used)]]
    runs = used // spare
    rows = count // (runs + 1)
    return rows, [
        [(at * rows, 0, 0, used), (runs * rows, used, at * spare, (at + 1) * spare)] for at in range(runs)
    ]


def packed_rows(count, bins):
    rows, parts = packing(count, bins)
    return rows * len(parts)


def unpack(picked, bins):
    used = 4 * bins
    spare = LANES - used
    if not spare:
        return picked
    runs = used // spare
    rows = picked.shape[0] // runs
    rest = [picked[at * rows : (at + 1) * rows, used:] for at in range(runs)]
    return jnp.concatenate([picked[:, :used], jnp.concatenate(rest, axis=1)])


def pick(place_ref, counts_ref, listed, flat_ref, bins, mq, *picked_refs):
    cells = counts_ref.shape[0]
    quarter, group = place_of(place_ref, cells // 4)
    own = quarter ^ mq
    high, low = own // 2, own % 2
    cell = high * (cells // 2) + group * 2 + low
    count = listed.shape[0] // 2
    runs = LANES // width(bins)
    run_bits, bin_bits, lane_bits = (n.bit_length() - 1 for n in (runs, width(bins), LANES))
    first, second = listed[:count].astype(jnp.int32), listed[count:].astype(jnp.int32)
    far_counts = [counts_ref[cell ^ 1], counts_ref[cell ^ (cells // 2)]]
    odd = lax.broadcasted_iota(jnp.int32, (count, LANES), 0) & 1
    live = (first < counts_ref[cell]) & (second < jnp.where(odd == 1, far_counts[1], far_counts[0]))
    left, right = jnp.where(high == low, first, second), jnp.where(high == low, second, first)
    spot = jnp.where(live, (left >> run_bits) * SLOTS + right, -1)
    turned = (spot * runs + (left & (runs - 1))).T
    lane = lax.broadcasted_iota(jnp.int32, (LANES, LANES), 1)
    run = lane >> bin_bits
    sides = ((high, high), (low, 1 - low))
    found = []
    for step_round in range(2):
        hot, here = [], []
        for at in range(step_round, count, 2):
            both = jnp.broadcast_to(turned[:, at : at + 1], (LANES, LANES))
            here.append((both & (runs - 1)) == run)
            offset = (both >> run_bits) - lane
            hot.append(
                jnp.concatenate(
                    [
                        jnp.where(offset == start, 1.0, 0.0).astype(jnp.bfloat16)
                        for start in range(0, flat_ref.shape[2], LANES)
                    ],
                    axis=1,
                )
            )
        block = flat_ref[sides[step_round][0], sides[step_round][1]]
        wide = jnp.dot(jnp.concatenate(hot), block, preferred_element_type=jnp.float32)
        masked = []
        for chunk, mask in enumerate(here):
            part = wide[chunk * LANES : (chunk + 1) * LANES]
            masked.append(
                jnp.concatenate(
                    [
                        jnp.where(mask, part[:, :LANES], 0.0).astype(jnp.bfloat16),
                        jnp.where(mask, part[:, LANES:], 0.0).astype(jnp.bfloat16),
                    ],
                    axis=1,
                )
            )
        found.append(jnp.concatenate(masked))
    found = jnp.concatenate(found, axis=1)
    spread = lax.broadcasted_iota(jnp.int32, (4 * LANES, LANES), 0)
    kept = lax.broadcasted_iota(jnp.int32, (4 * LANES, LANES), 1)
    bin_of = spread & (width(bins) - 1)
    value = jnp.where(bin_of < bins, (spread >> lane_bits) * bins + bin_of, -1)
    rows, parts = packing(found.shape[0], bins)
    picked = []
    for entries in parts:
        total = 0.0
        for start, at, least, end in entries:
            fold = (value >= least) & (value < end) & (kept == value + (at - least))
            total += jnp.dot(
                found[start : start + rows],
                jnp.where(fold, 1.0, 0.0).astype(jnp.bfloat16),
                preferred_element_type=jnp.float32,
            )
        picked.append(total.astype(jnp.bfloat16))
    picked = jnp.concatenate(picked)
    each = picked.shape[0] // len(picked_refs)
    for at, ref in enumerate(picked_refs):
        ref[...] = picked[at * each : (at + 1) * each]


def padded(traces):
    return -(-traces // 16) * 16


def add_cross(pieces, trace_ref, bins, sums_ref, before_ref=None):
    slots, rows = 2 * SLOTS, 2 * bins
    traces = trace_ref.shape[0] // rows
    start = 0
    for piece, at, size in pieces:
        trace_ref[start : start + size] = piece[at : at + size].astype(jnp.float32)
        start += size
    if start < traces * rows:
        trace_ref[start:] = jnp.zeros((traces * rows - start, LANES), jnp.float32)
    lower = lax.broadcasted_iota(jnp.int32, (traces, LANES), 1) < slots
    for k in range(bins):
        real = trace_ref[pl.ds(k, traces, stride=rows), :]
        imag = trace_ref[pl.ds(bins + k, traces, stride=rows), :]
        left = jnp.concatenate([real, imag]).astype(jnp.bfloat16)[:, :slots]
        right = jnp.concatenate(
            [
                jnp.where(lower, pltpu.roll(real, slots, 1), imag),
                jnp.where(lower, pltpu.roll(imag, slots, 1), -real),
            ]
        ).astype(jnp.bfloat16)
        cross = lax.dot_general(left, right, TN, preferred_element_type=jnp.float32)
        if before_ref is not None:
            cross += before_ref[k * slots : (k + 1) * slots]
        sums_ref[k * slots : (k + 1) * slots] = cross


def turn_blocks(cross_ref, bins, flat_ref):
    slots, runs = 2 * SLOTS, LANES // width(bins)
    empty = jnp.zeros((width(bins) - bins, LANES), jnp.float32)
    for own in range(2):
        for at in range(SLOTS // runs):
            block = []
            for i in range(runs):
                block.append(cross_ref[pl.ds(own * SLOTS + at * runs + i, bins, stride=slots), :])
                block += [empty] * (bins < width(bins))
            block = jnp.concatenate(block).T.astype(jnp.bfloat16)
            for part in range(2):
                for far in range(2):
                    start = (part * 2 + far) * SLOTS
                    flat_ref[
                        own, far, at * SLOTS : (at + 1) * SLOTS, part * LANES : (part + 1) * LANES
                    ] = block[start : start + SLOTS]


def side_part(ref):
    return (ref, 0, 2 * COMPS * 2 * PART)


def side_full(ref):
    return (ref, 2 * COMPS * 2 * PART, 2 * COMPS * 2 * FULL)


def cross_full(ref):
    return (ref, 0, 2 * COMPS * 2 * FULL)


def part_kernel(after_ref, *refs):
    piece_refs, (flat_ref, trace_ref, cross_ref) = refs[:-3], refs[-3:]
    add_cross([side_part(ref) for ref in piece_refs], trace_ref, PART, cross_ref)
    turn_blocks(cross_ref, PART, flat_ref)


def far_kernel(bins, place_ref, counts_ref, listed_ref, flat_ref, after_ref, picked_0, picked_1):
    listed = listed_ref[cross_full(listed_ref)[2] :].astype(jnp.float32)
    listing = listed.shape[0] // 2
    pick(place_ref, counts_ref, listed[:listing], flat_ref, bins, 2, picked_0)
    pick(place_ref, counts_ref, listed[listing:], flat_ref, bins, 3, picked_1)


def early_kernel(own_ref, *refs):
    piece_refs, (sums_ref, trace_ref) = refs[:-2], refs[-2:]
    add_cross([side_full(own_ref)] + [cross_full(ref) for ref in piece_refs], trace_ref, FULL, sums_ref)


def side_kernel(after_0, after_1, before_ref, *refs):
    piece_refs, (sums_ref, trace_ref) = refs[:-2], refs[-2:]
    add_cross([side_full(ref) for ref in piece_refs], trace_ref, FULL, sums_ref, before_ref)


def full_kernel(place_ref, counts_ref, listed_ref, after_0, after_2, before_ref, *refs):
    piece_refs, (flat_ref, picked_0, picked_1, trace_ref, cross_ref) = refs[:-5], refs[-5:]
    add_cross([cross_full(ref) for ref in piece_refs], trace_ref, FULL, cross_ref, before_ref)
    turn_blocks(cross_ref, FULL, flat_ref)
    listed = listed_ref[cross_full(listed_ref)[2] :].astype(jnp.float32)
    listing = listed.shape[0] // 2
    pick(place_ref, counts_ref, listed[:listing], flat_ref, FULL, 2, picked_0)
    pick(place_ref, counts_ref, listed[listing:], flat_ref, FULL, 3, picked_1)


def near_kernel(bins, sent, place_ref, counts_ref, own_pairs_ref, near_pairs_ref, flat_ref, *refs):
    picked_0, *picked_1 = refs[-1 - sent :]
    pick(place_ref, counts_ref, listing_of(near_pairs_ref, LANES), flat_ref, bins, 1, *picked_1)
    pick(place_ref, counts_ref, listing_of(own_pairs_ref, LANES), flat_ref, bins, 0, picked_0)


def both_rounds(rows, sign):
    row = lax.broadcasted_iota(jnp.int32, rows.shape, 0)
    rows = rows * jnp.where(row < rows.shape[0] // 2, 1.0, sign)
    empty = jnp.zeros_like(rows)
    return jnp.concatenate(
        [jnp.concatenate([rows, empty], axis=1), jnp.concatenate([empty, rows], axis=1)]
    )


def halves(table):
    high = table.astype(jnp.bfloat16)
    return high, (table - high.astype(jnp.float32)).astype(jnp.bfloat16)


def first_lags_kernel(groups, place_ref, inverse_ref, *refs):
    part_0, part_2, part_3, full_0, part_1, *full_1, lags_ref, table_ref = refs
    samples = inverse_ref.shape[1]
    quarter, _ = place_of(place_ref, groups)
    low = quarter % 2
    sign = jnp.where(quarter // 2 == low, 1.0, -1.0)

    def part_table(which):
        start = pl.multiple_of((low ^ which) * 2 * PART, 2 * PART)
        return halves(both_rounds(inverse_ref[pl.ds(start, 2 * PART), :], sign))

    def full_table(mq):
        start = pl.multiple_of(4 * PART + (quarter ^ mq) * 2 * FULL, 2 * FULL)
        return halves(both_rounds(inverse_ref[pl.ds(start, 2 * FULL), :], sign))

    near, other = part_table(0), part_table(1)
    lags = 0.0
    full_1 = jnp.concatenate([ref[...] for ref in full_1])
    for picked, bins, table in (
        (part_0[...], PART, near),
        (part_2[...], PART, near),
        (part_1[...], PART, other),
        (part_3[...], PART, other),
        (full_0[...], FULL, full_table(0)),
        (full_1, FULL, full_table(1)),
    ):
        picked = unpack(picked, bins)
        for half in table:
            lags += jnp.dot(picked, half, preferred_element_type=jnp.float32)
    for step_round in range(2):
        lags_ref[step_round] = lags[:, step_round * samples : (step_round + 1) * samples]
    for at in range(2):
        table_ref[at] = full_table(2 + at)[0]


def lag_kernel(first_ref, table_ref, *refs):
    picked_refs, lags_ref = refs[:-1], refs[-1]
    samples = lags_ref.shape[2]
    more = 0.0
    for at, ref in enumerate(picked_refs):
        more += jnp.dot(unpack(ref[...], FULL), table_ref[at], preferred_element_type=jnp.float32)
    for step_round in range(2):
        lags_ref[step_round] = (
            first_ref[step_round] + more[:, step_round * samples : (step_round + 1) * samples]
        )


def on_device(windows, counts, pairs):
    comps, _, events, samples = windows.shape
    cells = lax.axis_size("cell")
    half, groups = cells // 2, cells // 4
    count = pairs.shape[2]
    inverse = jnp.asarray(inverse_table(samples, cells))
    place = lax.axis_index("cell").astype(jnp.int32).reshape(1)

    def swap(x, mask):
        return lax.ppermute(x, "cell", [(i, i ^ mask) for i in range(cells)])

    def shape(*dims, dtype=jnp.bfloat16):
        return jax.ShapeDtypeStruct(dims, dtype)

    vmem = pl.BlockSpec(memory_space=pltpu.VMEM)
    smem = pl.BlockSpec(memory_space=pltpu.SMEM)
    params = pltpu.CompilerParams(vmem_limit_bytes=VMEM_LIMIT)

    def cost(microseconds):
        return pl.CostEstimate(
            flops=int(microseconds * 1e9), bytes_accessed=2**20, transcendentals=0
        )

    windows = windows.reshape(comps, 2, groups, 2 * SLOTS, samples)
    near_windows, near_pairs = swap(windows, 1), swap(pairs, 1)
    part_rows, full_rows = comps * 2 * PART, comps * 2 * FULL
    part_spectra, full_spectra, table = pl.pallas_call(
        own_kernel,
        out_shape=[
            shape(groups, part_rows, LANES),
            shape(2 * groups, full_rows, LANES),
            shape(2 * PART + 4 * FULL, samples),
        ],
        in_specs=[smem, vmem],
        out_specs=[vmem] * 3,
        compiler_params=params,
        cost_estimate=cost(1),
        name="own_spectra",
    )(place, windows)
    listing = 2 * pairs.size // LANES
    pieces = pl.pallas_call(
        near_spectra_kernel,
        out_shape=[shape(2 * (part_rows + full_rows), LANES)] * groups
        + [shape(2 * full_rows + listing * (mg < 2), LANES) for mg in range(groups)],
        in_specs=[smem] + [vmem] * 6,
        out_specs=[vmem] * (2 * groups),
        compiler_params=params,
        cost_estimate=cost(1),
        name="near_spectra",
    )(place, pairs, near_pairs, table, part_spectra, full_spectra, near_windows)
    arrived = [pieces[0]] + [swap(pieces[m], 2 * m) for m in range(1, 2 * groups)]
    sides, far = arrived[:groups], arrived[groups:]

    early, late = far[: groups - 2], far[groups - 2 :]
    part_packed = shape(packed_rows(count, PART), LANES)
    full_packed = shape(packed_rows(count, FULL), LANES)
    half_packed = shape(packed_rows(count, FULL) // 2, LANES)
    part_blocks = shape(2, 2, SLOTS * SLOTS * width(PART) // LANES, 2 * LANES)
    full_blocks = shape(2, 2, SLOTS * SLOTS * width(FULL) // LANES, 2 * LANES)
    sums = pl.pallas_call(
        early_kernel,
        out_shape=shape(2 * SLOTS * FULL, LANES, dtype=jnp.float32),
        in_specs=[vmem] * (1 + len(early)),
        out_specs=vmem,
        scratch_shapes=[
            pltpu.VMEM((padded((1 + len(early)) * 2 * comps) * 2 * FULL, LANES), jnp.float32)
        ],
        compiler_params=params,
        cost_estimate=cost(0.7),
        name="early",
    )(sides[0], *early)
    part_flat = pl.pallas_call(
        part_kernel,
        out_shape=part_blocks,
        in_specs=[pl.BlockSpec(memory_space=pl.ANY)] + [vmem] * groups,
        out_specs=vmem,
        scratch_shapes=[
            pltpu.VMEM((padded(groups * 2 * comps) * 2 * PART, LANES), jnp.float32),
            pltpu.VMEM((2 * SLOTS * PART, LANES), jnp.float32),
        ],
        compiler_params=params,
        cost_estimate=cost(0.001),
        name="part",
    )(sums, *sides)
    part_0, part_1 = pl.pallas_call(
        functools.partial(near_kernel, PART, 1),
        out_shape=[part_packed, part_packed],
        in_specs=[smem, smem] + [vmem] * 3,
        out_specs=[vmem] * 2,
        compiler_params=params,
        cost_estimate=cost(0.001),
        name="part_near",
    )(place, counts, pairs, near_pairs, part_flat)
    part_2, part_3 = pl.pallas_call(
        functools.partial(far_kernel, PART),
        out_shape=[part_packed, part_packed],
        in_specs=[smem, smem, vmem, vmem, pl.BlockSpec(memory_space=pl.ANY)],
        out_specs=[vmem, vmem],
        compiler_params=params,
        cost_estimate=cost(1),
        name="part_far",
    )(place, counts, far[0], part_flat, part_0)
    part_1 = swap(part_1, 1)
    sums = pl.pallas_call(
        side_kernel,
        out_shape=shape(2 * SLOTS * FULL, LANES, dtype=jnp.float32),
        in_specs=[pl.BlockSpec(memory_space=pl.ANY)] * 2 + [vmem] * groups,
        out_specs=vmem,
        scratch_shapes=[
            pltpu.VMEM((padded((groups - 1) * 2 * comps) * 2 * FULL, LANES), jnp.float32)
        ],
        compiler_params=params,
        cost_estimate=cost(0.001),
        name="side",
    )(part_0, part_2, sums, *sides[1:])
    sent, part_2, part_3 = part_2, swap(part_2, half), swap(part_3, half + 1)
    full_flat, full_2, full_3 = pl.pallas_call(
        full_kernel,
        out_shape=[full_blocks, full_packed, full_packed],
        in_specs=[smem, smem, vmem] + [pl.BlockSpec(memory_space=pl.ANY)] * 2 + [vmem] * (1 + len(late)),
        out_specs=[vmem] * 3,
        scratch_shapes=[
            pltpu.VMEM((padded(len(late) * 2 * comps) * 2 * FULL, LANES), jnp.float32),
            pltpu.VMEM((2 * SLOTS * FULL, LANES), jnp.float32),
        ],
        compiler_params=params,
        cost_estimate=cost(10),
        name="full",
    )(place, counts, far[0], part_0, sent, sums, *late)
    full_2, full_3 = swap(full_2, half), swap(full_3, half + 1)
    full_0, *full_1 = pl.pallas_call(
        functools.partial(near_kernel, FULL, 2),
        out_shape=[full_packed, half_packed, half_packed],
        in_specs=[smem, smem] + [vmem] * 3 + [pl.BlockSpec(memory_space=pl.ANY)] * 2,
        out_specs=[vmem] * 3,
        compiler_params=params,
        cost_estimate=cost(0.5),
        name="full_near",
    )(place, counts, pairs, near_pairs, full_flat, part_2, part_3)
    full_1 = [swap(x, 1) for x in full_1]

    first, tables = pl.pallas_call(
        functools.partial(first_lags_kernel, groups),
        out_shape=[
            shape(2, count, samples, dtype=jnp.float32),
            shape(2, 4 * FULL, 2 * samples),
        ],
        in_specs=[smem] + [vmem] * 8,
        out_specs=[vmem] * 2,
        compiler_params=params,
        cost_estimate=cost(0.001),
        name="first_lags",
    )(place, inverse, part_0, part_2, part_3, full_0, part_1, *full_1)
    return pl.pallas_call(
        lag_kernel,
        out_shape=shape(2, count, samples, dtype=jnp.float32),
        in_specs=[vmem] * 4,
        out_specs=vmem,
        compiler_params=params,
        cost_estimate=cost(1),
        name="lags",
    )(first, tables, full_2, full_3)


def solution(mesh):
    in_specs = (P(None, "cell", "grp", None), P("grp"), P(None, None, ("grp", "cell")))
    out_specs = P(None, ("grp", "cell"), None)
    return jax.shard_map(
        on_device, mesh=mesh, in_specs=in_specs, out_specs=out_specs, check_vma=False
    )
```

```python
import functools
import math

import jax
import jax.numpy as jnp
import numpy as np
from jax import lax
from jax.experimental import pallas as pl
from jax.experimental.pallas import tpu as pltpu
from jax.sharding import PartitionSpec as P

EPSILON = 1e-06
COSINE = (
    0.9999999999993376,
    -4.934802200431432,
    4.058712123240781,
    -1.3352627346923478,
    0.23533044681677665,
    -0.02580633847975355,
    0.0019285963125396874,
    -0.00010362767792380447,
    3.734915399663344e-06,
)
SLOTS = 32
LANES = 4 * SLOTS
COMPS = 3
NT = (((1,), (1,)), ((), ()))
TN = (((0,), (0,)), ((), ()))
VMEM_LIMIT = 40 * 1024 * 1024

PART = 16
FULL = 24


def inverse_table(samples, stations):
    bins = samples // 2
    turn = np.arange(bins)[:, None] * np.arange(samples)[None, :] % samples
    angle = turn * (2.0 * math.pi / samples)
    weight = np.where(np.arange(bins) == 0, 1.0, 2.0)[:, None] / samples
    weight = weight * math.sqrt(samples / (3.0 * stations))
    real, imag = weight * np.cos(angle), -weight * np.sin(angle)
    runs = [(at, PART) for at in range(0, 2 * PART, PART)]
    runs += [(at, FULL) for at in range(2 * PART, bins, FULL)]
    rows = [part[at : at + run] for at, run in runs for part in (real, imag)]
    return np.concatenate(rows).astype(np.float32)


def forward_rows(bins, samples):
    count = bins.shape[0]
    sample = lax.broadcasted_iota(jnp.int32, (2 * count, samples), 1)
    turn = jnp.concatenate([bins * sample[:count], bins * sample[:count] + samples // 4])
    turn &= samples - 1
    x = jnp.where(turn > samples // 2, turn - samples, turn).astype(jnp.float32) * (2.0 / samples)
    square = x * x
    value = jnp.full(square.shape, COSINE[-1], jnp.float32)
    for factor in COSINE[-2::-1]:
        value = value * square + factor
    return value.astype(jnp.bfloat16)


def place_of(place_ref, groups):
    position = place_ref[0]
    high, inner = position // (2 * groups), position % (2 * groups)
    return high * 2 + inner % 2, inner // 2


def listing_of(pairs_ref, lanes):
    ends = []
    for end in range(2):
        slots = pairs_ref[:, end, :].astype(jnp.float32)
        ends += [slots[:, at : at + lanes] for at in range(0, slots.shape[1], lanes)]
    return jnp.concatenate(ends)


def station_spectra(windows_ref, at, table):
    parts = []
    for comp in range(windows_ref.shape[0]):
        low = windows_ref[comp, 0, at]
        high = windows_ref[comp, 1, at]
        parts += [low[:SLOTS], high[SLOTS:], low[SLOTS:], high[:SLOTS]]
    traces = jnp.concatenate(parts)
    square = jnp.square(traces.astype(jnp.float32))
    square_hi = square.astype(jnp.bfloat16)
    square_lo = (square - square_hi.astype(jnp.float32)).astype(jnp.bfloat16)
    ones = jnp.ones((16, traces.shape[1]), jnp.bfloat16)
    energy = lax.dot_general(ones, square_hi, NT, preferred_element_type=jnp.float32)
    energy += lax.dot_general(ones, square_lo, NT, preferred_element_type=jnp.float32)
    scale = lax.rsqrt(energy[:1] + EPSILON)
    raw = lax.dot_general(table, traces, NT, preferred_element_type=jnp.float32)
    return (raw * scale).astype(jnp.bfloat16)


def own_kernel(place_ref, windows_ref, part_ref, full_ref, table_ref):
    groups, samples = windows_ref.shape[2], windows_ref.shape[4]
    quarter, group = place_of(place_ref, groups)
    bins = lax.broadcasted_iota(jnp.int32, (PART, samples), 0) + (quarter % 2) * PART
    table_ref[: 2 * PART] = forward_rows(bins, samples)
    for far in range(2):
        start = 2 * PART + (quarter ^ (2 * far)) * FULL
        bins = lax.broadcasted_iota(jnp.int32, (FULL, samples), 0) + start
        at = 2 * PART + 2 * FULL * far
        table_ref[at : at + 2 * FULL] = forward_rows(bins, samples)
    table = table_ref[...]
    for mg in range(groups):
        spectra = station_spectra(windows_ref, group ^ mg, table)
        for comp in range(COMPS):
            lanes = spectra[:, comp * LANES : (comp + 1) * LANES]
            part_ref[mg, comp * 2 * PART : (comp + 1) * 2 * PART] = lanes[: 2 * PART]
            for far in range(2):
                at = 2 * PART + 2 * FULL * far
                full_ref[far * groups + mg, comp * 2 * FULL : (comp + 1) * 2 * FULL] = lanes[at : at + 2 * FULL]


def near_spectra_kernel(
    place_ref, own_pairs_ref, near_pairs_ref, table_ref, part_ref, full_ref, windows_ref, *piece_refs
):
    groups = windows_ref.shape[2]
    _, group = place_of(place_ref, groups)
    table = table_ref[...]
    part_rows, full_rows = COMPS * 2 * PART, COMPS * 2 * FULL
    piece_refs[groups][2 * full_rows :] = jnp.concatenate(
        [listing_of(own_pairs_ref, LANES), listing_of(near_pairs_ref, LANES)]
    ).astype(jnp.bfloat16)
    for mg in range(groups):
        spectra = station_spectra(windows_ref, group ^ mg, table)
        side, cross = piece_refs[mg], piece_refs[groups + mg]
        side[:part_rows] = part_ref[mg]
        side[2 * part_rows : 2 * part_rows + full_rows] = full_ref[mg]
        cross[:full_rows] = full_ref[groups + mg]
        for comp in range(COMPS):
            lanes = spectra[:, comp * LANES : (comp + 1) * LANES]
            at = part_rows + comp * 2 * PART
            side[at : at + 2 * PART] = lanes[: 2 * PART]
            at = 2 * part_rows + full_rows + comp * 2 * FULL
            side[at : at + 2 * FULL] = lanes[2 * PART : 2 * PART + 2 * FULL]
            at = full_rows + comp * 2 * FULL
            cross[at : at + 2 * FULL] = lanes[2 * PART + 2 * FULL :]


def width(bins):
    return 1 << (bins - 1).bit_length()


def packing(count, bins):
    used = 4 * bins
    spare = LANES - used
    if not spare:
        return count, [[(0, 0, 0, used)]]
    runs = used // spare
    rows = count // (runs + 1)
    return rows, [
        [(at * rows, 0, 0, used), (runs * rows, used, at * spare, (at + 1) * spare)] for at in range(runs)
    ]


def packed_rows(count, bins):
    rows, parts = packing(count, bins)
    return rows * len(parts)


def unpack(picked, bins):
    used = 4 * bins
    spare = LANES - used
    if not spare:
        return picked
    runs = used // spare
    rows = picked.shape[0] // runs
    rest = [picked[at * rows : (at + 1) * rows, used:] for at in range(runs)]
    return jnp.concatenate([picked[:, :used], jnp.concatenate(rest, axis=1)])


def pick(place_ref, counts_ref, listed, flat_ref, bins, mq, *picked_refs):
    cells = counts_ref.shape[0]
    quarter, group = place_of(place_ref, cells // 4)
    own = quarter ^ mq
    high, low = own // 2, own % 2
    cell = high * (cells // 2) + group * 2 + low
    count = listed.shape[0] // 2
    runs = LANES // width(bins)
    run_bits, bin_bits, lane_bits = (n.bit_length() - 1 for n in (runs, width(bins), LANES))
    first, second = listed[:count].astype(jnp.int32), listed[count:].astype(jnp.int32)
    far_counts = [counts_ref[cell ^ 1], counts_ref[cell ^ (cells // 2)]]
    odd = lax.broadcasted_iota(jnp.int32, (count, LANES), 0) & 1
    live = (first < counts_ref[cell]) & (second < jnp.where(odd == 1, far_counts[1], far_counts[0]))
    left, right = jnp.where(high == low, first, second), jnp.where(high == low, second, first)
    spot = jnp.where(live, (left >> run_bits) * SLOTS + right, -1)
    turned = (spot * runs + (left & (runs - 1))).T
    lane = lax.broadcasted_iota(jnp.int32, (LANES, LANES), 1)
    run = lane >> bin_bits
    sides = ((high, high), (low, 1 - low))
    found = []
    for step_round in range(2):
        hot, here = [], []
        for at in range(step_round, count, 2):
            both = jnp.broadcast_to(turned[:, at : at + 1], (LANES, LANES))
            here.append((both & (runs - 1)) == run)
            offset = (both >> run_bits) - lane
            hot.append(
                jnp.concatenate(
                    [
                        jnp.where(offset == start, 1.0, 0.0).astype(jnp.bfloat16)
                        for start in range(0, flat_ref.shape[2], LANES)
                    ],
                    axis=1,
                )
            )
        block = flat_ref[sides[step_round][0], sides[step_round][1]]
        wide = jnp.dot(jnp.concatenate(hot), block, preferred_element_type=jnp.float32)
        masked = []
        for chunk, mask in enumerate(here):
            part = wide[chunk * LANES : (chunk + 1) * LANES]
            masked.append(
                jnp.concatenate(
                    [
                        jnp.where(mask, part[:, :LANES], 0.0).astype(jnp.bfloat16),
                        jnp.where(mask, part[:, LANES:], 0.0).astype(jnp.bfloat16),
                    ],
                    axis=1,
                )
            )
        found.append(jnp.concatenate(masked))
    found = jnp.concatenate(found, axis=1)
    spread = lax.broadcasted_iota(jnp.int32, (4 * LANES, LANES), 0)
    kept = lax.broadcasted_iota(jnp.int32, (4 * LANES, LANES), 1)
    bin_of = spread & (width(bins) - 1)
    value = jnp.where(bin_of < bins, (spread >> lane_bits) * bins + bin_of, -1)
    rows, parts = packing(found.shape[0], bins)
    picked = []
    for entries in parts:
        total = 0.0
        for start, at, least, end in entries:
            fold = (value >= least) & (value < end) & (kept == value + (at - least))
            total += jnp.dot(
                found[start : start + rows],
                jnp.where(fold, 1.0, 0.0).astype(jnp.bfloat16),
                preferred_element_type=jnp.float32,
            )
        picked.append(total.astype(jnp.bfloat16))
    picked = jnp.concatenate(picked)
    each = picked.shape[0] // len(picked_refs)
    for at, ref in enumerate(picked_refs):
        ref[...] = picked[at * each : (at + 1) * each]


def padded(traces):
    return -(-traces // 16) * 16


def add_cross(pieces, trace_ref, bins, sums_ref, before_ref=None):
    slots, rows = 2 * SLOTS, 2 * bins
    traces = trace_ref.shape[0] // rows
    start = 0
    for piece, at, size in pieces:
        trace_ref[start : start + size] = piece[at : at + size].astype(jnp.float32)
        start += size
    if start < traces * rows:
        trace_ref[start:] = jnp.zeros((traces * rows - start, LANES), jnp.float32)
    lower = lax.broadcasted_iota(jnp.int32, (traces, LANES), 1) < slots
    for k in range(bins):
        real = trace_ref[pl.ds(k, traces, stride=rows), :]
        imag = trace_ref[pl.ds(bins + k, traces, stride=rows), :]
        left = jnp.concatenate([real, imag]).astype(jnp.bfloat16)[:, :slots]
        right = jnp.concatenate(
            [
                jnp.where(lower, pltpu.roll(real, slots, 1), imag),
                jnp.where(lower, pltpu.roll(imag, slots, 1), -real),
            ]
        ).astype(jnp.bfloat16)
        cross = lax.dot_general(left, right, TN, preferred_element_type=jnp.float32)
        if before_ref is not None:
            cross += before_ref[k * slots : (k + 1) * slots]
        sums_ref[k * slots : (k + 1) * slots] = cross


def turn_blocks(cross_ref, bins, flat_ref):
    slots, runs = 2 * SLOTS, LANES // width(bins)
    empty = jnp.zeros((width(bins) - bins, LANES), jnp.float32)
    for own in range(2):
        for at in range(SLOTS // runs):
            block = []
            for i in range(runs):
                block.append(cross_ref[pl.ds(own * SLOTS + at * runs + i, bins, stride=slots), :])
                block += [empty] * (bins < width(bins))
            block = jnp.concatenate(block).astype(jnp.bfloat16).T
            for part in range(2):
                for far in range(2):
                    start = (part * 2 + far) * SLOTS
                    flat_ref[
                        own, far, at * SLOTS : (at + 1) * SLOTS, part * LANES : (part + 1) * LANES
                    ] = block[start : start + SLOTS]


def side_part(ref):
    return (ref, 0, 2 * COMPS * 2 * PART)


def side_full(ref):
    return (ref, 2 * COMPS * 2 * PART, 2 * COMPS * 2 * FULL)


def cross_full(ref):
    return (ref, 0, 2 * COMPS * 2 * FULL)


def part_kernel(*refs):
    piece_refs, (flat_ref, trace_ref, cross_ref) = refs[:-3], refs[-3:]
    add_cross([side_part(ref) for ref in piece_refs], trace_ref, PART, cross_ref)
    turn_blocks(cross_ref, PART, flat_ref)


def far_kernel(bins, place_ref, counts_ref, listed_ref, flat_ref, after_ref, picked_0, picked_1):
    listed = listed_ref[cross_full(listed_ref)[2] :].astype(jnp.float32)
    listing = listed.shape[0] // 2
    pick(place_ref, counts_ref, listed[:listing], flat_ref, bins, 2, picked_0)
    pick(place_ref, counts_ref, listed[listing:], flat_ref, bins, 3, picked_1)


def early_kernel(sides, after_0, after_1, *refs):
    piece_refs, (sums_ref, trace_ref) = refs[:-2], refs[-2:]
    pieces = [side_full(ref) for ref in piece_refs[:sides]] + [cross_full(ref) for ref in piece_refs[sides:]]
    add_cross(pieces, trace_ref, FULL, sums_ref)


def full_kernel(place_ref, counts_ref, listed_ref, after_0, after_2, before_ref, *refs):
    piece_refs, (flat_ref, picked_0, picked_1, trace_ref, cross_ref) = refs[:-5], refs[-5:]
    add_cross([cross_full(ref) for ref in piece_refs], trace_ref, FULL, cross_ref, before_ref)
    turn_blocks(cross_ref, FULL, flat_ref)
    listed = listed_ref[cross_full(listed_ref)[2] :].astype(jnp.float32)
    listing = listed.shape[0] // 2
    pick(place_ref, counts_ref, listed[:listing], flat_ref, FULL, 2, picked_0)
    pick(place_ref, counts_ref, listed[listing:], flat_ref, FULL, 3, picked_1)


def near_kernel(bins, sent, place_ref, counts_ref, own_pairs_ref, near_pairs_ref, flat_ref, *refs):
    picked_0, *picked_1 = refs[-1 - sent :]
    pick(place_ref, counts_ref, listing_of(near_pairs_ref, LANES), flat_ref, bins, 1, *picked_1)
    pick(place_ref, counts_ref, listing_of(own_pairs_ref, LANES), flat_ref, bins, 0, picked_0)


def both_rounds(rows, sign):
    row = lax.broadcasted_iota(jnp.int32, rows.shape, 0)
    rows = rows * jnp.where(row < rows.shape[0] // 2, 1.0, sign)
    empty = jnp.zeros_like(rows)
    return jnp.concatenate(
        [jnp.concatenate([rows, empty], axis=1), jnp.concatenate([empty, rows], axis=1)]
    )


def halves(table):
    high = table.astype(jnp.bfloat16)
    return high, (table - high.astype(jnp.float32)).astype(jnp.bfloat16)


def first_lags_kernel(groups, place_ref, inverse_ref, *refs):
    part_0, part_2, part_3, full_0, part_1, *full_1, lags_ref, table_ref = refs
    samples = inverse_ref.shape[1]
    quarter, _ = place_of(place_ref, groups)
    low = quarter % 2
    sign = jnp.where(quarter // 2 == low, 1.0, -1.0)

    def part_table(which):
        start = pl.multiple_of((low ^ which) * 2 * PART, 2 * PART)
        return halves(both_rounds(inverse_ref[pl.ds(start, 2 * PART), :], sign))

    def full_table(mq):
        start = pl.multiple_of(4 * PART + (quarter ^ mq) * 2 * FULL, 2 * FULL)
        return halves(both_rounds(inverse_ref[pl.ds(start, 2 * FULL), :], sign))

    near, other = part_table(0), part_table(1)
    lags = 0.0
    full_1 = jnp.concatenate([ref[...] for ref in full_1])
    for picked, bins, table in (
        (part_0[...], PART, near),
        (part_2[...], PART, near),
        (part_1[...], PART, other),
        (part_3[...], PART, other),
        (full_0[...], FULL, full_table(0)),
        (full_1, FULL, full_table(1)),
    ):
        picked = unpack(picked, bins)
        for half in table:
            lags += jnp.dot(picked, half, preferred_element_type=jnp.float32)
    for step_round in range(2):
        lags_ref[step_round] = lags[:, step_round * samples : (step_round + 1) * samples]
    for at in range(2):
        table_ref[at] = full_table(2 + at)[0]


def lag_kernel(first_ref, table_ref, *refs):
    picked_refs, (lags_ref, held_ref, sems) = refs[:-3], refs[-3:]
    samples = lags_ref.shape[2]
    runs = sems.shape[0]
    held = held_ref.shape[1] // runs
    picked = [unpack(ref[...], FULL) for ref in picked_refs]
    copies = []
    for run in range(runs):
        rows = slice(run * held, (run + 1) * held)
        more = 0.0
        for at, values in enumerate(picked):
            more += jnp.dot(values[rows], table_ref[at], preferred_element_type=jnp.float32)
        for step_round in range(2):
            held_ref[step_round, rows] = (
                first_ref[step_round, rows] + more[:, step_round * samples : (step_round + 1) * samples]
            )
        copies.append(
            pltpu.make_async_copy(held_ref.at[:, rows], lags_ref.at[:, rows], sems.at[run])
        )
        copies[-1].start()
    for copy in copies:
        copy.wait()


def on_device(windows, counts, pairs):
    comps, _, events, samples = windows.shape
    cells = lax.axis_size("cell")
    half, groups = cells // 2, cells // 4
    count = pairs.shape[2]
    inverse = jnp.asarray(inverse_table(samples, cells))
    place = lax.axis_index("cell").astype(jnp.int32).reshape(1)

    def swap(x, mask):
        return lax.ppermute(x, "cell", [(i, i ^ mask) for i in range(cells)])

    def shape(*dims, dtype=jnp.bfloat16):
        return jax.ShapeDtypeStruct(dims, dtype)

    vmem = pl.BlockSpec(memory_space=pltpu.VMEM)
    smem = pl.BlockSpec(memory_space=pltpu.SMEM)
    params = pltpu.CompilerParams(vmem_limit_bytes=VMEM_LIMIT)

    def cost(microseconds):
        return pl.CostEstimate(
            flops=int(microseconds * 1e9), bytes_accessed=2**20, transcendentals=0
        )

    windows = windows.reshape(comps, 2, groups, 2 * SLOTS, samples)
    near_windows, near_pairs = swap(windows, 1), swap(pairs, 1)
    part_rows, full_rows = comps * 2 * PART, comps * 2 * FULL
    part_spectra, full_spectra, table = pl.pallas_call(
        own_kernel,
        out_shape=[
            shape(groups, part_rows, LANES),
            shape(2 * groups, full_rows, LANES),
            shape(2 * PART + 4 * FULL, samples),
        ],
        in_specs=[smem, vmem],
        out_specs=[vmem] * 3,
        compiler_params=params,
        cost_estimate=cost(1),
        name="own_spectra",
    )(place, windows)
    listing = 2 * pairs.size // LANES
    pieces = pl.pallas_call(
        near_spectra_kernel,
        out_shape=[shape(2 * (part_rows + full_rows), LANES)] * groups
        + [shape(2 * full_rows + listing * (mg == 0), LANES) for mg in range(groups)],
        in_specs=[smem] + [vmem] * 6,
        out_specs=[vmem] * (2 * groups),
        compiler_params=params,
        cost_estimate=cost(1),
        name="near_spectra",
    )(place, pairs, near_pairs, table, part_spectra, full_spectra, near_windows)
    arrived = [pieces[0]] + [swap(pieces[m], 2 * m) for m in range(1, 2 * groups)]
    sides, far = arrived[:groups], arrived[groups:]

    early, late = far[: groups - 2], far[groups - 2 :]
    part_packed = shape(packed_rows(count, PART), LANES)
    full_packed = shape(packed_rows(count, FULL), LANES)
    half_packed = shape(packed_rows(count, FULL) // 2, LANES)
    part_blocks = shape(2, 2, SLOTS * SLOTS * width(PART) // LANES, 2 * LANES)
    full_blocks = shape(2, 2, SLOTS * SLOTS * width(FULL) // LANES, 2 * LANES)
    part_flat = pl.pallas_call(
        part_kernel,
        out_shape=part_blocks,
        in_specs=[vmem] * groups,
        out_specs=vmem,
        scratch_shapes=[
            pltpu.VMEM((padded(groups * 2 * comps) * 2 * PART, LANES), jnp.float32),
            pltpu.VMEM((2 * SLOTS * PART, LANES), jnp.float32),
        ],
        compiler_params=params,
        cost_estimate=cost(0.001),
        name="part",
    )(*sides)
    part_0, part_1 = pl.pallas_call(
        functools.partial(near_kernel, PART, 1),
        out_shape=[part_packed, part_packed],
        in_specs=[smem, smem] + [vmem] * 3,
        out_specs=[vmem] * 2,
        compiler_params=params,
        cost_estimate=cost(0.001),
        name="part_near",
    )(place, counts, pairs, near_pairs, part_flat)
    part_2, part_3 = pl.pallas_call(
        functools.partial(far_kernel, PART),
        out_shape=[part_packed, part_packed],
        in_specs=[smem, smem, vmem, vmem, pl.BlockSpec(memory_space=pl.ANY)],
        out_specs=[vmem, vmem],
        compiler_params=params,
        cost_estimate=cost(1),
        name="part_far",
    )(place, counts, far[0], part_flat, part_0)
    part_1 = swap(part_1, 1)
    sums = pl.pallas_call(
        functools.partial(early_kernel, groups),
        out_shape=shape(2 * SLOTS * FULL, LANES, dtype=jnp.float32),
        in_specs=[pl.BlockSpec(memory_space=pl.ANY)] * 2 + [vmem] * (groups + len(early)),
        out_specs=vmem,
        scratch_shapes=[
            pltpu.VMEM((padded((groups + len(early)) * 2 * comps) * 2 * FULL, LANES), jnp.float32)
        ],
        compiler_params=params,
        cost_estimate=cost(0.001),
        name="early",
    )(part_0, part_2, *sides, *early)
    sent, part_2, part_3 = part_2, swap(part_2, half), swap(part_3, half + 1)
    full_flat, full_2, full_3 = pl.pallas_call(
        full_kernel,
        out_shape=[full_blocks, full_packed, full_packed],
        in_specs=[smem, smem, vmem] + [pl.BlockSpec(memory_space=pl.ANY)] * 2 + [vmem] * (1 + len(late)),
        out_specs=[vmem] * 3,
        scratch_shapes=[
            pltpu.VMEM((padded(len(late) * 2 * comps) * 2 * FULL, LANES), jnp.float32),
            pltpu.VMEM((2 * SLOTS * FULL, LANES), jnp.float32),
        ],
        compiler_params=params,
        cost_estimate=cost(10),
        name="full",
    )(place, counts, far[0], part_0, sent, sums, *late)
    full_2, full_3 = swap(full_2, half), swap(full_3, half + 1)
    full_0, *full_1 = pl.pallas_call(
        functools.partial(near_kernel, FULL, 2),
        out_shape=[full_packed, half_packed, half_packed],
        in_specs=[smem, smem] + [vmem] * 3 + [pl.BlockSpec(memory_space=pl.ANY)] * 2,
        out_specs=[vmem] * 3,
        compiler_params=params,
        cost_estimate=cost(0.5),
        name="full_near",
    )(place, counts, pairs, near_pairs, full_flat, part_2, part_3)
    full_1 = [swap(x, 1) for x in full_1]

    first, tables = pl.pallas_call(
        functools.partial(first_lags_kernel, groups),
        out_shape=[
            shape(2, count, samples, dtype=jnp.float32),
            shape(2, 4 * FULL, 2 * samples),
        ],
        in_specs=[smem] + [vmem] * 8,
        out_specs=[vmem] * 2,
        compiler_params=params,
        cost_estimate=cost(0.001),
        name="first_lags",
    )(place, inverse, part_0, part_2, part_3, full_0, part_1, *full_1)
    return pl.pallas_call(
        lag_kernel,
        out_shape=shape(2, count, samples, dtype=jnp.float32),
        in_specs=[vmem] * 4,
        out_specs=pl.BlockSpec(memory_space=pl.ANY),
        scratch_shapes=[
            pltpu.VMEM((2, count, samples), jnp.float32),
            pltpu.SemaphoreType.DMA((4,)),
        ],
        compiler_params=params,
        cost_estimate=cost(1),
        name="lags",
    )(first, tables, full_2, full_3)


def solution(mesh):
    in_specs = (P(None, "cell", "grp", None), P("grp"), P(None, None, ("grp", "cell")))
    out_specs = P(None, ("grp", "cell"), None)
    return jax.shard_map(
        on_device, mesh=mesh, in_specs=in_specs, out_specs=out_specs, check_vma=False
    )
```

```python
import functools
import math

import jax
import jax.numpy as jnp
import numpy as np
from jax import lax
from jax.experimental import pallas as pl
from jax.experimental.pallas import tpu as pltpu
from jax.sharding import PartitionSpec as P

EPSILON = 1e-06
COSINE = (
    0.9999999999993376,
    -4.934802200431432,
    4.058712123240781,
    -1.3352627346923478,
    0.23533044681677665,
    -0.02580633847975355,
    0.0019285963125396874,
    -0.00010362767792380447,
    3.734915399663344e-06,
)
SLOTS = 32
LANES = 4 * SLOTS
COMPS = 3
NT = (((1,), (1,)), ((), ()))
TN = (((0,), (0,)), ((), ()))
VMEM_LIMIT = 40 * 1024 * 1024

PART = 16
FULL = 24


def inverse_table(samples, stations):
    bins = samples // 2
    turn = np.arange(bins)[:, None] * np.arange(samples)[None, :] % samples
    angle = turn * (2.0 * math.pi / samples)
    weight = np.where(np.arange(bins) == 0, 1.0, 2.0)[:, None] / samples
    weight = weight * math.sqrt(samples / (3.0 * stations))
    real, imag = weight * np.cos(angle), -weight * np.sin(angle)
    runs = [(at, PART) for at in range(0, 2 * PART, PART)]
    runs += [(at, FULL) for at in range(2 * PART, bins, FULL)]
    rows = [part[at : at + run] for at, run in runs for part in (real, imag)]
    return np.concatenate(rows).astype(np.float32)


def forward_rows(bins, samples):
    count = bins.shape[0]
    sample = lax.broadcasted_iota(jnp.int32, (2 * count, samples), 1)
    turn = jnp.concatenate([bins * sample[:count], bins * sample[:count] + samples // 4])
    turn &= samples - 1
    x = jnp.where(turn > samples // 2, turn - samples, turn).astype(jnp.float32) * (2.0 / samples)
    square = x * x
    value = jnp.full(square.shape, COSINE[-1], jnp.float32)
    for factor in COSINE[-2::-1]:
        value = value * square + factor
    return value.astype(jnp.bfloat16)


def place_of(place_ref, groups):
    position = place_ref[0]
    high, inner = position // (2 * groups), position % (2 * groups)
    return high * 2 + inner % 2, inner // 2


def listing_of(pairs_ref, lanes):
    ends = []
    for end in range(2):
        slots = pairs_ref[:, end, :].astype(jnp.float32)
        ends += [slots[:, at : at + lanes] for at in range(0, slots.shape[1], lanes)]
    return jnp.concatenate(ends)


def station_spectra(windows_ref, at, table):
    parts = []
    for comp in range(COMPS):
        low = windows_ref[comp, 0, at]
        high = windows_ref[comp, 1, at]
        parts += [low[:SLOTS], high[SLOTS:], low[SLOTS:], high[:SLOTS]]
    traces = jnp.concatenate(parts)
    energy = jnp.sum(jnp.square(traces.astype(jnp.float32)), axis=1, keepdims=True)
    raw = lax.dot_general(traces, table, NT, preferred_element_type=jnp.float32)
    spectra = (raw * lax.rsqrt(energy + EPSILON)).astype(jnp.bfloat16)
    return [spectra[comp * LANES : (comp + 1) * LANES].T for comp in range(COMPS)]


def own_kernel(place_ref, windows_ref, part_ref, full_ref, table_ref):
    groups, samples = windows_ref.shape[2], windows_ref.shape[4]
    quarter, group = place_of(place_ref, groups)
    bins = lax.broadcasted_iota(jnp.int32, (PART, samples), 0) + (quarter % 2) * PART
    table_ref[: 2 * PART] = forward_rows(bins, samples)
    for far in range(2):
        start = 2 * PART + (quarter ^ (2 * far)) * FULL
        bins = lax.broadcasted_iota(jnp.int32, (FULL, samples), 0) + start
        at = 2 * PART + 2 * FULL * far
        table_ref[at : at + 2 * FULL] = forward_rows(bins, samples)
    table = table_ref[...]
    for mg in range(groups):
        spectra = station_spectra(windows_ref, group ^ mg, table)
        for comp in range(COMPS):
            lanes = spectra[comp]
            part_ref[mg, comp * 2 * PART : (comp + 1) * 2 * PART] = lanes[: 2 * PART]
            for far in range(2):
                at = 2 * PART + 2 * FULL * far
                full_ref[far * groups + mg, comp * 2 * FULL : (comp + 1) * 2 * FULL] = lanes[at : at + 2 * FULL]


def near_spectra_kernel(
    place_ref, own_pairs_ref, near_pairs_ref, table_ref, part_ref, full_ref, windows_ref, *piece_refs
):
    groups = windows_ref.shape[2]
    _, group = place_of(place_ref, groups)
    table = table_ref[...]
    part_rows, full_rows = COMPS * 2 * PART, COMPS * 2 * FULL
    piece_refs[groups][2 * full_rows :] = jnp.concatenate(
        [listing_of(own_pairs_ref, LANES), listing_of(near_pairs_ref, LANES)]
    ).astype(jnp.bfloat16)
    for mg in range(groups):
        spectra = station_spectra(windows_ref, group ^ mg, table)
        side, cross = piece_refs[mg], piece_refs[groups + mg]
        side[:part_rows] = part_ref[mg]
        side[2 * part_rows : 2 * part_rows + full_rows] = full_ref[mg]
        cross[:full_rows] = full_ref[groups + mg]
        for comp in range(COMPS):
            lanes = spectra[comp]
            at = part_rows + comp * 2 * PART
            side[at : at + 2 * PART] = lanes[: 2 * PART]
            at = 2 * part_rows + full_rows + comp * 2 * FULL
            side[at : at + 2 * FULL] = lanes[2 * PART : 2 * PART + 2 * FULL]
            at = full_rows + comp * 2 * FULL
            cross[at : at + 2 * FULL] = lanes[2 * PART + 2 * FULL :]


def width(bins):
    return 1 << (bins - 1).bit_length()


def packing(count, bins):
    used = 4 * bins
    spare = LANES - used
    if not spare:
        return count, [[(0, 0, 0, used)]]
    runs = used // spare
    rows = count // (runs + 1)
    return rows, [
        [(at * rows, 0, 0, used), (runs * rows, used, at * spare, (at + 1) * spare)] for at in range(runs)
    ]


def packed_rows(count, bins):
    rows, parts = packing(count, bins)
    return rows * len(parts)


def unpack(picked, bins):
    used = 4 * bins
    spare = LANES - used
    if not spare:
        return picked
    runs = used // spare
    rows = picked.shape[0] // runs
    rest = [picked[at * rows : (at + 1) * rows, used:] for at in range(runs)]
    return jnp.concatenate([picked[:, :used], jnp.concatenate(rest, axis=1)])


def sides_of(place_ref, cells, mq):
    quarter, group = place_of(place_ref, cells // 4)
    own = quarter ^ mq
    high, low = own // 2, own % 2
    return high * (cells // 2) + group * 2 + low, high, low, ((high, high), (low, 1 - low))


def hots(place_ref, counts_ref, listed, rows, bins, mq):
    cells = counts_ref.shape[0]
    cell, high, low, _ = sides_of(place_ref, cells, mq)
    count = listed.shape[0] // 2
    runs = LANES // width(bins)
    run_bits, bin_bits = (n.bit_length() - 1 for n in (runs, width(bins)))
    first, second = listed[:count].astype(jnp.int32), listed[count:].astype(jnp.int32)
    far_counts = [counts_ref[cell ^ 1], counts_ref[cell ^ (cells // 2)]]
    odd = lax.broadcasted_iota(jnp.int32, (count, LANES), 0) & 1
    live = (first < counts_ref[cell]) & (second < jnp.where(odd == 1, far_counts[1], far_counts[0]))
    left, right = jnp.where(high == low, first, second), jnp.where(high == low, second, first)
    spot = jnp.where(live, (left >> run_bits) * SLOTS + right, -1)
    turned = (spot * runs + (left & (runs - 1))).T
    lane = lax.broadcasted_iota(jnp.int32, (LANES, LANES), 1)
    run = lane >> bin_bits
    found = []
    for step_round in range(2):
        hot, here = [], []
        for at in range(step_round, count, 2):
            both = jnp.broadcast_to(turned[:, at : at + 1], (LANES, LANES))
            here.append(jnp.where((both & (runs - 1)) == run, 1.0, 0.0).astype(jnp.bfloat16))
            offset = (both >> run_bits) - lane
            hot.append(
                jnp.concatenate(
                    [
                        jnp.where(offset == start, 1.0, 0.0).astype(jnp.bfloat16)
                        for start in range(0, rows, LANES)
                    ],
                    axis=1,
                )
            )
        found.append((jnp.concatenate(hot), jnp.concatenate(here)))
    return found


def folds_of(count, bins):
    return sorted({entry[1:] for entries in packing(count, bins)[1] for entry in entries})


def folds(count, bins):
    spread = lax.broadcasted_iota(jnp.int32, (4 * LANES, LANES), 0)
    kept = lax.broadcasted_iota(jnp.int32, (4 * LANES, LANES), 1)
    bin_of = spread & (width(bins) - 1)
    value = jnp.where(bin_of < bins, (spread >> (LANES.bit_length() - 1)) * bins + bin_of, -1)
    kinds = folds_of(count, bins)
    matrices = []
    for at, least, end in kinds:
        fold = (value >= least) & (value < end) & (kept == value + (at - least))
        matrices.append(jnp.where(fold, 1.0, 0.0).astype(jnp.bfloat16))
    return kinds, matrices


def picks(place_ref, cells, hot, kinds, matrices, flat_ref, bins, mq):
    _, _, _, sides = sides_of(place_ref, cells, mq)
    found = []
    for (rows, lanes), (own, far) in zip(hot, sides):
        wide = jnp.dot(rows, flat_ref[own, far], preferred_element_type=jnp.float32).astype(jnp.bfloat16)
        found += [wide[:, :LANES] * lanes, wide[:, LANES:] * lanes]
    found = jnp.concatenate(found, axis=1)
    held, parts = packing(found.shape[0], bins)
    picked = []
    for entries in parts:
        total = 0.0
        for start, *kind in entries:
            total += jnp.dot(
                found[start : start + held],
                matrices[kinds.index(tuple(kind))],
                preferred_element_type=jnp.float32,
            )
        picked.append(total.astype(jnp.bfloat16))
    return jnp.concatenate(picked)


def pick(place_ref, counts_ref, listed, flat_ref, bins, mq, *picked_refs):
    hot = hots(place_ref, counts_ref, listed, flat_ref.shape[2], bins, mq)
    kinds, matrices = folds(listed.shape[0] // 4 * LANES, bins)
    picked = picks(place_ref, counts_ref.shape[0], hot, kinds, matrices, flat_ref, bins, mq)
    each = picked.shape[0] // len(picked_refs)
    for at, ref in enumerate(picked_refs):
        ref[...] = picked[at * each : (at + 1) * each]


def padded(traces):
    return -(-traces // 16) * 16


def add_cross(pieces, trace_ref, bins, sums_ref, before_ref=None):
    slots, rows = 2 * SLOTS, 2 * bins
    traces = trace_ref.shape[0] // rows
    start = 0
    for piece, at, size in pieces:
        trace_ref[start : start + size] = piece[at : at + size].astype(jnp.float32)
        start += size
    if start < traces * rows:
        trace_ref[start:] = jnp.zeros((traces * rows - start, LANES), jnp.float32)
    lower = lax.broadcasted_iota(jnp.int32, (traces, LANES), 1) < slots
    for k in range(bins):
        real = trace_ref[pl.ds(k, traces, stride=rows), :]
        imag = trace_ref[pl.ds(bins + k, traces, stride=rows), :]
        left = jnp.concatenate([real, imag]).astype(jnp.bfloat16)[:, :slots]
        right = jnp.concatenate(
            [
                jnp.where(lower, pltpu.roll(real, slots, 1), imag),
                jnp.where(lower, pltpu.roll(imag, slots, 1), -real),
            ]
        ).astype(jnp.bfloat16)
        cross = lax.dot_general(left, right, TN, preferred_element_type=jnp.float32)
        if before_ref is not None:
            cross += before_ref[k * slots : (k + 1) * slots]
        sums_ref[k * slots : (k + 1) * slots] = cross


def turn_blocks(cross_ref, bins, flat_ref):
    slots, runs = 2 * SLOTS, LANES // width(bins)
    empty = jnp.zeros((width(bins) - bins, LANES), jnp.float32)
    for own in range(2):
        for at in range(SLOTS // runs):
            block = []
            for i in range(runs):
                block.append(cross_ref[pl.ds(own * SLOTS + at * runs + i, bins, stride=slots), :])
                block += [empty] * (bins < width(bins))
            block = jnp.concatenate(block).astype(jnp.bfloat16).T
            for part in range(2):
                for far in range(2):
                    start = (part * 2 + far) * SLOTS
                    flat_ref[
                        own, far, at * SLOTS : (at + 1) * SLOTS, part * LANES : (part + 1) * LANES
                    ] = block[start : start + SLOTS]


def side_part(ref):
    return (ref, 0, 2 * COMPS * 2 * PART)


def side_full(ref):
    return (ref, 2 * COMPS * 2 * PART, 2 * COMPS * 2 * FULL)


def cross_full(ref):
    return (ref, 0, 2 * COMPS * 2 * FULL)


def part_kernel(*refs):
    piece_refs, (flat_ref, trace_ref, cross_ref) = refs[:-3], refs[-3:]
    add_cross([side_part(ref) for ref in piece_refs], trace_ref, PART, cross_ref)
    turn_blocks(cross_ref, PART, flat_ref)


def far_kernel(bins, place_ref, counts_ref, listed_ref, flat_ref, after_ref, picked_0, picked_1):
    listed = listed_ref[cross_full(listed_ref)[2] :].astype(jnp.float32)
    listing = listed.shape[0] // 2
    pick(place_ref, counts_ref, listed[:listing], flat_ref, bins, 2, picked_0)
    pick(place_ref, counts_ref, listed[listing:], flat_ref, bins, 3, picked_1)


def early_kernel(sides, after_0, after_1, *refs):
    piece_refs, (sums_ref, trace_ref) = refs[:-2], refs[-2:]
    pieces = [side_full(ref) for ref in piece_refs[:sides]] + [cross_full(ref) for ref in piece_refs[sides:]]
    add_cross(pieces, trace_ref, FULL, sums_ref)


def ready_kernel(place_ref, counts_ref, listed_ref, after_ref, hot_ref, here_ref, fold_ref):
    listed = listed_ref[cross_full(listed_ref)[2] :].astype(jnp.float32)
    listing = listed.shape[0] // 2
    for at in range(2):
        part = listed[at * listing : (at + 1) * listing]
        for step_round, (hot, here) in enumerate(
            hots(place_ref, counts_ref, part, hot_ref.shape[3], FULL, 2 + at)
        ):
            hot_ref[at, step_round] = hot
            here_ref[at, step_round] = here
    for at, matrix in enumerate(folds(hot_ref.shape[2], FULL)[1]):
        fold_ref[at] = matrix


def full_kernel(cells, place_ref, hot_ref, here_ref, fold_ref, after_0, before_ref, *refs):
    piece_refs, (flat_ref, picked_0, picked_1, trace_ref, cross_ref) = refs[:-5], refs[-5:]
    add_cross([cross_full(ref) for ref in piece_refs], trace_ref, FULL, cross_ref, before_ref)
    turn_blocks(cross_ref, FULL, flat_ref)
    count = hot_ref.shape[2]
    kinds = folds_of(count, FULL)
    matrices = [fold_ref[at] for at in range(len(kinds))]
    for at, ref in enumerate((picked_0, picked_1)):
        hot = [(hot_ref[at, step_round], here_ref[at, step_round]) for step_round in range(2)]
        ref[...] = picks(place_ref, cells, hot, kinds, matrices, flat_ref, FULL, 2 + at)


def near_kernel(bins, sent, place_ref, counts_ref, own_pairs_ref, near_pairs_ref, flat_ref, *refs):
    picked_0, *picked_1 = refs[-1 - sent :]
    pick(place_ref, counts_ref, listing_of(near_pairs_ref, LANES), flat_ref, bins, 1, *picked_1)
    pick(place_ref, counts_ref, listing_of(own_pairs_ref, LANES), flat_ref, bins, 0, picked_0)


def both_rounds(rows, sign):
    row = lax.broadcasted_iota(jnp.int32, rows.shape, 0)
    rows = rows * jnp.where(row < rows.shape[0] // 2, 1.0, sign)
    empty = jnp.zeros_like(rows)
    return jnp.concatenate(
        [jnp.concatenate([rows, empty], axis=1), jnp.concatenate([empty, rows], axis=1)]
    )


def halves(table):
    high = table.astype(jnp.bfloat16)
    return high, (table - high.astype(jnp.float32)).astype(jnp.bfloat16)


def first_lags_kernel(groups, place_ref, inverse_ref, *refs):
    part_0, part_2, part_3, full_0, part_1, *full_1, lags_ref, table_ref = refs
    samples = inverse_ref.shape[1]
    quarter, _ = place_of(place_ref, groups)
    low = quarter % 2
    sign = jnp.where(quarter // 2 == low, 1.0, -1.0)

    def part_table(which):
        start = pl.multiple_of((low ^ which) * 2 * PART, 2 * PART)
        return halves(both_rounds(inverse_ref[pl.ds(start, 2 * PART), :], sign))

    def full_table(mq):
        start = pl.multiple_of(4 * PART + (quarter ^ mq) * 2 * FULL, 2 * FULL)
        return halves(both_rounds(inverse_ref[pl.ds(start, 2 * FULL), :], sign))

    near, other = part_table(0), part_table(1)
    lags = 0.0
    full_1 = jnp.concatenate([ref[...] for ref in full_1])
    for picked, bins, table in (
        (part_0[...], PART, near),
        (part_2[...], PART, near),
        (part_1[...], PART, other),
        (part_3[...], PART, other),
        (full_0[...], FULL, full_table(0)),
        (full_1, FULL, full_table(1)),
    ):
        picked = unpack(picked, bins)
        for half in table:
            lags += jnp.dot(picked, half, preferred_element_type=jnp.float32)
    for step_round in range(2):
        lags_ref[step_round] = lags[:, step_round * samples : (step_round + 1) * samples]
    for at in range(2):
        table_ref[at] = full_table(2 + at)[0]


def lag_kernel(first_ref, table_ref, *refs):
    picked_refs, (lags_ref, held_ref, sems) = refs[:-3], refs[-3:]
    samples = lags_ref.shape[2]
    runs = sems.shape[0]
    held = held_ref.shape[1] // runs
    picked = [unpack(ref[...], FULL) for ref in picked_refs]
    copies = []
    for run in range(runs):
        rows = slice(run * held, (run + 1) * held)
        more = 0.0
        for at, values in enumerate(picked):
            more += jnp.dot(values[rows], table_ref[at], preferred_element_type=jnp.float32)
        for step_round in range(2):
            held_ref[step_round, rows] = (
                first_ref[step_round, rows] + more[:, step_round * samples : (step_round + 1) * samples]
            )
        copies.append(
            pltpu.make_async_copy(held_ref.at[:, rows], lags_ref.at[:, rows], sems.at[run])
        )
        copies[-1].start()
    for copy in copies:
        copy.wait()


def on_device(windows, counts, pairs):
    comps, _, events, samples = windows.shape
    cells = lax.axis_size("cell")
    half, groups = cells // 2, cells // 4
    count = pairs.shape[2]
    inverse = jnp.asarray(inverse_table(samples, cells))
    place = lax.axis_index("cell").astype(jnp.int32).reshape(1)

    def swap(x, mask):
        return lax.ppermute(x, "cell", [(i, i ^ mask) for i in range(cells)])

    def shape(*dims, dtype=jnp.bfloat16):
        return jax.ShapeDtypeStruct(dims, dtype)

    vmem = pl.BlockSpec(memory_space=pltpu.VMEM)
    smem = pl.BlockSpec(memory_space=pltpu.SMEM)
    params = pltpu.CompilerParams(vmem_limit_bytes=VMEM_LIMIT)

    def cost(microseconds):
        return pl.CostEstimate(
            flops=int(microseconds * 1e9), bytes_accessed=2**20, transcendentals=0
        )

    windows = windows.reshape(comps, 2, groups, 2 * SLOTS, samples)
    near_windows, near_pairs = swap(windows, 1), swap(pairs, 1)
    part_rows, full_rows = comps * 2 * PART, comps * 2 * FULL
    part_spectra, full_spectra, table = pl.pallas_call(
        own_kernel,
        out_shape=[
            shape(groups, part_rows, LANES),
            shape(2 * groups, full_rows, LANES),
            shape(2 * PART + 4 * FULL, samples),
        ],
        in_specs=[smem, vmem],
        out_specs=[vmem] * 3,
        compiler_params=params,
        cost_estimate=cost(1),
        name="own_spectra",
    )(place, windows)
    listing = 2 * pairs.size // LANES
    pieces = pl.pallas_call(
        near_spectra_kernel,
        out_shape=[shape(2 * (part_rows + full_rows), LANES)] * groups
        + [shape(2 * full_rows + listing * (mg == 0), LANES) for mg in range(groups)],
        in_specs=[smem] + [vmem] * 6,
        out_specs=[vmem] * (2 * groups),
        compiler_params=params,
        cost_estimate=cost(1),
        name="near_spectra",
    )(place, pairs, near_pairs, table, part_spectra, full_spectra, near_windows)
    arrived = [pieces[0]] + [swap(pieces[m], 2 * m) for m in range(1, 2 * groups)]
    sides, far = arrived[:groups], arrived[groups:]

    early, late = far[: groups - 2], far[groups - 2 :]
    part_packed = shape(packed_rows(count, PART), LANES)
    full_packed = shape(packed_rows(count, FULL), LANES)
    half_packed = shape(packed_rows(count, FULL) // 2, LANES)
    part_blocks = shape(2, 2, SLOTS * SLOTS * width(PART) // LANES, 2 * LANES)
    full_blocks = shape(2, 2, SLOTS * SLOTS * width(FULL) // LANES, 2 * LANES)
    part_flat = pl.pallas_call(
        part_kernel,
        out_shape=part_blocks,
        in_specs=[vmem] * groups,
        out_specs=vmem,
        scratch_shapes=[
            pltpu.VMEM((padded(groups * 2 * comps) * 2 * PART, LANES), jnp.float32),
            pltpu.VMEM((2 * SLOTS * PART, LANES), jnp.float32),
        ],
        compiler_params=params,
        cost_estimate=cost(0.001),
        name="part",
    )(*sides)
    part_0, part_1 = pl.pallas_call(
        functools.partial(near_kernel, PART, 1),
        out_shape=[part_packed, part_packed],
        in_specs=[smem, smem] + [vmem] * 3,
        out_specs=[vmem] * 2,
        compiler_params=params,
        cost_estimate=cost(0.001),
        name="part_near",
    )(place, counts, pairs, near_pairs, part_flat)
    part_2, part_3 = pl.pallas_call(
        functools.partial(far_kernel, PART),
        out_shape=[part_packed, part_packed],
        in_specs=[smem, smem, vmem, vmem, pl.BlockSpec(memory_space=pl.ANY)],
        out_specs=[vmem, vmem],
        compiler_params=params,
        cost_estimate=cost(1),
        name="part_far",
    )(place, counts, far[0], part_flat, part_0)
    part_1 = swap(part_1, 1)
    sums = pl.pallas_call(
        functools.partial(early_kernel, groups),
        out_shape=shape(2 * SLOTS * FULL, LANES, dtype=jnp.float32),
        in_specs=[pl.BlockSpec(memory_space=pl.ANY)] * 2 + [vmem] * (groups + len(early)),
        out_specs=vmem,
        scratch_shapes=[
            pltpu.VMEM((padded((groups + len(early)) * 2 * comps) * 2 * FULL, LANES), jnp.float32)
        ],
        compiler_params=params,
        cost_estimate=cost(0.001),
        name="early",
    )(part_0, part_2, *sides, *early)
    part_2, part_3 = swap(part_2, half), swap(part_3, half + 1)
    ready = pl.pallas_call(
        ready_kernel,
        out_shape=[
            shape(2, 2, count, full_blocks.shape[2]),
            shape(2, 2, count, LANES),
            shape(len(folds_of(count, FULL)), 4 * LANES, LANES),
        ],
        in_specs=[smem, smem, vmem, pl.BlockSpec(memory_space=pl.ANY)],
        out_specs=[vmem] * 3,
        compiler_params=params,
        cost_estimate=cost(0.001),
        name="ready",
    )(place, counts, far[0], sums)
    full_flat, full_2, full_3 = pl.pallas_call(
        functools.partial(full_kernel, cells),
        out_shape=[full_blocks, full_packed, full_packed],
        in_specs=[smem] + [vmem] * 3 + [pl.BlockSpec(memory_space=pl.ANY)] + [vmem] * (1 + len(late)),
        out_specs=[vmem] * 3,
        scratch_shapes=[
            pltpu.VMEM((padded(len(late) * 2 * comps) * 2 * FULL, LANES), jnp.float32),
            pltpu.VMEM((2 * SLOTS * FULL, LANES), jnp.float32),
        ],
        compiler_params=params,
        cost_estimate=cost(10),
        name="full",
    )(place, *ready, part_0, sums, *late)
    full_2, full_3 = swap(full_2, half), swap(full_3, half + 1)
    full_0, *full_1 = pl.pallas_call(
        functools.partial(near_kernel, FULL, 2),
        out_shape=[full_packed, half_packed, half_packed],
        in_specs=[smem, smem] + [vmem] * 3 + [pl.BlockSpec(memory_space=pl.ANY)] * 2,
        out_specs=[vmem] * 3,
        compiler_params=params,
        cost_estimate=cost(0.5),
        name="full_near",
    )(place, counts, pairs, near_pairs, full_flat, part_2, part_3)
    full_1 = [swap(x, 1) for x in full_1]

    first, tables = pl.pallas_call(
        functools.partial(first_lags_kernel, groups),
        out_shape=[
            shape(2, count, samples, dtype=jnp.float32),
            shape(2, 4 * FULL, 2 * samples),
        ],
        in_specs=[smem] + [vmem] * 8,
        out_specs=[vmem] * 2,
        compiler_params=params,
        cost_estimate=cost(0.001),
        name="first_lags",
    )(place, inverse, part_0, part_2, part_3, full_0, part_1, *full_1)
    return pl.pallas_call(
        lag_kernel,
        out_shape=shape(2, count, samples, dtype=jnp.float32),
        in_specs=[vmem] * 4,
        out_specs=pl.BlockSpec(memory_space=pl.ANY),
        scratch_shapes=[
            pltpu.VMEM((2, count, samples), jnp.float32),
            pltpu.SemaphoreType.DMA((4,)),
        ],
        compiler_params=params,
        cost_estimate=cost(1),
        name="lags",
    )(first, tables, full_2, full_3)


def solution(mesh):
    in_specs = (P(None, "cell", "grp", None), P("grp"), P(None, None, ("grp", "cell")))
    out_specs = P(None, ("grp", "cell"), None)
    return jax.shard_map(
        on_device, mesh=mesh, in_specs=in_specs, out_specs=out_specs, check_vma=False
    )
```

```python
import functools
import math

import jax
import jax.numpy as jnp
import numpy as np
from jax import lax
from jax.experimental import pallas as pl
from jax.experimental.pallas import tpu as pltpu
from jax.sharding import PartitionSpec as P

EPSILON = 1e-06
COSINE = (
    0.9999999999993376,
    -4.934802200431432,
    4.058712123240781,
    -1.3352627346923478,
    0.23533044681677665,
    -0.02580633847975355,
    0.0019285963125396874,
    -0.00010362767792380447,
    3.734915399663344e-06,
)
SLOTS = 32
LANES = 4 * SLOTS
COMPS = 3
NT = (((1,), (1,)), ((), ()))
TN = (((0,), (0,)), ((), ()))
VMEM_LIMIT = 40 * 1024 * 1024

PART = 16
FULL = 24


def inverse_table(samples, stations):
    bins = samples // 2
    turn = np.arange(bins)[:, None] * np.arange(samples)[None, :] % samples
    angle = turn * (2.0 * math.pi / samples)
    weight = np.where(np.arange(bins) == 0, 1.0, 2.0)[:, None] / samples
    weight = weight * math.sqrt(samples / (3.0 * stations))
    real, imag = weight * np.cos(angle), -weight * np.sin(angle)
    runs = [(at, PART) for at in range(0, 2 * PART, PART)]
    runs += [(at, FULL) for at in range(2 * PART, bins, FULL)]
    rows = [part[at : at + run] for at, run in runs for part in (real, imag)]
    return np.concatenate(rows).astype(np.float32)


def forward_rows(bins, samples):
    count = bins.shape[0]
    sample = lax.broadcasted_iota(jnp.int32, (2 * count, samples), 1)
    turn = jnp.concatenate([bins * sample[:count], bins * sample[:count] + samples // 4])
    turn &= samples - 1
    x = jnp.where(turn > samples // 2, turn - samples, turn).astype(jnp.float32) * (2.0 / samples)
    square = x * x
    value = jnp.full(square.shape, COSINE[-1], jnp.float32)
    for factor in COSINE[-2::-1]:
        value = value * square + factor
    return value.astype(jnp.bfloat16)


def place_of(place_ref, groups):
    position = place_ref[0]
    high, inner = position // (2 * groups), position % (2 * groups)
    return high * 2 + inner % 2, inner // 2


def listing_of(pairs_ref, lanes):
    ends = []
    for end in range(2):
        slots = pairs_ref[:, end, :].astype(jnp.float32)
        ends += [slots[:, at : at + lanes] for at in range(0, slots.shape[1], lanes)]
    return jnp.concatenate(ends)


def station_spectra(windows_ref, at, table):
    parts = []
    for comp in range(COMPS):
        low = windows_ref[comp, 0, at]
        high = windows_ref[comp, 1, at]
        parts += [low[:SLOTS], high[SLOTS:], low[SLOTS:], high[:SLOTS]]
    traces = jnp.concatenate(parts)
    energy = jnp.sum(jnp.square(traces.astype(jnp.float32)), axis=1, keepdims=True)
    raw = lax.dot_general(traces, table, NT, preferred_element_type=jnp.float32)
    spectra = (raw * lax.rsqrt(energy + EPSILON)).astype(jnp.bfloat16)
    return [spectra[comp * LANES : (comp + 1) * LANES].T for comp in range(COMPS)]


def own_kernel(place_ref, windows_ref, part_ref, full_ref, table_ref):
    groups, samples = windows_ref.shape[2], windows_ref.shape[4]
    quarter, group = place_of(place_ref, groups)
    bins = lax.broadcasted_iota(jnp.int32, (PART, samples), 0) + (quarter % 2) * PART
    table_ref[: 2 * PART] = forward_rows(bins, samples)
    for far in range(2):
        start = 2 * PART + (quarter ^ (2 * far)) * FULL
        bins = lax.broadcasted_iota(jnp.int32, (FULL, samples), 0) + start
        at = 2 * PART + 2 * FULL * far
        table_ref[at : at + 2 * FULL] = forward_rows(bins, samples)
    table = table_ref[...]
    for mg in range(groups):
        spectra = station_spectra(windows_ref, group ^ mg, table)
        for comp in range(COMPS):
            lanes = spectra[comp]
            part_ref[mg, comp * 2 * PART : (comp + 1) * 2 * PART] = lanes[: 2 * PART]
            for far in range(2):
                at = 2 * PART + 2 * FULL * far
                full_ref[far * groups + mg, comp * 2 * FULL : (comp + 1) * 2 * FULL] = lanes[at : at + 2 * FULL]


def near_spectra_kernel(
    place_ref, own_pairs_ref, near_pairs_ref, table_ref, part_ref, full_ref, windows_ref, *piece_refs
):
    groups = windows_ref.shape[2]
    _, group = place_of(place_ref, groups)
    table = table_ref[...]
    part_rows, full_rows = COMPS * 2 * PART, COMPS * 2 * FULL
    piece_refs[groups][2 * full_rows :] = jnp.concatenate(
        [listing_of(own_pairs_ref, LANES), listing_of(near_pairs_ref, LANES)]
    ).astype(jnp.bfloat16)
    for mg in range(groups):
        spectra = station_spectra(windows_ref, group ^ mg, table)
        side, cross = piece_refs[mg], piece_refs[groups + mg]
        full, start = (side, 2 * part_rows) if mg < groups - 1 else (piece_refs[2 * groups], 0)
        side[:part_rows] = part_ref[mg]
        full[start : start + full_rows] = full_ref[mg]
        cross[:full_rows] = full_ref[groups + mg]
        for comp in range(COMPS):
            lanes = spectra[comp]
            at = part_rows + comp * 2 * PART
            side[at : at + 2 * PART] = lanes[: 2 * PART]
            at = start + full_rows + comp * 2 * FULL
            full[at : at + 2 * FULL] = lanes[2 * PART : 2 * PART + 2 * FULL]
            at = full_rows + comp * 2 * FULL
            cross[at : at + 2 * FULL] = lanes[2 * PART + 2 * FULL :]


def width(bins):
    return 1 << (bins - 1).bit_length()


def packing(count, bins):
    used = 4 * bins
    spare = LANES - used
    if not spare:
        return count, [[(0, 0, 0, used)]]
    runs = used // spare
    rows = count // (runs + 1)
    return rows, [
        [(at * rows, 0, 0, used), (runs * rows, used, at * spare, (at + 1) * spare)] for at in range(runs)
    ]


def packed_rows(count, bins):
    rows, parts = packing(count, bins)
    return rows * len(parts)


def unpack(picked, bins):
    used = 4 * bins
    spare = LANES - used
    if not spare:
        return picked
    runs = used // spare
    rows = picked.shape[0] // runs
    rest = [picked[at * rows : (at + 1) * rows, used:] for at in range(runs)]
    return jnp.concatenate([picked[:, :used], jnp.concatenate(rest, axis=1)])


def sides_of(place_ref, cells, mq):
    quarter, group = place_of(place_ref, cells // 4)
    own = quarter ^ mq
    high, low = own // 2, own % 2
    return high * (cells // 2) + group * 2 + low, high, low, ((high, high), (low, 1 - low))


def hots(place_ref, counts_ref, listed, rows, bins, mq):
    cells = counts_ref.shape[0]
    cell, high, low, _ = sides_of(place_ref, cells, mq)
    count = listed.shape[0] // 2
    runs = LANES // width(bins)
    run_bits, bin_bits = (n.bit_length() - 1 for n in (runs, width(bins)))
    first, second = listed[:count].astype(jnp.int32), listed[count:].astype(jnp.int32)
    far_counts = [counts_ref[cell ^ 1], counts_ref[cell ^ (cells // 2)]]
    odd = lax.broadcasted_iota(jnp.int32, (count, LANES), 0) & 1
    live = (first < counts_ref[cell]) & (second < jnp.where(odd == 1, far_counts[1], far_counts[0]))
    left, right = jnp.where(high == low, first, second), jnp.where(high == low, second, first)
    spot = jnp.where(live, (left >> run_bits) * SLOTS + right, -1)
    turned = (spot * runs + (left & (runs - 1))).T
    lane = lax.broadcasted_iota(jnp.int32, (LANES, LANES), 1)
    run = lane >> bin_bits
    found = []
    for step_round in range(2):
        hot, here = [], []
        for at in range(step_round, count, 2):
            both = jnp.broadcast_to(turned[:, at : at + 1], (LANES, LANES))
            here.append(jnp.where((both & (runs - 1)) == run, 1.0, 0.0).astype(jnp.bfloat16))
            offset = (both >> run_bits) - lane
            hot.append(
                jnp.concatenate(
                    [
                        jnp.where(offset == start, 1.0, 0.0).astype(jnp.bfloat16)
                        for start in range(0, rows, LANES)
                    ],
                    axis=1,
                )
            )
        found.append((jnp.concatenate(hot), jnp.concatenate(here)))
    return found


def folds_of(count, bins):
    return sorted({entry[1:] for entries in packing(count, bins)[1] for entry in entries})


def folds(count, bins):
    spread = lax.broadcasted_iota(jnp.int32, (4 * LANES, LANES), 0)
    kept = lax.broadcasted_iota(jnp.int32, (4 * LANES, LANES), 1)
    bin_of = spread & (width(bins) - 1)
    value = jnp.where(bin_of < bins, (spread >> (LANES.bit_length() - 1)) * bins + bin_of, -1)
    kinds = folds_of(count, bins)
    matrices = []
    for at, least, end in kinds:
        fold = (value >= least) & (value < end) & (kept == value + (at - least))
        matrices.append(jnp.where(fold, 1.0, 0.0).astype(jnp.bfloat16))
    return kinds, matrices


def picks(place_ref, cells, hot, kinds, matrices, flat_ref, bins, mq):
    _, _, _, sides = sides_of(place_ref, cells, mq)
    found = []
    for (rows, lanes), (own, far) in zip(hot, sides):
        wide = jnp.dot(rows, flat_ref[own, far], preferred_element_type=jnp.float32).astype(jnp.bfloat16)
        found += [wide[:, :LANES] * lanes, wide[:, LANES:] * lanes]
    found = jnp.concatenate(found, axis=1)
    held, parts = packing(found.shape[0], bins)
    picked = []
    for entries in parts:
        total = 0.0
        for start, *kind in entries:
            total += jnp.dot(
                found[start : start + held],
                matrices[kinds.index(tuple(kind))],
                preferred_element_type=jnp.float32,
            )
        picked.append(total.astype(jnp.bfloat16))
    return jnp.concatenate(picked)


def pick(place_ref, counts_ref, listed, flat_ref, bins, mq, *picked_refs):
    hot = hots(place_ref, counts_ref, listed, flat_ref.shape[2], bins, mq)
    kinds, matrices = folds(listed.shape[0] // 4 * LANES, bins)
    picked = picks(place_ref, counts_ref.shape[0], hot, kinds, matrices, flat_ref, bins, mq)
    each = picked.shape[0] // len(picked_refs)
    for at, ref in enumerate(picked_refs):
        ref[...] = picked[at * each : (at + 1) * each]


def padded(traces):
    return -(-traces // 16) * 16


def add_cross(pieces, trace_ref, bins, sums_ref, before_ref=None):
    slots, rows = 2 * SLOTS, 2 * bins
    traces = trace_ref.shape[0] // rows
    start = 0
    for piece, at, size in pieces:
        trace_ref[start : start + size] = piece[at : at + size].astype(jnp.float32)
        start += size
    if start < traces * rows:
        trace_ref[start:] = jnp.zeros((traces * rows - start, LANES), jnp.float32)
    lower = lax.broadcasted_iota(jnp.int32, (traces, LANES), 1) < slots
    for k in range(bins):
        real = trace_ref[pl.ds(k, traces, stride=rows), :]
        imag = trace_ref[pl.ds(bins + k, traces, stride=rows), :]
        left = jnp.concatenate([real, imag]).astype(jnp.bfloat16)[:, :slots]
        right = jnp.concatenate(
            [
                jnp.where(lower, pltpu.roll(real, slots, 1), imag),
                jnp.where(lower, pltpu.roll(imag, slots, 1), -real),
            ]
        ).astype(jnp.bfloat16)
        cross = lax.dot_general(left, right, TN, preferred_element_type=jnp.float32)
        if before_ref is not None:
            cross += before_ref[k * slots : (k + 1) * slots]
        sums_ref[k * slots : (k + 1) * slots] = cross


def turn_blocks(cross_ref, bins, flat_ref):
    slots, runs = 2 * SLOTS, LANES // width(bins)
    empty = jnp.zeros((width(bins) - bins, LANES), jnp.float32)
    for own in range(2):
        for at in range(SLOTS // runs):
            block = []
            for i in range(runs):
                block.append(cross_ref[pl.ds(own * SLOTS + at * runs + i, bins, stride=slots), :])
                block += [empty] * (bins < width(bins))
            block = jnp.concatenate(block).astype(jnp.bfloat16).T
            for part in range(2):
                for far in range(2):
                    start = (part * 2 + far) * SLOTS
                    flat_ref[
                        own, far, at * SLOTS : (at + 1) * SLOTS, part * LANES : (part + 1) * LANES
                    ] = block[start : start + SLOTS]


def side_part(ref):
    return (ref, 0, 2 * COMPS * 2 * PART)


def side_full(ref):
    return (ref, 2 * COMPS * 2 * PART, 2 * COMPS * 2 * FULL)


def cross_full(ref):
    return (ref, 0, 2 * COMPS * 2 * FULL)


def part_kernel(*refs):
    piece_refs, (flat_ref, trace_ref, cross_ref) = refs[:-3], refs[-3:]
    add_cross([side_part(ref) for ref in piece_refs], trace_ref, PART, cross_ref)
    turn_blocks(cross_ref, PART, flat_ref)


def far_kernel(bins, place_ref, counts_ref, listed_ref, flat_ref, after_ref, picked_0, picked_1):
    listed = listed_ref[cross_full(listed_ref)[2] :].astype(jnp.float32)
    listing = listed.shape[0] // 2
    pick(place_ref, counts_ref, listed[:listing], flat_ref, bins, 2, picked_0)
    pick(place_ref, counts_ref, listed[listing:], flat_ref, bins, 3, picked_1)


def early_kernel(sides, after_0, after_1, *refs):
    piece_refs, (sums_ref, trace_ref) = refs[:-2], refs[-2:]
    pieces = [side_full(ref) for ref in piece_refs[:sides]] + [cross_full(ref) for ref in piece_refs[sides:]]
    add_cross(pieces, trace_ref, FULL, sums_ref)


def ready_kernel(place_ref, counts_ref, listed_ref, after_ref, hot_ref, here_ref, fold_ref):
    listed = listed_ref[cross_full(listed_ref)[2] :].astype(jnp.float32)
    listing = listed.shape[0] // 2
    for at in range(2):
        part = listed[at * listing : (at + 1) * listing]
        for step_round, (hot, here) in enumerate(
            hots(place_ref, counts_ref, part, hot_ref.shape[3], FULL, 2 + at)
        ):
            hot_ref[at, step_round] = hot
            here_ref[at, step_round] = here
    for at, matrix in enumerate(folds(hot_ref.shape[2], FULL)[1]):
        fold_ref[at] = matrix


def full_kernel(cells, place_ref, hot_ref, here_ref, fold_ref, after_0, before_ref, *refs):
    piece_refs, (flat_ref, picked_0, picked_1, trace_ref, cross_ref) = refs[:-5], refs[-5:]
    add_cross([cross_full(ref) for ref in piece_refs], trace_ref, FULL, cross_ref, before_ref)
    turn_blocks(cross_ref, FULL, flat_ref)
    count = hot_ref.shape[2]
    kinds = folds_of(count, FULL)
    matrices = [fold_ref[at] for at in range(len(kinds))]
    for at, ref in enumerate((picked_0, picked_1)):
        hot = [(hot_ref[at, step_round], here_ref[at, step_round]) for step_round in range(2)]
        ref[...] = picks(place_ref, cells, hot, kinds, matrices, flat_ref, FULL, 2 + at)


def near_kernel(bins, sent, place_ref, counts_ref, own_pairs_ref, near_pairs_ref, flat_ref, *refs):
    picked_0, *picked_1 = refs[-1 - sent :]
    pick(place_ref, counts_ref, listing_of(near_pairs_ref, LANES), flat_ref, bins, 1, *picked_1)
    pick(place_ref, counts_ref, listing_of(own_pairs_ref, LANES), flat_ref, bins, 0, picked_0)


def both_rounds(rows, sign):
    row = lax.broadcasted_iota(jnp.int32, rows.shape, 0)
    rows = rows * jnp.where(row < rows.shape[0] // 2, 1.0, sign)
    empty = jnp.zeros_like(rows)
    return jnp.concatenate(
        [jnp.concatenate([rows, empty], axis=1), jnp.concatenate([empty, rows], axis=1)]
    )


def halves(table):
    high = table.astype(jnp.bfloat16)
    return high, (table - high.astype(jnp.float32)).astype(jnp.bfloat16)


def first_lags_kernel(groups, place_ref, inverse_ref, *refs):
    part_0, part_2, part_3, full_0, part_1, *full_1, lags_ref, table_ref = refs
    samples = inverse_ref.shape[1]
    quarter, _ = place_of(place_ref, groups)
    low = quarter % 2
    sign = jnp.where(quarter // 2 == low, 1.0, -1.0)

    def part_table(which):
        start = pl.multiple_of((low ^ which) * 2 * PART, 2 * PART)
        return halves(both_rounds(inverse_ref[pl.ds(start, 2 * PART), :], sign))

    def full_table(mq):
        start = pl.multiple_of(4 * PART + (quarter ^ mq) * 2 * FULL, 2 * FULL)
        return halves(both_rounds(inverse_ref[pl.ds(start, 2 * FULL), :], sign))

    near, other = part_table(0), part_table(1)
    lags = 0.0
    full_1 = jnp.concatenate([ref[...] for ref in full_1])
    for picked, bins, table in (
        (part_0[...], PART, near),
        (part_2[...], PART, near),
        (part_1[...], PART, other),
        (part_3[...], PART, other),
        (full_0[...], FULL, full_table(0)),
        (full_1, FULL, full_table(1)),
    ):
        picked = unpack(picked, bins)
        for half in table:
            lags += jnp.dot(picked, half, preferred_element_type=jnp.float32)
    for step_round in range(2):
        lags_ref[step_round] = lags[:, step_round * samples : (step_round + 1) * samples]
    for at in range(2):
        table_ref[at] = full_table(2 + at)[0]


def lag_kernel(first_ref, table_ref, *refs):
    picked_refs, (lags_ref, held_ref, sems) = refs[:-3], refs[-3:]
    samples = lags_ref.shape[2]
    runs = sems.shape[0]
    held = held_ref.shape[1] // runs
    picked = [unpack(ref[...], FULL) for ref in picked_refs]
    copies = []
    for run in range(runs):
        rows = slice(run * held, (run + 1) * held)
        more = 0.0
        for at, values in enumerate(picked):
            more += jnp.dot(values[rows], table_ref[at], preferred_element_type=jnp.float32)
        for step_round in range(2):
            held_ref[step_round, rows] = (
                first_ref[step_round, rows] + more[:, step_round * samples : (step_round + 1) * samples]
            )
        copies.append(
            pltpu.make_async_copy(held_ref.at[:, rows], lags_ref.at[:, rows], sems.at[run])
        )
        copies[-1].start()
    for copy in copies:
        copy.wait()


def on_device(windows, counts, pairs):
    comps, _, events, samples = windows.shape
    cells = lax.axis_size("cell")
    half, groups = cells // 2, cells // 4
    count = pairs.shape[2]
    inverse = jnp.asarray(inverse_table(samples, cells))
    place = lax.axis_index("cell").astype(jnp.int32).reshape(1)

    def swap(x, mask):
        return lax.ppermute(x, "cell", [(i, i ^ mask) for i in range(cells)])

    def shape(*dims, dtype=jnp.bfloat16):
        return jax.ShapeDtypeStruct(dims, dtype)

    vmem = pl.BlockSpec(memory_space=pltpu.VMEM)
    smem = pl.BlockSpec(memory_space=pltpu.SMEM)
    params = pltpu.CompilerParams(vmem_limit_bytes=VMEM_LIMIT)

    def cost(microseconds):
        return pl.CostEstimate(
            flops=int(microseconds * 1e9), bytes_accessed=2**20, transcendentals=0
        )

    windows = windows.reshape(comps, 2, groups, 2 * SLOTS, samples)
    near_windows, near_pairs = swap(windows, 1), swap(pairs, 1)
    part_rows, full_rows = comps * 2 * PART, comps * 2 * FULL
    part_spectra, full_spectra, table = pl.pallas_call(
        own_kernel,
        out_shape=[
            shape(groups, part_rows, LANES),
            shape(2 * groups, full_rows, LANES),
            shape(2 * PART + 4 * FULL, samples),
        ],
        in_specs=[smem, vmem],
        out_specs=[vmem] * 3,
        compiler_params=params,
        cost_estimate=cost(1),
        name="own_spectra",
    )(place, windows)
    listing = 2 * pairs.size // LANES
    pieces = pl.pallas_call(
        near_spectra_kernel,
        out_shape=[shape(2 * (part_rows + full_rows), LANES)] * (groups - 1)
        + [shape(2 * part_rows, LANES)]
        + [shape(2 * full_rows + listing * (mg == 0), LANES) for mg in range(groups)]
        + [shape(2 * full_rows, LANES)],
        in_specs=[smem] + [vmem] * 6,
        out_specs=[vmem] * (2 * groups + 1),
        compiler_params=params,
        cost_estimate=cost(1),
        name="near_spectra",
    )(place, pairs, near_pairs, table, part_spectra, full_spectra, near_windows)
    arrived = [pieces[0]] + [swap(pieces[m], 2 * m) for m in range(1, 2 * groups)]
    sides, far = arrived[:groups], arrived[groups:]
    side_rest = swap(pieces[2 * groups], 2 * (groups - 1))

    early, late = far[: groups - 2], far[groups - 2 :]
    part_packed = shape(packed_rows(count, PART), LANES)
    full_packed = shape(packed_rows(count, FULL), LANES)
    half_packed = shape(packed_rows(count, FULL) // 2, LANES)
    part_blocks = shape(2, 2, SLOTS * SLOTS * width(PART) // LANES, 2 * LANES)
    full_blocks = shape(2, 2, SLOTS * SLOTS * width(FULL) // LANES, 2 * LANES)
    part_flat = pl.pallas_call(
        part_kernel,
        out_shape=part_blocks,
        in_specs=[vmem] * groups,
        out_specs=vmem,
        scratch_shapes=[
            pltpu.VMEM((padded(groups * 2 * comps) * 2 * PART, LANES), jnp.float32),
            pltpu.VMEM((2 * SLOTS * PART, LANES), jnp.float32),
        ],
        compiler_params=params,
        cost_estimate=cost(0.001),
        name="part",
    )(*sides)
    part_0, part_1 = pl.pallas_call(
        functools.partial(near_kernel, PART, 1),
        out_shape=[part_packed, part_packed],
        in_specs=[smem, smem] + [vmem] * 3,
        out_specs=[vmem] * 2,
        compiler_params=params,
        cost_estimate=cost(0.001),
        name="part_near",
    )(place, counts, pairs, near_pairs, part_flat)
    part_2, part_3 = pl.pallas_call(
        functools.partial(far_kernel, PART),
        out_shape=[part_packed, part_packed],
        in_specs=[smem, smem, vmem, vmem, pl.BlockSpec(memory_space=pl.ANY)],
        out_specs=[vmem, vmem],
        compiler_params=params,
        cost_estimate=cost(1),
        name="part_far",
    )(place, counts, far[0], part_flat, part_0)
    part_1 = swap(part_1, 1)
    sums = pl.pallas_call(
        functools.partial(early_kernel, groups - 1),
        out_shape=shape(2 * SLOTS * FULL, LANES, dtype=jnp.float32),
        in_specs=[pl.BlockSpec(memory_space=pl.ANY)] * 2 + [vmem] * (groups + len(early)),
        out_specs=vmem,
        scratch_shapes=[
            pltpu.VMEM((padded((groups + len(early)) * 2 * comps) * 2 * FULL, LANES), jnp.float32)
        ],
        compiler_params=params,
        cost_estimate=cost(0.001),
        name="early",
    )(part_0, part_2, *sides[:-1], *early, side_rest)
    part_2, part_3 = swap(part_2, half), swap(part_3, half + 1)
    ready = pl.pallas_call(
        ready_kernel,
        out_shape=[
            shape(2, 2, count, full_blocks.shape[2]),
            shape(2, 2, count, LANES),
            shape(len(folds_of(count, FULL)), 4 * LANES, LANES),
        ],
        in_specs=[smem, smem, vmem, pl.BlockSpec(memory_space=pl.ANY)],
        out_specs=[vmem] * 3,
        compiler_params=params,
        cost_estimate=cost(0.001),
        name="ready",
    )(place, counts, far[0], sums)
    full_flat, full_2, full_3 = pl.pallas_call(
        functools.partial(full_kernel, cells),
        out_shape=[full_blocks, full_packed, full_packed],
        in_specs=[smem] + [vmem] * 3 + [pl.BlockSpec(memory_space=pl.ANY)] + [vmem] * (1 + len(late)),
        out_specs=[vmem] * 3,
        scratch_shapes=[
            pltpu.VMEM((padded(len(late) * 2 * comps) * 2 * FULL, LANES), jnp.float32),
            pltpu.VMEM((2 * SLOTS * FULL, LANES), jnp.float32),
        ],
        compiler_params=params,
        cost_estimate=cost(10),
        name="full",
    )(place, *ready, part_0, sums, *late)
    full_2, full_3 = swap(full_2, half), swap(full_3, half + 1)
    full_0, *full_1 = pl.pallas_call(
        functools.partial(near_kernel, FULL, 2),
        out_shape=[full_packed, half_packed, half_packed],
        in_specs=[smem, smem] + [vmem] * 3 + [pl.BlockSpec(memory_space=pl.ANY)] * 2,
        out_specs=[vmem] * 3,
        compiler_params=params,
        cost_estimate=cost(0.5),
        name="full_near",
    )(place, counts, pairs, near_pairs, full_flat, part_2, part_3)
    full_1 = [swap(x, 1) for x in full_1]

    first, tables = pl.pallas_call(
        functools.partial(first_lags_kernel, groups),
        out_shape=[
            shape(2, count, samples, dtype=jnp.float32),
            shape(2, 4 * FULL, 2 * samples),
        ],
        in_specs=[smem] + [vmem] * 8,
        out_specs=[vmem] * 2,
        compiler_params=params,
        cost_estimate=cost(0.001),
        name="first_lags",
    )(place, inverse, part_0, part_2, part_3, full_0, part_1, *full_1)
    return pl.pallas_call(
        lag_kernel,
        out_shape=shape(2, count, samples, dtype=jnp.float32),
        in_specs=[vmem] * 4,
        out_specs=pl.BlockSpec(memory_space=pl.ANY),
        scratch_shapes=[
            pltpu.VMEM((2, count, samples), jnp.float32),
            pltpu.SemaphoreType.DMA((4,)),
        ],
        compiler_params=params,
        cost_estimate=cost(1),
        name="lags",
    )(first, tables, full_2, full_3)


def solution(mesh):
    in_specs = (P(None, "cell", "grp", None), P("grp"), P(None, None, ("grp", "cell")))
    out_specs = P(None, ("grp", "cell"), None)
    return jax.shard_map(
        on_device, mesh=mesh, in_specs=in_specs, out_specs=out_specs, check_vma=False
    )
```

```python
import functools
import math

import jax
import jax.numpy as jnp
import numpy as np
from jax import lax
from jax.experimental import pallas as pl
from jax.experimental.pallas import tpu as pltpu
from jax.sharding import PartitionSpec as P

EPSILON = 1e-06
COSINE = (
    0.9999999999993376,
    -4.934802200431432,
    4.058712123240781,
    -1.3352627346923478,
    0.23533044681677665,
    -0.02580633847975355,
    0.0019285963125396874,
    -0.00010362767792380447,
    3.734915399663344e-06,
)
SLOTS = 32
LANES = 4 * SLOTS
COMPS = 3
NT = (((1,), (1,)), ((), ()))
TN = (((0,), (0,)), ((), ()))
VMEM_LIMIT = 40 * 1024 * 1024

PART = 24
FULL = 20


def inverse_table(samples, stations):
    bins = samples // 2
    turn = np.arange(bins)[:, None] * np.arange(samples)[None, :] % samples
    angle = turn * (2.0 * math.pi / samples)
    weight = np.where(np.arange(bins) == 0, 1.0, 2.0)[:, None] / samples
    weight = weight * math.sqrt(samples / (3.0 * stations))
    real, imag = weight * np.cos(angle), -weight * np.sin(angle)
    runs = [(at, PART) for at in range(0, 2 * PART, PART)]
    runs += [(at, FULL) for at in range(2 * PART, bins, FULL)]
    rows = [part[at : at + run] for at, run in runs for part in (real, imag)]
    return np.concatenate(rows).astype(np.float32)


def forward_rows(start, count, samples):
    row = lax.broadcasted_iota(jnp.int32, (2 * count, samples), 0)
    sample = lax.broadcasted_iota(jnp.int32, (2 * count, samples), 1)
    imag = row >= count
    turn = (row + start - jnp.where(imag, count, 0)) * sample + jnp.where(imag, samples // 4, 0)
    turn &= samples - 1
    x = jnp.where(turn > samples // 2, turn - samples, turn).astype(jnp.float32) * (2.0 / samples)
    square = x * x
    value = jnp.full(square.shape, COSINE[-1], jnp.float32)
    for factor in COSINE[-2::-1]:
        value = value * square + factor
    return value


def place_of(place_ref, groups):
    position = place_ref[0]
    high, inner = position // (2 * groups), position % (2 * groups)
    return high * 2 + inner % 2, inner // 2


def listing_of(pairs_ref, lanes):
    ends = []
    for end in range(2):
        slots = pairs_ref[:, end, :].astype(jnp.float32)
        ends += [slots[:, at : at + lanes] for at in range(0, slots.shape[1], lanes)]
    return jnp.concatenate(ends)


def station_spectra(windows_ref, at, table):
    parts = []
    for comp in range(COMPS):
        low = windows_ref[comp, 0, at]
        high = windows_ref[comp, 1, at]
        parts += [low[:SLOTS], high[SLOTS:], low[SLOTS:], high[:SLOTS]]
    traces = jnp.concatenate(parts)
    energy = jnp.sum(jnp.square(traces.astype(jnp.float32)), axis=1, keepdims=True)
    raw = lax.dot_general(traces, table, NT, preferred_element_type=jnp.float32)
    spectra = raw * lax.rsqrt(energy + EPSILON)
    return [spectra[comp * LANES : (comp + 1) * LANES].T for comp in range(COMPS)]


def rows_of(spectra, start, count):
    return jnp.concatenate([lanes[start : start + count] for lanes in spectra])


def own_kernel(place_ref, windows_ref, part_ref, full_ref, table_ref):
    groups, samples = windows_ref.shape[2], windows_ref.shape[4]
    quarter, group = place_of(place_ref, groups)
    table = [forward_rows((quarter % 2) * PART, PART, samples)]
    for far in range(2):
        table.append(forward_rows(2 * PART + (quarter ^ (2 * far)) * FULL, FULL, samples))
    table = jnp.concatenate(table).astype(jnp.bfloat16)
    table_ref[...] = table
    held = full_ref.shape[1] - COMPS * 2 * FULL
    for mg in range(groups):
        spectra = station_spectra(windows_ref, group ^ mg, table)
        part_ref[mg] = rows_of(spectra, 0, 2 * PART).astype(jnp.bfloat16)
        for far in range(2):
            rows = rows_of(spectra, 2 * PART + 2 * FULL * far, 2 * FULL)
            if held:
                rows = jnp.concatenate([rows, jnp.zeros((held, LANES), jnp.float32)])
            full_ref[far * groups + mg] = rows.astype(jnp.bfloat16)


def near_spectra_kernel(
    place_ref, own_pairs_ref, near_pairs_ref, table_ref, part_ref, full_ref, windows_ref, *piece_refs
):
    groups = windows_ref.shape[2]
    _, group = place_of(place_ref, groups)
    table = table_ref[...]
    part_rows, full_rows = COMPS * 2 * PART, COMPS * 2 * FULL
    piece_refs[groups][2 * full_rows :] = jnp.concatenate(
        [listing_of(own_pairs_ref, LANES), listing_of(near_pairs_ref, LANES)]
    ).astype(jnp.bfloat16)
    for mg in range(groups):
        spectra = station_spectra(windows_ref, group ^ mg, table)
        side = piece_refs[mg]
        side[:part_rows] = part_ref[mg]
        side[part_rows : 2 * part_rows] = rows_of(spectra, 0, 2 * PART).astype(jnp.bfloat16)
        for far, (piece, start) in enumerate(((side, 2 * part_rows), (piece_refs[groups + mg], 0))):
            own = full_ref[far * groups + mg].astype(jnp.float32)[:full_rows]
            near = rows_of(spectra, 2 * PART + 2 * FULL * far, 2 * FULL)
            piece[start : start + 2 * full_rows] = jnp.concatenate([own, near]).astype(jnp.bfloat16)


def width(bins):
    return 1 << (bins - 1).bit_length()


def packing(count, bins):
    used = 4 * bins
    spare = LANES - used
    runs, rest = used // math.gcd(used, LANES), spare // math.gcd(used, LANES)
    rows = count // (runs + rest)
    parts = []
    for run in range(runs):
        parts.append([(run * rows, 0, 0, used)])
        for extra in range(rest):
            start, end = max(run * spare, extra * used), min((run + 1) * spare, (extra + 1) * used)
            if start < end:
                lane = used + start - run * spare
                parts[-1].append(((runs + extra) * rows, lane, start - extra * used, end - extra * used))
    return rows, parts


def packed_rows(count, bins):
    rows, parts = packing(count, bins)
    return rows * len(parts)


def unpack(picked, bins):
    used = 4 * bins
    runs, rest = used // math.gcd(used, LANES), (LANES - used) // math.gcd(used, LANES)
    rows = picked.shape[0] // runs
    if not rest:
        return picked
    spare = jnp.concatenate([picked[run * rows : (run + 1) * rows, used:] for run in range(runs)], axis=1)
    return jnp.concatenate(
        [picked[:, :used]] + [spare[:, extra * used : (extra + 1) * used] for extra in range(rest)]
    )


def sides_of(place_ref, cells, mq):
    quarter, group = place_of(place_ref, cells // 4)
    own = quarter ^ mq
    high, low = own // 2, own % 2
    return high * (cells // 2) + group * 2 + low, high, low, ((high, high), (low, 1 - low))


def hots(place_ref, counts_ref, listed, rows, bins, mq):
    cells = counts_ref.shape[0]
    cell, high, low, _ = sides_of(place_ref, cells, mq)
    count = listed.shape[0] // 2
    runs = LANES // width(bins)
    run_bits, bin_bits = (n.bit_length() - 1 for n in (runs, width(bins)))
    first, second = listed[:count].astype(jnp.int32), listed[count:].astype(jnp.int32)
    far_counts = [counts_ref[cell ^ 1], counts_ref[cell ^ (cells // 2)]]
    odd = lax.broadcasted_iota(jnp.int32, (count, LANES), 0) & 1
    live = (first < counts_ref[cell]) & (second < jnp.where(odd == 1, far_counts[1], far_counts[0]))
    left, right = jnp.where(high == low, first, second), jnp.where(high == low, second, first)
    spot = jnp.where(live, (left >> run_bits) * SLOTS + right, -1)
    turned = (spot * runs + (left & (runs - 1))).T
    lane = lax.broadcasted_iota(jnp.int32, (LANES, LANES), 1)
    run = lane >> bin_bits
    found = []
    for step_round in range(2):
        hot, here = [], []
        for at in range(step_round, count, 2):
            both = jnp.broadcast_to(turned[:, at : at + 1], (LANES, LANES))
            here.append(jnp.where((both & (runs - 1)) == run, 1.0, 0.0).astype(jnp.bfloat16))
            offset = (both >> run_bits) - lane
            hot.append(
                jnp.concatenate(
                    [
                        jnp.where(offset == start, 1.0, 0.0).astype(jnp.bfloat16)
                        for start in range(0, rows, LANES)
                    ],
                    axis=1,
                )
            )
        found.append((jnp.concatenate(hot), jnp.concatenate(here)))
    return found


def folds_of(count, bins):
    return sorted({entry[1:] for entries in packing(count, bins)[1] for entry in entries})


def folds(count, bins):
    spread = lax.broadcasted_iota(jnp.int32, (4 * LANES, LANES), 0)
    kept = lax.broadcasted_iota(jnp.int32, (4 * LANES, LANES), 1)
    bin_of = spread & (width(bins) - 1)
    value = jnp.where(bin_of < bins, (spread >> (LANES.bit_length() - 1)) * bins + bin_of, -1)
    kinds = folds_of(count, bins)
    matrices = []
    for at, least, end in kinds:
        fold = (value >= least) & (value < end) & (kept == value + (at - least))
        matrices.append(jnp.where(fold, 1.0, 0.0).astype(jnp.bfloat16))
    return kinds, matrices


def picks(place_ref, cells, hot, kinds, matrices, flat_ref, bins, mq):
    _, _, _, sides = sides_of(place_ref, cells, mq)
    found = []
    for (rows, lanes), (own, far) in zip(hot, sides):
        wide = jnp.dot(rows, flat_ref[own, far], preferred_element_type=jnp.float32).astype(jnp.bfloat16)
        found += [wide[:, :LANES] * lanes, wide[:, LANES:] * lanes]
    found = jnp.concatenate(found, axis=1)
    held, parts = packing(found.shape[0], bins)
    picked = []
    for entries in parts:
        total = 0.0
        for start, *kind in entries:
            total += jnp.dot(
                found[start : start + held],
                matrices[kinds.index(tuple(kind))],
                preferred_element_type=jnp.float32,
            )
        picked.append(total.astype(jnp.bfloat16))
    return jnp.concatenate(picked)


def pick(place_ref, counts_ref, listed, flat_ref, bins, mq, *picked_refs):
    hot = hots(place_ref, counts_ref, listed, flat_ref.shape[2], bins, mq)
    kinds, matrices = folds(listed.shape[0] // 4 * LANES, bins)
    picked = picks(place_ref, counts_ref.shape[0], hot, kinds, matrices, flat_ref, bins, mq)
    each = picked.shape[0] // len(picked_refs)
    for at, ref in enumerate(picked_refs):
        ref[...] = picked[at * each : (at + 1) * each]


def whole(count, tile):
    return -(-count // tile) * tile


def padded(traces):
    return whole(traces, 16)


def add_cross(pieces, trace_ref, bins, sums_ref, before_ref=None):
    slots, rows = 2 * SLOTS, 2 * bins
    traces = trace_ref.shape[0] // rows
    start = 0
    for piece, at, size in pieces:
        trace_ref[start : start + size] = piece[at : at + size].astype(jnp.float32)
        start += size
    if start < traces * rows:
        trace_ref[start:] = jnp.zeros((traces * rows - start, LANES), jnp.float32)
    lower = lax.broadcasted_iota(jnp.int32, (traces, LANES), 1) < slots
    for k in range(bins):
        real = trace_ref[pl.ds(k, traces, stride=rows), :]
        imag = trace_ref[pl.ds(bins + k, traces, stride=rows), :]
        left = jnp.concatenate([real, imag]).astype(jnp.bfloat16)[:, :slots]
        right = jnp.concatenate(
            [
                jnp.where(lower, pltpu.roll(real, slots, 1), imag),
                jnp.where(lower, pltpu.roll(imag, slots, 1), -real),
            ]
        ).astype(jnp.bfloat16)
        cross = lax.dot_general(left, right, TN, preferred_element_type=jnp.float32)
        if before_ref is not None:
            cross += before_ref[k * slots : (k + 1) * slots]
        sums_ref[k * slots : (k + 1) * slots] = cross


def turn_blocks(cross_ref, bins, flat_ref):
    slots, runs = 2 * SLOTS, LANES // width(bins)
    held = cross_ref.shape[0] // slots
    if held > bins:
        cross_ref[bins * slots :] = jnp.zeros(((held - bins) * slots, LANES), jnp.float32)
    empty = jnp.zeros((width(bins) - held, LANES), jnp.float32)
    for own in range(2):
        for at in range(SLOTS // runs):
            block = []
            for i in range(runs):
                block.append(cross_ref[pl.ds(own * SLOTS + at * runs + i, held, stride=slots), :])
                block += [empty] * (held < width(bins))
            block = jnp.concatenate(block).astype(jnp.bfloat16).T
            for part in range(2):
                for far in range(2):
                    start = (part * 2 + far) * SLOTS
                    flat_ref[
                        own, far, at * SLOTS : (at + 1) * SLOTS, part * LANES : (part + 1) * LANES
                    ] = block[start : start + SLOTS]


def side_part(ref):
    return (ref, 0, 2 * COMPS * 2 * PART)


def side_full(ref):
    return (ref, 2 * COMPS * 2 * PART, 2 * COMPS * 2 * FULL)


def cross_full(ref):
    return (ref, 0, 2 * COMPS * 2 * FULL)


def part_kernel(*refs):
    piece_refs, (flat_ref, trace_ref, cross_ref) = refs[:-3], refs[-3:]
    add_cross([side_part(ref) for ref in piece_refs], trace_ref, PART, cross_ref)
    turn_blocks(cross_ref, PART, flat_ref)


def far_kernel(bins, place_ref, counts_ref, listed_ref, flat_ref, after_ref, picked_0, picked_1):
    listed = listed_ref[cross_full(listed_ref)[2] :].astype(jnp.float32)
    listing = listed.shape[0] // 2
    pick(place_ref, counts_ref, listed[:listing], flat_ref, bins, 2, picked_0)
    pick(place_ref, counts_ref, listed[listing:], flat_ref, bins, 3, picked_1)


def early_kernel(sides, after_0, after_1, *refs):
    piece_refs, (sums_ref, trace_ref) = refs[:-2], refs[-2:]
    pieces = [side_full(ref) for ref in piece_refs[:sides]] + [cross_full(ref) for ref in piece_refs[sides:]]
    add_cross(pieces, trace_ref, FULL, sums_ref)


def ready_kernel(place_ref, counts_ref, listed_ref, after_ref, hot_ref, here_ref, fold_ref):
    listed = listed_ref[cross_full(listed_ref)[2] :].astype(jnp.float32)
    listing = listed.shape[0] // 2
    for at in range(2):
        part = listed[at * listing : (at + 1) * listing]
        for step_round, (hot, here) in enumerate(
            hots(place_ref, counts_ref, part, hot_ref.shape[3], FULL, 2 + at)
        ):
            hot_ref[at, step_round] = hot
            here_ref[at, step_round] = here
    for at, matrix in enumerate(folds(hot_ref.shape[2], FULL)[1]):
        fold_ref[at] = matrix


def full_kernel(cells, place_ref, hot_ref, here_ref, fold_ref, after_0, before_ref, *refs):
    piece_refs, (flat_ref, picked_0, picked_1, trace_ref, cross_ref) = refs[:-5], refs[-5:]
    add_cross([cross_full(ref) for ref in piece_refs], trace_ref, FULL, cross_ref, before_ref)
    turn_blocks(cross_ref, FULL, flat_ref)
    count = hot_ref.shape[2]
    kinds = folds_of(count, FULL)
    matrices = [fold_ref[at] for at in range(len(kinds))]
    for at, ref in enumerate((picked_0, picked_1)):
        hot = [(hot_ref[at, step_round], here_ref[at, step_round]) for step_round in range(2)]
        ref[...] = picks(place_ref, cells, hot, kinds, matrices, flat_ref, FULL, 2 + at)


def near_kernel(bins, sent, place_ref, counts_ref, own_pairs_ref, near_pairs_ref, flat_ref, *refs):
    picked_0, *picked_1 = refs[-1 - sent :]
    pick(place_ref, counts_ref, listing_of(near_pairs_ref, LANES), flat_ref, bins, 1, *picked_1)
    pick(place_ref, counts_ref, listing_of(own_pairs_ref, LANES), flat_ref, bins, 0, picked_0)


def both_rounds(rows, sign):
    row = lax.broadcasted_iota(jnp.int32, rows.shape, 0)
    rows = rows * jnp.where(row < rows.shape[0] // 2, 1.0, sign)
    empty = jnp.zeros_like(rows)
    return jnp.concatenate(
        [jnp.concatenate([rows, empty], axis=1), jnp.concatenate([empty, rows], axis=1)]
    )


def halves(table):
    high = table.astype(jnp.bfloat16)
    return high, (table - high.astype(jnp.float32)).astype(jnp.bfloat16)


def first_lags_kernel(groups, place_ref, inverse_ref, *refs):
    part_0, part_2, part_3, full_0, part_1, *full_1, lags_ref, table_ref = refs
    samples = inverse_ref.shape[1]
    quarter, _ = place_of(place_ref, groups)
    low = quarter % 2
    sign = jnp.where(quarter // 2 == low, 1.0, -1.0)

    def part_table(which):
        start = pl.multiple_of((low ^ which) * 2 * PART, 2 * PART)
        return halves(both_rounds(inverse_ref[pl.ds(start, 2 * PART), :], sign))

    def full_table(mq):
        start = pl.multiple_of(4 * PART + (quarter ^ mq) * 2 * FULL, 2 * FULL)
        return halves(both_rounds(inverse_ref[pl.ds(start, 2 * FULL), :], sign))

    near, other = part_table(0), part_table(1)
    lags = 0.0
    full_1 = jnp.concatenate([ref[...] for ref in full_1])
    for picked, bins, table in (
        (part_0[...], PART, near),
        (part_2[...], PART, near),
        (part_1[...], PART, other),
        (part_3[...], PART, other),
        (full_0[...], FULL, full_table(0)),
        (full_1, FULL, full_table(1)),
    ):
        picked = unpack(picked, bins)
        for half in table:
            lags += jnp.dot(picked, half, preferred_element_type=jnp.float32)
    for step_round in range(2):
        lags_ref[step_round] = lags[:, step_round * samples : (step_round + 1) * samples]
    for at in range(2):
        table_ref[at] = full_table(2 + at)[0]


def lag_kernel(first_ref, table_ref, *refs):
    picked_refs, (lags_ref, held_ref, sems) = refs[:-3], refs[-3:]
    samples = lags_ref.shape[2]
    runs = sems.shape[0]
    held = held_ref.shape[1] // runs
    picked = [unpack(ref[...], FULL) for ref in picked_refs]
    copies = []
    for run in range(runs):
        rows = slice(run * held, (run + 1) * held)
        more = 0.0
        for at, values in enumerate(picked):
            more += jnp.dot(values[rows], table_ref[at], preferred_element_type=jnp.float32)
        for step_round in range(2):
            held_ref[step_round, rows] = (
                first_ref[step_round, rows] + more[:, step_round * samples : (step_round + 1) * samples]
            )
        copies.append(
            pltpu.make_async_copy(held_ref.at[:, rows], lags_ref.at[:, rows], sems.at[run])
        )
        copies[-1].start()
    for copy in copies:
        copy.wait()


def on_device(windows, counts, pairs):
    comps, _, events, samples = windows.shape
    cells = lax.axis_size("cell")
    half, groups = cells // 2, cells // 4
    count = pairs.shape[2]
    inverse = jnp.asarray(inverse_table(samples, cells))
    place = lax.axis_index("cell").astype(jnp.int32).reshape(1)

    def swap(x, mask):
        return lax.ppermute(x, "cell", [(i, i ^ mask) for i in range(cells)])

    def shape(*dims, dtype=jnp.bfloat16):
        return jax.ShapeDtypeStruct(dims, dtype)

    vmem = pl.BlockSpec(memory_space=pltpu.VMEM)
    smem = pl.BlockSpec(memory_space=pltpu.SMEM)
    params = pltpu.CompilerParams(vmem_limit_bytes=VMEM_LIMIT)

    def cost(microseconds):
        return pl.CostEstimate(
            flops=int(microseconds * 1e9), bytes_accessed=2**20, transcendentals=0
        )

    windows = windows.reshape(comps, 2, groups, 2 * SLOTS, samples)
    near_windows, near_pairs = swap(windows, 1), swap(pairs, 1)
    part_rows, full_rows = comps * 2 * PART, comps * 2 * FULL
    part_spectra, full_spectra, table = pl.pallas_call(
        own_kernel,
        out_shape=[
            shape(groups, part_rows, LANES),
            shape(2 * groups, whole(full_rows, 16), LANES),
            shape(2 * PART + 4 * FULL, samples),
        ],
        in_specs=[smem, vmem],
        out_specs=[vmem] * 3,
        compiler_params=params,
        cost_estimate=cost(1),
        name="own_spectra",
    )(place, windows)
    listing = 2 * pairs.size // LANES
    pieces = pl.pallas_call(
        near_spectra_kernel,
        out_shape=[shape(2 * (part_rows + full_rows), LANES)] * groups
        + [shape(2 * full_rows + listing * (mg == 0), LANES) for mg in range(groups)],
        in_specs=[smem] + [vmem] * 6,
        out_specs=[vmem] * (2 * groups),
        compiler_params=params,
        cost_estimate=cost(1),
        name="near_spectra",
    )(place, pairs, near_pairs, table, part_spectra, full_spectra, near_windows)
    arrived = [pieces[0]] + [swap(pieces[m], 2 * m) for m in range(1, 2 * groups)]
    sides, far = arrived[:groups], arrived[groups:]

    early, late = far[: groups - 2], far[groups - 2 :]
    part_packed = shape(packed_rows(count, PART), LANES)
    full_packed = shape(packed_rows(count, FULL), LANES)
    half_packed = shape(packed_rows(count, FULL) // 2, LANES)
    part_blocks = shape(2, 2, SLOTS * SLOTS * width(PART) // LANES, 2 * LANES)
    full_blocks = shape(2, 2, SLOTS * SLOTS * width(FULL) // LANES, 2 * LANES)
    part_flat = pl.pallas_call(
        part_kernel,
        out_shape=part_blocks,
        in_specs=[vmem] * groups,
        out_specs=vmem,
        scratch_shapes=[
            pltpu.VMEM((padded(groups * 2 * comps) * 2 * PART, LANES), jnp.float32),
            pltpu.VMEM((2 * SLOTS * whole(PART, 8), LANES), jnp.float32),
        ],
        compiler_params=params,
        cost_estimate=cost(0.001),
        name="part",
    )(*sides)
    part_0, part_1 = pl.pallas_call(
        functools.partial(near_kernel, PART, 1),
        out_shape=[part_packed, part_packed],
        in_specs=[smem, smem] + [vmem] * 3,
        out_specs=[vmem] * 2,
        compiler_params=params,
        cost_estimate=cost(0.001),
        name="part_near",
    )(place, counts, pairs, near_pairs, part_flat)
    part_2, part_3 = pl.pallas_call(
        functools.partial(far_kernel, PART),
        out_shape=[part_packed, part_packed],
        in_specs=[smem, smem, vmem, vmem, pl.BlockSpec(memory_space=pl.ANY)],
        out_specs=[vmem, vmem],
        compiler_params=params,
        cost_estimate=cost(1),
        name="part_far",
    )(place, counts, far[0], part_flat, part_0)
    part_1 = swap(part_1, 1)
    sums = pl.pallas_call(
        functools.partial(early_kernel, groups),
        out_shape=shape(2 * SLOTS * FULL, LANES, dtype=jnp.float32),
        in_specs=[pl.BlockSpec(memory_space=pl.ANY)] * 2 + [vmem] * (groups + len(early)),
        out_specs=vmem,
        scratch_shapes=[
            pltpu.VMEM((padded((groups + len(early)) * 2 * comps) * 2 * FULL, LANES), jnp.float32)
        ],
        compiler_params=params,
        cost_estimate=cost(0.001),
        name="early",
    )(part_0, part_2, *sides, *early)
    part_2, part_3 = swap(part_2, half), swap(part_3, half + 1)
    ready = pl.pallas_call(
        ready_kernel,
        out_shape=[
            shape(2, 2, count, full_blocks.shape[2]),
            shape(2, 2, count, LANES),
            shape(len(folds_of(count, FULL)), 4 * LANES, LANES),
        ],
        in_specs=[smem, smem, vmem, pl.BlockSpec(memory_space=pl.ANY)],
        out_specs=[vmem] * 3,
        compiler_params=params,
        cost_estimate=cost(0.001),
        name="ready",
    )(place, counts, far[0], sums)
    full_flat, full_2, full_3 = pl.pallas_call(
        functools.partial(full_kernel, cells),
        out_shape=[full_blocks, full_packed, full_packed],
        in_specs=[smem] + [vmem] * 3 + [pl.BlockSpec(memory_space=pl.ANY)] + [vmem] * (1 + len(late)),
        out_specs=[vmem] * 3,
        scratch_shapes=[
            pltpu.VMEM((padded(len(late) * 2 * comps) * 2 * FULL, LANES), jnp.float32),
            pltpu.VMEM((2 * SLOTS * whole(FULL, 8), LANES), jnp.float32),
        ],
        compiler_params=params,
        cost_estimate=cost(10),
        name="full",
    )(place, *ready, part_0, sums, *late)
    full_2, full_3 = swap(full_2, half), swap(full_3, half + 1)
    full_0, *full_1 = pl.pallas_call(
        functools.partial(near_kernel, FULL, 2),
        out_shape=[full_packed, half_packed, half_packed],
        in_specs=[smem, smem] + [vmem] * 3 + [pl.BlockSpec(memory_space=pl.ANY)] * 2,
        out_specs=[vmem] * 3,
        compiler_params=params,
        cost_estimate=cost(0.5),
        name="full_near",
    )(place, counts, pairs, near_pairs, full_flat, part_2, part_3)
    full_1 = [swap(x, 1) for x in full_1]

    first, tables = pl.pallas_call(
        functools.partial(first_lags_kernel, groups),
        out_shape=[
            shape(2, count, samples, dtype=jnp.float32),
            shape(2, 4 * FULL, 2 * samples),
        ],
        in_specs=[smem] + [vmem] * 8,
        out_specs=[vmem] * 2,
        compiler_params=params,
        cost_estimate=cost(0.001),
        name="first_lags",
    )(place, inverse, part_0, part_2, part_3, full_0, part_1, *full_1)
    return pl.pallas_call(
        lag_kernel,
        out_shape=shape(2, count, samples, dtype=jnp.float32),
        in_specs=[vmem] * 4,
        out_specs=pl.BlockSpec(memory_space=pl.ANY),
        scratch_shapes=[
            pltpu.VMEM((2, count, samples), jnp.float32),
            pltpu.SemaphoreType.DMA((4,)),
        ],
        compiler_params=params,
        cost_estimate=cost(1),
        name="lags",
    )(first, tables, full_2, full_3)


def solution(mesh):
    in_specs = (P(None, "cell", "grp", None), P("grp"), P(None, None, ("grp", "cell")))
    out_specs = P(None, ("grp", "cell"), None)
    return jax.shard_map(
        on_device, mesh=mesh, in_specs=in_specs, out_specs=out_specs, check_vma=False
    )
```

```python
import functools
import math

import jax
import jax.numpy as jnp
import numpy as np
from jax import lax
from jax.experimental import pallas as pl
from jax.experimental.pallas import tpu as pltpu
from jax.sharding import PartitionSpec as P

EPSILON = 1e-06
COSINE = (
    0.9999999999993376,
    -4.934802200431432,
    4.058712123240781,
    -1.3352627346923478,
    0.23533044681677665,
    -0.02580633847975355,
    0.0019285963125396874,
    -0.00010362767792380447,
    3.734915399663344e-06,
)
SLOTS = 32
LANES = 4 * SLOTS
COMPS = 3
NT = (((1,), (1,)), ((), ()))
TN = (((0,), (0,)), ((), ()))
VMEM_LIMIT = 40 * 1024 * 1024

PART = 24
FULL = 20


def inverse_table(samples, stations):
    bins = samples // 2
    turn = np.arange(bins)[:, None] * np.arange(samples)[None, :] % samples
    angle = turn * (2.0 * math.pi / samples)
    weight = np.where(np.arange(bins) == 0, 1.0, 2.0)[:, None] / samples
    weight = weight * math.sqrt(samples / (3.0 * stations))
    real, imag = weight * np.cos(angle), -weight * np.sin(angle)
    runs = [(at, PART) for at in range(0, 2 * PART, PART)]
    runs += [(at, FULL) for at in range(2 * PART, bins, FULL)]
    rows = [part[at : at + run] for at, run in runs for part in (real, imag)]
    return np.concatenate(rows).astype(np.float32)


def forward_rows(start, count, samples):
    row = lax.broadcasted_iota(jnp.int32, (2 * count, samples), 0)
    sample = lax.broadcasted_iota(jnp.int32, (2 * count, samples), 1)
    imag = row >= count
    turn = (row + start - jnp.where(imag, count, 0)) * sample + jnp.where(imag, samples // 4, 0)
    turn &= samples - 1
    x = jnp.where(turn > samples // 2, turn - samples, turn).astype(jnp.float32) * (2.0 / samples)
    square = x * x
    value = jnp.full(square.shape, COSINE[-1], jnp.float32)
    for factor in COSINE[-2::-1]:
        value = value * square + factor
    return value


def place_of(place_ref, groups):
    position = place_ref[0]
    high, inner = position // (2 * groups), position % (2 * groups)
    return high * 2 + inner % 2, inner // 2


def listing_of(pairs_ref, lanes):
    ends = []
    for end in range(2):
        slots = pairs_ref[:, end, :].astype(jnp.float32)
        ends += [slots[:, at : at + lanes] for at in range(0, slots.shape[1], lanes)]
    return jnp.concatenate(ends)


def station_spectra(windows_ref, at, table):
    parts = []
    for comp in range(COMPS):
        low = windows_ref[comp, 0, at]
        high = windows_ref[comp, 1, at]
        parts += [low[:SLOTS], high[SLOTS:], low[SLOTS:], high[:SLOTS]]
    traces = jnp.concatenate(parts)
    energy = jnp.sum(jnp.square(traces.astype(jnp.float32)), axis=1, keepdims=True)
    raw = lax.dot_general(traces, table, NT, preferred_element_type=jnp.float32)
    spectra = raw * lax.rsqrt(energy + EPSILON)
    return [spectra[comp * LANES : (comp + 1) * LANES].T for comp in range(COMPS)]


def rows_of(spectra, start, count):
    return jnp.concatenate([lanes[start : start + count] for lanes in spectra])


def own_kernel(place_ref, windows_ref, part_ref, full_ref, table_ref):
    groups, samples = windows_ref.shape[2], windows_ref.shape[4]
    quarter, group = place_of(place_ref, groups)
    table = [forward_rows((quarter % 2) * PART, PART, samples)]
    for far in range(2):
        table.append(forward_rows(2 * PART + (quarter ^ (2 * far)) * FULL, FULL, samples))
    table = jnp.concatenate(table).astype(jnp.bfloat16)
    table_ref[...] = table
    held = full_ref.shape[1] - COMPS * 2 * FULL
    for mg in range(groups):
        spectra = station_spectra(windows_ref, group ^ mg, table)
        part_ref[mg] = rows_of(spectra, 0, 2 * PART).astype(jnp.bfloat16)
        for far in range(2):
            rows = rows_of(spectra, 2 * PART + 2 * FULL * far, 2 * FULL)
            if held:
                rows = jnp.concatenate([rows, jnp.zeros((held, LANES), jnp.float32)])
            full_ref[far * groups + mg] = rows.astype(jnp.bfloat16)


def near_spectra_kernel(
    place_ref, own_pairs_ref, near_pairs_ref, table_ref, part_ref, full_ref, windows_ref, *piece_refs
):
    groups = windows_ref.shape[2]
    _, group = place_of(place_ref, groups)
    table = table_ref[...]
    part_rows, full_rows = COMPS * 2 * PART, COMPS * 2 * FULL
    piece_refs[groups][2 * full_rows :] = jnp.concatenate(
        [listing_of(own_pairs_ref, LANES), listing_of(near_pairs_ref, LANES)]
    ).astype(jnp.bfloat16)
    for mg in range(groups):
        spectra = station_spectra(windows_ref, group ^ mg, table)
        side = piece_refs[mg]
        side[:part_rows] = part_ref[mg]
        side[part_rows : 2 * part_rows] = rows_of(spectra, 0, 2 * PART).astype(jnp.bfloat16)
        for far, (piece, start) in enumerate(((side, 2 * part_rows), (piece_refs[groups + mg], 0))):
            own = full_ref[far * groups + mg].astype(jnp.float32)[:full_rows]
            near = rows_of(spectra, 2 * PART + 2 * FULL * far, 2 * FULL)
            piece[start : start + 2 * full_rows] = jnp.concatenate([own, near]).astype(jnp.bfloat16)


def width(bins):
    return 1 << (bins - 1).bit_length()


def packing(count, bins):
    used = 4 * bins
    spare = LANES - used
    runs, rest = used // math.gcd(used, LANES), spare // math.gcd(used, LANES)
    rows = count // (runs + rest)
    parts = []
    for run in range(runs):
        parts.append([(run * rows, 0, 0, used)])
        for extra in range(rest):
            start, end = max(run * spare, extra * used), min((run + 1) * spare, (extra + 1) * used)
            if start < end:
                lane = used + start - run * spare
                parts[-1].append(((runs + extra) * rows, lane, start - extra * used, end - extra * used))
    return rows, parts


def packed_rows(count, bins):
    rows, parts = packing(count, bins)
    return rows * len(parts)


def unpack(picked, bins):
    used = 4 * bins
    runs, rest = used // math.gcd(used, LANES), (LANES - used) // math.gcd(used, LANES)
    rows = picked.shape[0] // runs
    if not rest:
        return picked
    spare = jnp.concatenate([picked[run * rows : (run + 1) * rows, used:] for run in range(runs)], axis=1)
    return jnp.concatenate(
        [picked[:, :used]] + [spare[:, extra * used : (extra + 1) * used] for extra in range(rest)]
    )


def sides_of(place_ref, cells, mq):
    quarter, group = place_of(place_ref, cells // 4)
    own = quarter ^ mq
    high, low = own // 2, own % 2
    return high * (cells // 2) + group * 2 + low, high, low, ((high, high), (low, 1 - low))


def hots(place_ref, counts_ref, listed, rows, bins, mq):
    cells = counts_ref.shape[0]
    cell, high, low, _ = sides_of(place_ref, cells, mq)
    count = listed.shape[0] // 2
    runs = LANES // width(bins)
    run_bits, bin_bits = (n.bit_length() - 1 for n in (runs, width(bins)))
    first, second = listed[:count].astype(jnp.int32), listed[count:].astype(jnp.int32)
    far_counts = [counts_ref[cell ^ 1], counts_ref[cell ^ (cells // 2)]]
    odd = lax.broadcasted_iota(jnp.int32, (count, LANES), 0) & 1
    live = (first < counts_ref[cell]) & (second < jnp.where(odd == 1, far_counts[1], far_counts[0]))
    left, right = jnp.where(high == low, first, second), jnp.where(high == low, second, first)
    spot = jnp.where(live, (left >> run_bits) * SLOTS + right, -1)
    turned = (spot * runs + (left & (runs - 1))).T
    lane = lax.broadcasted_iota(jnp.int32, (LANES, LANES), 1)
    run = lane >> bin_bits
    found = []
    for step_round in range(2):
        hot, here = [], []
        for at in range(step_round, count, 2):
            both = jnp.broadcast_to(turned[:, at : at + 1], (LANES, LANES))
            here.append(jnp.where((both & (runs - 1)) == run, 1.0, 0.0).astype(jnp.bfloat16))
            offset = (both >> run_bits) - lane
            hot.append(
                jnp.concatenate(
                    [
                        jnp.where(offset == start, 1.0, 0.0).astype(jnp.bfloat16)
                        for start in range(0, rows, LANES)
                    ],
                    axis=1,
                )
            )
        found.append((jnp.concatenate(hot), jnp.concatenate(here)))
    return found


def folds_of(count, bins):
    return sorted({entry[1:] for entries in packing(count, bins)[1] for entry in entries})


def folds(count, bins):
    spread = lax.broadcasted_iota(jnp.int32, (4 * LANES, LANES), 0)
    kept = lax.broadcasted_iota(jnp.int32, (4 * LANES, LANES), 1)
    bin_of = spread & (width(bins) - 1)
    value = jnp.where(bin_of < bins, (spread >> (LANES.bit_length() - 1)) * bins + bin_of, -1)
    kinds = folds_of(count, bins)
    matrices = []
    for at, least, end in kinds:
        fold = (value >= least) & (value < end) & (kept == value + (at - least))
        matrices.append(jnp.where(fold, 1.0, 0.0).astype(jnp.bfloat16))
    return kinds, matrices


def picks(place_ref, cells, hot, kinds, matrices, flat_ref, bins, mq):
    _, _, _, sides = sides_of(place_ref, cells, mq)
    found = []
    for (rows, lanes), (own, far) in zip(hot, sides):
        wide = jnp.dot(rows, flat_ref[own, far], preferred_element_type=jnp.float32).astype(jnp.bfloat16)
        found += [wide[:, :LANES] * lanes, wide[:, LANES:] * lanes]
    found = jnp.concatenate(found, axis=1)
    held, parts = packing(found.shape[0], bins)
    picked = []
    for entries in parts:
        total = 0.0
        for start, *kind in entries:
            total += jnp.dot(
                found[start : start + held],
                matrices[kinds.index(tuple(kind))],
                preferred_element_type=jnp.float32,
            )
        picked.append(total.astype(jnp.bfloat16))
    return jnp.concatenate(picked)


def pick(place_ref, counts_ref, listed, flat_ref, bins, mq, *picked_refs):
    hot = hots(place_ref, counts_ref, listed, flat_ref.shape[2], bins, mq)
    kinds, matrices = folds(listed.shape[0] // 4 * LANES, bins)
    picked = picks(place_ref, counts_ref.shape[0], hot, kinds, matrices, flat_ref, bins, mq)
    each = picked.shape[0] // len(picked_refs)
    for at, ref in enumerate(picked_refs):
        ref[...] = picked[at * each : (at + 1) * each]


def whole(count, tile):
    return -(-count // tile) * tile


def padded(traces):
    return whole(traces, 16)


def add_cross(pieces, trace_ref, bins, sums_ref, before_ref=None):
    slots, rows = 2 * SLOTS, 2 * bins
    traces = trace_ref.shape[0] // rows
    start = 0
    for piece, at, size in pieces:
        trace_ref[start : start + size] = piece[at : at + size].astype(jnp.float32)
        start += size
    if start < traces * rows:
        trace_ref[start:] = jnp.zeros((traces * rows - start, LANES), jnp.float32)
    lower = lax.broadcasted_iota(jnp.int32, (traces, LANES), 1) < slots
    for k in range(bins):
        real = trace_ref[pl.ds(k, traces, stride=rows), :]
        imag = trace_ref[pl.ds(bins + k, traces, stride=rows), :]
        left = jnp.concatenate([real, imag]).astype(jnp.bfloat16)[:, :slots]
        right = jnp.concatenate(
            [
                jnp.where(lower, pltpu.roll(real, slots, 1), imag),
                jnp.where(lower, pltpu.roll(imag, slots, 1), -real),
            ]
        ).astype(jnp.bfloat16)
        cross = lax.dot_general(left, right, TN, preferred_element_type=jnp.float32)
        if before_ref is not None:
            cross += before_ref[k * slots : (k + 1) * slots]
        sums_ref[k * slots : (k + 1) * slots] = cross


def turn_blocks(cross_ref, bins, flat_ref):
    slots, runs = 2 * SLOTS, LANES // width(bins)
    held = cross_ref.shape[0] // slots
    if held > bins:
        cross_ref[bins * slots :] = jnp.zeros(((held - bins) * slots, LANES), jnp.float32)
    empty = jnp.zeros((width(bins) - held, LANES), jnp.float32)
    for own in range(2):
        for at in range(SLOTS // runs):
            block = []
            for i in range(runs):
                block.append(cross_ref[pl.ds(own * SLOTS + at * runs + i, held, stride=slots), :])
                block += [empty] * (held < width(bins))
            block = jnp.concatenate(block).astype(jnp.bfloat16).T
            for part in range(2):
                for far in range(2):
                    start = (part * 2 + far) * SLOTS
                    flat_ref[
                        own, far, at * SLOTS : (at + 1) * SLOTS, part * LANES : (part + 1) * LANES
                    ] = block[start : start + SLOTS]


def side_part(ref):
    return (ref, 0, 2 * COMPS * 2 * PART)


def side_full(ref):
    return (ref, 2 * COMPS * 2 * PART, 2 * COMPS * 2 * FULL)


def cross_full(ref):
    return (ref, 0, 2 * COMPS * 2 * FULL)


def part_kernel(*refs):
    piece_refs, (flat_ref, trace_ref, cross_ref) = refs[:-3], refs[-3:]
    add_cross([side_part(ref) for ref in piece_refs], trace_ref, PART, cross_ref)
    turn_blocks(cross_ref, PART, flat_ref)


def far_kernel(bins, place_ref, counts_ref, listed_ref, flat_ref, after_ref, picked_0, picked_1):
    listed = listed_ref[cross_full(listed_ref)[2] :].astype(jnp.float32)
    listing = listed.shape[0] // 2
    pick(place_ref, counts_ref, listed[:listing], flat_ref, bins, 2, picked_0)
    pick(place_ref, counts_ref, listed[listing:], flat_ref, bins, 3, picked_1)


def early_kernel(sides, after_0, after_1, *refs):
    piece_refs, (sums_ref, trace_ref) = refs[:-2], refs[-2:]
    pieces = [side_full(ref) for ref in piece_refs[:sides]] + [cross_full(ref) for ref in piece_refs[sides:]]
    add_cross(pieces, trace_ref, FULL, sums_ref)


def ready_kernel(place_ref, counts_ref, listed_ref, after_ref, hot_ref, here_ref, fold_ref):
    listed = listed_ref[cross_full(listed_ref)[2] :].astype(jnp.float32)
    listing = listed.shape[0] // 2
    for at in range(2):
        part = listed[at * listing : (at + 1) * listing]
        for step_round, (hot, here) in enumerate(
            hots(place_ref, counts_ref, part, hot_ref.shape[3], FULL, 2 + at)
        ):
            hot_ref[at, step_round] = hot
            here_ref[at, step_round] = here
    for at, matrix in enumerate(folds(hot_ref.shape[2], FULL)[1]):
        fold_ref[at] = matrix


def full_kernel(cells, place_ref, hot_ref, here_ref, fold_ref, after_0, before_ref, *refs):
    piece_refs, (flat_ref, picked_0, picked_1, trace_ref, cross_ref) = refs[:-5], refs[-5:]
    add_cross([cross_full(ref) for ref in piece_refs], trace_ref, FULL, cross_ref, before_ref)
    turn_blocks(cross_ref, FULL, flat_ref)
    count = hot_ref.shape[2]
    kinds = folds_of(count, FULL)
    matrices = [fold_ref[at] for at in range(len(kinds))]
    for at, ref in enumerate((picked_0, picked_1)):
        hot = [(hot_ref[at, step_round], here_ref[at, step_round]) for step_round in range(2)]
        ref[...] = picks(place_ref, cells, hot, kinds, matrices, flat_ref, FULL, 2 + at)


def near_kernel(bins, sent, place_ref, counts_ref, own_pairs_ref, near_pairs_ref, flat_ref, *refs):
    picked_0, *picked_1 = refs[-1 - sent :]
    pick(place_ref, counts_ref, listing_of(near_pairs_ref, LANES), flat_ref, bins, 1, *picked_1)
    pick(place_ref, counts_ref, listing_of(own_pairs_ref, LANES), flat_ref, bins, 0, picked_0)


def both_rounds(rows, sign):
    row = lax.broadcasted_iota(jnp.int32, rows.shape, 0)
    rows = rows * jnp.where(row < rows.shape[0] // 2, 1.0, sign)
    empty = jnp.zeros_like(rows)
    return jnp.concatenate(
        [jnp.concatenate([rows, empty], axis=1), jnp.concatenate([empty, rows], axis=1)]
    )


def halves(table):
    high = table.astype(jnp.bfloat16)
    return high, (table - high.astype(jnp.float32)).astype(jnp.bfloat16)


def tables_of(groups, place_ref, inverse_ref):
    quarter, _ = place_of(place_ref, groups)
    low = quarter % 2
    sign = jnp.where(quarter // 2 == low, 1.0, -1.0)

    def part_table(which):
        start = pl.multiple_of((low ^ which) * 2 * PART, 2 * PART)
        return halves(both_rounds(inverse_ref[pl.ds(start, 2 * PART), :], sign))

    def full_table(mq):
        start = pl.multiple_of(4 * PART + (quarter ^ mq) * 2 * FULL, 2 * FULL)
        return halves(both_rounds(inverse_ref[pl.ds(start, 2 * FULL), :], sign))

    return part_table, full_table


def sum_lags(terms):
    lags = 0.0
    for picked, bins, table in terms:
        picked = unpack(picked, bins)
        for half in table:
            lags += jnp.dot(picked, half, preferred_element_type=jnp.float32)
    return lags


def part_lags_kernel(groups, place_ref, inverse_ref, part_0, part_2, part_3, part_1, lags_ref):
    samples = inverse_ref.shape[1]
    part_table, _ = tables_of(groups, place_ref, inverse_ref)
    near, other = part_table(0), part_table(1)
    lags = sum_lags(
        [
            (part_0[...], PART, near),
            (part_2[...], PART, near),
            (part_1[...], PART, other),
            (part_3[...], PART, other),
        ]
    )
    for step_round in range(2):
        lags_ref[step_round] = lags[:, step_round * samples : (step_round + 1) * samples]


def first_lags_kernel(groups, place_ref, inverse_ref, before_ref, full_0, *refs):
    full_1, (lags_ref, table_ref) = refs[:-2], refs[-2:]
    samples = inverse_ref.shape[1]
    _, full_table = tables_of(groups, place_ref, inverse_ref)
    full_1 = jnp.concatenate([ref[...] for ref in full_1])
    lags = sum_lags([(full_0[...], FULL, full_table(0)), (full_1, FULL, full_table(1))])
    for step_round in range(2):
        lags_ref[step_round] = (
            before_ref[step_round] + lags[:, step_round * samples : (step_round + 1) * samples]
        )
    for at in range(2):
        table_ref[at] = full_table(2 + at)[0]


def lag_kernel(first_ref, table_ref, *refs):
    picked_refs, (lags_ref, held_ref, sems) = refs[:-3], refs[-3:]
    samples = lags_ref.shape[2]
    runs = sems.shape[0]
    held = held_ref.shape[1] // runs
    picked = [unpack(ref[...], FULL) for ref in picked_refs]
    copies = []
    for run in range(runs):
        rows = slice(run * held, (run + 1) * held)
        more = 0.0
        for at, values in enumerate(picked):
            more += jnp.dot(values[rows], table_ref[at], preferred_element_type=jnp.float32)
        for step_round in range(2):
            held_ref[step_round, rows] = (
                first_ref[step_round, rows] + more[:, step_round * samples : (step_round + 1) * samples]
            )
        copies.append(
            pltpu.make_async_copy(held_ref.at[:, rows], lags_ref.at[:, rows], sems.at[run])
        )
        copies[-1].start()
    for copy in copies:
        copy.wait()


def on_device(windows, counts, pairs):
    comps, _, events, samples = windows.shape
    cells = lax.axis_size("cell")
    half, groups = cells // 2, cells // 4
    count = pairs.shape[2]
    inverse = jnp.asarray(inverse_table(samples, cells))
    place = lax.axis_index("cell").astype(jnp.int32).reshape(1)

    def swap(x, mask):
        return lax.ppermute(x, "cell", [(i, i ^ mask) for i in range(cells)])

    def shape(*dims, dtype=jnp.bfloat16):
        return jax.ShapeDtypeStruct(dims, dtype)

    vmem = pl.BlockSpec(memory_space=pltpu.VMEM)
    smem = pl.BlockSpec(memory_space=pltpu.SMEM)
    params = pltpu.CompilerParams(vmem_limit_bytes=VMEM_LIMIT)

    def cost(microseconds):
        return pl.CostEstimate(
            flops=int(microseconds * 1e9), bytes_accessed=2**20, transcendentals=0
        )

    windows = windows.reshape(comps, 2, groups, 2 * SLOTS, samples)
    near_windows, near_pairs = swap(windows, 1), swap(pairs, 1)
    part_rows, full_rows = comps * 2 * PART, comps * 2 * FULL
    part_spectra, full_spectra, table = pl.pallas_call(
        own_kernel,
        out_shape=[
            shape(groups, part_rows, LANES),
            shape(2 * groups, whole(full_rows, 16), LANES),
            shape(2 * PART + 4 * FULL, samples),
        ],
        in_specs=[smem, vmem],
        out_specs=[vmem] * 3,
        compiler_params=params,
        cost_estimate=cost(1),
        name="own_spectra",
    )(place, windows)
    listing = 2 * pairs.size // LANES
    pieces = pl.pallas_call(
        near_spectra_kernel,
        out_shape=[shape(2 * (part_rows + full_rows), LANES)] * groups
        + [shape(2 * full_rows + listing * (mg == 0), LANES) for mg in range(groups)],
        in_specs=[smem] + [vmem] * 6,
        out_specs=[vmem] * (2 * groups),
        compiler_params=params,
        cost_estimate=cost(1),
        name="near_spectra",
    )(place, pairs, near_pairs, table, part_spectra, full_spectra, near_windows)
    arrived = [pieces[0]] + [swap(pieces[m], 2 * m) for m in range(1, 2 * groups)]
    sides, far = arrived[:groups], arrived[groups:]

    early, late = far[: groups - 2], far[groups - 2 :]
    part_packed = shape(packed_rows(count, PART), LANES)
    full_packed = shape(packed_rows(count, FULL), LANES)
    half_packed = shape(packed_rows(count, FULL) // 2, LANES)
    part_blocks = shape(2, 2, SLOTS * SLOTS * width(PART) // LANES, 2 * LANES)
    full_blocks = shape(2, 2, SLOTS * SLOTS * width(FULL) // LANES, 2 * LANES)
    part_flat = pl.pallas_call(
        part_kernel,
        out_shape=part_blocks,
        in_specs=[vmem] * groups,
        out_specs=vmem,
        scratch_shapes=[
            pltpu.VMEM((padded(groups * 2 * comps) * 2 * PART, LANES), jnp.float32),
            pltpu.VMEM((2 * SLOTS * whole(PART, 8), LANES), jnp.float32),
        ],
        compiler_params=params,
        cost_estimate=cost(0.001),
        name="part",
    )(*sides)
    part_0, part_1 = pl.pallas_call(
        functools.partial(near_kernel, PART, 1),
        out_shape=[part_packed, part_packed],
        in_specs=[smem, smem] + [vmem] * 3,
        out_specs=[vmem] * 2,
        compiler_params=params,
        cost_estimate=cost(0.001),
        name="part_near",
    )(place, counts, pairs, near_pairs, part_flat)
    part_2, part_3 = pl.pallas_call(
        functools.partial(far_kernel, PART),
        out_shape=[part_packed, part_packed],
        in_specs=[smem, smem, vmem, vmem, pl.BlockSpec(memory_space=pl.ANY)],
        out_specs=[vmem, vmem],
        compiler_params=params,
        cost_estimate=cost(1),
        name="part_far",
    )(place, counts, far[0], part_flat, part_0)
    part_1 = swap(part_1, 1)
    sums = pl.pallas_call(
        functools.partial(early_kernel, groups),
        out_shape=shape(2 * SLOTS * FULL, LANES, dtype=jnp.float32),
        in_specs=[pl.BlockSpec(memory_space=pl.ANY)] * 2 + [vmem] * (groups + len(early)),
        out_specs=vmem,
        scratch_shapes=[
            pltpu.VMEM((padded((groups + len(early)) * 2 * comps) * 2 * FULL, LANES), jnp.float32)
        ],
        compiler_params=params,
        cost_estimate=cost(0.001),
        name="early",
    )(part_0, part_2, *sides, *early)
    part_2, part_3 = swap(part_2, half), swap(part_3, half + 1)
    ready = pl.pallas_call(
        ready_kernel,
        out_shape=[
            shape(2, 2, count, full_blocks.shape[2]),
            shape(2, 2, count, LANES),
            shape(len(folds_of(count, FULL)), 4 * LANES, LANES),
        ],
        in_specs=[smem, smem, vmem, pl.BlockSpec(memory_space=pl.ANY)],
        out_specs=[vmem] * 3,
        compiler_params=params,
        cost_estimate=cost(0.001),
        name="ready",
    )(place, counts, far[0], sums)
    full_flat, full_2, full_3 = pl.pallas_call(
        functools.partial(full_kernel, cells),
        out_shape=[full_blocks, full_packed, full_packed],
        in_specs=[smem] + [vmem] * 3 + [pl.BlockSpec(memory_space=pl.ANY)] + [vmem] * (1 + len(late)),
        out_specs=[vmem] * 3,
        scratch_shapes=[
            pltpu.VMEM((padded(len(late) * 2 * comps) * 2 * FULL, LANES), jnp.float32),
            pltpu.VMEM((2 * SLOTS * whole(FULL, 8), LANES), jnp.float32),
        ],
        compiler_params=params,
        cost_estimate=cost(10),
        name="full",
    )(place, *ready, part_0, sums, *late)
    full_2, full_3 = swap(full_2, half), swap(full_3, half + 1)
    full_0, *full_1 = pl.pallas_call(
        functools.partial(near_kernel, FULL, 2),
        out_shape=[full_packed, half_packed, half_packed],
        in_specs=[smem, smem] + [vmem] * 3,
        out_specs=[vmem] * 3,
        compiler_params=params,
        cost_estimate=cost(0.5),
        name="full_near",
    )(place, counts, pairs, near_pairs, full_flat)
    full_1 = [swap(x, 1) for x in full_1]

    part_lags = pl.pallas_call(
        functools.partial(part_lags_kernel, groups),
        out_shape=shape(2, count, samples, dtype=jnp.float32),
        in_specs=[smem] + [vmem] * 5,
        out_specs=vmem,
        compiler_params=params,
        cost_estimate=cost(0.001),
        name="part_lags",
    )(place, inverse, part_0, part_2, part_3, part_1)
    first, tables = pl.pallas_call(
        functools.partial(first_lags_kernel, groups),
        out_shape=[
            shape(2, count, samples, dtype=jnp.float32),
            shape(2, 4 * FULL, 2 * samples),
        ],
        in_specs=[smem] + [vmem] * 5,
        out_specs=[vmem] * 2,
        compiler_params=params,
        cost_estimate=cost(0.001),
        name="first_lags",
    )(place, inverse, part_lags, full_0, *full_1)
    return pl.pallas_call(
        lag_kernel,
        out_shape=shape(2, count, samples, dtype=jnp.float32),
        in_specs=[vmem] * 4,
        out_specs=pl.BlockSpec(memory_space=pl.ANY),
        scratch_shapes=[
            pltpu.VMEM((2, count, samples), jnp.float32),
            pltpu.SemaphoreType.DMA((4,)),
        ],
        compiler_params=params,
        cost_estimate=cost(1),
        name="lags",
    )(first, tables, full_2, full_3)


def solution(mesh):
    in_specs = (P(None, "cell", "grp", None), P("grp"), P(None, None, ("grp", "cell")))
    out_specs = P(None, ("grp", "cell"), None)
    return jax.shard_map(
        on_device, mesh=mesh, in_specs=in_specs, out_specs=out_specs, check_vma=False
    )
```

```python
import functools
import math

import jax
import jax.numpy as jnp
import numpy as np
from jax import lax
from jax.experimental import pallas as pl
from jax.experimental.pallas import tpu as pltpu
from jax.sharding import PartitionSpec as P

EPSILON = 1e-06
COSINE = (
    0.9999999999993376,
    -4.934802200431432,
    4.058712123240781,
    -1.3352627346923478,
    0.23533044681677665,
    -0.02580633847975355,
    0.0019285963125396874,
    -0.00010362767792380447,
    3.734915399663344e-06,
)
SLOTS = 32
LANES = 4 * SLOTS
COMPS = 3
NT = (((1,), (1,)), ((), ()))
TN = (((0,), (0,)), ((), ()))
VMEM_LIMIT = 40 * 1024 * 1024

PART = 24
FULL = 20


def inverse_table(samples, stations):
    bins = samples // 2
    turn = np.arange(bins)[:, None] * np.arange(samples)[None, :] % samples
    angle = turn * (2.0 * math.pi / samples)
    weight = np.where(np.arange(bins) == 0, 1.0, 2.0)[:, None] / samples
    weight = weight * math.sqrt(samples / (3.0 * stations))
    real, imag = weight * np.cos(angle), -weight * np.sin(angle)
    runs = [(at, PART) for at in range(0, 2 * PART, PART)]
    runs += [(at, FULL) for at in range(2 * PART, bins, FULL)]
    rows = [part[at : at + run] for at, run in runs for part in (real, imag)]
    return np.concatenate(rows).astype(np.float32)


def forward_rows(start, count, samples):
    row = lax.broadcasted_iota(jnp.int32, (2 * count, samples), 0)
    sample = lax.broadcasted_iota(jnp.int32, (2 * count, samples), 1)
    imag = row >= count
    turn = (row + start - jnp.where(imag, count, 0)) * sample + jnp.where(imag, samples // 4, 0)
    turn &= samples - 1
    x = jnp.where(turn > samples // 2, turn - samples, turn).astype(jnp.float32) * (2.0 / samples)
    square = x * x
    value = jnp.full(square.shape, COSINE[-1], jnp.float32)
    for factor in COSINE[-2::-1]:
        value = value * square + factor
    return value


def place_of(place_ref, groups):
    position = place_ref[0]
    high, inner = position // (2 * groups), position % (2 * groups)
    return high * 2 + inner % 2, inner // 2


def listing_of(pairs_ref, lanes):
    ends = []
    for end in range(2):
        slots = pairs_ref[:, end, :].astype(jnp.float32)
        ends += [slots[:, at : at + lanes] for at in range(0, slots.shape[1], lanes)]
    return jnp.concatenate(ends)


def station_spectra(windows_ref, at, table):
    parts = []
    for comp in range(COMPS):
        low = windows_ref[comp, 0, at]
        high = windows_ref[comp, 1, at]
        parts += [low[:SLOTS], high[SLOTS:], low[SLOTS:], high[:SLOTS]]
    traces = jnp.concatenate(parts)
    energy = jnp.sum(jnp.square(traces.astype(jnp.float32)), axis=1, keepdims=True)
    raw = lax.dot_general(traces, table, NT, preferred_element_type=jnp.float32)
    spectra = raw * lax.rsqrt(energy + EPSILON)
    return [spectra[comp * LANES : (comp + 1) * LANES].T for comp in range(COMPS)]


def rows_of(spectra, start, count):
    return jnp.concatenate([lanes[start : start + count] for lanes in spectra])


def own_kernel(place_ref, windows_ref, part_ref, full_ref, table_ref):
    groups, samples = windows_ref.shape[2], windows_ref.shape[4]
    quarter, group = place_of(place_ref, groups)
    table = [forward_rows((quarter % 2) * PART, PART, samples)]
    for far in range(2):
        table.append(forward_rows(2 * PART + (quarter ^ (2 * far)) * FULL, FULL, samples))
    table = jnp.concatenate(table).astype(jnp.bfloat16)
    table_ref[...] = table
    held = full_ref.shape[1] - COMPS * 2 * FULL
    for mg in range(groups):
        spectra = station_spectra(windows_ref, group ^ mg, table)
        part_ref[mg] = rows_of(spectra, 0, 2 * PART).astype(jnp.bfloat16)
        for far in range(2):
            rows = rows_of(spectra, 2 * PART + 2 * FULL * far, 2 * FULL)
            if held:
                rows = jnp.concatenate([rows, jnp.zeros((held, LANES), jnp.float32)])
            full_ref[far * groups + mg] = rows.astype(jnp.bfloat16)


def near_spectra_kernel(
    place_ref, own_pairs_ref, near_pairs_ref, table_ref, part_ref, full_ref, windows_ref, *piece_refs
):
    groups = windows_ref.shape[2]
    _, group = place_of(place_ref, groups)
    table = table_ref[...]
    part_rows, full_rows = COMPS * 2 * PART, COMPS * 2 * FULL
    piece_refs[groups][2 * full_rows :] = jnp.concatenate(
        [listing_of(own_pairs_ref, LANES), listing_of(near_pairs_ref, LANES)]
    ).astype(jnp.bfloat16)
    for mg in range(groups):
        spectra = station_spectra(windows_ref, group ^ mg, table)
        side = piece_refs[mg]
        side[:part_rows] = part_ref[mg]
        side[part_rows : 2 * part_rows] = rows_of(spectra, 0, 2 * PART).astype(jnp.bfloat16)
        for far, (piece, start) in enumerate(((side, 2 * part_rows), (piece_refs[groups + mg], 0))):
            own = full_ref[far * groups + mg].astype(jnp.float32)[:full_rows]
            near = rows_of(spectra, 2 * PART + 2 * FULL * far, 2 * FULL)
            piece[start : start + 2 * full_rows] = jnp.concatenate([own, near]).astype(jnp.bfloat16)


def width(bins):
    return 1 << (bins - 1).bit_length()


def packing(count, bins):
    used = 4 * bins
    spare = LANES - used
    runs, rest = used // math.gcd(used, LANES), spare // math.gcd(used, LANES)
    rows = count // (runs + rest)
    parts = []
    for run in range(runs):
        parts.append([(run * rows, 0, 0, used)])
        for extra in range(rest):
            start, end = max(run * spare, extra * used), min((run + 1) * spare, (extra + 1) * used)
            if start < end:
                lane = used + start - run * spare
                parts[-1].append(((runs + extra) * rows, lane, start - extra * used, end - extra * used))
    return rows, parts


def packed_rows(count, bins):
    rows, parts = packing(count, bins)
    return rows * len(parts)


def unpack(picked, bins):
    used = 4 * bins
    runs, rest = used // math.gcd(used, LANES), (LANES - used) // math.gcd(used, LANES)
    rows = picked.shape[0] // runs
    if not rest:
        return picked
    spare = jnp.concatenate([picked[run * rows : (run + 1) * rows, used:] for run in range(runs)], axis=1)
    return jnp.concatenate(
        [picked[:, :used]] + [spare[:, extra * used : (extra + 1) * used] for extra in range(rest)]
    )


def sides_of(place_ref, cells, mq):
    quarter, group = place_of(place_ref, cells // 4)
    own = quarter ^ mq
    high, low = own // 2, own % 2
    return high * (cells // 2) + group * 2 + low, high, low, ((high, high), (low, 1 - low))


def hots(place_ref, counts_ref, listed, rows, bins, mq):
    cells = counts_ref.shape[0]
    cell, high, low, _ = sides_of(place_ref, cells, mq)
    count = listed.shape[0] // 2
    runs = LANES // width(bins)
    run_bits, bin_bits = (n.bit_length() - 1 for n in (runs, width(bins)))
    first, second = listed[:count].astype(jnp.int32), listed[count:].astype(jnp.int32)
    far_counts = [counts_ref[cell ^ 1], counts_ref[cell ^ (cells // 2)]]
    odd = lax.broadcasted_iota(jnp.int32, (count, LANES), 0) & 1
    live = (first < counts_ref[cell]) & (second < jnp.where(odd == 1, far_counts[1], far_counts[0]))
    left, right = jnp.where(high == low, first, second), jnp.where(high == low, second, first)
    spot = jnp.where(live, (left >> run_bits) * SLOTS + right, -1)
    turned = (spot * runs + (left & (runs - 1))).T
    lane = lax.broadcasted_iota(jnp.int32, (LANES, LANES), 1)
    run = lane >> bin_bits
    found = []
    for step_round in range(2):
        hot, here = [], []
        for at in range(step_round, count, 2):
            both = jnp.broadcast_to(turned[:, at : at + 1], (LANES, LANES))
            here.append(jnp.where((both & (runs - 1)) == run, 1.0, 0.0).astype(jnp.bfloat16))
            offset = (both >> run_bits) - lane
            hot.append(
                jnp.concatenate(
                    [
                        jnp.where(offset == start, 1.0, 0.0).astype(jnp.bfloat16)
                        for start in range(0, rows, LANES)
                    ],
                    axis=1,
                )
            )
        found.append((jnp.concatenate(hot), jnp.concatenate(here)))
    return found


def folds_of(count, bins):
    return sorted({entry[1:] for entries in packing(count, bins)[1] for entry in entries})


def folds(count, bins):
    spread = lax.broadcasted_iota(jnp.int32, (4 * LANES, LANES), 0)
    kept = lax.broadcasted_iota(jnp.int32, (4 * LANES, LANES), 1)
    bin_of = spread & (width(bins) - 1)
    value = jnp.where(bin_of < bins, (spread >> (LANES.bit_length() - 1)) * bins + bin_of, -1)
    kinds = folds_of(count, bins)
    matrices = []
    for at, least, end in kinds:
        fold = (value >= least) & (value < end) & (kept == value + (at - least))
        matrices.append(jnp.where(fold, 1.0, 0.0).astype(jnp.bfloat16))
    return kinds, matrices


def picks(place_ref, cells, hot, kinds, matrices, flat_ref, bins, mq):
    _, _, _, sides = sides_of(place_ref, cells, mq)
    found = []
    for (rows, lanes), (own, far) in zip(hot, sides):
        wide = jnp.dot(rows, flat_ref[own, far], preferred_element_type=jnp.float32).astype(jnp.bfloat16)
        found += [wide[:, :LANES] * lanes, wide[:, LANES:] * lanes]
    found = jnp.concatenate(found, axis=1)
    held, parts = packing(found.shape[0], bins)
    picked = []
    for entries in parts:
        total = 0.0
        for start, *kind in entries:
            total += jnp.dot(
                found[start : start + held],
                matrices[kinds.index(tuple(kind))],
                preferred_element_type=jnp.float32,
            )
        picked.append(total.astype(jnp.bfloat16))
    return jnp.concatenate(picked)


def pick(place_ref, counts_ref, listed, flat_ref, bins, mq, *picked_refs):
    hot = hots(place_ref, counts_ref, listed, flat_ref.shape[2], bins, mq)
    kinds, matrices = folds(listed.shape[0] // 4 * LANES, bins)
    picked = picks(place_ref, counts_ref.shape[0], hot, kinds, matrices, flat_ref, bins, mq)
    each = picked.shape[0] // len(picked_refs)
    for at, ref in enumerate(picked_refs):
        ref[...] = picked[at * each : (at + 1) * each]


def whole(count, tile):
    return -(-count // tile) * tile


def padded(traces):
    return whole(traces, 16)


def add_cross(pieces, trace_ref, bins, sums_ref, before_ref=None):
    slots, rows = 2 * SLOTS, 2 * bins
    traces = trace_ref.shape[0] // rows
    start = 0
    for piece, at, size in pieces:
        trace_ref[start : start + size] = piece[at : at + size].astype(jnp.float32)
        start += size
    if start < traces * rows:
        trace_ref[start:] = jnp.zeros((traces * rows - start, LANES), jnp.float32)
    lower = lax.broadcasted_iota(jnp.int32, (traces, LANES), 1) < slots
    for k in range(bins):
        real = trace_ref[pl.ds(k, traces, stride=rows), :]
        imag = trace_ref[pl.ds(bins + k, traces, stride=rows), :]
        left = jnp.concatenate([real, imag]).astype(jnp.bfloat16)[:, :slots]
        right = jnp.concatenate(
            [
                jnp.where(lower, pltpu.roll(real, slots, 1), imag),
                jnp.where(lower, pltpu.roll(imag, slots, 1), -real),
            ]
        ).astype(jnp.bfloat16)
        cross = lax.dot_general(left, right, TN, preferred_element_type=jnp.float32)
        if before_ref is not None:
            cross += before_ref[k * slots : (k + 1) * slots]
        sums_ref[k * slots : (k + 1) * slots] = cross


def turn_blocks(cross_ref, bins, flat_ref):
    slots, runs = 2 * SLOTS, LANES // width(bins)
    held = cross_ref.shape[0] // slots
    if held > bins:
        cross_ref[bins * slots :] = jnp.zeros(((held - bins) * slots, LANES), jnp.float32)
    empty = jnp.zeros((width(bins) - held, LANES), jnp.float32)
    for own in range(2):
        for at in range(SLOTS // runs):
            block = []
            for i in range(runs):
                block.append(cross_ref[pl.ds(own * SLOTS + at * runs + i, held, stride=slots), :])
                block += [empty] * (held < width(bins))
            block = jnp.concatenate(block).astype(jnp.bfloat16).T
            for part in range(2):
                for far in range(2):
                    start = (part * 2 + far) * SLOTS
                    flat_ref[
                        own, far, at * SLOTS : (at + 1) * SLOTS, part * LANES : (part + 1) * LANES
                    ] = block[start : start + SLOTS]


def side_part(ref):
    return (ref, 0, 2 * COMPS * 2 * PART)


def side_full(ref):
    return (ref, 2 * COMPS * 2 * PART, 2 * COMPS * 2 * FULL)


def cross_full(ref):
    return (ref, 0, 2 * COMPS * 2 * FULL)


def part_kernel(*refs):
    piece_refs, (flat_ref, trace_ref, cross_ref) = refs[:-3], refs[-3:]
    add_cross([side_part(ref) for ref in piece_refs], trace_ref, PART, cross_ref)
    turn_blocks(cross_ref, PART, flat_ref)


def far_kernel(bins, place_ref, counts_ref, listed_ref, flat_ref, picked_0, picked_1):
    listed = listed_ref[cross_full(listed_ref)[2] :].astype(jnp.float32)
    listing = listed.shape[0] // 2
    pick(place_ref, counts_ref, listed[:listing], flat_ref, bins, 2, picked_0)
    pick(place_ref, counts_ref, listed[listing:], flat_ref, bins, 3, picked_1)


def early_kernel(sides, after_0, after_1, *refs):
    piece_refs, (sums_ref, trace_ref) = refs[:-2], refs[-2:]
    pieces = [side_full(ref) for ref in piece_refs[:sides]] + [cross_full(ref) for ref in piece_refs[sides:]]
    add_cross(pieces, trace_ref, FULL, sums_ref)


def full_kernel(place_ref, counts_ref, listed_ref, before_ref, *refs):
    piece_refs, (flat_ref, picked_0, picked_1, trace_ref, cross_ref) = refs[:-5], refs[-5:]
    add_cross([cross_full(ref) for ref in piece_refs], trace_ref, FULL, cross_ref, before_ref)
    turn_blocks(cross_ref, FULL, flat_ref)
    listed = listed_ref[cross_full(listed_ref)[2] :].astype(jnp.float32)
    listing = listed.shape[0] // 2
    pick(place_ref, counts_ref, listed[:listing], flat_ref, FULL, 2, picked_0)
    pick(place_ref, counts_ref, listed[listing:], flat_ref, FULL, 3, picked_1)


def near_kernel(bins, sent, place_ref, counts_ref, own_pairs_ref, near_pairs_ref, flat_ref, *refs):
    picked_0, *picked_1 = refs[-1 - sent :]
    pick(place_ref, counts_ref, listing_of(near_pairs_ref, LANES), flat_ref, bins, 1, *picked_1)
    pick(place_ref, counts_ref, listing_of(own_pairs_ref, LANES), flat_ref, bins, 0, picked_0)


def both_rounds(rows, sign):
    row = lax.broadcasted_iota(jnp.int32, rows.shape, 0)
    rows = rows * jnp.where(row < rows.shape[0] // 2, 1.0, sign)
    empty = jnp.zeros_like(rows)
    return jnp.concatenate(
        [jnp.concatenate([rows, empty], axis=1), jnp.concatenate([empty, rows], axis=1)]
    )


def halves(table):
    high = table.astype(jnp.bfloat16)
    return high, (table - high.astype(jnp.float32)).astype(jnp.bfloat16)


def tables_of(groups, place_ref, inverse_ref):
    quarter, _ = place_of(place_ref, groups)
    low = quarter % 2
    sign = jnp.where(quarter // 2 == low, 1.0, -1.0)

    def part_table(which):
        start = pl.multiple_of((low ^ which) * 2 * PART, 2 * PART)
        return halves(both_rounds(inverse_ref[pl.ds(start, 2 * PART), :], sign))

    def full_table(mq):
        start = pl.multiple_of(4 * PART + (quarter ^ mq) * 2 * FULL, 2 * FULL)
        return halves(both_rounds(inverse_ref[pl.ds(start, 2 * FULL), :], sign))

    return part_table, full_table


def sum_lags(terms):
    lags = 0.0
    for picked, bins, table in terms:
        picked = unpack(picked, bins)
        for half in table:
            lags += jnp.dot(picked, half, preferred_element_type=jnp.float32)
    return lags


def part_lags_kernel(groups, place_ref, inverse_ref, part_0, part_2, part_3, part_1, lags_ref):
    samples = inverse_ref.shape[1]
    part_table, _ = tables_of(groups, place_ref, inverse_ref)
    near, other = part_table(0), part_table(1)
    lags = sum_lags(
        [
            (part_0[...], PART, near),
            (part_2[...], PART, near),
            (part_1[...], PART, other),
            (part_3[...], PART, other),
        ]
    )
    for step_round in range(2):
        lags_ref[step_round] = lags[:, step_round * samples : (step_round + 1) * samples]


def first_lags_kernel(groups, place_ref, inverse_ref, before_ref, full_0, *refs):
    full_1, (lags_ref, table_ref) = refs[:-2], refs[-2:]
    samples = inverse_ref.shape[1]
    _, full_table = tables_of(groups, place_ref, inverse_ref)
    full_1 = jnp.concatenate([ref[...] for ref in full_1])
    lags = sum_lags([(full_0[...], FULL, full_table(0)), (full_1, FULL, full_table(1))])
    for step_round in range(2):
        lags_ref[step_round] = (
            before_ref[step_round] + lags[:, step_round * samples : (step_round + 1) * samples]
        )
    for at in range(2):
        table_ref[at] = full_table(2 + at)[0]


def lag_kernel(first_ref, table_ref, *refs):
    picked_refs, (lags_ref, held_ref, sems) = refs[:-3], refs[-3:]
    samples = lags_ref.shape[2]
    runs = sems.shape[0]
    held = held_ref.shape[1] // runs
    picked = [unpack(ref[...], FULL) for ref in picked_refs]
    copies = []
    for run in range(runs):
        rows = slice(run * held, (run + 1) * held)
        more = 0.0
        for at, values in enumerate(picked):
            more += jnp.dot(values[rows], table_ref[at], preferred_element_type=jnp.float32)
        for step_round in range(2):
            held_ref[step_round, rows] = (
                first_ref[step_round, rows] + more[:, step_round * samples : (step_round + 1) * samples]
            )
        copies.append(
            pltpu.make_async_copy(held_ref.at[:, rows], lags_ref.at[:, rows], sems.at[run])
        )
        copies[-1].start()
    for copy in copies:
        copy.wait()


def on_device(windows, counts, pairs):
    comps, _, events, samples = windows.shape
    cells = lax.axis_size("cell")
    half, groups = cells // 2, cells // 4
    count = pairs.shape[2]
    inverse = jnp.asarray(inverse_table(samples, cells))
    place = lax.axis_index("cell").astype(jnp.int32).reshape(1)

    def swap(x, mask):
        return lax.ppermute(x, "cell", [(i, i ^ mask) for i in range(cells)])

    def shape(*dims, dtype=jnp.bfloat16):
        return jax.ShapeDtypeStruct(dims, dtype)

    vmem = pl.BlockSpec(memory_space=pltpu.VMEM)
    smem = pl.BlockSpec(memory_space=pltpu.SMEM)
    params = pltpu.CompilerParams(vmem_limit_bytes=VMEM_LIMIT)

    def cost(microseconds):
        return pl.CostEstimate(
            flops=int(microseconds * 1e9), bytes_accessed=2**20, transcendentals=0
        )

    windows = windows.reshape(comps, 2, groups, 2 * SLOTS, samples)
    near_windows, near_pairs = swap(windows, 1), swap(pairs, 1)
    part_rows, full_rows = comps * 2 * PART, comps * 2 * FULL
    part_spectra, full_spectra, table = pl.pallas_call(
        own_kernel,
        out_shape=[
            shape(groups, part_rows, LANES),
            shape(2 * groups, whole(full_rows, 16), LANES),
            shape(2 * PART + 4 * FULL, samples),
        ],
        in_specs=[smem, vmem],
        out_specs=[vmem] * 3,
        compiler_params=params,
        cost_estimate=cost(1),
        name="own_spectra",
    )(place, windows)
    listing = 2 * pairs.size // LANES
    pieces = pl.pallas_call(
        near_spectra_kernel,
        out_shape=[shape(2 * (part_rows + full_rows), LANES)] * groups
        + [shape(2 * full_rows + listing * (mg == 0), LANES) for mg in range(groups)],
        in_specs=[smem] + [vmem] * 6,
        out_specs=[vmem] * (2 * groups),
        compiler_params=params,
        cost_estimate=cost(1),
        name="near_spectra",
    )(place, pairs, near_pairs, table, part_spectra, full_spectra, near_windows)
    arrived = [pieces[0]] + [swap(pieces[m], 2 * m) for m in range(1, 2 * groups)]
    sides, far = arrived[:groups], arrived[groups:]

    early, late = far[: groups - 2], far[groups - 2 :]
    part_packed = shape(packed_rows(count, PART), LANES)
    full_packed = shape(packed_rows(count, FULL), LANES)
    half_packed = shape(packed_rows(count, FULL) // 2, LANES)
    part_blocks = shape(2, 2, SLOTS * SLOTS * width(PART) // LANES, 2 * LANES)
    full_blocks = shape(2, 2, SLOTS * SLOTS * width(FULL) // LANES, 2 * LANES)
    part_flat = pl.pallas_call(
        part_kernel,
        out_shape=part_blocks,
        in_specs=[vmem] * groups,
        out_specs=vmem,
        scratch_shapes=[
            pltpu.VMEM((padded(groups * 2 * comps) * 2 * PART, LANES), jnp.float32),
            pltpu.VMEM((2 * SLOTS * whole(PART, 8), LANES), jnp.float32),
        ],
        compiler_params=params,
        cost_estimate=cost(0.001),
        name="part",
    )(*sides)
    part_0, part_1 = pl.pallas_call(
        functools.partial(near_kernel, PART, 1),
        out_shape=[part_packed, part_packed],
        in_specs=[smem, smem] + [vmem] * 3,
        out_specs=[vmem] * 2,
        compiler_params=params,
        cost_estimate=cost(0.001),
        name="part_near",
    )(place, counts, pairs, near_pairs, part_flat)
    part_2, part_3 = pl.pallas_call(
        functools.partial(far_kernel, PART),
        out_shape=[part_packed, part_packed],
        in_specs=[smem, smem, vmem, vmem],
        out_specs=[vmem, vmem],
        compiler_params=params,
        cost_estimate=cost(1),
        name="part_far",
    )(place, counts, far[0], part_flat)
    part_1 = swap(part_1, 1)
    sums = pl.pallas_call(
        functools.partial(early_kernel, groups),
        out_shape=shape(2 * SLOTS * FULL, LANES, dtype=jnp.float32),
        in_specs=[pl.BlockSpec(memory_space=pl.ANY)] * 2 + [vmem] * (groups + len(early)),
        out_specs=vmem,
        scratch_shapes=[
            pltpu.VMEM((padded((groups + len(early)) * 2 * comps) * 2 * FULL, LANES), jnp.float32)
        ],
        compiler_params=params,
        cost_estimate=cost(0.001),
        name="early",
    )(part_0, part_2, *sides, *early)
    part_2, part_3 = swap(part_2, half), swap(part_3, half + 1)
    full_flat, full_2, full_3 = pl.pallas_call(
        full_kernel,
        out_shape=[full_blocks, full_packed, full_packed],
        in_specs=[smem, smem] + [vmem] * (2 + len(late)),
        out_specs=[vmem] * 3,
        scratch_shapes=[
            pltpu.VMEM((padded(len(late) * 2 * comps) * 2 * FULL, LANES), jnp.float32),
            pltpu.VMEM((2 * SLOTS * whole(FULL, 8), LANES), jnp.float32),
        ],
        compiler_params=params,
        cost_estimate=cost(10),
        name="full",
    )(place, counts, far[0], sums, *late)
    full_2, full_3 = swap(full_2, half), swap(full_3, half + 1)
    full_0, *full_1 = pl.pallas_call(
        functools.partial(near_kernel, FULL, 2),
        out_shape=[full_packed, half_packed, half_packed],
        in_specs=[smem, smem] + [vmem] * 3,
        out_specs=[vmem] * 3,
        compiler_params=params,
        cost_estimate=cost(0.5),
        name="full_near",
    )(place, counts, pairs, near_pairs, full_flat)
    full_1 = [swap(x, 1) for x in full_1]

    part_lags = pl.pallas_call(
        functools.partial(part_lags_kernel, groups),
        out_shape=shape(2, count, samples, dtype=jnp.float32),
        in_specs=[smem] + [vmem] * 5,
        out_specs=vmem,
        compiler_params=params,
        cost_estimate=cost(0.001),
        name="part_lags",
    )(place, inverse, part_0, part_2, part_3, part_1)
    first, tables = pl.pallas_call(
        functools.partial(first_lags_kernel, groups),
        out_shape=[
            shape(2, count, samples, dtype=jnp.float32),
            shape(2, 4 * FULL, 2 * samples),
        ],
        in_specs=[smem] + [vmem] * 5,
        out_specs=[vmem] * 2,
        compiler_params=params,
        cost_estimate=cost(0.001),
        name="first_lags",
    )(place, inverse, part_lags, full_0, *full_1)
    return pl.pallas_call(
        lag_kernel,
        out_shape=shape(2, count, samples, dtype=jnp.float32),
        in_specs=[vmem] * 4,
        out_specs=pl.BlockSpec(memory_space=pl.ANY),
        scratch_shapes=[
            pltpu.VMEM((2, count, samples), jnp.float32),
            pltpu.SemaphoreType.DMA((4,)),
        ],
        compiler_params=params,
        cost_estimate=cost(1),
        name="lags",
    )(first, tables, full_2, full_3)


def solution(mesh):
    in_specs = (P(None, "cell", "grp", None), P("grp"), P(None, None, ("grp", "cell")))
    out_specs = P(None, ("grp", "cell"), None)
    return jax.shard_map(
        on_device, mesh=mesh, in_specs=in_specs, out_specs=out_specs, check_vma=False
    )
```

```python
import functools
import math

import jax
import jax.numpy as jnp
import numpy as np
from jax import lax
from jax.experimental import pallas as pl
from jax.experimental.pallas import tpu as pltpu
from jax.sharding import PartitionSpec as P

EPSILON = 1e-06
COSINE = (
    0.9999999999993376,
    -4.934802200431432,
    4.058712123240781,
    -1.3352627346923478,
    0.23533044681677665,
    -0.02580633847975355,
    0.0019285963125396874,
    -0.00010362767792380447,
    3.734915399663344e-06,
)
SLOTS = 32
LANES = 4 * SLOTS
COMPS = 3
NT = (((1,), (1,)), ((), ()))
TN = (((0,), (0,)), ((), ()))
VMEM_LIMIT = 40 * 1024 * 1024

PART = 24
FULL = 20


def inverse_table(samples, stations):
    bins = samples // 2
    turn = np.arange(bins)[:, None] * np.arange(samples)[None, :] % samples
    angle = turn * (2.0 * math.pi / samples)
    weight = np.where(np.arange(bins) == 0, 1.0, 2.0)[:, None] / samples
    weight = weight * math.sqrt(samples / (3.0 * stations))
    real, imag = weight * np.cos(angle), -weight * np.sin(angle)
    runs = [(at, PART) for at in range(0, 2 * PART, PART)]
    runs += [(at, FULL) for at in range(2 * PART, bins, FULL)]
    rows = [part[at : at + run] for at, run in runs for part in (real, imag)]
    return np.concatenate(rows).astype(np.float32)


def forward_rows(start, count, samples):
    row = lax.broadcasted_iota(jnp.int32, (2 * count, samples), 0)
    sample = lax.broadcasted_iota(jnp.int32, (2 * count, samples), 1)
    imag = row >= count
    turn = (row + start - jnp.where(imag, count, 0)) * sample + jnp.where(imag, samples // 4, 0)
    turn &= samples - 1
    x = jnp.where(turn > samples // 2, turn - samples, turn).astype(jnp.float32) * (2.0 / samples)
    square = x * x
    value = jnp.full(square.shape, COSINE[-1], jnp.float32)
    for factor in COSINE[-2::-1]:
        value = value * square + factor
    return value


def place_of(place_ref, groups):
    position = place_ref[0]
    high, inner = position // (2 * groups), position % (2 * groups)
    return high * 2 + inner % 2, inner // 2


def listing_of(pairs_ref, lanes):
    ends = []
    for end in range(2):
        slots = pairs_ref[:, end, :].astype(jnp.float32)
        ends += [slots[:, at : at + lanes] for at in range(0, slots.shape[1], lanes)]
    return jnp.concatenate(ends)


def station_spectra(windows_ref, at, table):
    parts = []
    for comp in range(COMPS):
        low = windows_ref[comp, 0, at]
        high = windows_ref[comp, 1, at]
        parts += [low[:SLOTS], high[SLOTS:], low[SLOTS:], high[:SLOTS]]
    traces = jnp.concatenate(parts)
    energy = jnp.sum(jnp.square(traces.astype(jnp.float32)), axis=1, keepdims=True)
    raw = lax.dot_general(traces, table, NT, preferred_element_type=jnp.float32)
    spectra = raw * lax.rsqrt(energy + EPSILON)
    return [spectra[comp * LANES : (comp + 1) * LANES].T for comp in range(COMPS)]


def rows_of(spectra, start, count):
    return jnp.concatenate([lanes[start : start + count] for lanes in spectra])


def own_kernel(place_ref, windows_ref, part_ref, full_ref, table_ref, *fold_refs):
    groups, samples = windows_ref.shape[2], windows_ref.shape[4]
    quarter, group = place_of(place_ref, groups)
    table = [forward_rows((quarter % 2) * PART, PART, samples)]
    for far in range(2):
        table.append(forward_rows(2 * PART + (quarter ^ (2 * far)) * FULL, FULL, samples))
    table = jnp.concatenate(table).astype(jnp.bfloat16)
    table_ref[...] = table
    held = full_ref.shape[1] - COMPS * 2 * FULL
    for fold_ref, bins in zip(fold_refs, (PART, FULL)):
        for at, matrix in enumerate(folds(fold_ref.shape[1], bins)[1]):
            fold_ref[at] = matrix
    for mg in range(groups):
        spectra = station_spectra(windows_ref, group ^ mg, table)
        part_ref[mg] = rows_of(spectra, 0, 2 * PART).astype(jnp.bfloat16)
        for far in range(2):
            rows = rows_of(spectra, 2 * PART + 2 * FULL * far, 2 * FULL)
            if held:
                rows = jnp.concatenate([rows, jnp.zeros((held, LANES), jnp.float32)])
            full_ref[far * groups + mg] = rows.astype(jnp.bfloat16)


def near_spectra_kernel(
    place_ref, own_pairs_ref, near_pairs_ref, table_ref, part_ref, full_ref, windows_ref, *piece_refs
):
    groups = windows_ref.shape[2]
    _, group = place_of(place_ref, groups)
    table = table_ref[...]
    part_rows, full_rows = COMPS * 2 * PART, COMPS * 2 * FULL
    piece_refs[groups][2 * full_rows :] = jnp.concatenate(
        [listing_of(own_pairs_ref, LANES), listing_of(near_pairs_ref, LANES)]
    ).astype(jnp.bfloat16)
    for mg in range(groups):
        spectra = station_spectra(windows_ref, group ^ mg, table)
        side = piece_refs[mg]
        side[:part_rows] = part_ref[mg]
        side[part_rows : 2 * part_rows] = rows_of(spectra, 0, 2 * PART).astype(jnp.bfloat16)
        for far, (piece, start) in enumerate(((side, 2 * part_rows), (piece_refs[groups + mg], 0))):
            own = full_ref[far * groups + mg].astype(jnp.float32)[:full_rows]
            near = rows_of(spectra, 2 * PART + 2 * FULL * far, 2 * FULL)
            piece[start : start + 2 * full_rows] = jnp.concatenate([own, near]).astype(jnp.bfloat16)


def width(bins):
    return 1 << (bins - 1).bit_length()


def packing(count, bins):
    used = 4 * bins
    spare = LANES - used
    runs, rest = used // math.gcd(used, LANES), spare // math.gcd(used, LANES)
    rows = count // (runs + rest)
    parts = []
    for run in range(runs):
        parts.append([(run * rows, 0, 0, used)])
        for extra in range(rest):
            start, end = max(run * spare, extra * used), min((run + 1) * spare, (extra + 1) * used)
            if start < end:
                lane = used + start - run * spare
                parts[-1].append(((runs + extra) * rows, lane, start - extra * used, end - extra * used))
    return rows, parts


def packed_rows(count, bins):
    rows, parts = packing(count, bins)
    return rows * len(parts)


def unpack(picked, bins):
    used = 4 * bins
    runs, rest = used // math.gcd(used, LANES), (LANES - used) // math.gcd(used, LANES)
    rows = picked.shape[0] // runs
    if not rest:
        return picked
    spare = jnp.concatenate([picked[run * rows : (run + 1) * rows, used:] for run in range(runs)], axis=1)
    return jnp.concatenate(
        [picked[:, :used]] + [spare[:, extra * used : (extra + 1) * used] for extra in range(rest)]
    )


def sides_of(place_ref, cells, mq):
    quarter, group = place_of(place_ref, cells // 4)
    own = quarter ^ mq
    high, low = own // 2, own % 2
    return high * (cells // 2) + group * 2 + low, high, low, ((high, high), (low, 1 - low))


def hots(place_ref, counts_ref, listed, rows, bins, mq):
    cells = counts_ref.shape[0]
    cell, high, low, _ = sides_of(place_ref, cells, mq)
    count = listed.shape[0] // 2
    runs = LANES // width(bins)
    run_bits, bin_bits = (n.bit_length() - 1 for n in (runs, width(bins)))
    first, second = listed[:count].astype(jnp.int32), listed[count:].astype(jnp.int32)
    far_counts = [counts_ref[cell ^ 1], counts_ref[cell ^ (cells // 2)]]
    odd = lax.broadcasted_iota(jnp.int32, (count, LANES), 0) & 1
    live = (first < counts_ref[cell]) & (second < jnp.where(odd == 1, far_counts[1], far_counts[0]))
    left, right = jnp.where(high == low, first, second), jnp.where(high == low, second, first)
    spot = jnp.where(live, (left >> run_bits) * SLOTS + right, -1)
    turned = (spot * runs + (left & (runs - 1))).T
    lane = lax.broadcasted_iota(jnp.int32, (LANES, LANES), 1)
    run = lane >> bin_bits
    found = []
    for step_round in range(2):
        hot, here = [], []
        for at in range(step_round, count, 2):
            both = jnp.broadcast_to(turned[:, at : at + 1], (LANES, LANES))
            here.append(jnp.where((both & (runs - 1)) == run, 1.0, 0.0).astype(jnp.bfloat16))
            offset = (both >> run_bits) - lane
            hot.append(
                jnp.concatenate(
                    [
                        jnp.where(offset == start, 1.0, 0.0).astype(jnp.bfloat16)
                        for start in range(0, rows, LANES)
                    ],
                    axis=1,
                )
            )
        found.append((jnp.concatenate(hot), jnp.concatenate(here)))
    return found


def folds_of(count, bins):
    return sorted({entry[1:] for entries in packing(count, bins)[1] for entry in entries})


def folds(count, bins):
    spread = lax.broadcasted_iota(jnp.int32, (4 * LANES, LANES), 0)
    kept = lax.broadcasted_iota(jnp.int32, (4 * LANES, LANES), 1)
    bin_of = spread & (width(bins) - 1)
    value = jnp.where(bin_of < bins, (spread >> (LANES.bit_length() - 1)) * bins + bin_of, -1)
    kinds = folds_of(count, bins)
    matrices = []
    for at, least, end in kinds:
        fold = (value >= least) & (value < end) & (kept == value + (at - least))
        matrices.append(jnp.where(fold, 1.0, 0.0).astype(jnp.bfloat16))
    return kinds, matrices


def picks(place_ref, cells, hot, kinds, matrices, flat_ref, bins, mq):
    _, _, _, sides = sides_of(place_ref, cells, mq)
    found = []
    for (rows, lanes), (own, far) in zip(hot, sides):
        wide = jnp.dot(rows, flat_ref[own, far], preferred_element_type=jnp.float32).astype(jnp.bfloat16)
        found += [wide[:, :LANES] * lanes, wide[:, LANES:] * lanes]
    found = jnp.concatenate(found, axis=1)
    held, parts = packing(found.shape[0], bins)
    picked = []
    for entries in parts:
        total = 0.0
        for start, *kind in entries:
            total += jnp.dot(
                found[start : start + held],
                matrices[kinds.index(tuple(kind))],
                preferred_element_type=jnp.float32,
            )
        picked.append(total.astype(jnp.bfloat16))
    return jnp.concatenate(picked)


def pick(place_ref, counts_ref, listed, flat_ref, fold_ref, bins, mq, *picked_refs):
    hot = hots(place_ref, counts_ref, listed, flat_ref.shape[2], bins, mq)
    kinds = folds_of(listed.shape[0] // 4 * LANES, bins)
    matrices = [fold_ref[at] for at in range(len(kinds))]
    picked = picks(place_ref, counts_ref.shape[0], hot, kinds, matrices, flat_ref, bins, mq)
    each = picked.shape[0] // len(picked_refs)
    for at, ref in enumerate(picked_refs):
        ref[...] = picked[at * each : (at + 1) * each]


def whole(count, tile):
    return -(-count // tile) * tile


def padded(traces):
    return whole(traces, 16)


def add_cross(pieces, trace_ref, bins, sums_ref, before_ref=None):
    slots, rows = 2 * SLOTS, 2 * bins
    traces = trace_ref.shape[0] // rows
    start = 0
    for piece, at, size in pieces:
        trace_ref[start : start + size] = piece[at : at + size].astype(jnp.float32)
        start += size
    if start < traces * rows:
        trace_ref[start:] = jnp.zeros((traces * rows - start, LANES), jnp.float32)
    lower = lax.broadcasted_iota(jnp.int32, (traces, LANES), 1) < slots
    for k in range(bins):
        real = trace_ref[pl.ds(k, traces, stride=rows), :]
        imag = trace_ref[pl.ds(bins + k, traces, stride=rows), :]
        left = jnp.concatenate([real, imag]).astype(jnp.bfloat16)[:, :slots]
        right = jnp.concatenate(
            [
                jnp.where(lower, pltpu.roll(real, slots, 1), imag),
                jnp.where(lower, pltpu.roll(imag, slots, 1), -real),
            ]
        ).astype(jnp.bfloat16)
        cross = lax.dot_general(left, right, TN, preferred_element_type=jnp.float32)
        if before_ref is not None:
            cross += before_ref[k * slots : (k + 1) * slots]
        sums_ref[k * slots : (k + 1) * slots] = cross


def turn_blocks(cross_ref, bins, flat_ref):
    slots, runs = 2 * SLOTS, LANES // width(bins)
    held = cross_ref.shape[0] // slots
    if held > bins:
        cross_ref[bins * slots :] = jnp.zeros(((held - bins) * slots, LANES), jnp.float32)
    empty = jnp.zeros((width(bins) - held, LANES), jnp.float32)
    for own in range(2):
        for at in range(SLOTS // runs):
            block = []
            for i in range(runs):
                block.append(cross_ref[pl.ds(own * SLOTS + at * runs + i, held, stride=slots), :])
                block += [empty] * (held < width(bins))
            block = jnp.concatenate(block).astype(jnp.bfloat16).T
            for part in range(2):
                for far in range(2):
                    start = (part * 2 + far) * SLOTS
                    flat_ref[
                        own, far, at * SLOTS : (at + 1) * SLOTS, part * LANES : (part + 1) * LANES
                    ] = block[start : start + SLOTS]


def side_part(ref):
    return (ref, 0, 2 * COMPS * 2 * PART)


def side_full(ref):
    return (ref, 2 * COMPS * 2 * PART, 2 * COMPS * 2 * FULL)


def cross_full(ref):
    return (ref, 0, 2 * COMPS * 2 * FULL)


def part_kernel(*refs):
    piece_refs, (flat_ref, trace_ref, cross_ref) = refs[:-3], refs[-3:]
    add_cross([side_part(ref) for ref in piece_refs], trace_ref, PART, cross_ref)
    turn_blocks(cross_ref, PART, flat_ref)


def far_kernel(bins, place_ref, counts_ref, listed_ref, flat_ref, fold_ref, picked_0, picked_1):
    listed = listed_ref[cross_full(listed_ref)[2] :].astype(jnp.float32)
    listing = listed.shape[0] // 2
    pick(place_ref, counts_ref, listed[:listing], flat_ref, fold_ref, bins, 2, picked_0)
    pick(place_ref, counts_ref, listed[listing:], flat_ref, fold_ref, bins, 3, picked_1)


def early_kernel(sides, after_0, after_1, *refs):
    piece_refs, (sums_ref, trace_ref) = refs[:-2], refs[-2:]
    pieces = [side_full(ref) for ref in piece_refs[:sides]] + [cross_full(ref) for ref in piece_refs[sides:]]
    add_cross(pieces, trace_ref, FULL, sums_ref)


def full_kernel(place_ref, counts_ref, listed_ref, fold_ref, before_ref, *refs):
    piece_refs, (flat_ref, picked_0, picked_1, trace_ref, cross_ref) = refs[:-5], refs[-5:]
    add_cross([cross_full(ref) for ref in piece_refs], trace_ref, FULL, cross_ref, before_ref)
    turn_blocks(cross_ref, FULL, flat_ref)
    listed = listed_ref[cross_full(listed_ref)[2] :].astype(jnp.float32)
    listing = listed.shape[0] // 2
    pick(place_ref, counts_ref, listed[:listing], flat_ref, fold_ref, FULL, 2, picked_0)
    pick(place_ref, counts_ref, listed[listing:], flat_ref, fold_ref, FULL, 3, picked_1)


def near_kernel(bins, sent, place_ref, counts_ref, own_pairs_ref, near_pairs_ref, flat_ref, fold_ref, *refs):
    picked_0, *picked_1 = refs[-1 - sent :]
    pick(place_ref, counts_ref, listing_of(near_pairs_ref, LANES), flat_ref, fold_ref, bins, 1, *picked_1)
    pick(place_ref, counts_ref, listing_of(own_pairs_ref, LANES), flat_ref, fold_ref, bins, 0, picked_0)


def both_rounds(rows, sign):
    row = lax.broadcasted_iota(jnp.int32, rows.shape, 0)
    rows = rows * jnp.where(row < rows.shape[0] // 2, 1.0, sign)
    empty = jnp.zeros_like(rows)
    return jnp.concatenate(
        [jnp.concatenate([rows, empty], axis=1), jnp.concatenate([empty, rows], axis=1)]
    )


def halves(table):
    high = table.astype(jnp.bfloat16)
    return high, (table - high.astype(jnp.float32)).astype(jnp.bfloat16)


def tables_of(groups, place_ref, inverse_ref):
    quarter, _ = place_of(place_ref, groups)
    low = quarter % 2
    sign = jnp.where(quarter // 2 == low, 1.0, -1.0)

    def part_table(which):
        start = pl.multiple_of((low ^ which) * 2 * PART, 2 * PART)
        return halves(both_rounds(inverse_ref[pl.ds(start, 2 * PART), :], sign))

    def full_table(mq):
        start = pl.multiple_of(4 * PART + (quarter ^ mq) * 2 * FULL, 2 * FULL)
        return halves(both_rounds(inverse_ref[pl.ds(start, 2 * FULL), :], sign))

    return part_table, full_table


def sum_lags(terms):
    lags = 0.0
    for picked, bins, table in terms:
        picked = unpack(picked, bins)
        for half in table:
            lags += jnp.dot(picked, half, preferred_element_type=jnp.float32)
    return lags


def part_lags_kernel(groups, place_ref, inverse_ref, part_0, part_2, part_3, part_1, lags_ref):
    samples = inverse_ref.shape[1]
    part_table, _ = tables_of(groups, place_ref, inverse_ref)
    near, other = part_table(0), part_table(1)
    lags = sum_lags(
        [
            (part_0[...], PART, near),
            (part_2[...], PART, near),
            (part_1[...], PART, other),
            (part_3[...], PART, other),
        ]
    )
    for step_round in range(2):
        lags_ref[step_round] = lags[:, step_round * samples : (step_round + 1) * samples]


def first_lags_kernel(groups, place_ref, inverse_ref, before_ref, full_0, *refs):
    full_1, (lags_ref, table_ref) = refs[:-2], refs[-2:]
    samples = inverse_ref.shape[1]
    _, full_table = tables_of(groups, place_ref, inverse_ref)
    full_1 = jnp.concatenate([ref[...] for ref in full_1])
    lags = sum_lags([(full_0[...], FULL, full_table(0)), (full_1, FULL, full_table(1))])
    for step_round in range(2):
        lags_ref[step_round] = (
            before_ref[step_round] + lags[:, step_round * samples : (step_round + 1) * samples]
        )
    for at in range(2):
        table_ref[at] = full_table(2 + at)[0]


def lag_kernel(first_ref, table_ref, *refs):
    picked_refs, (lags_ref, held_ref, sems) = refs[:-3], refs[-3:]
    samples = lags_ref.shape[2]
    runs = sems.shape[0]
    held = held_ref.shape[1] // runs
    picked = [unpack(ref[...], FULL) for ref in picked_refs]
    copies = []
    for run in range(runs):
        rows = slice(run * held, (run + 1) * held)
        more = 0.0
        for at, values in enumerate(picked):
            more += jnp.dot(values[rows], table_ref[at], preferred_element_type=jnp.float32)
        for step_round in range(2):
            held_ref[step_round, rows] = (
                first_ref[step_round, rows] + more[:, step_round * samples : (step_round + 1) * samples]
            )
        copies.append(
            pltpu.make_async_copy(held_ref.at[:, rows], lags_ref.at[:, rows], sems.at[run])
        )
        copies[-1].start()
    for copy in copies:
        copy.wait()


def on_device(windows, counts, pairs):
    comps, _, events, samples = windows.shape
    cells = lax.axis_size("cell")
    half, groups = cells // 2, cells // 4
    count = pairs.shape[2]
    inverse = jnp.asarray(inverse_table(samples, cells))
    place = lax.axis_index("cell").astype(jnp.int32).reshape(1)

    def swap(x, mask):
        return lax.ppermute(x, "cell", [(i, i ^ mask) for i in range(cells)])

    def shape(*dims, dtype=jnp.bfloat16):
        return jax.ShapeDtypeStruct(dims, dtype)

    vmem = pl.BlockSpec(memory_space=pltpu.VMEM)
    smem = pl.BlockSpec(memory_space=pltpu.SMEM)
    params = pltpu.CompilerParams(vmem_limit_bytes=VMEM_LIMIT)

    def cost(microseconds):
        return pl.CostEstimate(
            flops=int(microseconds * 1e9), bytes_accessed=2**20, transcendentals=0
        )

    windows = windows.reshape(comps, 2, groups, 2 * SLOTS, samples)
    near_windows, near_pairs = swap(windows, 1), swap(pairs, 1)
    part_rows, full_rows = comps * 2 * PART, comps * 2 * FULL
    part_spectra, full_spectra, table, part_fold, full_fold = pl.pallas_call(
        own_kernel,
        out_shape=[
            shape(groups, part_rows, LANES),
            shape(2 * groups, whole(full_rows, 16), LANES),
            shape(2 * PART + 4 * FULL, samples),
            shape(len(folds_of(count, PART)), 4 * LANES, LANES),
            shape(len(folds_of(count, FULL)), 4 * LANES, LANES),
        ],
        in_specs=[smem, vmem],
        out_specs=[vmem] * 5,
        compiler_params=params,
        cost_estimate=cost(1),
        name="own_spectra",
    )(place, windows)
    listing = 2 * pairs.size // LANES
    pieces = pl.pallas_call(
        near_spectra_kernel,
        out_shape=[shape(2 * (part_rows + full_rows), LANES)] * groups
        + [shape(2 * full_rows + listing * (mg == 0), LANES) for mg in range(groups)],
        in_specs=[smem] + [vmem] * 6,
        out_specs=[vmem] * (2 * groups),
        compiler_params=params,
        cost_estimate=cost(1),
        name="near_spectra",
    )(place, pairs, near_pairs, table, part_spectra, full_spectra, near_windows)
    arrived = [pieces[0]] + [swap(pieces[m], 2 * m) for m in range(1, 2 * groups)]
    sides, far = arrived[:groups], arrived[groups:]

    early, late = far[: groups - 2], far[groups - 2 :]
    part_packed = shape(packed_rows(count, PART), LANES)
    full_packed = shape(packed_rows(count, FULL), LANES)
    half_packed = shape(packed_rows(count, FULL) // 2, LANES)
    part_blocks = shape(2, 2, SLOTS * SLOTS * width(PART) // LANES, 2 * LANES)
    full_blocks = shape(2, 2, SLOTS * SLOTS * width(FULL) // LANES, 2 * LANES)
    part_flat = pl.pallas_call(
        part_kernel,
        out_shape=part_blocks,
        in_specs=[vmem] * groups,
        out_specs=vmem,
        scratch_shapes=[
            pltpu.VMEM((padded(groups * 2 * comps) * 2 * PART, LANES), jnp.float32),
            pltpu.VMEM((2 * SLOTS * whole(PART, 8), LANES), jnp.float32),
        ],
        compiler_params=params,
        cost_estimate=cost(0.001),
        name="part",
    )(*sides)
    part_0, part_1 = pl.pallas_call(
        functools.partial(near_kernel, PART, 1),
        out_shape=[part_packed, part_packed],
        in_specs=[smem, smem] + [vmem] * 4,
        out_specs=[vmem] * 2,
        compiler_params=params,
        cost_estimate=cost(0.001),
        name="part_near",
    )(place, counts, pairs, near_pairs, part_flat, part_fold)
    part_2, part_3 = pl.pallas_call(
        functools.partial(far_kernel, PART),
        out_shape=[part_packed, part_packed],
        in_specs=[smem, smem, vmem, vmem, vmem],
        out_specs=[vmem, vmem],
        compiler_params=params,
        cost_estimate=cost(1),
        name="part_far",
    )(place, counts, far[0], part_flat, part_fold)
    part_1 = swap(part_1, 1)
    sums = pl.pallas_call(
        functools.partial(early_kernel, groups),
        out_shape=shape(2 * SLOTS * FULL, LANES, dtype=jnp.float32),
        in_specs=[pl.BlockSpec(memory_space=pl.ANY)] * 2 + [vmem] * (groups + len(early)),
        out_specs=vmem,
        scratch_shapes=[
            pltpu.VMEM((padded((groups + len(early)) * 2 * comps) * 2 * FULL, LANES), jnp.float32)
        ],
        compiler_params=params,
        cost_estimate=cost(0.001),
        name="early",
    )(part_0, part_2, *sides, *early)
    part_2, part_3 = swap(part_2, half), swap(part_3, half + 1)
    full_flat, full_2, full_3 = pl.pallas_call(
        full_kernel,
        out_shape=[full_blocks, full_packed, full_packed],
        in_specs=[smem, smem] + [vmem] * (3 + len(late)),
        out_specs=[vmem] * 3,
        scratch_shapes=[
            pltpu.VMEM((padded(len(late) * 2 * comps) * 2 * FULL, LANES), jnp.float32),
            pltpu.VMEM((2 * SLOTS * whole(FULL, 8), LANES), jnp.float32),
        ],
        compiler_params=params,
        cost_estimate=cost(10),
        name="full",
    )(place, counts, far[0], full_fold, sums, *late)
    full_2, full_3 = swap(full_2, half), swap(full_3, half + 1)
    full_0, *full_1 = pl.pallas_call(
        functools.partial(near_kernel, FULL, 2),
        out_shape=[full_packed, half_packed, half_packed],
        in_specs=[smem, smem] + [vmem] * 4,
        out_specs=[vmem] * 3,
        compiler_params=params,
        cost_estimate=cost(0.5),
        name="full_near",
    )(place, counts, pairs, near_pairs, full_flat, full_fold)
    full_1 = [swap(x, 1) for x in full_1]

    part_lags = pl.pallas_call(
        functools.partial(part_lags_kernel, groups),
        out_shape=shape(2, count, samples, dtype=jnp.float32),
        in_specs=[smem] + [vmem] * 5,
        out_specs=vmem,
        compiler_params=params,
        cost_estimate=cost(0.001),
        name="part_lags",
    )(place, inverse, part_0, part_2, part_3, part_1)
    first, tables = pl.pallas_call(
        functools.partial(first_lags_kernel, groups),
        out_shape=[
            shape(2, count, samples, dtype=jnp.float32),
            shape(2, 4 * FULL, 2 * samples),
        ],
        in_specs=[smem] + [vmem] * 5,
        out_specs=[vmem] * 2,
        compiler_params=params,
        cost_estimate=cost(0.001),
        name="first_lags",
    )(place, inverse, part_lags, full_0, *full_1)
    return pl.pallas_call(
        lag_kernel,
        out_shape=shape(2, count, samples, dtype=jnp.float32),
        in_specs=[vmem] * 4,
        out_specs=pl.BlockSpec(memory_space=pl.ANY),
        scratch_shapes=[
            pltpu.VMEM((2, count, samples), jnp.float32),
            pltpu.SemaphoreType.DMA((4,)),
        ],
        compiler_params=params,
        cost_estimate=cost(1),
        name="lags",
    )(first, tables, full_2, full_3)


def solution(mesh):
    in_specs = (P(None, "cell", "grp", None), P("grp"), P(None, None, ("grp", "cell")))
    out_specs = P(None, ("grp", "cell"), None)
    return jax.shard_map(
        on_device, mesh=mesh, in_specs=in_specs, out_specs=out_specs, check_vma=False
    )
```

```python
import functools
import math

import jax
import jax.numpy as jnp
import numpy as np
from jax import lax
from jax.experimental import pallas as pl
from jax.experimental.pallas import tpu as pltpu
from jax.sharding import PartitionSpec as P

EPSILON = 1e-06
COSINE = (
    0.9999999999993376,
    -4.934802200431432,
    4.058712123240781,
    -1.3352627346923478,
    0.23533044681677665,
    -0.02580633847975355,
    0.0019285963125396874,
    -0.00010362767792380447,
    3.734915399663344e-06,
)
SLOTS = 32
LANES = 4 * SLOTS
COMPS = 3
NT = (((1,), (1,)), ((), ()))
TN = (((0,), (0,)), ((), ()))
VMEM_LIMIT = 40 * 1024 * 1024

PART = 24
FULL = 20


def inverse_table(samples, stations):
    bins = samples // 2
    turn = np.arange(bins)[:, None] * np.arange(samples)[None, :] % samples
    angle = turn * (2.0 * math.pi / samples)
    weight = np.where(np.arange(bins) == 0, 1.0, 2.0)[:, None] / samples
    weight = weight * math.sqrt(samples / (3.0 * stations))
    real, imag = weight * np.cos(angle), -weight * np.sin(angle)
    runs = [(at, PART) for at in range(0, 2 * PART, PART)]
    runs += [(at, FULL) for at in range(2 * PART, bins, FULL)]
    rows = [part[at : at + run] for at, run in runs for part in (real, imag)]
    return np.concatenate(rows).astype(np.float32)


def forward_rows(start, count, samples):
    row = lax.broadcasted_iota(jnp.int32, (2 * count, samples), 0)
    sample = lax.broadcasted_iota(jnp.int32, (2 * count, samples), 1)
    imag = row >= count
    turn = (row + start - jnp.where(imag, count, 0)) * sample + jnp.where(imag, samples // 4, 0)
    turn &= samples - 1
    x = jnp.where(turn > samples // 2, turn - samples, turn).astype(jnp.float32) * (2.0 / samples)
    square = x * x
    value = jnp.full(square.shape, COSINE[-1], jnp.float32)
    for factor in COSINE[-2::-1]:
        value = value * square + factor
    return value


def place_of(place_ref, groups):
    position = place_ref[0]
    high, inner = position // (2 * groups), position % (2 * groups)
    return high * 2 + inner % 2, inner // 2


def listing_of(pairs_ref, lanes):
    ends = []
    for end in range(2):
        slots = pairs_ref[:, end, :].astype(jnp.float32)
        ends += [slots[:, at : at + lanes] for at in range(0, slots.shape[1], lanes)]
    return jnp.concatenate(ends)


def station_spectra(windows_ref, at, table):
    parts = []
    for comp in range(COMPS):
        low = windows_ref[comp, 0, at]
        high = windows_ref[comp, 1, at]
        parts += [low[:SLOTS], high[SLOTS:], low[SLOTS:], high[:SLOTS]]
    traces = jnp.concatenate(parts)
    energy = jnp.sum(jnp.square(traces.astype(jnp.float32)), axis=1, keepdims=True)
    raw = lax.dot_general(traces, table, NT, preferred_element_type=jnp.float32)
    spectra = raw * lax.rsqrt(energy + EPSILON)
    return [spectra[comp * LANES : (comp + 1) * LANES].T for comp in range(COMPS)]


def rows_of(spectra, start, count):
    return jnp.concatenate([lanes[start : start + count] for lanes in spectra])


def own_kernel(place_ref, windows_ref, part_ref, full_ref, table_ref):
    groups, samples = windows_ref.shape[2], windows_ref.shape[4]
    quarter, group = place_of(place_ref, groups)
    table = [forward_rows((quarter % 2) * PART, PART, samples)]
    for far in range(2):
        table.append(forward_rows(2 * PART + (quarter ^ (2 * far)) * FULL, FULL, samples))
    table = jnp.concatenate(table).astype(jnp.bfloat16)
    table_ref[...] = table
    held = full_ref.shape[1] - COMPS * 2 * FULL
    for mg in range(groups):
        spectra = station_spectra(windows_ref, group ^ mg, table)
        part_ref[mg] = rows_of(spectra, 0, 2 * PART).astype(jnp.bfloat16)
        for far in range(2):
            rows = rows_of(spectra, 2 * PART + 2 * FULL * far, 2 * FULL)
            if held:
                rows = jnp.concatenate([rows, jnp.zeros((held, LANES), jnp.float32)])
            full_ref[far * groups + mg] = rows.astype(jnp.bfloat16)


def near_spectra_kernel(
    place_ref, own_pairs_ref, near_pairs_ref, table_ref, part_ref, full_ref, windows_ref, *piece_refs
):
    groups = windows_ref.shape[2]
    _, group = place_of(place_ref, groups)
    table = table_ref[...]
    part_rows, full_rows = COMPS * 2 * PART, COMPS * 2 * FULL
    piece_refs[groups][2 * full_rows :] = jnp.concatenate(
        [listing_of(own_pairs_ref, LANES), listing_of(near_pairs_ref, LANES)]
    ).astype(jnp.bfloat16)
    for mg in range(groups):
        spectra = station_spectra(windows_ref, group ^ mg, table)
        side = piece_refs[mg]
        side[:part_rows] = part_ref[mg]
        side[part_rows : 2 * part_rows] = rows_of(spectra, 0, 2 * PART).astype(jnp.bfloat16)
        for far, (piece, start) in enumerate(((side, 2 * part_rows), (piece_refs[groups + mg], 0))):
            own = full_ref[far * groups + mg].astype(jnp.float32)[:full_rows]
            near = rows_of(spectra, 2 * PART + 2 * FULL * far, 2 * FULL)
            piece[start : start + 2 * full_rows] = jnp.concatenate([own, near]).astype(jnp.bfloat16)


def width(bins):
    return 1 << (bins - 1).bit_length()


def packing(count, bins):
    used = 4 * bins
    spare = LANES - used
    runs, rest = used // math.gcd(used, LANES), spare // math.gcd(used, LANES)
    rows = count // (runs + rest)
    parts = []
    for run in range(runs):
        parts.append([(run * rows, 0, 0, used)])
        for extra in range(rest):
            start, end = max(run * spare, extra * used), min((run + 1) * spare, (extra + 1) * used)
            if start < end:
                lane = used + start - run * spare
                parts[-1].append(((runs + extra) * rows, lane, start - extra * used, end - extra * used))
    return rows, parts


def packed_rows(count, bins):
    rows, parts = packing(count, bins)
    return rows * len(parts)


def unpack(picked, bins):
    used = 4 * bins
    runs, rest = used // math.gcd(used, LANES), (LANES - used) // math.gcd(used, LANES)
    rows = picked.shape[0] // runs
    if not rest:
        return picked
    spare = jnp.concatenate([picked[run * rows : (run + 1) * rows, used:] for run in range(runs)], axis=1)
    return jnp.concatenate(
        [picked[:, :used]] + [spare[:, extra * used : (extra + 1) * used] for extra in range(rest)]
    )


def sides_of(place_ref, cells, mq):
    quarter, group = place_of(place_ref, cells // 4)
    own = quarter ^ mq
    high, low = own // 2, own % 2
    return high * (cells // 2) + group * 2 + low, high, low, ((high, high), (low, 1 - low))


def hots(place_ref, counts_ref, listed, rows, bins, mq):
    cells = counts_ref.shape[0]
    cell, high, low, _ = sides_of(place_ref, cells, mq)
    count = listed.shape[0] // 2
    runs = LANES // width(bins)
    run_bits, bin_bits = (n.bit_length() - 1 for n in (runs, width(bins)))
    first, second = listed[:count].astype(jnp.int32), listed[count:].astype(jnp.int32)
    far_counts = [counts_ref[cell ^ 1], counts_ref[cell ^ (cells // 2)]]
    odd = lax.broadcasted_iota(jnp.int32, (count, LANES), 0) & 1
    live = (first < counts_ref[cell]) & (second < jnp.where(odd == 1, far_counts[1], far_counts[0]))
    left, right = jnp.where(high == low, first, second), jnp.where(high == low, second, first)
    spot = jnp.where(live, (left >> run_bits) * SLOTS + right, -1)
    turned = (spot * runs + (left & (runs - 1))).T
    lane = lax.broadcasted_iota(jnp.int32, (LANES, LANES), 1)
    run = lane >> bin_bits
    found = []
    for step_round in range(2):
        hot, here = [], []
        for at in range(step_round, count, 2):
            both = jnp.broadcast_to(turned[:, at : at + 1], (LANES, LANES))
            here.append(jnp.where((both & (runs - 1)) == run, 1.0, 0.0).astype(jnp.bfloat16))
            offset = (both >> run_bits) - lane
            hot.append(
                jnp.concatenate(
                    [
                        jnp.where(offset == start, 1.0, 0.0).astype(jnp.bfloat16)
                        for start in range(0, rows, LANES)
                    ],
                    axis=1,
                )
            )
        found.append((jnp.concatenate(hot), jnp.concatenate(here)))
    return found


def folds_of(count, bins):
    return sorted({entry[1:] for entries in packing(count, bins)[1] for entry in entries})


def folds(count, bins):
    spread = lax.broadcasted_iota(jnp.int32, (4 * LANES, LANES), 0)
    kept = lax.broadcasted_iota(jnp.int32, (4 * LANES, LANES), 1)
    bin_of = spread & (width(bins) - 1)
    value = jnp.where(bin_of < bins, (spread >> (LANES.bit_length() - 1)) * bins + bin_of, -1)
    kinds = folds_of(count, bins)
    matrices = []
    for at, least, end in kinds:
        fold = (value >= least) & (value < end) & (kept == value + (at - least))
        matrices.append(jnp.where(fold, 1.0, 0.0).astype(jnp.bfloat16))
    return kinds, matrices


def picks(place_ref, cells, hot, kinds, matrices, flat_ref, bins, mq):
    _, _, _, sides = sides_of(place_ref, cells, mq)
    found = []
    for (rows, lanes), (own, far) in zip(hot, sides):
        wide = jnp.dot(rows, flat_ref[own, far], preferred_element_type=jnp.float32).astype(jnp.bfloat16)
        found += [wide[:, :LANES] * lanes, wide[:, LANES:] * lanes]
    found = jnp.concatenate(found, axis=1)
    held, parts = packing(found.shape[0], bins)
    picked = []
    for entries in parts:
        total = 0.0
        for start, *kind in entries:
            total += jnp.dot(
                found[start : start + held],
                matrices[kinds.index(tuple(kind))],
                preferred_element_type=jnp.float32,
            )
        picked.append(total.astype(jnp.bfloat16))
    return jnp.concatenate(picked)


def pick(place_ref, counts_ref, listed, flat_ref, bins, mq, *picked_refs):
    hot = hots(place_ref, counts_ref, listed, flat_ref.shape[2], bins, mq)
    kinds, matrices = folds(listed.shape[0] // 4 * LANES, bins)
    picked = picks(place_ref, counts_ref.shape[0], hot, kinds, matrices, flat_ref, bins, mq)
    each = picked.shape[0] // len(picked_refs)
    for at, ref in enumerate(picked_refs):
        ref[...] = picked[at * each : (at + 1) * each]


def whole(count, tile):
    return -(-count // tile) * tile


def padded(traces):
    return whole(traces, 16)


def add_cross(pieces, trace_ref, bins, sums_ref, before_ref=None):
    slots, rows = 2 * SLOTS, 2 * bins
    traces = trace_ref.shape[0] // rows
    start = 0
    for piece, at, size in pieces:
        trace_ref[start : start + size] = piece[at : at + size].astype(jnp.float32)
        start += size
    if start < traces * rows:
        trace_ref[start:] = jnp.zeros((traces * rows - start, LANES), jnp.float32)
    lower = lax.broadcasted_iota(jnp.int32, (traces, LANES), 1) < slots
    for k in range(bins):
        real = trace_ref[pl.ds(k, traces, stride=rows), :]
        imag = trace_ref[pl.ds(bins + k, traces, stride=rows), :]
        left = jnp.concatenate([real, imag]).astype(jnp.bfloat16)[:, :slots]
        right = jnp.concatenate(
            [
                jnp.where(lower, pltpu.roll(real, slots, 1), imag),
                jnp.where(lower, pltpu.roll(imag, slots, 1), -real),
            ]
        ).astype(jnp.bfloat16)
        cross = lax.dot_general(left, right, TN, preferred_element_type=jnp.float32)
        if before_ref is not None:
            cross += before_ref[k * slots : (k + 1) * slots]
        sums_ref[k * slots : (k + 1) * slots] = cross


def turn_blocks(cross_ref, bins, flat_ref):
    slots, runs = 2 * SLOTS, LANES // width(bins)
    held = cross_ref.shape[0] // slots
    if held > bins:
        cross_ref[bins * slots :] = jnp.zeros(((held - bins) * slots, LANES), jnp.float32)
    empty = jnp.zeros((width(bins) - held, LANES), jnp.float32)
    for own in range(2):
        for at in range(SLOTS // runs):
            block = []
            for i in range(runs):
                block.append(cross_ref[pl.ds(own * SLOTS + at * runs + i, held, stride=slots), :])
                block += [empty] * (held < width(bins))
            block = jnp.concatenate(block).astype(jnp.bfloat16).T
            for part in range(2):
                for far in range(2):
                    start = (part * 2 + far) * SLOTS
                    flat_ref[
                        own, far, at * SLOTS : (at + 1) * SLOTS, part * LANES : (part + 1) * LANES
                    ] = block[start : start + SLOTS]


def side_part(ref):
    return (ref, 0, 2 * COMPS * 2 * PART)


def side_full(ref):
    return (ref, 2 * COMPS * 2 * PART, 2 * COMPS * 2 * FULL)


def cross_full(ref):
    return (ref, 0, 2 * COMPS * 2 * FULL)


def part_kernel(*refs):
    piece_refs, (flat_ref, trace_ref, cross_ref) = refs[:-3], refs[-3:]
    add_cross([side_part(ref) for ref in piece_refs], trace_ref, PART, cross_ref)
    turn_blocks(cross_ref, PART, flat_ref)


def far_kernel(bins, place_ref, counts_ref, listed_ref, flat_ref, picked_0, picked_1):
    listed = listed_ref[cross_full(listed_ref)[2] :].astype(jnp.float32)
    listing = listed.shape[0] // 2
    pick(place_ref, counts_ref, listed[:listing], flat_ref, bins, 2, picked_0)
    pick(place_ref, counts_ref, listed[listing:], flat_ref, bins, 3, picked_1)


def full_kernel(sides, place_ref, counts_ref, listed_ref, after_0, after_1, *refs):
    piece_refs, (flat_ref, picked_0, picked_1, trace_ref, cross_ref) = refs[:-5], refs[-5:]
    pieces = [side_full(ref) for ref in piece_refs[:sides]] + [cross_full(ref) for ref in piece_refs[sides:]]
    add_cross(pieces, trace_ref, FULL, cross_ref)
    turn_blocks(cross_ref, FULL, flat_ref)
    listed = listed_ref[cross_full(listed_ref)[2] :].astype(jnp.float32)
    listing = listed.shape[0] // 2
    pick(place_ref, counts_ref, listed[:listing], flat_ref, FULL, 2, picked_0)
    pick(place_ref, counts_ref, listed[listing:], flat_ref, FULL, 3, picked_1)


def near_kernel(bins, sent, place_ref, counts_ref, own_pairs_ref, near_pairs_ref, flat_ref, *refs):
    picked_0, *picked_1 = refs[-1 - sent :]
    pick(place_ref, counts_ref, listing_of(near_pairs_ref, LANES), flat_ref, bins, 1, *picked_1)
    pick(place_ref, counts_ref, listing_of(own_pairs_ref, LANES), flat_ref, bins, 0, picked_0)


def both_rounds(rows, sign):
    row = lax.broadcasted_iota(jnp.int32, rows.shape, 0)
    rows = rows * jnp.where(row < rows.shape[0] // 2, 1.0, sign)
    empty = jnp.zeros_like(rows)
    return jnp.concatenate(
        [jnp.concatenate([rows, empty], axis=1), jnp.concatenate([empty, rows], axis=1)]
    )


def halves(table):
    high = table.astype(jnp.bfloat16)
    return high, (table - high.astype(jnp.float32)).astype(jnp.bfloat16)


def tables_of(groups, place_ref, inverse_ref):
    quarter, _ = place_of(place_ref, groups)
    low = quarter % 2
    sign = jnp.where(quarter // 2 == low, 1.0, -1.0)

    def part_table(which):
        start = pl.multiple_of((low ^ which) * 2 * PART, 2 * PART)
        return halves(both_rounds(inverse_ref[pl.ds(start, 2 * PART), :], sign))

    def full_table(mq):
        start = pl.multiple_of(4 * PART + (quarter ^ mq) * 2 * FULL, 2 * FULL)
        return halves(both_rounds(inverse_ref[pl.ds(start, 2 * FULL), :], sign))

    return part_table, full_table


def sum_lags(terms):
    lags = 0.0
    for picked, bins, table in terms:
        picked = unpack(picked, bins)
        for half in table:
            lags += jnp.dot(picked, half, preferred_element_type=jnp.float32)
    return lags


def part_lags_kernel(groups, place_ref, inverse_ref, part_0, part_2, part_3, part_1, lags_ref):
    samples = inverse_ref.shape[1]
    part_table, _ = tables_of(groups, place_ref, inverse_ref)
    near, other = part_table(0), part_table(1)
    lags = sum_lags(
        [
            (part_0[...], PART, near),
            (part_2[...], PART, near),
            (part_1[...], PART, other),
            (part_3[...], PART, other),
        ]
    )
    for step_round in range(2):
        lags_ref[step_round] = lags[:, step_round * samples : (step_round + 1) * samples]


def first_lags_kernel(groups, place_ref, inverse_ref, before_ref, full_0, *refs):
    full_1, (lags_ref, table_ref) = refs[:-2], refs[-2:]
    samples = inverse_ref.shape[1]
    _, full_table = tables_of(groups, place_ref, inverse_ref)
    full_1 = jnp.concatenate([ref[...] for ref in full_1])
    lags = sum_lags([(full_0[...], FULL, full_table(0)), (full_1, FULL, full_table(1))])
    for step_round in range(2):
        lags_ref[step_round] = (
            before_ref[step_round] + lags[:, step_round * samples : (step_round + 1) * samples]
        )
    for at in range(2):
        table_ref[at] = full_table(2 + at)[0]


def lag_kernel(first_ref, table_ref, *refs):
    picked_refs, (lags_ref, held_ref, sems) = refs[:-3], refs[-3:]
    samples = lags_ref.shape[2]
    runs = sems.shape[0]
    held = held_ref.shape[1] // runs
    picked = [unpack(ref[...], FULL) for ref in picked_refs]
    copies = []
    for run in range(runs):
        rows = slice(run * held, (run + 1) * held)
        more = 0.0
        for at, values in enumerate(picked):
            more += jnp.dot(values[rows], table_ref[at], preferred_element_type=jnp.float32)
        for step_round in range(2):
            held_ref[step_round, rows] = (
                first_ref[step_round, rows] + more[:, step_round * samples : (step_round + 1) * samples]
            )
        copies.append(
            pltpu.make_async_copy(held_ref.at[:, rows], lags_ref.at[:, rows], sems.at[run])
        )
        copies[-1].start()
    for copy in copies:
        copy.wait()


def on_device(windows, counts, pairs):
    comps, _, events, samples = windows.shape
    cells = lax.axis_size("cell")
    half, groups = cells // 2, cells // 4
    count = pairs.shape[2]
    inverse = jnp.asarray(inverse_table(samples, cells))
    place = lax.axis_index("cell").astype(jnp.int32).reshape(1)

    def swap(x, mask):
        return lax.ppermute(x, "cell", [(i, i ^ mask) for i in range(cells)])

    def shape(*dims, dtype=jnp.bfloat16):
        return jax.ShapeDtypeStruct(dims, dtype)

    vmem = pl.BlockSpec(memory_space=pltpu.VMEM)
    smem = pl.BlockSpec(memory_space=pltpu.SMEM)
    params = pltpu.CompilerParams(vmem_limit_bytes=VMEM_LIMIT)

    def cost(microseconds):
        return pl.CostEstimate(
            flops=int(microseconds * 1e9), bytes_accessed=2**20, transcendentals=0
        )

    windows = windows.reshape(comps, 2, groups, 2 * SLOTS, samples)
    near_windows, near_pairs = swap(windows, 1), swap(pairs, 1)
    part_rows, full_rows = comps * 2 * PART, comps * 2 * FULL
    part_spectra, full_spectra, table = pl.pallas_call(
        own_kernel,
        out_shape=[
            shape(groups, part_rows, LANES),
            shape(2 * groups, whole(full_rows, 16), LANES),
            shape(2 * PART + 4 * FULL, samples),
        ],
        in_specs=[smem, vmem],
        out_specs=[vmem] * 3,
        compiler_params=params,
        cost_estimate=cost(1),
        name="own_spectra",
    )(place, windows)
    listing = 2 * pairs.size // LANES
    pieces = pl.pallas_call(
        near_spectra_kernel,
        out_shape=[shape(2 * (part_rows + full_rows), LANES)] * groups
        + [shape(2 * full_rows + listing * (mg == 0), LANES) for mg in range(groups)],
        in_specs=[smem] + [vmem] * 6,
        out_specs=[vmem] * (2 * groups),
        compiler_params=params,
        cost_estimate=cost(1),
        name="near_spectra",
    )(place, pairs, near_pairs, table, part_spectra, full_spectra, near_windows)
    arrived = [pieces[0]] + [swap(pieces[m], 2 * m) for m in range(1, 2 * groups)]
    sides, far = arrived[:groups], arrived[groups:]

    part_packed = shape(packed_rows(count, PART), LANES)
    full_packed = shape(packed_rows(count, FULL), LANES)
    half_packed = shape(packed_rows(count, FULL) // 2, LANES)
    part_blocks = shape(2, 2, SLOTS * SLOTS * width(PART) // LANES, 2 * LANES)
    full_blocks = shape(2, 2, SLOTS * SLOTS * width(FULL) // LANES, 2 * LANES)
    part_flat = pl.pallas_call(
        part_kernel,
        out_shape=part_blocks,
        in_specs=[vmem] * groups,
        out_specs=vmem,
        scratch_shapes=[
            pltpu.VMEM((padded(groups * 2 * comps) * 2 * PART, LANES), jnp.float32),
            pltpu.VMEM((2 * SLOTS * whole(PART, 8), LANES), jnp.float32),
        ],
        compiler_params=params,
        cost_estimate=cost(0.001),
        name="part",
    )(*sides)
    part_0, part_1 = pl.pallas_call(
        functools.partial(near_kernel, PART, 1),
        out_shape=[part_packed, part_packed],
        in_specs=[smem, smem] + [vmem] * 3,
        out_specs=[vmem] * 2,
        compiler_params=params,
        cost_estimate=cost(0.001),
        name="part_near",
    )(place, counts, pairs, near_pairs, part_flat)
    part_2, part_3 = pl.pallas_call(
        functools.partial(far_kernel, PART),
        out_shape=[part_packed, part_packed],
        in_specs=[smem, smem, vmem, vmem],
        out_specs=[vmem, vmem],
        compiler_params=params,
        cost_estimate=cost(1),
        name="part_far",
    )(place, counts, far[0], part_flat)
    part_1 = swap(part_1, 1)
    sent, part_2, part_3 = part_2, swap(part_2, half), swap(part_3, half + 1)
    full_flat, full_2, full_3 = pl.pallas_call(
        functools.partial(full_kernel, groups),
        out_shape=[full_blocks, full_packed, full_packed],
        in_specs=[smem, smem, vmem]
        + [pl.BlockSpec(memory_space=pl.ANY)] * 2
        + [vmem] * (2 * groups),
        out_specs=[vmem] * 3,
        scratch_shapes=[
            pltpu.VMEM((padded(2 * groups * 2 * comps) * 2 * FULL, LANES), jnp.float32),
            pltpu.VMEM((2 * SLOTS * whole(FULL, 8), LANES), jnp.float32),
        ],
        compiler_params=params,
        cost_estimate=cost(10),
        name="full",
    )(place, counts, far[0], part_0, sent, *sides, *far)
    full_2, full_3 = swap(full_2, half), swap(full_3, half + 1)
    full_0, *full_1 = pl.pallas_call(
        functools.partial(near_kernel, FULL, 2),
        out_shape=[full_packed, half_packed, half_packed],
        in_specs=[smem, smem] + [vmem] * 3,
        out_specs=[vmem] * 3,
        compiler_params=params,
        cost_estimate=cost(0.5),
        name="full_near",
    )(place, counts, pairs, near_pairs, full_flat)
    full_1 = [swap(x, 1) for x in full_1]

    part_lags = pl.pallas_call(
        functools.partial(part_lags_kernel, groups),
        out_shape=shape(2, count, samples, dtype=jnp.float32),
        in_specs=[smem] + [vmem] * 5,
        out_specs=vmem,
        compiler_params=params,
        cost_estimate=cost(0.001),
        name="part_lags",
    )(place, inverse, part_0, part_2, part_3, part_1)
    first, tables = pl.pallas_call(
        functools.partial(first_lags_kernel, groups),
        out_shape=[
            shape(2, count, samples, dtype=jnp.float32),
            shape(2, 4 * FULL, 2 * samples),
        ],
        in_specs=[smem] + [vmem] * 5,
        out_specs=[vmem] * 2,
        compiler_params=params,
        cost_estimate=cost(0.001),
        name="first_lags",
    )(place, inverse, part_lags, full_0, *full_1)
    return pl.pallas_call(
        lag_kernel,
        out_shape=shape(2, count, samples, dtype=jnp.float32),
        in_specs=[vmem] * 4,
        out_specs=pl.BlockSpec(memory_space=pl.ANY),
        scratch_shapes=[
            pltpu.VMEM((2, count, samples), jnp.float32),
            pltpu.SemaphoreType.DMA((4,)),
        ],
        compiler_params=params,
        cost_estimate=cost(1),
        name="lags",
    )(first, tables, full_2, full_3)


def solution(mesh):
    in_specs = (P(None, "cell", "grp", None), P("grp"), P(None, None, ("grp", "cell")))
    out_specs = P(None, ("grp", "cell"), None)
    return jax.shard_map(
        on_device, mesh=mesh, in_specs=in_specs, out_specs=out_specs, check_vma=False
    )
```

```python
import functools
import math

import jax
import jax.numpy as jnp
import numpy as np
from jax import lax
from jax.experimental import pallas as pl
from jax.experimental.pallas import tpu as pltpu
from jax.sharding import PartitionSpec as P

EPSILON = 1e-06
COSINE = (
    0.9999999999993376,
    -4.934802200431432,
    4.058712123240781,
    -1.3352627346923478,
    0.23533044681677665,
    -0.02580633847975355,
    0.0019285963125396874,
    -0.00010362767792380447,
    3.734915399663344e-06,
)
SLOTS = 32
LANES = 4 * SLOTS
COMPS = 3
NT = (((1,), (1,)), ((), ()))
TN = (((0,), (0,)), ((), ()))
VMEM_LIMIT = 40 * 1024 * 1024

PART = 24
FULL = 20


def inverse_table(samples, stations):
    bins = samples // 2
    turn = np.arange(bins)[:, None] * np.arange(samples)[None, :] % samples
    angle = turn * (2.0 * math.pi / samples)
    weight = np.where(np.arange(bins) == 0, 1.0, 2.0)[:, None] / samples
    weight = weight * math.sqrt(samples / (3.0 * stations))
    real, imag = weight * np.cos(angle), -weight * np.sin(angle)
    runs = [(at, PART) for at in range(0, 2 * PART, PART)]
    runs += [(at, FULL) for at in range(2 * PART, bins, FULL)]
    rows = [part[at : at + run] for at, run in runs for part in (real, imag)]
    return np.concatenate(rows).astype(np.float32)


def forward_rows(start, count, samples):
    row = lax.broadcasted_iota(jnp.int32, (2 * count, samples), 0)
    sample = lax.broadcasted_iota(jnp.int32, (2 * count, samples), 1)
    imag = row >= count
    turn = (row + start - jnp.where(imag, count, 0)) * sample + jnp.where(imag, samples // 4, 0)
    turn &= samples - 1
    x = jnp.where(turn > samples // 2, turn - samples, turn).astype(jnp.float32) * (2.0 / samples)
    square = x * x
    value = jnp.full(square.shape, COSINE[-1], jnp.float32)
    for factor in COSINE[-2::-1]:
        value = value * square + factor
    return value


def place_of(place_ref, groups):
    position = place_ref[0]
    high, inner = position // (2 * groups), position % (2 * groups)
    return high * 2 + inner % 2, inner // 2


def listing_of(pairs_ref, lanes):
    ends = []
    for end in range(2):
        slots = pairs_ref[:, end, :].astype(jnp.float32)
        ends += [slots[:, at : at + lanes] for at in range(0, slots.shape[1], lanes)]
    return jnp.concatenate(ends)


def station_spectra(windows_ref, at, table):
    parts = []
    for comp in range(COMPS):
        low = windows_ref[comp, 0, at]
        high = windows_ref[comp, 1, at]
        parts += [low[:SLOTS], high[SLOTS:], low[SLOTS:], high[:SLOTS]]
    traces = jnp.concatenate(parts)
    energy = jnp.sum(jnp.square(traces.astype(jnp.float32)), axis=1, keepdims=True)
    raw = lax.dot_general(traces, table, NT, preferred_element_type=jnp.float32)
    spectra = (raw * lax.rsqrt(energy + EPSILON)).astype(jnp.bfloat16)
    turned = [spectra[comp * LANES : (comp + 1) * LANES].T for comp in range(COMPS)]
    return [lanes.astype(jnp.float32) for lanes in turned]


def rows_of(spectra, start, count):
    return jnp.concatenate([lanes[start : start + count] for lanes in spectra])


def own_kernel(place_ref, windows_ref, part_ref, full_ref, table_ref):
    groups, samples = windows_ref.shape[2], windows_ref.shape[4]
    quarter, group = place_of(place_ref, groups)
    table = [forward_rows((quarter % 2) * PART, PART, samples)]
    for far in range(2):
        table.append(forward_rows(2 * PART + (quarter ^ (2 * far)) * FULL, FULL, samples))
    table = jnp.concatenate(table).astype(jnp.bfloat16)
    table_ref[...] = table
    held = full_ref.shape[1] - COMPS * 2 * FULL
    for mg in range(groups):
        spectra = station_spectra(windows_ref, group ^ mg, table)
        part_ref[mg] = rows_of(spectra, 0, 2 * PART).astype(jnp.bfloat16)
        for far in range(2):
            rows = rows_of(spectra, 2 * PART + 2 * FULL * far, 2 * FULL)
            if held:
                rows = jnp.concatenate([rows, jnp.zeros((held, LANES), jnp.float32)])
            full_ref[far * groups + mg] = rows.astype(jnp.bfloat16)


def near_spectra_kernel(
    place_ref, own_pairs_ref, near_pairs_ref, table_ref, part_ref, full_ref, windows_ref, *piece_refs
):
    groups = windows_ref.shape[2]
    _, group = place_of(place_ref, groups)
    table = table_ref[...]
    part_rows, full_rows = COMPS * 2 * PART, COMPS * 2 * FULL
    piece_refs[groups][2 * full_rows :] = jnp.concatenate(
        [listing_of(own_pairs_ref, LANES), listing_of(near_pairs_ref, LANES)]
    ).astype(jnp.bfloat16)
    for mg in range(groups):
        spectra = station_spectra(windows_ref, group ^ mg, table)
        side = piece_refs[mg]
        side[:part_rows] = part_ref[mg]
        side[part_rows : 2 * part_rows] = rows_of(spectra, 0, 2 * PART).astype(jnp.bfloat16)
        for far, (piece, start) in enumerate(((side, 2 * part_rows), (piece_refs[groups + mg], 0))):
            own = full_ref[far * groups + mg].astype(jnp.float32)[:full_rows]
            near = rows_of(spectra, 2 * PART + 2 * FULL * far, 2 * FULL)
            piece[start : start + 2 * full_rows] = jnp.concatenate([own, near]).astype(jnp.bfloat16)


def width(bins):
    return 1 << (bins - 1).bit_length()


def packing(count, bins):
    used = 4 * bins
    spare = LANES - used
    runs, rest = used // math.gcd(used, LANES), spare // math.gcd(used, LANES)
    rows = count // (runs + rest)
    parts = []
    for run in range(runs):
        parts.append([(run * rows, 0, 0, used)])
        for extra in range(rest):
            start, end = max(run * spare, extra * used), min((run + 1) * spare, (extra + 1) * used)
            if start < end:
                lane = used + start - run * spare
                parts[-1].append(((runs + extra) * rows, lane, start - extra * used, end - extra * used))
    return rows, parts


def packed_rows(count, bins):
    rows, parts = packing(count, bins)
    return rows * len(parts)


def unpack(picked, bins):
    used = 4 * bins
    runs, rest = used // math.gcd(used, LANES), (LANES - used) // math.gcd(used, LANES)
    rows = picked.shape[0] // runs
    if not rest:
        return picked
    spare = jnp.concatenate([picked[run * rows : (run + 1) * rows, used:] for run in range(runs)], axis=1)
    return jnp.concatenate(
        [picked[:, :used]] + [spare[:, extra * used : (extra + 1) * used] for extra in range(rest)]
    )


def sides_of(place_ref, cells, mq):
    quarter, group = place_of(place_ref, cells // 4)
    own = quarter ^ mq
    high, low = own // 2, own % 2
    return high * (cells // 2) + group * 2 + low, high, low, ((high, high), (low, 1 - low))


def hots(place_ref, counts_ref, listed, rows, bins, mq):
    cells = counts_ref.shape[0]
    cell, high, low, _ = sides_of(place_ref, cells, mq)
    count = listed.shape[0] // 2
    runs = LANES // width(bins)
    run_bits, bin_bits = (n.bit_length() - 1 for n in (runs, width(bins)))
    first, second = listed[:count].astype(jnp.int32), listed[count:].astype(jnp.int32)
    far_counts = [counts_ref[cell ^ 1], counts_ref[cell ^ (cells // 2)]]
    odd = lax.broadcasted_iota(jnp.int32, (count, LANES), 0) & 1
    live = (first < counts_ref[cell]) & (second < jnp.where(odd == 1, far_counts[1], far_counts[0]))
    left, right = jnp.where(high == low, first, second), jnp.where(high == low, second, first)
    spot = jnp.where(live, (left >> run_bits) * SLOTS + right, -1)
    turned = (spot * runs + (left & (runs - 1))).T
    lane = lax.broadcasted_iota(jnp.int32, (LANES, LANES), 1)
    run = lane >> bin_bits
    found = []
    for step_round in range(2):
        hot, here = [], []
        for at in range(step_round, count, 2):
            both = jnp.broadcast_to(turned[:, at : at + 1], (LANES, LANES))
            here.append(jnp.where((both & (runs - 1)) == run, 1.0, 0.0).astype(jnp.bfloat16))
            offset = (both >> run_bits) - lane
            hot.append(
                jnp.concatenate(
                    [
                        jnp.where(offset == start, 1.0, 0.0).astype(jnp.bfloat16)
                        for start in range(0, rows, LANES)
                    ],
                    axis=1,
                )
            )
        found.append((jnp.concatenate(hot), jnp.concatenate(here)))
    return found


def folds_of(count, bins):
    return sorted({entry[1:] for entries in packing(count, bins)[1] for entry in entries})


def folds(count, bins):
    spread = lax.broadcasted_iota(jnp.int32, (4 * LANES, LANES), 0)
    kept = lax.broadcasted_iota(jnp.int32, (4 * LANES, LANES), 1)
    bin_of = spread & (width(bins) - 1)
    value = jnp.where(bin_of < bins, (spread >> (LANES.bit_length() - 1)) * bins + bin_of, -1)
    kinds = folds_of(count, bins)
    matrices = []
    for at, least, end in kinds:
        fold = (value >= least) & (value < end) & (kept == value + (at - least))
        matrices.append(jnp.where(fold, 1.0, 0.0).astype(jnp.bfloat16))
    return kinds, matrices


def picks(place_ref, cells, hot, kinds, matrices, flat_ref, bins, mq):
    _, _, _, sides = sides_of(place_ref, cells, mq)
    found = []
    for (rows, lanes), (own, far) in zip(hot, sides):
        wide = jnp.dot(rows, flat_ref[own, far], preferred_element_type=jnp.float32).astype(jnp.bfloat16)
        found += [wide[:, :LANES] * lanes, wide[:, LANES:] * lanes]
    found = jnp.concatenate(found, axis=1)
    held, parts = packing(found.shape[0], bins)
    picked = []
    for entries in parts:
        total = 0.0
        for start, *kind in entries:
            total += jnp.dot(
                found[start : start + held],
                matrices[kinds.index(tuple(kind))],
                preferred_element_type=jnp.float32,
            )
        picked.append(total.astype(jnp.bfloat16))
    return jnp.concatenate(picked)


def pick(place_ref, counts_ref, listed, flat_ref, bins, mq, *picked_refs):
    hot = hots(place_ref, counts_ref, listed, flat_ref.shape[2], bins, mq)
    kinds, matrices = folds(listed.shape[0] // 4 * LANES, bins)
    picked = picks(place_ref, counts_ref.shape[0], hot, kinds, matrices, flat_ref, bins, mq)
    each = picked.shape[0] // len(picked_refs)
    for at, ref in enumerate(picked_refs):
        ref[...] = picked[at * each : (at + 1) * each]


def whole(count, tile):
    return -(-count // tile) * tile


def padded(traces):
    return whole(traces, 16)


def add_cross(pieces, trace_ref, bins, sums_ref, before_ref=None):
    slots, rows = 2 * SLOTS, 2 * bins
    traces = trace_ref.shape[0] // rows
    start = 0
    for piece, at, size in pieces:
        trace_ref[start : start + size] = piece[at : at + size].astype(jnp.float32)
        start += size
    if start < traces * rows:
        trace_ref[start:] = jnp.zeros((traces * rows - start, LANES), jnp.float32)
    lower = lax.broadcasted_iota(jnp.int32, (traces, LANES), 1) < slots
    for k in range(bins):
        real = trace_ref[pl.ds(k, traces, stride=rows), :]
        imag = trace_ref[pl.ds(bins + k, traces, stride=rows), :]
        left = jnp.concatenate([real, imag]).astype(jnp.bfloat16)[:, :slots]
        right = jnp.concatenate(
            [
                jnp.where(lower, pltpu.roll(real, slots, 1), imag),
                jnp.where(lower, pltpu.roll(imag, slots, 1), -real),
            ]
        ).astype(jnp.bfloat16)
        cross = lax.dot_general(left, right, TN, preferred_element_type=jnp.float32)
        if before_ref is not None:
            cross += before_ref[k * slots : (k + 1) * slots]
        sums_ref[k * slots : (k + 1) * slots] = cross


def turn_blocks(cross_ref, bins, flat_ref):
    slots, runs = 2 * SLOTS, LANES // width(bins)
    held = cross_ref.shape[0] // slots
    if held > bins:
        cross_ref[bins * slots :] = jnp.zeros(((held - bins) * slots, LANES), jnp.float32)
    empty = jnp.zeros((width(bins) - held, LANES), jnp.float32)
    for own in range(2):
        for at in range(SLOTS // runs):
            block = []
            for i in range(runs):
                block.append(cross_ref[pl.ds(own * SLOTS + at * runs + i, held, stride=slots), :])
                block += [empty] * (held < width(bins))
            block = jnp.concatenate(block).astype(jnp.bfloat16).T
            for part in range(2):
                for far in range(2):
                    start = (part * 2 + far) * SLOTS
                    flat_ref[
                        own, far, at * SLOTS : (at + 1) * SLOTS, part * LANES : (part + 1) * LANES
                    ] = block[start : start + SLOTS]


def side_part(ref):
    return (ref, 0, 2 * COMPS * 2 * PART)


def side_full(ref):
    return (ref, 2 * COMPS * 2 * PART, 2 * COMPS * 2 * FULL)


def cross_full(ref):
    return (ref, 0, 2 * COMPS * 2 * FULL)


def part_kernel(*refs):
    piece_refs, (flat_ref, trace_ref, cross_ref) = refs[:-3], refs[-3:]
    add_cross([side_part(ref) for ref in piece_refs], trace_ref, PART, cross_ref)
    turn_blocks(cross_ref, PART, flat_ref)


def far_kernel(bins, place_ref, counts_ref, listed_ref, flat_ref, picked_0, picked_1):
    listed = listed_ref[cross_full(listed_ref)[2] :].astype(jnp.float32)
    listing = listed.shape[0] // 2
    pick(place_ref, counts_ref, listed[:listing], flat_ref, bins, 2, picked_0)
    pick(place_ref, counts_ref, listed[listing:], flat_ref, bins, 3, picked_1)


def full_kernel(sides, place_ref, counts_ref, listed_ref, after_0, after_1, *refs):
    piece_refs, (flat_ref, picked_0, picked_1, trace_ref, cross_ref) = refs[:-5], refs[-5:]
    pieces = [side_full(ref) for ref in piece_refs[:sides]] + [cross_full(ref) for ref in piece_refs[sides:]]
    add_cross(pieces, trace_ref, FULL, cross_ref)
    turn_blocks(cross_ref, FULL, flat_ref)
    listed = listed_ref[cross_full(listed_ref)[2] :].astype(jnp.float32)
    listing = listed.shape[0] // 2
    pick(place_ref, counts_ref, listed[:listing], flat_ref, FULL, 2, picked_0)
    pick(place_ref, counts_ref, listed[listing:], flat_ref, FULL, 3, picked_1)


def near_kernel(bins, sent, place_ref, counts_ref, own_pairs_ref, near_pairs_ref, flat_ref, *refs):
    picked_0, *picked_1 = refs[-1 - sent :]
    pick(place_ref, counts_ref, listing_of(near_pairs_ref, LANES), flat_ref, bins, 1, *picked_1)
    pick(place_ref, counts_ref, listing_of(own_pairs_ref, LANES), flat_ref, bins, 0, picked_0)


def both_rounds(rows, sign):
    row = lax.broadcasted_iota(jnp.int32, rows.shape, 0)
    rows = rows * jnp.where(row < rows.shape[0] // 2, 1.0, sign)
    empty = jnp.zeros_like(rows)
    return jnp.concatenate(
        [jnp.concatenate([rows, empty], axis=1), jnp.concatenate([empty, rows], axis=1)]
    )


def halves(table):
    high = table.astype(jnp.bfloat16)
    return high, (table - high.astype(jnp.float32)).astype(jnp.bfloat16)


def tables_of(groups, place_ref, inverse_ref):
    quarter, _ = place_of(place_ref, groups)
    low = quarter % 2
    sign = jnp.where(quarter // 2 == low, 1.0, -1.0)

    def part_table(which):
        start = pl.multiple_of((low ^ which) * 2 * PART, 2 * PART)
        return halves(both_rounds(inverse_ref[pl.ds(start, 2 * PART), :], sign))

    def full_table(mq):
        start = pl.multiple_of(4 * PART + (quarter ^ mq) * 2 * FULL, 2 * FULL)
        return halves(both_rounds(inverse_ref[pl.ds(start, 2 * FULL), :], sign))

    return part_table, full_table


def sum_lags(terms):
    lags = 0.0
    for picked, bins, table in terms:
        picked = unpack(picked, bins)
        for half in table:
            lags += jnp.dot(picked, half, preferred_element_type=jnp.float32)
    return lags


def part_lags_kernel(groups, place_ref, inverse_ref, part_0, part_2, part_3, part_1, lags_ref):
    samples = inverse_ref.shape[1]
    part_table, _ = tables_of(groups, place_ref, inverse_ref)
    near, other = part_table(0), part_table(1)
    lags = sum_lags(
        [
            (part_0[...], PART, near),
            (part_2[...], PART, near),
            (part_1[...], PART, other),
            (part_3[...], PART, other),
        ]
    )
    for step_round in range(2):
        lags_ref[step_round] = lags[:, step_round * samples : (step_round + 1) * samples]


def first_lags_kernel(groups, place_ref, inverse_ref, before_ref, full_0, *refs):
    full_1, (lags_ref, table_ref) = refs[:-2], refs[-2:]
    samples = inverse_ref.shape[1]
    _, full_table = tables_of(groups, place_ref, inverse_ref)
    full_1 = jnp.concatenate([ref[...] for ref in full_1])
    lags = sum_lags([(full_0[...], FULL, full_table(0)), (full_1, FULL, full_table(1))])
    for step_round in range(2):
        lags_ref[step_round] = (
            before_ref[step_round] + lags[:, step_round * samples : (step_round + 1) * samples]
        )
    for at in range(2):
        table_ref[at] = full_table(2 + at)[0]


def lag_kernel(first_ref, table_ref, *refs):
    picked_refs, (lags_ref, held_ref, sems) = refs[:-3], refs[-3:]
    samples = lags_ref.shape[2]
    runs = sems.shape[0]
    held = held_ref.shape[1] // runs
    picked = [unpack(ref[...], FULL) for ref in picked_refs]
    copies = []
    for run in range(runs):
        rows = slice(run * held, (run + 1) * held)
        more = 0.0
        for at, values in enumerate(picked):
            more += jnp.dot(values[rows], table_ref[at], preferred_element_type=jnp.float32)
        for step_round in range(2):
            held_ref[step_round, rows] = (
                first_ref[step_round, rows] + more[:, step_round * samples : (step_round + 1) * samples]
            )
        copies.append(
            pltpu.make_async_copy(held_ref.at[:, rows], lags_ref.at[:, rows], sems.at[run])
        )
        copies[-1].start()
    for copy in copies:
        copy.wait()


def on_device(windows, counts, pairs):
    comps, _, events, samples = windows.shape
    cells = lax.axis_size("cell")
    half, groups = cells // 2, cells // 4
    count = pairs.shape[2]
    inverse = jnp.asarray(inverse_table(samples, cells))
    place = lax.axis_index("cell").astype(jnp.int32).reshape(1)

    def swap(x, mask):
        return lax.ppermute(x, "cell", [(i, i ^ mask) for i in range(cells)])

    def shape(*dims, dtype=jnp.bfloat16):
        return jax.ShapeDtypeStruct(dims, dtype)

    vmem = pl.BlockSpec(memory_space=pltpu.VMEM)
    smem = pl.BlockSpec(memory_space=pltpu.SMEM)
    params = pltpu.CompilerParams(vmem_limit_bytes=VMEM_LIMIT)

    def cost(microseconds):
        return pl.CostEstimate(
            flops=int(microseconds * 1e9), bytes_accessed=2**20, transcendentals=0
        )

    windows = windows.reshape(comps, 2, groups, 2 * SLOTS, samples)
    near_windows, near_pairs = swap(windows, 1), swap(pairs, 1)
    part_rows, full_rows = comps * 2 * PART, comps * 2 * FULL
    part_spectra, full_spectra, table = pl.pallas_call(
        own_kernel,
        out_shape=[
            shape(groups, part_rows, LANES),
            shape(2 * groups, whole(full_rows, 16), LANES),
            shape(2 * PART + 4 * FULL, samples),
        ],
        in_specs=[smem, vmem],
        out_specs=[vmem] * 3,
        compiler_params=params,
        cost_estimate=cost(1),
        name="own_spectra",
    )(place, windows)
    listing = 2 * pairs.size // LANES
    pieces = pl.pallas_call(
        near_spectra_kernel,
        out_shape=[shape(2 * (part_rows + full_rows), LANES)] * groups
        + [shape(2 * full_rows + listing * (mg == 0), LANES) for mg in range(groups)],
        in_specs=[smem] + [vmem] * 6,
        out_specs=[vmem] * (2 * groups),
        compiler_params=params,
        cost_estimate=cost(1),
        name="near_spectra",
    )(place, pairs, near_pairs, table, part_spectra, full_spectra, near_windows)
    arrived = [pieces[0]] + [swap(pieces[m], 2 * m) for m in range(1, 2 * groups)]
    sides, far = arrived[:groups], arrived[groups:]

    part_packed = shape(packed_rows(count, PART), LANES)
    full_packed = shape(packed_rows(count, FULL), LANES)
    half_packed = shape(packed_rows(count, FULL) // 2, LANES)
    part_blocks = shape(2, 2, SLOTS * SLOTS * width(PART) // LANES, 2 * LANES)
    full_blocks = shape(2, 2, SLOTS * SLOTS * width(FULL) // LANES, 2 * LANES)
    part_flat = pl.pallas_call(
        part_kernel,
        out_shape=part_blocks,
        in_specs=[vmem] * groups,
        out_specs=vmem,
        scratch_shapes=[
            pltpu.VMEM((padded(groups * 2 * comps) * 2 * PART, LANES), jnp.float32),
            pltpu.VMEM((2 * SLOTS * whole(PART, 8), LANES), jnp.float32),
        ],
        compiler_params=params,
        cost_estimate=cost(0.001),
        name="part",
    )(*sides)
    part_0, part_1 = pl.pallas_call(
        functools.partial(near_kernel, PART, 1),
        out_shape=[part_packed, part_packed],
        in_specs=[smem, smem] + [vmem] * 3,
        out_specs=[vmem] * 2,
        compiler_params=params,
        cost_estimate=cost(0.001),
        name="part_near",
    )(place, counts, pairs, near_pairs, part_flat)
    part_2, part_3 = pl.pallas_call(
        functools.partial(far_kernel, PART),
        out_shape=[part_packed, part_packed],
        in_specs=[smem, smem, vmem, vmem],
        out_specs=[vmem, vmem],
        compiler_params=params,
        cost_estimate=cost(1),
        name="part_far",
    )(place, counts, far[0], part_flat)
    part_1 = swap(part_1, 1)
    sent, part_2, part_3 = part_2, swap(part_2, half), swap(part_3, half + 1)
    full_flat, full_2, full_3 = pl.pallas_call(
        functools.partial(full_kernel, groups),
        out_shape=[full_blocks, full_packed, full_packed],
        in_specs=[smem, smem, vmem]
        + [pl.BlockSpec(memory_space=pl.ANY)] * 2
        + [vmem] * (2 * groups),
        out_specs=[vmem] * 3,
        scratch_shapes=[
            pltpu.VMEM((padded(2 * groups * 2 * comps) * 2 * FULL, LANES), jnp.float32),
            pltpu.VMEM((2 * SLOTS * whole(FULL, 8), LANES), jnp.float32),
        ],
        compiler_params=params,
        cost_estimate=cost(10),
        name="full",
    )(place, counts, far[0], part_0, sent, *sides, *far)
    full_2, full_3 = swap(full_2, half), swap(full_3, half + 1)
    full_0, *full_1 = pl.pallas_call(
        functools.partial(near_kernel, FULL, 2),
        out_shape=[full_packed, half_packed, half_packed],
        in_specs=[smem, smem] + [vmem] * 3,
        out_specs=[vmem] * 3,
        compiler_params=params,
        cost_estimate=cost(0.5),
        name="full_near",
    )(place, counts, pairs, near_pairs, full_flat)
    full_1 = [swap(x, 1) for x in full_1]

    part_lags = pl.pallas_call(
        functools.partial(part_lags_kernel, groups),
        out_shape=shape(2, count, samples, dtype=jnp.float32),
        in_specs=[smem] + [vmem] * 5,
        out_specs=vmem,
        compiler_params=params,
        cost_estimate=cost(0.001),
        name="part_lags",
    )(place, inverse, part_0, part_2, part_3, part_1)
    first, tables = pl.pallas_call(
        functools.partial(first_lags_kernel, groups),
        out_shape=[
            shape(2, count, samples, dtype=jnp.float32),
            shape(2, 4 * FULL, 2 * samples),
        ],
        in_specs=[smem] + [vmem] * 5,
        out_specs=[vmem] * 2,
        compiler_params=params,
        cost_estimate=cost(0.001),
        name="first_lags",
    )(place, inverse, part_lags, full_0, *full_1)
    return pl.pallas_call(
        lag_kernel,
        out_shape=shape(2, count, samples, dtype=jnp.float32),
        in_specs=[vmem] * 4,
        out_specs=pl.BlockSpec(memory_space=pl.ANY),
        scratch_shapes=[
            pltpu.VMEM((2, count, samples), jnp.float32),
            pltpu.SemaphoreType.DMA((4,)),
        ],
        compiler_params=params,
        cost_estimate=cost(1),
        name="lags",
    )(first, tables, full_2, full_3)


def solution(mesh):
    in_specs = (P(None, "cell", "grp", None), P("grp"), P(None, None, ("grp", "cell")))
    out_specs = P(None, ("grp", "cell"), None)
    return jax.shard_map(
        on_device, mesh=mesh, in_specs=in_specs, out_specs=out_specs, check_vma=False
    )
```
